32 devices in a mesh: parts: 2 (over y), gx: 4 (over z), gy: 2 (over x), gz: 2 (over core).
Axes of the slice: x: 2, y: 2, z: 4, core: 2. Of those that a mesh axis runs over, the one named last changes fastest.
Arguments:
- adjoint_rhs: float32 [2, 20, 64, 1024], P(None, None, ('parts', 'gx'), ('gy', 'gz')), parts along dimension 2, may hold values from -40 to 40
- viscosity: float32 [20, 64, 1024], P(None, ('parts', 'gx'), ('gy', 'gz')), parts along dimension 1, may hold values from 0.03 to 0.3
- friction: float32 [64, 1024], P(('parts', 'gx'), ('gy', 'gz')), parts along dimension 0, may hold values from 0.05 to 1
- ice_mask: int32 [64, 1024], P(('parts', 'gx'), ('gy', 'gz')), parts along dimension 0, may hold values 0 or 1
- grounded: int32 [64, 1024], P(('parts', 'gx'), ('gy', 'gz')), parts along dimension 0, may hold values 0 or 1
- basal_velocity: float32 [2, 64, 1024], P(None, ('parts', 'gx'), ('gy', 'gz')), parts along dimension 1, may hold values from -6 to 6
Outputs:
- adjoint_solution: float32 [2, 20, 64, 1024], P(None, None, ('parts', 'gx'), ('gy', 'gz')), parts along dimension 2
- adjoint_residual: float32 [2, 20, 64, 1024], P(None, None, ('parts', 'gx'), ('gy', 'gz')), parts along dimension 2
- hessian_action: float32 [64, 1024], P(('parts', 'gx'), ('gy', 'gz')), parts along dimension 0
The draws below stay inside these ranges and needn't reach their ends.
There are 2 independent parts, one for each index of `parts`. The reference program is written for one: setup_inputs(seed, part) draws one part's arguments, and reference() takes and returns one part's arrays. A program takes and returns all parts, laid end to end along the dimension named above; each array names one. Nothing has to cross between parts.
All inputs are finite; a program needn't handle non-finite values. No bound on the sum of `ice_mask` or of `grounded` on one device may be relied on, other than what follows from the above.
Results may differ from the reference program's by a relative error of at most 0.00015.
Values sent between devices are 32-bit elements; how exact they have to be, the bound alone decides.
No kernel may reach another device: no remote copies, remote signals or barrier semaphores. Data moves between devices by JAX's collectives and lax.ppermute only.
A program may use at most 64 MiB of HBM per device.

```python
import math
import jax
import jax.numpy as jnp
from jax import lax

L = 20
ITERS = 2
NX = 32
NY = 1024


def draw_adjoint_rhs(key, part):
    key = jax.random.fold_in(key, 7)
    first = jax.random.fold_in(key, 0)
    along_rows = jnp.arange(NX, dtype=jnp.float32) / NX
    along_columns = jnp.arange(NY, dtype=jnp.float32) / NY
    values = jnp.clip(jax.random.normal(first, (2, L, NX, NY), jnp.float32), -4.0, 4.0)
    ramp = jnp.power(3.0, 0.5 * (along_rows - 0.5))[:, None] * jnp.power(3.0, 0.5 * (along_columns - 0.5))[None, :]
    return values * ramp


def place_ends(drawn, stream_key, smallest, largest):
    longest = drawn.shape.index(max(drawn.shape))
    spots = []
    for shift in (0, 1):
        where = [jax.random.randint(jax.random.fold_in(stream_key, axis), (), 0, length) for axis, length in enumerate(drawn.shape)]
        where[longest] = (where[longest] + shift) % drawn.shape[longest]
        spots.append(tuple(where))
    return drawn.at[spots[0]].set(smallest).at[spots[1]].set(largest)


def steps_of(stream_key, dims, shards, low, high):
    def one(dim, blocks):
        steps = jax.random.uniform(jax.random.fold_in(jax.random.fold_in(stream_key, 6), dim), (blocks,), jnp.float32, low / len(shards), high / len(shards))
        return jnp.repeat(jnp.exp(steps), dims[dim] // blocks).reshape((-1,) + (1,) * (len(dims) - dim - 1))

    level = one(*shards[0])
    for cut in shards[1:]:
        level = level * one(*cut)
    return level


def gaussian(key, extent, scale, reach, cuts=(), kind=jnp.bfloat16):
    gain = steps_of(key, extent, cuts, -0.22, 0.18) if cuts else 1.0
    values = jax.random.normal(key, extent, jnp.float32) * scale * gain
    return jnp.minimum(jnp.maximum(values, -reach), reach).astype(kind)


def setup_inputs(seed: int = 0, part: int = 0) -> dict:
    key_list = jax.random.split(jax.random.key(seed), 7)
    own_keys = jax.random.split(jax.random.fold_in(key_list[6], part), 7)
    return {
        "adjoint_rhs": draw_adjoint_rhs(jax.random.fold_in(jax.random.fold_in(key_list[6], part), 71), part),
        "viscosity": jnp.clip(jnp.exp(math.log(0.3) - 2.3025852 * jax.random.uniform(own_keys[1], (L, NX, NY), jnp.float32) ** steps_of(own_keys[1], (L, NX, NY), ((1, 4), (2, 4)), -0.2, 0.2)), 0.03, 0.3),
        "friction": jnp.clip(jnp.exp(math.log(1.0) - 2.9957323 * jax.random.uniform(own_keys[2], (NX, NY), jnp.float32) ** steps_of(own_keys[2], (NX, NY), ((0, 4), (1, 4)), -0.2, 0.2)), 0.05, 1.0),
        "ice_mask": place_ends((jax.random.randint(own_keys[3], (NX, NY), 0, 8) < 7).astype(jnp.int32), jax.random.fold_in(own_keys[3], 1), 0, 1),
        "grounded": place_ends((jax.random.randint(own_keys[4], (NX, NY), 0, 4) < 3).astype(jnp.int32), jax.random.fold_in(own_keys[4], 1), 0, 1),
        "basal_velocity": gaussian(own_keys[5], (2, NX, NY), 1.0, 6.0, ((1, 4), (2, 4)), jnp.float32),
    }


vertical_weight = 2.0

def neighbour(values, axis, offset):
    length = values.shape[axis]
    widths = [(0, 0)] * values.ndim
    widths[axis] = (1, 1)
    padded = jnp.pad(values, widths)
    return lax.slice_in_dim(padded, 1 + offset, 1 + offset + length, axis=axis)

def operate(vector_in, viscosity, ice_cover, basal_drag):
    masked = vector_in * ice_cover
    eta_next_row = 0.5 * (viscosity + neighbour(viscosity, 1, 1))
    eta_prev_row = 0.5 * (viscosity + neighbour(viscosity, 1, -1))
    eta_next_col = 0.5 * (viscosity + neighbour(viscosity, 2, 1))
    eta_prev_col = 0.5 * (viscosity + neighbour(viscosity, 2, -1))
    across_rows = eta_next_row * (masked - neighbour(masked, 2, 1)) + eta_prev_row * (masked - neighbour(masked, 2, -1))
    across_columns = eta_next_col * (masked - neighbour(masked, 3, 1)) + eta_prev_col * (masked - neighbour(masked, 3, -1))
    layer_eta = 0.5 * (viscosity[1:] + viscosity[:-1])
    layer_flux = layer_eta * (masked[:, 1:] - masked[:, :-1])
    vertical = jnp.pad(-layer_flux, ((0, 0), (0, 1), (0, 0), (0, 0))) + jnp.pad(layer_flux, ((0, 0), (1, 0), (0, 0), (0, 0)))
    bed_term = jnp.pad((basal_drag * masked[:, 0])[:, None], ((0, 0), (0, masked.shape[1] - 1), (0, 0), (0, 0)))
    cross_first = viscosity * (0.5 * (neighbour(masked[1], 2, 1) - neighbour(masked[1], 2, -1)))
    mixed_first = -(neighbour(cross_first, 1, 1) - neighbour(cross_first, 1, -1))
    cross_second = viscosity * (0.5 * (neighbour(masked[0], 1, 1) - neighbour(masked[0], 1, -1)))
    mixed_second = -(neighbour(cross_second, 2, 1) - neighbour(cross_second, 2, -1))
    row_gain = jnp.array([4.0, 1.0], jnp.float32).reshape(2, 1, 1, 1)
    column_gain = jnp.array([1.0, 4.0], jnp.float32).reshape(2, 1, 1, 1)
    operator_sum = row_gain * across_rows + column_gain * across_columns + vertical_weight * vertical + bed_term + jnp.stack([mixed_first, mixed_second])
    return ice_cover * operator_sum + (1.0 - ice_cover) * vector_in

def reference(adjoint_rhs, viscosity, friction, ice_mask, grounded, basal_velocity):
    ice_cover = ice_mask.astype(jnp.float32)
    basal_drag = friction * grounded.astype(jnp.float32)

    def apply_op(vector_in):
        return operate(vector_in, viscosity, ice_cover, basal_drag)
    right_side = adjoint_rhs
    quasi = right_side
    search = right_side
    applied = apply_op(search)
    carried = applied
    update = jnp.zeros_like(right_side)
    iterate = jnp.zeros_like(right_side)
    rho_now = jnp.sum(right_side * right_side)
    tau_now = jnp.sqrt(rho_now)
    theta_now = jnp.zeros((), jnp.float32)
    eta_now = jnp.zeros((), jnp.float32)
    alpha_step = jnp.ones((), jnp.float32)
    search_next = search
    for half_step in range(2 * ITERS):
        if half_step % 2 == 0:
            alpha_step = rho_now / jnp.sum(carried * right_side)
            search_next = search - alpha_step * carried
        quasi = quasi - alpha_step * applied
        update = search + theta_now * theta_now / alpha_step * eta_now * update
        theta_now = jnp.sqrt(jnp.sum(quasi * quasi)) / tau_now
        cosine = 1.0 / jnp.sqrt(1.0 + theta_now * theta_now)
        tau_now = tau_now * theta_now * cosine
        eta_now = cosine * cosine * alpha_step
        iterate = iterate + eta_now * update
        if half_step % 2 == 0:
            search = search_next
            applied = apply_op(search)
        elif half_step < 2 * ITERS - 1:
            rho_next = jnp.sum(quasi * right_side)
            beta_step = rho_next / rho_now
            search_new = quasi + beta_step * search
            applied_new = apply_op(search_new)
            carried = applied_new + beta_step * (applied + beta_step * carried)
            search = search_new
            applied = applied_new
            rho_now = rho_next
    residual_out = adjoint_rhs - apply_op(iterate)
    hessian_out = ice_cover * basal_drag * (basal_velocity[0] * iterate[0, 0] + basal_velocity[1] * iterate[1, 0])
    return (iterate, residual_out, hessian_out)
```

```python
import functools

import jax
import jax.numpy as jnp
from jax import lax
from jax.experimental import pallas as pl
from jax.experimental.pallas import tpu as pltpu
from jax.sharding import PartitionSpec as P

STEPS = 4
HALO = 4
ROWS = 8
LANES = 128
VMEM = pltpu.CompilerParams(vmem_limit_bytes=40 * 1024 * 1024)


def call(kernel, outs, scratch=()):
    return pl.pallas_call(
        kernel,
        out_shape=[jax.ShapeDtypeStruct(s, jnp.float32) for s in outs],
        scratch_shapes=[pltpu.VMEM(s, jnp.float32) for s in scratch],
        compiler_params=VMEM,
    )


def own_planes(rhs, eta, friction, ice, grounded):
    layers = eta.shape[0]
    cover = ice[...].astype(jnp.float32)
    drag = friction[...] * grounded[...].astype(jnp.float32)

    def plane(p):
        if p < 2 * layers:
            return rhs[p // layers, p % layers] * cover
        if p < 3 * layers:
            return eta[p - 2 * layers]
        return cover if p == 3 * layers else drag

    return plane


def pair_of(q, layers):
    if q < layers:
        return q, q + layers
    if q < layers + layers // 2:
        return q + layers, q + layers + layers // 2
    return 3 * layers, 3 * layers + 1


def pack_kernel(rhs, eta, friction, ice, grounded, to_left, to_right, to_prev, to_next):
    layers = eta.shape[0]
    plane = own_planes(rhs, eta, friction, ice, grounded)
    lane = lax.broadcasted_iota(jnp.int32, (ROWS, LANES), 1)
    row = lax.broadcasted_iota(jnp.int32, (ROWS, LANES), 0)
    upper = row < HALO
    width = to_prev.shape[0]
    left = [jnp.zeros((ROWS, LANES), jnp.float32) for _ in range(2)]
    right = [jnp.zeros((ROWS, LANES), jnp.float32) for _ in range(2)]
    for q in range(width // 2):
        first, second = pair_of(q, layers)
        x, y = plane(first), plane(second)
        for half in range(2):
            xs = x[:, half * LANES : (half + 1) * LANES]
            ys = y[:, half * LANES : (half + 1) * LANES]
            to_prev[2 * q + half] = jnp.where(upper, xs, pltpu.roll(ys, HALO, 0))
            to_next[2 * q + half] = jnp.where(upper, pltpu.roll(ys, HALO, 0), xs)
        for p, v in ((first, x), (second, y)):
            group, place = p // 32, HALO * (p % 32)
            mine = (lane >= place) & (lane < place + HALO)
            head, tail = v[:, :LANES], v[:, LANES:]
            shift = (place + HALO) % LANES
            left[group] = jnp.where(mine, pltpu.roll(head, place, 1) if place else head, left[group])
            right[group] = jnp.where(mine, pltpu.roll(tail, shift, 1) if shift else tail, right[group])
    for group in range(2):
        to_left[group] = left[group]
        to_right[group] = right[group]


def two_sum(a, b):
    s = a + b
    t = s - a
    return s, (a - (s - t)) + (b - t)


def join(x, y):
    s, e = two_sum(x[0], y[0])
    e = e + (x[1] + y[1])
    h = s + e
    return h, e - (h - s)


def times(scalar, x):
    def cut(v):
        t = v * 4097.0
        h = t - (t - v)
        return h, v - h

    p = scalar * x[0]
    sh, sl = cut(scalar)
    xh, xl = cut(x[0])
    e = ((sh * xh - p) + sh * xl + sl * xh) + sl * xl
    return p, e + scalar * x[1]


def power_kernel(
    rhs, eta, friction, ice, grounded, from_next, from_prev, columns,
    powers, moments,
    field_a, field_b, eta_row, eta_col, eta_half, eta_up, cover, drag,
):
    layers = eta.shape[0]
    plane = own_planes(rhs, eta, friction, ice, grounded)
    lane = lax.broadcasted_iota(jnp.int32, (ROWS, LANES), 1)
    row = lax.broadcasted_iota(jnp.int32, (ROWS, LANES), 0)
    upper = row < HALO
    strips = from_next.shape[0] - 4
    corner = [jnp.where(upper, from_next[strips + t], from_prev[strips + t]) for t in range(4)]
    beside = [columns[t] for t in range(4)]

    def side(tiles, p):
        group, place = p // 32, HALO * (p % 32)
        a, b = (LANES - place) % LANES, LANES - place - HALO
        right = pltpu.roll(tiles[group], a, 1) if a else tiles[group]
        left = pltpu.roll(tiles[2 + group], b, 1) if b else tiles[2 + group]
        return jnp.where(lane < HALO, right, jnp.where(lane >= LANES - HALO, left, 0.0))

    def fill(p, dst):
        dst[0:ROWS, 0 : 2 * LANES] = plane(p)
        dst[0:ROWS, 2 * LANES :] = side(beside, p)
        dst[ROWS:, 2 * LANES :] = side(corner, p)

    def target(p):
        if p < 2 * layers:
            return field_a.at[p // layers, p % layers]
        if p < 3 * layers:
            return eta_half.at[p - 2 * layers]
        return cover if p == 3 * layers else drag

    for q in range(strips // 2):
        first, second = pair_of(q, layers)
        for half in range(2):
            below, above = from_next[2 * q + half], from_prev[2 * q + half]
            cut = slice(half * LANES, (half + 1) * LANES)
            target(first)[ROWS:, cut] = jnp.where(upper, below, above)
            target(second)[ROWS:, cut] = pltpu.roll(jnp.where(upper, above, below), HALO, 0)
        fill(first, target(first))
        fill(second, target(second))

    def row_next(v):
        return pltpu.roll(v, 2 * ROWS - 1, 0)

    def row_prev(v):
        return pltpu.roll(v, 1, 0)

    def col_next(v):
        return pltpu.roll(v, 3 * LANES - 1, 1)

    def col_prev(v):
        return pltpu.roll(v, 1, 1)

    for k in range(layers):
        e = eta_half[k]
        eta_row[k] = 2.0 * (e + row_next(e))
        eta_col[k] = 0.5 * (e + col_next(e))
        eta_up[k] = e + eta_half[k + 1] if k + 1 < layers else jnp.zeros_like(e)
        if k:
            eta_half[k - 1] = 0.5 * eta_half[k - 1]
    eta_half[layers - 1] = 0.5 * eta_half[layers - 1]

    own = (slice(0, ROWS), slice(0, 2 * LANES))
    bare = 1.0 - ice[...].astype(jnp.float32)

    def apply(t, src, dst):
        def layer(k, carry):
            below0, below1, odd, even = carry
            g0, g1 = src[0, k], src[1, k]
            after = jnp.minimum(k + 1, layers - 1)
            e_row, e_col, e_half, e_up = eta_row[k], eta_col[k], eta_half[k], eta_up[k]
            up0 = e_up * (g0 - src[0, after])
            up1 = e_up * (g1 - src[1, after])
            g0n, g1n = row_next(g0), col_next(g1)
            f = e_half * (g1n - col_prev(g1))
            h = e_half * (g0n - row_prev(g0))
            flux = e_row * (g0 - g0n)
            out0 = flux - row_next(f) - row_prev(flux - f)
            flux = e_col * (g0 - col_next(g0))
            out0 = out0 + (flux - col_prev(flux)) + (up0 - below0)
            flux = (4.0 * e_col) * (g1 - g1n)
            out1 = flux - col_next(h) - col_prev(flux - h)
            flux = (0.25 * e_row) * (g1 - row_next(g1))
            out1 = out1 + (flux - row_prev(flux)) + (up1 - below1)
            m = cover[...]
            out0, out1 = m * out0, m * out1
            if t < STEPS:
                dst[0, k], dst[1, k] = out0, out1
            for c, g, out in ((0, g0, out0), (1, g1, out1)):
                outside = rhs[c, k] * bare
                before = g[own] + outside
                now = out[own] + outside
                powers[t - 1, c, k] = now
                odd = odd + before * now
                even = even + now * now
            return up0, up1, odd, even

        zero = jnp.zeros((ROWS, 2 * LANES), jnp.float32)
        d = drag[...]
        start = (-d * src[0, 0], -d * src[1, 0], zero, zero)
        return lax.fori_loop(0, layers, layer, start)[2:]

    square = jnp.zeros((ROWS, 2 * LANES), jnp.float32)
    for c in range(2):
        for k in range(layers):
            square = square + rhs[c, k] * rhs[c, k]
    sums = [square]
    src, dst = field_a, field_b
    for t in range(1, STEPS + 1):
        sums.extend(apply(t, src, dst))
        src, dst = dst, src

    tall = lax.broadcasted_iota(jnp.int32, (2 * ROWS, LANES), 0)
    high = jnp.zeros((2 * ROWS, LANES), jnp.float32)
    low = jnp.zeros((2 * ROWS, LANES), jnp.float32)
    for j, total in enumerate(sums):
        pair = two_sum(total[:, :LANES], total[:, LANES:])
        for step in (4, 2, 1):
            pair = join(pair, tuple(pltpu.roll(v, step, 0) for v in pair))
        high = jnp.where(tall == j, jnp.concatenate([pair[0]] * 2, 0), high)
        low = jnp.where(tall == j, jnp.concatenate([pair[1]] * 2, 0), low)
    moments[0] = high
    moments[1] = low


def add_kernel(*refs):
    *ins, out = refs
    total = (ins[0][0], ins[0][1])
    for x in ins[1:]:
        total = join(total, (x[0], x[1]))
    out[0], out[1] = total


def solve(total):
    for step in (64, 32, 16, 8, 4, 2, 1):
        total = join(total, tuple(pltpu.roll(v, step, 1) for v in total))

    def spread(v, j):
        return jnp.broadcast_to(v[j : j + 1], (ROWS, LANES))

    centre = spread(total[0], 1) / spread(total[0], 0)
    wide = jnp.concatenate([centre, centre], 0)
    mu = [spread(total[0], 0)]
    for _ in range(2 * STEPS):
        step = times(wide, total)
        total = join(tuple(pltpu.roll(v, 2 * ROWS - 1, 0) for v in total), (-step[0], -step[1]))
        mu.append(spread(total[0], 0))

    def plus(a, b):
        n = max(len(a), len(b))
        return [a[i] + b[i] if i < min(len(a), len(b)) else (a[i] if i < len(a) else b[i]) for i in range(n)]

    def scaled(s, a):
        return [s * x for x in a]

    def operator(a):
        return plus([centre * x for x in a], [jnp.zeros_like(centre)] + a)

    def dot(a, b):
        square = [None] * (len(a) + len(b) - 1)
        for i, x in enumerate(a):
            for j, y in enumerate(b):
                z = x * y
                square[i + j] = z if square[i + j] is None else square[i + j] + z
        value = square[0] * mu[0]
        for n in range(1, len(square)):
            value = value + square[n] * mu[n]
        return value

    one = jnp.ones_like(centre)
    right = [one]
    quasi, search, update, iterate = right, right, [], []
    applied = operator(search)
    carried = applied
    rho = mu[0]
    tau_sq = rho
    alpha = theta_sq = eta = None
    for half in range(STEPS):
        if half % 2 == 0:
            alpha = rho / dot(carried, right)
            search_next = plus(search, scaled(-alpha, carried))
        quasi = plus(quasi, scaled(-alpha, applied))
        if half:
            update = plus(search, scaled(theta_sq / alpha * eta, update))
        else:
            update = search
        theta_sq = dot(quasi, quasi) / tau_sq
        cosine_sq = 1.0 / (1.0 + theta_sq)
        tau_sq = tau_sq * theta_sq * cosine_sq
        eta = cosine_sq * alpha
        iterate = plus(iterate, scaled(eta, update))
        if half % 2 == 0:
            search = search_next
            applied = operator(search)
        elif half < STEPS - 1:
            rho_next = dot(quasi, right)
            beta = rho_next / rho
            search = plus(quasi, scaled(beta, search))
            applied_next = operator(search)
            carried = plus(applied_next, scaled(beta, plus(applied, scaled(beta, carried))))
            applied, rho = applied_next, rho_next
    powers = [iterate[-1]]
    for c in iterate[-2::-1]:
        powers = plus([c] + powers, scaled(-centre, powers))
    return powers


def final_kernel(rhs, powers, friction, ice, grounded, speed, *rest):
    *parts, iterate, residual, hessian = rest
    layers = rhs.shape[1]
    total = (parts[0][0], parts[0][1])
    for x in parts[1:]:
        total = join(total, (x[0], x[1]))
    factors = [jnp.concatenate([c, c], 1) for c in solve(total)]
    for c in range(2):
        for k in range(layers):
            r = rhs[c, k]
            vectors = [r] + [powers[t, c, k] for t in range(STEPS)]
            x = factors[0] * vectors[0]
            y = factors[0] * vectors[1]
            for t in range(1, STEPS):
                x = x + factors[t] * vectors[t]
                y = y + factors[t] * vectors[t + 1]
            iterate[c, k] = x
            residual[c, k] = r - y
    weight = ice[...].astype(jnp.float32) * (friction[...] * grounded[...].astype(jnp.float32))
    hessian[...] = weight * (speed[0] * iterate[0, 0] + speed[1] * iterate[1, 0])


def shifted(x, axis, step):
    count = lax.axis_size(axis)
    pairs = [(i, i + step) for i in range(count) if 0 <= i + step < count]
    return lax.ppermute(x, axis, pairs)


def exchange(x, axis):
    count = lax.axis_size(axis)
    stride = 1
    rounds = []
    while stride < count:
        size = 4 if (count // stride) % 4 == 0 else 2
        rounds.append((stride, size))
        stride *= size
    for at, (stride, size) in enumerate(rounds):
        parts = [x]
        for turn in range(1, size):
            pairs = []
            for i in range(count):
                place = (i // stride) % size
                pairs.append((i, i + ((place + turn) % size - place) * stride))
            parts.append(lax.ppermute(x, axis, pairs))
        if at == len(rounds) - 1:
            return parts
        x = call(add_kernel, [x.shape])(*parts)[0]
    return [x]


def body(adjoint_rhs, viscosity, friction, ice_mask, grounded, basal_velocity):
    layers = viscosity.shape[0]
    fields = (adjoint_rhs, viscosity, friction, ice_mask, grounded)
    tile = (ROWS, LANES)
    strips = (2 * (layers + layers // 2 + 1),) + tile
    to_left, to_right, to_prev, to_next = call(pack_kernel, [(2,) + tile, (2,) + tile, strips, strips])(*fields)
    columns = jnp.concatenate(
        [shifted(to_left, ("gy", "gz"), -1), shifted(to_right, ("gy", "gz"), 1)], axis=0
    )
    from_next = shifted(jnp.concatenate([to_prev, columns], axis=0), "gx", -1)
    from_prev = shifted(jnp.concatenate([to_next, columns], axis=0), "gx", 1)
    block = (layers, 2 * ROWS, 3 * LANES)
    powers, sums = call(
        power_kernel,
        [(STEPS,) + adjoint_rhs.shape, (2, 2 * ROWS, LANES)],
        [(2,) + block] * 2 + [block] * 4 + [block[1:]] * 2,
    )(*fields, from_next, from_prev, columns)
    parts = exchange(sums, ("gy", "gz"))
    if len(parts) > 1:
        sums = call(add_kernel, [sums.shape])(*parts)[0]
    parts = exchange(sums, "gx")
    return tuple(
        call(final_kernel, [adjoint_rhs.shape, adjoint_rhs.shape, friction.shape])(
            adjoint_rhs, powers, friction, ice_mask, grounded, basal_velocity, *parts
        )
    )


def solution(mesh):
    in_specs = (
        P(None, None, ("parts", "gx"), ("gy", "gz")),
        P(None, ("parts", "gx"), ("gy", "gz")),
        P(("parts", "gx"), ("gy", "gz")),
        P(("parts", "gx"), ("gy", "gz")),
        P(("parts", "gx"), ("gy", "gz")),
        P(None, ("parts", "gx"), ("gy", "gz")),
    )
    out_specs = (
        P(None, None, ("parts", "gx"), ("gy", "gz")),
        P(None, None, ("parts", "gx"), ("gy", "gz")),
        P(("parts", "gx"), ("gy", "gz")),
    )
    return jax.shard_map(body, mesh=mesh, in_specs=in_specs, out_specs=out_specs, check_vma=False)
```

```python
import functools

import jax
import jax.numpy as jnp
from jax import lax
from jax.experimental import pallas as pl
from jax.experimental.pallas import tpu as pltpu
from jax.sharding import PartitionSpec as P

STEPS = 4
HALO = 4
ROWS = 8
LANES = 128
UNROLL = 4
VMEM = pltpu.CompilerParams(vmem_limit_bytes=40 * 1024 * 1024)


def call(kernel, outs, scratch=(), **more):
    return pl.pallas_call(
        kernel,
        out_shape=[jax.ShapeDtypeStruct(s, jnp.float32) if isinstance(s, tuple) else s for s in outs],
        scratch_shapes=[pltpu.VMEM(s, jnp.float32) if isinstance(s, tuple) else s for s in scratch],
        compiler_params=VMEM,
        **more,
    )


def own_planes(rhs, eta, friction, ice, grounded):
    layers = eta.shape[0]
    cover = ice[...].astype(jnp.float32)
    drag = friction[...] * grounded[...].astype(jnp.float32)

    def plane(p):
        if p < 2 * layers:
            return rhs[p // layers, p % layers] * cover
        if p < 3 * layers:
            return eta[p - 2 * layers]
        return cover if p == 3 * layers else drag

    return plane


def pair_of(q, layers):
    if q < layers:
        return q, q + layers
    if q < layers + layers // 2:
        return q + layers, q + layers + layers // 2
    return 3 * layers, 3 * layers + 1


def pack_kernel(*refs):
    sources, held, (to_left, to_right, to_prev, to_next, arrived) = refs[:6], refs[6:12], refs[12:]
    copies = [pltpu.make_async_copy(a, b, arrived.at[i]) for i, (a, b) in enumerate(zip(sources, held))]
    for copy in copies:
        copy.start()
    for copy in copies:
        copy.wait()
    rhs, eta, friction, ice, grounded, _ = held
    layers = eta.shape[0]
    plane = own_planes(rhs, eta, friction, ice, grounded)
    lane = lax.broadcasted_iota(jnp.int32, (ROWS, LANES), 1)
    row = lax.broadcasted_iota(jnp.int32, (ROWS, LANES), 0)
    upper = row < HALO
    width = to_prev.shape[0]
    left = [jnp.zeros((ROWS, LANES), jnp.float32) for _ in range(2)]
    right = [jnp.zeros((ROWS, LANES), jnp.float32) for _ in range(2)]
    for q in range(width // 2):
        first, second = pair_of(q, layers)
        x, y = plane(first), plane(second)
        for half in range(2):
            xs = x[:, half * LANES : (half + 1) * LANES]
            ys = y[:, half * LANES : (half + 1) * LANES]
            to_prev[2 * q + half] = jnp.where(upper, xs, pltpu.roll(ys, HALO, 0))
            to_next[2 * q + half] = jnp.where(upper, pltpu.roll(ys, HALO, 0), xs)
        for p, v in ((first, x), (second, y)):
            group, place = p // 32, HALO * (p % 32)
            mine = (lane >= place) & (lane < place + HALO)
            head, tail = v[:, :LANES], v[:, LANES:]
            shift = (place + HALO) % LANES
            left[group] = jnp.where(mine, pltpu.roll(head, place, 1) if place else head, left[group])
            right[group] = jnp.where(mine, pltpu.roll(tail, shift, 1) if shift else tail, right[group])
    for group in range(2):
        to_left[group] = left[group]
        to_right[group] = right[group]


def two_sum(a, b):
    s = a + b
    t = s - a
    return s, (a - (s - t)) + (b - t)


def join(x, y):
    s, e = two_sum(x[0], y[0])
    e = e + (x[1] + y[1])
    h = s + e
    return h, e - (h - s)


def times(scalar, x):
    def cut(v):
        t = v * 4097.0
        h = t - (t - v)
        return h, v - h

    p = scalar * x[0]
    sh, sl = cut(scalar)
    xh, xl = cut(x[0])
    e = ((sh * xh - p) + sh * xl + sl * xh) + sl * xl
    return p, e + scalar * x[1]


def power_kernel(
    rhs, eta, friction, ice, grounded, from_next, from_prev, columns, next_columns, prev_columns,
    powers, moments,
    field_a, field_b, eta_row, eta_col, eta_half, eta_up, cover, drag,
):
    layers = eta.shape[0]
    plane = own_planes(rhs, eta, friction, ice, grounded)
    lane = lax.broadcasted_iota(jnp.int32, (ROWS, LANES), 1)
    row = lax.broadcasted_iota(jnp.int32, (ROWS, LANES), 0)
    upper = row < HALO
    strips = from_next.shape[0]
    corner = [jnp.where(upper, next_columns[t], prev_columns[t]) for t in range(4)]
    beside = [columns[t] for t in range(4)]

    def side(tiles, p):
        group, place = p // 32, HALO * (p % 32)
        a, b = (LANES - place) % LANES, LANES - place - HALO
        right = pltpu.roll(tiles[group], a, 1) if a else tiles[group]
        left = pltpu.roll(tiles[2 + group], b, 1) if b else tiles[2 + group]
        return jnp.where(lane < HALO, right, jnp.where(lane >= LANES - HALO, left, 0.0))

    def fill(p, dst):
        dst[0:ROWS, 0 : 2 * LANES] = plane(p)
        dst[0:ROWS, 2 * LANES :] = side(beside, p)
        dst[ROWS:, 2 * LANES :] = side(corner, p)

    def target(p):
        if p < 2 * layers:
            return field_a.at[p // layers, p % layers]
        if p < 3 * layers:
            return eta_half.at[p - 2 * layers]
        return cover if p == 3 * layers else drag

    for q in range(strips // 2):
        first, second = pair_of(q, layers)
        for half in range(2):
            below, above = from_next[2 * q + half], from_prev[2 * q + half]
            cut = slice(half * LANES, (half + 1) * LANES)
            target(first)[ROWS:, cut] = jnp.where(upper, below, above)
            target(second)[ROWS:, cut] = pltpu.roll(jnp.where(upper, above, below), HALO, 0)
        fill(first, target(first))
        fill(second, target(second))

    def row_next(v):
        return pltpu.roll(v, 2 * ROWS - 1, 0)

    def row_prev(v):
        return pltpu.roll(v, 1, 0)

    def col_next(v):
        return pltpu.roll(v, 3 * LANES - 1, 1)

    def col_prev(v):
        return pltpu.roll(v, 1, 1)

    for k in range(layers):
        e = eta_half[k]
        eta_row[k] = 2.0 * (e + row_next(e))
        eta_col[k] = 0.5 * (e + col_next(e))
        eta_up[k] = e + eta_half[k + 1] if k + 1 < layers else jnp.zeros_like(e)
        if k:
            eta_half[k - 1] = 0.5 * eta_half[k - 1]
    eta_half[layers - 1] = 0.5 * eta_half[layers - 1]

    own = (slice(0, ROWS), slice(0, 2 * LANES))
    bare = 1.0 - ice[...].astype(jnp.float32)

    def apply(t, src, dst):
        def layer(k, carry):
            below0, below1, odd, even = carry
            g0, g1 = src[0, k], src[1, k]
            after = jnp.minimum(k + 1, layers - 1)
            e_row, e_col, e_half, e_up = eta_row[k], eta_col[k], eta_half[k], eta_up[k]
            up0 = e_up * (g0 - src[0, after])
            up1 = e_up * (g1 - src[1, after])
            g0n, g1n = row_next(g0), col_next(g1)
            f = e_half * (g1n - col_prev(g1))
            h = e_half * (g0n - row_prev(g0))
            flux = e_row * (g0 - g0n)
            out0 = flux - row_next(f) - row_prev(flux - f)
            flux = e_col * (g0 - col_next(g0))
            out0 = out0 + (flux - col_prev(flux)) + (up0 - below0)
            flux = (4.0 * e_col) * (g1 - g1n)
            out1 = flux - col_next(h) - col_prev(flux - h)
            flux = (0.25 * e_row) * (g1 - row_next(g1))
            out1 = out1 + (flux - row_prev(flux)) + (up1 - below1)
            m = cover[...]
            out0, out1 = m * out0, m * out1
            if t < STEPS:
                dst[0, k], dst[1, k] = out0, out1
            for c, g, out in ((0, g0, out0), (1, g1, out1)):
                outside = rhs[c, k] * bare
                before = g[own] + outside
                now = out[own] + outside
                powers[t - 1, c, k] = now
                odd = odd + before * now
                even = even + now * now
            return up0, up1, odd, even

        zero = jnp.zeros((ROWS, 2 * LANES), jnp.float32)
        d = drag[...]
        start = (-d * src[0, 0], -d * src[1, 0], zero, zero)

        def block(b, carry):
            for i in range(UNROLL):
                carry = layer(b * UNROLL + i, carry)
            return carry

        return lax.fori_loop(0, layers // UNROLL, block, start)[2:]

    square = jnp.zeros((ROWS, 2 * LANES), jnp.float32)
    for c in range(2):
        for k in range(layers):
            square = square + rhs[c, k] * rhs[c, k]
    sums = [square]
    src, dst = field_a, field_b
    for t in range(1, STEPS + 1):
        sums.extend(apply(t, src, dst))
        src, dst = dst, src

    tall = lax.broadcasted_iota(jnp.int32, (2 * ROWS, LANES), 0)
    high = jnp.zeros((2 * ROWS, LANES), jnp.float32)
    low = jnp.zeros((2 * ROWS, LANES), jnp.float32)
    for j, total in enumerate(sums):
        pair = two_sum(total[:, :LANES], total[:, LANES:])
        for step in (4, 2, 1):
            pair = join(pair, tuple(pltpu.roll(v, step, 0) for v in pair))
        high = jnp.where(tall == j, jnp.concatenate([pair[0]] * 2, 0), high)
        low = jnp.where(tall == j, jnp.concatenate([pair[1]] * 2, 0), low)
    moments[0] = high
    moments[1] = low


def add_kernel(*refs):
    *ins, out = refs
    total = (ins[0][0], ins[0][1])
    for x in ins[1:]:
        total = join(total, (x[0], x[1]))
    out[0], out[1] = total


def solve(total):
    for step in (64, 32, 16, 8, 4, 2, 1):
        total = join(total, tuple(pltpu.roll(v, step, 1) for v in total))

    def spread(v, j):
        return jnp.broadcast_to(v[j : j + 1], (ROWS, LANES))

    centre = spread(total[0], 1) / spread(total[0], 0)
    wide = jnp.concatenate([centre, centre], 0)
    mu = [spread(total[0], 0)]
    for _ in range(2 * STEPS):
        step = times(wide, total)
        total = join(tuple(pltpu.roll(v, 2 * ROWS - 1, 0) for v in total), (-step[0], -step[1]))
        mu.append(spread(total[0], 0))

    def plus(a, b):
        n = max(len(a), len(b))
        return [a[i] + b[i] if i < min(len(a), len(b)) else (a[i] if i < len(a) else b[i]) for i in range(n)]

    def scaled(s, a):
        return [s * x for x in a]

    def operator(a):
        return plus([centre * x for x in a], [jnp.zeros_like(centre)] + a)

    def dot(a, b):
        square = [None] * (len(a) + len(b) - 1)
        for i, x in enumerate(a):
            for j, y in enumerate(b):
                z = x * y
                square[i + j] = z if square[i + j] is None else square[i + j] + z
        value = square[0] * mu[0]
        for n in range(1, len(square)):
            value = value + square[n] * mu[n]
        return value

    one = jnp.ones_like(centre)
    right = [one]
    quasi, search, update, iterate = right, right, [], []
    applied = operator(search)
    carried = applied
    rho = mu[0]
    tau_sq = rho
    alpha = theta_sq = eta = None
    for half in range(STEPS):
        if half % 2 == 0:
            alpha = rho / dot(carried, right)
            search_next = plus(search, scaled(-alpha, carried))
        quasi = plus(quasi, scaled(-alpha, applied))
        if half:
            update = plus(search, scaled(theta_sq / alpha * eta, update))
        else:
            update = search
        theta_sq = dot(quasi, quasi) / tau_sq
        cosine_sq = 1.0 / (1.0 + theta_sq)
        tau_sq = tau_sq * theta_sq * cosine_sq
        eta = cosine_sq * alpha
        iterate = plus(iterate, scaled(eta, update))
        if half % 2 == 0:
            search = search_next
            applied = operator(search)
        elif half < STEPS - 1:
            rho_next = dot(quasi, right)
            beta = rho_next / rho
            search = plus(quasi, scaled(beta, search))
            applied_next = operator(search)
            carried = plus(applied_next, scaled(beta, plus(applied, scaled(beta, carried))))
            applied, rho = applied_next, rho_next
    powers = [iterate[-1]]
    for c in iterate[-2::-1]:
        powers = plus([c] + powers, scaled(-centre, powers))
    return powers


def final_kernel(rhs, powers, friction, ice, grounded, speed, *rest):
    *parts, iterate, residual, hessian = rest
    layers = rhs.shape[1]
    total = (parts[0][0], parts[0][1])
    for x in parts[1:]:
        total = join(total, (x[0], x[1]))
    factors = [jnp.concatenate([c, c], 1) for c in solve(total)]
    for c in range(2):
        for k in range(layers):
            r = rhs[c, k]
            vectors = [r] + [powers[t, c, k] for t in range(STEPS)]
            x = factors[0] * vectors[0]
            y = factors[0] * vectors[1]
            for t in range(1, STEPS):
                x = x + factors[t] * vectors[t]
                y = y + factors[t] * vectors[t + 1]
            iterate[c, k] = x
            residual[c, k] = r - y
    weight = ice[...].astype(jnp.float32) * (friction[...] * grounded[...].astype(jnp.float32))
    hessian[...] = weight * (speed[0] * iterate[0, 0] + speed[1] * iterate[1, 0])


def shifted(x, axis, step):
    count = lax.axis_size(axis)
    pairs = [(i, i + step) for i in range(count) if 0 <= i + step < count]
    return lax.ppermute(x, axis, pairs)


def exchange(x, axis):
    count = lax.axis_size(axis)
    stride = 1
    rounds = []
    while stride < count:
        size = 4 if (count // stride) % 4 == 0 else 2
        rounds.append((stride, size))
        stride *= size
    for at, (stride, size) in enumerate(rounds):
        parts = [x]
        for turn in range(1, size):
            pairs = []
            for i in range(count):
                place = (i // stride) % size
                pairs.append((i, i + ((place + turn) % size - place) * stride))
            parts.append(lax.ppermute(x, axis, pairs))
        if at == len(rounds) - 1:
            return parts
        x = call(add_kernel, [x.shape])(*parts)[0]
    return [x]


def body(adjoint_rhs, viscosity, friction, ice_mask, grounded, basal_velocity):
    layers = viscosity.shape[0]
    inputs = (adjoint_rhs, viscosity, friction, ice_mask, grounded, basal_velocity)
    tile = (ROWS, LANES)
    strips = (2 * (layers + layers // 2 + 1),) + tile
    *held, to_left, to_right, to_prev, to_next = call(
        pack_kernel,
        [jax.ShapeDtypeStruct(x.shape, x.dtype) for x in inputs] + [(2,) + tile, (2,) + tile, strips, strips],
        [pltpu.SemaphoreType.DMA((len(inputs),))],
        in_specs=[pl.BlockSpec(memory_space=pltpu.HBM)] * len(inputs),
    )(*inputs)
    rhs, eta, friction, ice_mask, grounded, speed = held
    from_next = shifted(to_prev, "gx", -1)
    from_prev = shifted(to_next, "gx", 1)
    columns = jnp.concatenate(
        [shifted(to_left, ("gy", "gz"), -1), shifted(to_right, ("gy", "gz"), 1)], axis=0
    )
    next_columns = shifted(columns, "gx", -1)
    prev_columns = shifted(columns, "gx", 1)
    block = (layers, 2 * ROWS, 3 * LANES)
    powers, sums = call(
        power_kernel,
        [(STEPS,) + adjoint_rhs.shape, (2, 2 * ROWS, LANES)],
        [(2,) + block] * 2 + [block] * 4 + [block[1:]] * 2,
    )(*held[:5], from_next, from_prev, columns, next_columns, prev_columns)
    parts = exchange(sums, ("gy", "gz"))
    if len(parts) > 1:
        sums = call(add_kernel, [sums.shape])(*parts)[0]
    parts = exchange(sums, "gx")
    return tuple(
        call(final_kernel, [adjoint_rhs.shape, adjoint_rhs.shape, friction.shape])(
            rhs, powers, friction, ice_mask, grounded, speed, *parts
        )
    )


def solution(mesh):
    in_specs = (
        P(None, None, ("parts", "gx"), ("gy", "gz")),
        P(None, ("parts", "gx"), ("gy", "gz")),
        P(("parts", "gx"), ("gy", "gz")),
        P(("parts", "gx"), ("gy", "gz")),
        P(("parts", "gx"), ("gy", "gz")),
        P(None, ("parts", "gx"), ("gy", "gz")),
    )
    out_specs = (
        P(None, None, ("parts", "gx"), ("gy", "gz")),
        P(None, None, ("parts", "gx"), ("gy", "gz")),
        P(("parts", "gx"), ("gy", "gz")),
    )
    return jax.shard_map(body, mesh=mesh, in_specs=in_specs, out_specs=out_specs, check_vma=False)
```

```python
import functools

import jax
import jax.numpy as jnp
from jax import lax
from jax.experimental import pallas as pl
from jax.experimental.pallas import tpu as pltpu
from jax.sharding import PartitionSpec as P

STEPS = 4
HALO = 4
ROWS = 8
LANES = 128
UNROLL = 4


def call(kernel, outs, scratch=(), **more):
    return pl.pallas_call(
        kernel,
        out_shape=[jax.ShapeDtypeStruct(s, jnp.float32) if isinstance(s, tuple) else s for s in outs],
        scratch_shapes=[pltpu.VMEM(s, jnp.float32) if isinstance(s, tuple) else s for s in scratch],
        compiler_params=pltpu.CompilerParams(vmem_limit_bytes=40 * 1024 * 1024),
        **more,
    )


def own_planes(rhs, eta, friction, ice, grounded):
    layers = eta.shape[0]
    cover = ice[...].astype(jnp.float32)
    drag = friction[...] * grounded[...].astype(jnp.float32)

    def plane(p):
        if p < 2 * layers:
            return rhs[p // layers, p % layers] * cover
        if p < 3 * layers:
            return eta[p - 2 * layers]
        return cover if p == 3 * layers else drag

    return plane


def pair_of(q, layers):
    if q < layers:
        return q, q + layers
    if q < layers + layers // 2:
        return q + layers, q + layers + layers // 2
    return 3 * layers, 3 * layers + 1


def pack_kernel(*refs):
    sources, held, (to_left, to_right, to_prev, to_next, arrived) = refs[:6], refs[6:12], refs[12:]
    copies = [pltpu.make_async_copy(a, b, arrived.at[i]) for i, (a, b) in enumerate(zip(sources, held))]
    for copy in copies:
        copy.start()
    for copy in copies:
        copy.wait()
    rhs, eta, friction, ice, grounded, _ = held
    layers = eta.shape[0]
    plane = own_planes(rhs, eta, friction, ice, grounded)
    lane = lax.broadcasted_iota(jnp.int32, (ROWS, LANES), 1)
    row = lax.broadcasted_iota(jnp.int32, (ROWS, LANES), 0)
    upper = row < HALO
    width = to_prev.shape[0]
    left = [jnp.zeros((ROWS, LANES), jnp.float32) for _ in range(2)]
    right = [jnp.zeros((ROWS, LANES), jnp.float32) for _ in range(2)]
    for q in range(width // 2):
        first, second = pair_of(q, layers)
        x, y = plane(first), plane(second)
        for half in range(2):
            xs = x[:, half * LANES : (half + 1) * LANES]
            ys = y[:, half * LANES : (half + 1) * LANES]
            to_prev[2 * q + half] = jnp.where(upper, xs, pltpu.roll(ys, HALO, 0))
            to_next[2 * q + half] = jnp.where(upper, pltpu.roll(ys, HALO, 0), xs)
        for p, v in ((first, x), (second, y)):
            group, place = p // 32, HALO * (p % 32)
            mine = (lane >= place) & (lane < place + HALO)
            head, tail = v[:, :LANES], v[:, LANES:]
            shift = (place + HALO) % LANES
            left[group] = jnp.where(mine, pltpu.roll(head, place, 1) if place else head, left[group])
            right[group] = jnp.where(mine, pltpu.roll(tail, shift, 1) if shift else tail, right[group])
    for group in range(2):
        to_left[group] = left[group]
        to_right[group] = right[group]


def two_sum(a, b):
    s = a + b
    t = s - a
    return s, (a - (s - t)) + (b - t)


def join(x, y):
    s, e = two_sum(x[0], y[0])
    e = e + (x[1] + y[1])
    h = s + e
    return h, e - (h - s)


def times(scalar, x):
    def cut(v):
        t = v * 4097.0
        h = t - (t - v)
        return h, v - h

    p = scalar * x[0]
    sh, sl = cut(scalar)
    xh, xl = cut(x[0])
    e = ((sh * xh - p) + sh * xl + sl * xh) + sl * xl
    return p, e + scalar * x[1]


def power_kernel(
    rhs, eta, friction, ice, grounded, from_next, from_prev, columns, next_columns, prev_columns,
    powers, moments,
    field_a, field_b, eta_row, eta_col, eta_half, eta_up, cover, drag,
):
    layers = eta.shape[0]
    plane = own_planes(rhs, eta, friction, ice, grounded)
    lane = lax.broadcasted_iota(jnp.int32, (ROWS, LANES), 1)
    row = lax.broadcasted_iota(jnp.int32, (ROWS, LANES), 0)
    upper = row < HALO
    strips = from_next.shape[0]
    corner = [jnp.where(upper, next_columns[t], prev_columns[t]) for t in range(4)]
    beside = [columns[t] for t in range(4)]

    def side(tiles, p):
        group, place = p // 32, HALO * (p % 32)
        a, b = (LANES - place) % LANES, LANES - place - HALO
        right = pltpu.roll(tiles[group], a, 1) if a else tiles[group]
        left = pltpu.roll(tiles[2 + group], b, 1) if b else tiles[2 + group]
        return jnp.where(lane < HALO, right, jnp.where(lane >= LANES - HALO, left, 0.0))

    def fill(p, dst):
        dst[0:ROWS, 0 : 2 * LANES] = plane(p)
        dst[0:ROWS, 2 * LANES :] = side(beside, p)
        dst[ROWS:, 2 * LANES :] = side(corner, p)

    def target(p):
        if p < 2 * layers:
            return field_a.at[p // layers, p % layers]
        if p < 3 * layers:
            return eta_half.at[p - 2 * layers]
        return cover if p == 3 * layers else drag

    for q in range(strips // 2):
        first, second = pair_of(q, layers)
        for half in range(2):
            below, above = from_next[2 * q + half], from_prev[2 * q + half]
            cut = slice(half * LANES, (half + 1) * LANES)
            target(first)[ROWS:, cut] = jnp.where(upper, below, above)
            target(second)[ROWS:, cut] = pltpu.roll(jnp.where(upper, above, below), HALO, 0)
        fill(first, target(first))
        fill(second, target(second))

    def row_next(v):
        return pltpu.roll(v, 2 * ROWS - 1, 0)

    def row_prev(v):
        return pltpu.roll(v, 1, 0)

    def col_next(v):
        return pltpu.roll(v, 3 * LANES - 1, 1)

    def col_prev(v):
        return pltpu.roll(v, 1, 1)

    for k in range(layers):
        e = eta_half[k]
        eta_row[k] = 2.0 * (e + row_next(e))
        eta_col[k] = 0.5 * (e + col_next(e))
        eta_up[k] = e + eta_half[k + 1] if k + 1 < layers else jnp.zeros_like(e)
        if k:
            eta_half[k - 1] = 0.5 * eta_half[k - 1]
    eta_half[layers - 1] = 0.5 * eta_half[layers - 1]

    own = (slice(0, ROWS), slice(0, 2 * LANES))
    bare = 1.0 - ice[...].astype(jnp.float32)

    def apply(t, src, dst):
        def layer(k, carry):
            below0, below1, odd, even = carry
            g0, g1 = src[0, k], src[1, k]
            after = jnp.minimum(k + 1, layers - 1)
            e_row, e_col, e_half, e_up = eta_row[k], eta_col[k], eta_half[k], eta_up[k]
            up0 = e_up * (g0 - src[0, after])
            up1 = e_up * (g1 - src[1, after])
            g0n, g1n = row_next(g0), col_next(g1)
            f = e_half * (g1n - col_prev(g1))
            h = e_half * (g0n - row_prev(g0))
            flux = e_row * (g0 - g0n)
            out0 = flux - row_next(f) - row_prev(flux - f)
            flux = e_col * (g0 - col_next(g0))
            out0 = out0 + (flux - col_prev(flux)) + (up0 - below0)
            flux = (4.0 * e_col) * (g1 - g1n)
            out1 = flux - col_next(h) - col_prev(flux - h)
            flux = (0.25 * e_row) * (g1 - row_next(g1))
            out1 = out1 + (flux - row_prev(flux)) + (up1 - below1)
            m = cover[...]
            out0, out1 = m * out0, m * out1
            if t < STEPS:
                dst[0, k], dst[1, k] = out0, out1
            for c, g, out in ((0, g0, out0), (1, g1, out1)):
                outside = rhs[c, k] * bare
                before = g[own] + outside
                now = out[own] + outside
                powers[t - 1, c, k] = now
                odd = odd + before * now
                even = even + now * now
            return up0, up1, odd, even

        zero = jnp.zeros((ROWS, 2 * LANES), jnp.float32)
        d = drag[...]
        start = (-d * src[0, 0], -d * src[1, 0], zero, zero)

        def block(b, carry):
            for i in range(UNROLL):
                carry = layer(b * UNROLL + i, carry)
            return carry

        return lax.fori_loop(0, layers // UNROLL, block, start)[2:]

    square = jnp.zeros((ROWS, 2 * LANES), jnp.float32)
    for c in range(2):
        for k in range(layers):
            square = square + rhs[c, k] * rhs[c, k]
    sums = [square]
    src, dst = field_a, field_b
    for t in range(1, STEPS + 1):
        sums.extend(apply(t, src, dst))
        src, dst = dst, src

    tall = lax.broadcasted_iota(jnp.int32, (2 * ROWS, LANES), 0)
    high = jnp.zeros((2 * ROWS, LANES), jnp.float32)
    low = jnp.zeros((2 * ROWS, LANES), jnp.float32)
    for j, total in enumerate(sums):
        pair = two_sum(total[:, :LANES], total[:, LANES:])
        for step in (4, 2, 1):
            pair = join(pair, tuple(pltpu.roll(v, step, 0) for v in pair))
        high = jnp.where(tall == j, jnp.concatenate([pair[0]] * 2, 0), high)
        low = jnp.where(tall == j, jnp.concatenate([pair[1]] * 2, 0), low)
    moments[0] = high
    moments[1] = low


def add_kernel(*refs):
    *ins, out = refs
    total = (ins[0][0], ins[0][1])
    for x in ins[1:]:
        total = join(total, (x[0], x[1]))
    out[0], out[1] = total


def solve(total):
    for step in (64, 32, 16, 8, 4, 2, 1):
        total = join(total, tuple(pltpu.roll(v, step, 1) for v in total))

    def spread(v, j):
        return jnp.broadcast_to(v[j : j + 1], (ROWS, LANES))

    centre = spread(total[0], 1) / spread(total[0], 0)
    wide = jnp.concatenate([centre, centre], 0)
    mu = [spread(total[0], 0)]
    for _ in range(2 * STEPS):
        step = times(wide, total)
        total = join(tuple(pltpu.roll(v, 2 * ROWS - 1, 0) for v in total), (-step[0], -step[1]))
        mu.append(spread(total[0], 0))

    def plus(a, b):
        n = max(len(a), len(b))
        return [a[i] + b[i] if i < min(len(a), len(b)) else (a[i] if i < len(a) else b[i]) for i in range(n)]

    def scaled(s, a):
        return [s * x for x in a]

    def operator(a):
        return plus([centre * x for x in a], [jnp.zeros_like(centre)] + a)

    def dot(a, b):
        square = [None] * (len(a) + len(b) - 1)
        for i, x in enumerate(a):
            for j, y in enumerate(b):
                z = x * y
                square[i + j] = z if square[i + j] is None else square[i + j] + z
        value = square[0] * mu[0]
        for n in range(1, len(square)):
            value = value + square[n] * mu[n]
        return value

    one = jnp.ones_like(centre)
    right = [one]
    quasi, search, update, iterate = right, right, [], []
    applied = operator(search)
    carried = applied
    rho = mu[0]
    tau_sq = rho
    alpha = theta_sq = eta = None
    for half in range(STEPS):
        if half % 2 == 0:
            alpha = rho / dot(carried, right)
            search_next = plus(search, scaled(-alpha, carried))
        quasi = plus(quasi, scaled(-alpha, applied))
        if half:
            update = plus(search, scaled(theta_sq / alpha * eta, update))
        else:
            update = search
        theta_sq = dot(quasi, quasi) / tau_sq
        cosine_sq = 1.0 / (1.0 + theta_sq)
        tau_sq = tau_sq * theta_sq * cosine_sq
        eta = cosine_sq * alpha
        iterate = plus(iterate, scaled(eta, update))
        if half % 2 == 0:
            search = search_next
            applied = operator(search)
        elif half < STEPS - 1:
            rho_next = dot(quasi, right)
            beta = rho_next / rho
            search = plus(quasi, scaled(beta, search))
            applied_next = operator(search)
            carried = plus(applied_next, scaled(beta, plus(applied, scaled(beta, carried))))
            applied, rho = applied_next, rho_next
    powers = [iterate[-1]]
    for c in iterate[-2::-1]:
        powers = plus([c] + powers, scaled(-centre, powers))
    return powers


def final_kernel(rhs, powers, friction, ice, grounded, speed, *rest):
    *parts, iterate, residual, hessian = rest
    layers = rhs.shape[1]
    total = (parts[0][0], parts[0][1])
    for x in parts[1:]:
        total = join(total, (x[0], x[1]))
    factors = [jnp.concatenate([c, c], 1) for c in solve(total)]
    for c in range(2):
        for k in range(layers):
            r = rhs[c, k]
            vectors = [r] + [powers[t, c, k] for t in range(STEPS)]
            x = factors[0] * vectors[0]
            y = factors[0] * vectors[1]
            for t in range(1, STEPS):
                x = x + factors[t] * vectors[t]
                y = y + factors[t] * vectors[t + 1]
            iterate[c, k] = x
            residual[c, k] = r - y
    weight = ice[...].astype(jnp.float32) * (friction[...] * grounded[...].astype(jnp.float32))
    hessian[...] = weight * (speed[0] * iterate[0, 0] + speed[1] * iterate[1, 0])


def shifted(x, axis, step):
    count = lax.axis_size(axis)
    pairs = [(i, i + step) for i in range(count) if 0 <= i + step < count]
    return lax.ppermute(x, axis, pairs)


def exchange(x, axis):
    count = lax.axis_size(axis)
    stride = 1
    rounds = []
    while stride < count:
        size = 4 if (count // stride) % 4 == 0 else 2
        rounds.append((stride, size))
        stride *= size
    for at, (stride, size) in enumerate(rounds):
        parts = [x]
        for turn in range(1, size):
            pairs = []
            for i in range(count):
                place = (i // stride) % size
                pairs.append((i, i + ((place + turn) % size - place) * stride))
            parts.append(lax.ppermute(x, axis, pairs))
        if at == len(rounds) - 1:
            return parts
        x = call(add_kernel, [x.shape])(*parts)[0]
    return [x]


def body(adjoint_rhs, viscosity, friction, ice_mask, grounded, basal_velocity):
    layers = viscosity.shape[0]
    inputs = (adjoint_rhs, viscosity, friction, ice_mask, grounded, basal_velocity)
    tile = (ROWS, LANES)
    strips = (2 * (layers + layers // 2 + 1),) + tile
    *held, to_left, to_right, to_prev, to_next = call(
        pack_kernel,
        [jax.ShapeDtypeStruct(x.shape, x.dtype) for x in inputs] + [(2,) + tile, (2,) + tile, strips, strips],
        [pltpu.SemaphoreType.DMA((len(inputs),))],
        in_specs=[pl.BlockSpec(memory_space=pltpu.HBM)] * len(inputs),
    )(*[pltpu.with_memory_space_constraint(x, pltpu.HBM) for x in inputs])
    from_next = shifted(to_prev, "gx", -1)
    from_prev = shifted(to_next, "gx", 1)
    columns = jnp.concatenate(
        [shifted(to_left, ("gy", "gz"), -1), shifted(to_right, ("gy", "gz"), 1)], axis=0
    )
    next_columns = shifted(columns, "gx", -1)
    prev_columns = shifted(columns, "gx", 1)
    block = (layers, 2 * ROWS, 3 * LANES)
    powers, sums = call(
        power_kernel,
        [(STEPS,) + adjoint_rhs.shape, (2, 2 * ROWS, LANES)],
        [(2,) + block] * 2 + [block] * 4 + [block[1:]] * 2,
    )(*held[:5], from_next, from_prev, columns, next_columns, prev_columns)
    parts = exchange(sums, ("gy", "gz"))
    if len(parts) > 1:
        sums = call(add_kernel, [sums.shape])(*parts)[0]
    parts = exchange(sums, "gx")
    rhs, _, friction, ice_mask, grounded, speed = held
    return tuple(
        call(final_kernel, [adjoint_rhs.shape, adjoint_rhs.shape, friction.shape])(
            rhs, powers, friction, ice_mask, grounded, speed, *parts
        )
    )


def solution(mesh):
    in_specs = (
        P(None, None, ("parts", "gx"), ("gy", "gz")),
        P(None, ("parts", "gx"), ("gy", "gz")),
        P(("parts", "gx"), ("gy", "gz")),
        P(("parts", "gx"), ("gy", "gz")),
        P(("parts", "gx"), ("gy", "gz")),
        P(None, ("parts", "gx"), ("gy", "gz")),
    )
    out_specs = (
        P(None, None, ("parts", "gx"), ("gy", "gz")),
        P(None, None, ("parts", "gx"), ("gy", "gz")),
        P(("parts", "gx"), ("gy", "gz")),
    )
    return jax.shard_map(body, mesh=mesh, in_specs=in_specs, out_specs=out_specs, check_vma=False)
```

```python
import functools

import jax
import jax.numpy as jnp
from jax import lax
from jax.experimental import pallas as pl
from jax.experimental.pallas import tpu as pltpu
from jax.sharding import PartitionSpec as P

STEPS = 4
HALO = 4
ROWS = 8
LANES = 128
UNROLL = 4


def call(kernel, outs, scratch=(), **more):
    return pl.pallas_call(
        kernel,
        out_shape=[jax.ShapeDtypeStruct(s, jnp.float32) if isinstance(s, tuple) else s for s in outs],
        scratch_shapes=[pltpu.VMEM(s, jnp.float32) if isinstance(s, tuple) else s for s in scratch],
        compiler_params=pltpu.CompilerParams(vmem_limit_bytes=40 * 1024 * 1024),
        **more,
    )


def place_of(axis):
    place, count = lax.axis_index(axis), lax.axis_size(axis)
    even = place % 2 == 0
    has_a = jnp.logical_or(jnp.logical_not(even), place < count - 1)
    has_b = jnp.where(even, place > 0, place < count - 1)
    return even, has_a, has_b


def swapped(x, axis, first):
    count = lax.axis_size(axis)
    pairs = []
    for i in range(count):
        other = i + 1 if (i - first) % 2 == 0 else i - 1
        pairs.append((i, other if 0 <= other < count else i))
    return lax.ppermute(x, axis, pairs)


def own_planes(rhs, eta, friction, ice, grounded):
    layers = eta.shape[0]
    cover = ice[...].astype(jnp.float32)
    drag = friction[...] * grounded[...].astype(jnp.float32)

    def plane(p):
        if p < 2 * layers:
            return rhs[p // layers, p % layers] * cover
        if p < 3 * layers:
            return eta[p - 2 * layers]
        return cover if p == 3 * layers else drag

    return plane


def pair_of(q, layers):
    if q < layers:
        return q, q + layers
    if q < layers + layers // 2:
        return q + layers, q + layers + layers // 2
    return 3 * layers, 3 * layers + 1


def pack_kernel(*refs):
    sources, held, (column_a, column_b, strip_a, strip_b, arrived) = refs[:6], refs[6:12], refs[12:]
    copies = [pltpu.make_async_copy(a, b, arrived.at[i]) for i, (a, b) in enumerate(zip(sources, held))]
    for copy in copies:
        copy.start()
    for copy in copies:
        copy.wait()
    rhs, eta, friction, ice, grounded, _ = held
    layers = eta.shape[0]
    plane = own_planes(rhs, eta, friction, ice, grounded)
    lane = lax.broadcasted_iota(jnp.int32, (ROWS, LANES), 1)
    row = lax.broadcasted_iota(jnp.int32, (ROWS, LANES), 0)
    rows_even, _, _ = place_of("gx")
    columns_even, _, _ = place_of(("gy", "gz"))
    upper_a = (row < HALO) != rows_even
    width = strip_a.shape[0]
    left = [jnp.zeros((ROWS, LANES), jnp.float32) for _ in range(2)]
    right = [jnp.zeros((ROWS, LANES), jnp.float32) for _ in range(2)]
    for q in range(width // 2):
        first, second = pair_of(q, layers)
        x, y = plane(first), plane(second)
        for half in range(2):
            xs = x[:, half * LANES : (half + 1) * LANES]
            ys = y[:, half * LANES : (half + 1) * LANES]
            ys = pltpu.roll(ys, HALO, 0)
            strip_a[2 * q + half] = jnp.where(upper_a, xs, ys)
            strip_b[2 * q + half] = jnp.where(upper_a, ys, xs)
        for p, v in ((first, x), (second, y)):
            group, place = p // 32, HALO * (p % 32)
            mine = (lane >= place) & (lane < place + HALO)
            head, tail = v[:, :LANES], v[:, LANES:]
            shift = (place + HALO) % LANES
            left[group] = jnp.where(mine, pltpu.roll(head, place, 1) if place else head, left[group])
            right[group] = jnp.where(mine, pltpu.roll(tail, shift, 1) if shift else tail, right[group])
    for group in range(2):
        column_a[group] = jnp.where(columns_even, right[group], left[group])
        column_b[group] = jnp.where(columns_even, left[group], right[group])


def two_sum(a, b):
    s = a + b
    t = s - a
    return s, (a - (s - t)) + (b - t)


def join(x, y):
    s, e = two_sum(x[0], y[0])
    e = e + (x[1] + y[1])
    h = s + e
    return h, e - (h - s)


def times(scalar, x):
    def cut(v):
        t = v * 4097.0
        h = t - (t - v)
        return h, v - h

    p = scalar * x[0]
    sh, sl = cut(scalar)
    xh, xl = cut(x[0])
    e = ((sh * xh - p) + sh * xl + sl * xh) + sl * xl
    return p, e + scalar * x[1]


def power_kernel(
    rhs, eta, friction, ice, grounded, strip_a, strip_b, columns, columns_a, columns_b,
    powers, moments,
    field_a, field_b, eta_row, eta_col, eta_half, eta_up, cover, drag,
):
    layers = eta.shape[0]
    plane = own_planes(rhs, eta, friction, ice, grounded)
    lane = lax.broadcasted_iota(jnp.int32, (ROWS, LANES), 1)
    row = lax.broadcasted_iota(jnp.int32, (ROWS, LANES), 0)
    strips = strip_a.shape[0]
    even, has_a, has_b = place_of("gx")
    upper_a = (row < HALO) == even

    def below_and_above(from_a, from_b):
        return jnp.where(upper_a, jnp.where(has_a, from_a, 0.0), jnp.where(has_b, from_b, 0.0))

    def above_and_below(from_a, from_b):
        return jnp.where(upper_a, jnp.where(has_b, from_b, 0.0), jnp.where(has_a, from_a, 0.0))

    even, came_a, came_b = place_of(("gy", "gz"))

    def right_and_left(tiles):
        from_a = [jnp.where(came_a, tiles[t], 0.0) for t in (0, 1)]
        from_b = [jnp.where(came_b, tiles[t], 0.0) for t in (2, 3)]
        right = [jnp.where(even, x, y) for x, y in zip(from_a, from_b)]
        left = [jnp.where(even, y, x) for x, y in zip(from_a, from_b)]
        return right + left

    corner = right_and_left([below_and_above(columns_a[t], columns_b[t]) for t in range(4)])
    beside = right_and_left([columns[t] for t in range(4)])

    def side(tiles, p):
        group, place = p // 32, HALO * (p % 32)
        a, b = (LANES - place) % LANES, LANES - place - HALO
        right = pltpu.roll(tiles[group], a, 1) if a else tiles[group]
        left = pltpu.roll(tiles[2 + group], b, 1) if b else tiles[2 + group]
        return jnp.where(lane < HALO, right, jnp.where(lane >= LANES - HALO, left, 0.0))

    def fill(p, dst):
        dst[0:ROWS, 0 : 2 * LANES] = plane(p)
        dst[0:ROWS, 2 * LANES :] = side(beside, p)
        dst[ROWS:, 2 * LANES :] = side(corner, p)

    def target(p):
        if p < 2 * layers:
            return field_a.at[p // layers, p % layers]
        if p < 3 * layers:
            return eta_half.at[p - 2 * layers]
        return cover if p == 3 * layers else drag

    for q in range(strips // 2):
        first, second = pair_of(q, layers)
        for half in range(2):
            from_a, from_b = strip_a[2 * q + half], strip_b[2 * q + half]
            cut = slice(half * LANES, (half + 1) * LANES)
            target(first)[ROWS:, cut] = below_and_above(from_a, from_b)
            target(second)[ROWS:, cut] = pltpu.roll(above_and_below(from_a, from_b), HALO, 0)
        fill(first, target(first))
        fill(second, target(second))

    def row_next(v):
        return pltpu.roll(v, 2 * ROWS - 1, 0)

    def row_prev(v):
        return pltpu.roll(v, 1, 0)

    def col_next(v):
        return pltpu.roll(v, 3 * LANES - 1, 1)

    def col_prev(v):
        return pltpu.roll(v, 1, 1)

    for k in range(layers):
        e = eta_half[k]
        eta_row[k] = 2.0 * (e + row_next(e))
        eta_col[k] = 0.5 * (e + col_next(e))
        eta_up[k] = e + eta_half[k + 1] if k + 1 < layers else jnp.zeros_like(e)
        if k:
            eta_half[k - 1] = 0.5 * eta_half[k - 1]
    eta_half[layers - 1] = 0.5 * eta_half[layers - 1]

    own = (slice(0, ROWS), slice(0, 2 * LANES))
    bare = 1.0 - ice[...].astype(jnp.float32)

    def apply(t, src, dst):
        def layer(k, carry):
            below0, below1, odd, even = carry
            g0, g1 = src[0, k], src[1, k]
            after = jnp.minimum(k + 1, layers - 1)
            e_row, e_col, e_half, e_up = eta_row[k], eta_col[k], eta_half[k], eta_up[k]
            up0 = e_up * (g0 - src[0, after])
            up1 = e_up * (g1 - src[1, after])
            g0n, g1n = row_next(g0), col_next(g1)
            f = e_half * (g1n - col_prev(g1))
            h = e_half * (g0n - row_prev(g0))
            flux = e_row * (g0 - g0n)
            out0 = flux - row_next(f) - row_prev(flux - f)
            flux = e_col * (g0 - col_next(g0))
            out0 = out0 + (flux - col_prev(flux)) + (up0 - below0)
            flux = (4.0 * e_col) * (g1 - g1n)
            out1 = flux - col_next(h) - col_prev(flux - h)
            flux = (0.25 * e_row) * (g1 - row_next(g1))
            out1 = out1 + (flux - row_prev(flux)) + (up1 - below1)
            m = cover[...]
            out0, out1 = m * out0, m * out1
            if t < STEPS:
                dst[0, k], dst[1, k] = out0, out1
            for c, g, out in ((0, g0, out0), (1, g1, out1)):
                outside = rhs[c, k] * bare
                before = g[own] + outside
                now = out[own] + outside
                powers[t - 1, c, k] = now
                odd = odd + before * now
                even = even + now * now
            return up0, up1, odd, even

        zero = jnp.zeros((ROWS, 2 * LANES), jnp.float32)
        d = drag[...]
        start = (-d * src[0, 0], -d * src[1, 0], zero, zero)

        def block(b, carry):
            for i in range(UNROLL):
                carry = layer(b * UNROLL + i, carry)
            return carry

        return lax.fori_loop(0, layers // UNROLL, block, start)[2:]

    square = jnp.zeros((ROWS, 2 * LANES), jnp.float32)
    for c in range(2):
        for k in range(layers):
            square = square + rhs[c, k] * rhs[c, k]
    sums = [square]
    src, dst = field_a, field_b
    for t in range(1, STEPS + 1):
        sums.extend(apply(t, src, dst))
        src, dst = dst, src

    tall = lax.broadcasted_iota(jnp.int32, (2 * ROWS, LANES), 0)
    high = jnp.zeros((2 * ROWS, LANES), jnp.float32)
    low = jnp.zeros((2 * ROWS, LANES), jnp.float32)
    for j, total in enumerate(sums):
        pair = two_sum(total[:, :LANES], total[:, LANES:])
        for step in (4, 2, 1):
            pair = join(pair, tuple(pltpu.roll(v, step, 0) for v in pair))
        high = jnp.where(tall == j, jnp.concatenate([pair[0]] * 2, 0), high)
        low = jnp.where(tall == j, jnp.concatenate([pair[1]] * 2, 0), low)
    moments[0] = high
    moments[1] = low


def add_kernel(*refs):
    *ins, out = refs
    total = (ins[0][0], ins[0][1])
    for x in ins[1:]:
        total = join(total, (x[0], x[1]))
    out[0], out[1] = total


def solve(total):
    for step in (64, 32, 16, 8, 4, 2, 1):
        total = join(total, tuple(pltpu.roll(v, step, 1) for v in total))

    def spread(v, j):
        return jnp.broadcast_to(v[j : j + 1], (ROWS, LANES))

    centre = spread(total[0], 1) / spread(total[0], 0)
    wide = jnp.concatenate([centre, centre], 0)
    mu = [spread(total[0], 0)]
    for _ in range(2 * STEPS):
        step = times(wide, total)
        total = join(tuple(pltpu.roll(v, 2 * ROWS - 1, 0) for v in total), (-step[0], -step[1]))
        mu.append(spread(total[0], 0))

    def plus(a, b):
        n = max(len(a), len(b))
        return [a[i] + b[i] if i < min(len(a), len(b)) else (a[i] if i < len(a) else b[i]) for i in range(n)]

    def scaled(s, a):
        return [s * x for x in a]

    def operator(a):
        return plus([centre * x for x in a], [jnp.zeros_like(centre)] + a)

    def dot(a, b):
        square = [None] * (len(a) + len(b) - 1)
        for i, x in enumerate(a):
            for j, y in enumerate(b):
                z = x * y
                square[i + j] = z if square[i + j] is None else square[i + j] + z
        value = square[0] * mu[0]
        for n in range(1, len(square)):
            value = value + square[n] * mu[n]
        return value

    one = jnp.ones_like(centre)
    right = [one]
    quasi, search, update, iterate = right, right, [], []
    applied = operator(search)
    carried = applied
    rho = mu[0]
    tau_sq = rho
    alpha = theta_sq = eta = None
    for half in range(STEPS):
        if half % 2 == 0:
            alpha = rho / dot(carried, right)
            search_next = plus(search, scaled(-alpha, carried))
        quasi = plus(quasi, scaled(-alpha, applied))
        if half:
            update = plus(search, scaled(theta_sq / alpha * eta, update))
        else:
            update = search
        theta_sq = dot(quasi, quasi) / tau_sq
        cosine_sq = 1.0 / (1.0 + theta_sq)
        tau_sq = tau_sq * theta_sq * cosine_sq
        eta = cosine_sq * alpha
        iterate = plus(iterate, scaled(eta, update))
        if half % 2 == 0:
            search = search_next
            applied = operator(search)
        elif half < STEPS - 1:
            rho_next = dot(quasi, right)
            beta = rho_next / rho
            search = plus(quasi, scaled(beta, search))
            applied_next = operator(search)
            carried = plus(applied_next, scaled(beta, plus(applied, scaled(beta, carried))))
            applied, rho = applied_next, rho_next
    powers = [iterate[-1]]
    for c in iterate[-2::-1]:
        powers = plus([c] + powers, scaled(-centre, powers))
    return powers


def final_kernel(rhs, powers, friction, ice, grounded, speed, *rest):
    *parts, iterate, residual, hessian = rest
    layers = rhs.shape[1]
    total = (parts[0][0], parts[0][1])
    for x in parts[1:]:
        total = join(total, (x[0], x[1]))
    factors = [jnp.concatenate([c, c], 1) for c in solve(total)]
    for c in range(2):
        for k in range(layers):
            r = rhs[c, k]
            vectors = [r] + [powers[t, c, k] for t in range(STEPS)]
            x = factors[0] * vectors[0]
            y = factors[0] * vectors[1]
            for t in range(1, STEPS):
                x = x + factors[t] * vectors[t]
                y = y + factors[t] * vectors[t + 1]
            iterate[c, k] = x
            residual[c, k] = r - y
    weight = ice[...].astype(jnp.float32) * (friction[...] * grounded[...].astype(jnp.float32))
    hessian[...] = weight * (speed[0] * iterate[0, 0] + speed[1] * iterate[1, 0])


def exchange(x, axis):
    count = lax.axis_size(axis)
    stride = 1
    rounds = []
    while stride < count:
        size = 4 if (count // stride) % 4 == 0 else 2
        rounds.append((stride, size))
        stride *= size
    for at, (stride, size) in enumerate(rounds):
        parts = [x]
        for turn in range(1, size):
            pairs = []
            for i in range(count):
                place = (i // stride) % size
                pairs.append((i, i + ((place ^ turn) - place) * stride))
            parts.append(lax.ppermute(x, axis, pairs))
        if at == len(rounds) - 1:
            return parts
        x = call(add_kernel, [x.shape])(*parts)[0]
    return [x]


def body(adjoint_rhs, viscosity, friction, ice_mask, grounded, basal_velocity):
    layers = viscosity.shape[0]
    inputs = (adjoint_rhs, viscosity, friction, ice_mask, grounded, basal_velocity)
    tile = (ROWS, LANES)
    strips = (2 * (layers + layers // 2 + 1),) + tile
    *held, column_a, column_b, strip_a, strip_b = call(
        pack_kernel,
        [jax.ShapeDtypeStruct(x.shape, x.dtype) for x in inputs] + [(2,) + tile, (2,) + tile, strips, strips],
        [pltpu.SemaphoreType.DMA((len(inputs),))],
        in_specs=[pl.BlockSpec(memory_space=pltpu.HBM)] * len(inputs),
    )(*[pltpu.with_memory_space_constraint(x, pltpu.HBM) for x in inputs])
    strip_a, strip_b = swapped(strip_a, "gx", 0), swapped(strip_b, "gx", 1)
    beside = ("gy", "gz")
    columns = jnp.concatenate([swapped(column_a, beside, 0), swapped(column_b, beside, 1)], axis=0)
    columns_a, columns_b = swapped(columns, "gx", 0), swapped(columns, "gx", 1)
    block = (layers, 2 * ROWS, 3 * LANES)
    powers, sums = call(
        power_kernel,
        [(STEPS,) + adjoint_rhs.shape, (2, 2 * ROWS, LANES)],
        [(2,) + block] * 2 + [block] * 4 + [block[1:]] * 2,
    )(*held[:5], strip_a, strip_b, columns, columns_a, columns_b)
    parts = exchange(sums, ("gy", "gz"))
    if len(parts) > 1:
        sums = call(add_kernel, [sums.shape])(*parts)[0]
    parts = exchange(sums, "gx")
    rhs, _, friction, ice_mask, grounded, speed = held
    return tuple(
        call(final_kernel, [adjoint_rhs.shape, adjoint_rhs.shape, friction.shape])(
            rhs, powers, friction, ice_mask, grounded, speed, *parts
        )
    )


def solution(mesh):
    in_specs = (
        P(None, None, ("parts", "gx"), ("gy", "gz")),
        P(None, ("parts", "gx"), ("gy", "gz")),
        P(("parts", "gx"), ("gy", "gz")),
        P(("parts", "gx"), ("gy", "gz")),
        P(("parts", "gx"), ("gy", "gz")),
        P(None, ("parts", "gx"), ("gy", "gz")),
    )
    out_specs = (
        P(None, None, ("parts", "gx"), ("gy", "gz")),
        P(None, None, ("parts", "gx"), ("gy", "gz")),
        P(("parts", "gx"), ("gy", "gz")),
    )
    return jax.shard_map(body, mesh=mesh, in_specs=in_specs, out_specs=out_specs, check_vma=False)
```

```python
import functools

import jax
import jax.numpy as jnp
from jax import lax
from jax.experimental import pallas as pl
from jax.experimental.pallas import tpu as pltpu
from jax.sharding import PartitionSpec as P

STEPS = 4
HALO = 4
ROWS = 8
LANES = 128
UNROLL = 4
GROUP = ("gx", "gy", "gz")


def call(kernel, outs, scratch=(), **more):
    return pl.pallas_call(
        kernel,
        out_shape=[jax.ShapeDtypeStruct(s, jnp.float32) if isinstance(s, tuple) else s for s in outs],
        scratch_shapes=[pltpu.VMEM(s, jnp.float32) if isinstance(s, tuple) else s for s in scratch],
        compiler_params=pltpu.CompilerParams(vmem_limit_bytes=40 * 1024 * 1024),
        **more,
    )


def place_of(axis):
    place, count = lax.axis_index(axis), lax.axis_size(axis)
    even = place % 2 == 0
    has_a = jnp.logical_or(jnp.logical_not(even), place < count - 1)
    has_b = jnp.where(even, place > 0, place < count - 1)
    return even, has_a, has_b


def swapped(x, axis, first):
    count = lax.axis_size(axis)
    pairs = []
    for i in range(count):
        other = i + 1 if (i - first) % 2 == 0 else i - 1
        pairs.append((i, other if 0 <= other < count else i))
    return lax.ppermute(x, axis, pairs)


def own_planes(rhs, eta, friction, ice, grounded):
    layers = eta.shape[0]
    cover = ice[...].astype(jnp.float32)
    drag = friction[...] * grounded[...].astype(jnp.float32)

    def plane(p):
        if p < 2 * layers:
            return rhs[p // layers, p % layers] * cover
        if p < 3 * layers:
            return eta[p - 2 * layers]
        return cover if p == 3 * layers else drag

    return plane


def pair_of(q, layers):
    if q < layers:
        return q, q + layers
    if q < layers + layers // 2:
        return q + layers, q + layers + layers // 2
    return 3 * layers, 3 * layers + 1


def pack_kernel(*refs):
    sources, held, (column_a, column_b, strip_a, strip_b, arrived) = refs[:6], refs[6:12], refs[12:]
    copies = [pltpu.make_async_copy(a, b, arrived.at[i]) for i, (a, b) in enumerate(zip(sources, held))]
    for copy in copies:
        copy.start()
    for copy in copies:
        copy.wait()
    rhs, eta, friction, ice, grounded, _ = held
    layers = eta.shape[0]
    plane = own_planes(rhs, eta, friction, ice, grounded)
    lane = lax.broadcasted_iota(jnp.int32, (ROWS, LANES), 1)
    row = lax.broadcasted_iota(jnp.int32, (ROWS, LANES), 0)
    rows_even, _, _ = place_of("gx")
    columns_even, _, _ = place_of(("gy", "gz"))
    upper_a = (row < HALO) != rows_even
    width = strip_a.shape[0]
    left = [jnp.zeros((ROWS, LANES), jnp.float32) for _ in range(2)]
    right = [jnp.zeros((ROWS, LANES), jnp.float32) for _ in range(2)]
    for q in range(width // 2):
        first, second = pair_of(q, layers)
        x, y = plane(first), plane(second)
        for half in range(2):
            xs = x[:, half * LANES : (half + 1) * LANES]
            ys = y[:, half * LANES : (half + 1) * LANES]
            ys = pltpu.roll(ys, HALO, 0)
            strip_a[2 * q + half] = jnp.where(upper_a, xs, ys)
            strip_b[2 * q + half] = jnp.where(upper_a, ys, xs)
        for p, v in ((first, x), (second, y)):
            group, place = p // 32, HALO * (p % 32)
            mine = (lane >= place) & (lane < place + HALO)
            head, tail = v[:, :LANES], v[:, LANES:]
            shift = (place + HALO) % LANES
            left[group] = jnp.where(mine, pltpu.roll(head, place, 1) if place else head, left[group])
            right[group] = jnp.where(mine, pltpu.roll(tail, shift, 1) if shift else tail, right[group])
    for group in range(2):
        column_a[group] = jnp.where(columns_even, right[group], left[group])
        column_b[group] = jnp.where(columns_even, left[group], right[group])


def two_sum(a, b):
    s = a + b
    t = s - a
    return s, (a - (s - t)) + (b - t)


def join(x, y):
    s, e = two_sum(x[0], y[0])
    e = e + (x[1] + y[1])
    h = s + e
    return h, e - (h - s)


def times(scalar, x):
    def cut(v):
        t = v * 4097.0
        h = t - (t - v)
        return h, v - h

    p = scalar * x[0]
    sh, sl = cut(scalar)
    xh, xl = cut(x[0])
    e = ((sh * xh - p) + sh * xl + sl * xh) + sl * xl
    return p, e + scalar * x[1]


def power_kernel(
    rhs, eta, friction, ice, grounded, strip_a, strip_b, columns, columns_a, columns_b,
    powers, moments,
    field_a, field_b, eta_row, eta_col, eta_half, eta_up, cover, drag,
):
    layers = eta.shape[0]
    plane = own_planes(rhs, eta, friction, ice, grounded)
    lane = lax.broadcasted_iota(jnp.int32, (ROWS, LANES), 1)
    row = lax.broadcasted_iota(jnp.int32, (ROWS, LANES), 0)
    strips = strip_a.shape[0]
    even, has_a, has_b = place_of("gx")
    upper_a = (row < HALO) == even

    def below_and_above(from_a, from_b):
        return jnp.where(upper_a, jnp.where(has_a, from_a, 0.0), jnp.where(has_b, from_b, 0.0))

    def above_and_below(from_a, from_b):
        return jnp.where(upper_a, jnp.where(has_b, from_b, 0.0), jnp.where(has_a, from_a, 0.0))

    even, came_a, came_b = place_of(("gy", "gz"))

    def right_and_left(tiles):
        from_a = [jnp.where(came_a, tiles[t], 0.0) for t in (0, 1)]
        from_b = [jnp.where(came_b, tiles[t], 0.0) for t in (2, 3)]
        right = [jnp.where(even, x, y) for x, y in zip(from_a, from_b)]
        left = [jnp.where(even, y, x) for x, y in zip(from_a, from_b)]
        return right + left

    corner = right_and_left([below_and_above(columns_a[t], columns_b[t]) for t in range(4)])
    beside = right_and_left([columns[t] for t in range(4)])

    def side(tiles, p):
        group, place = p // 32, HALO * (p % 32)
        a, b = (LANES - place) % LANES, LANES - place - HALO
        right = pltpu.roll(tiles[group], a, 1) if a else tiles[group]
        left = pltpu.roll(tiles[2 + group], b, 1) if b else tiles[2 + group]
        return jnp.where(lane < HALO, right, jnp.where(lane >= LANES - HALO, left, 0.0))

    def fill(p, dst):
        dst[0:ROWS, 0 : 2 * LANES] = plane(p)
        dst[0:ROWS, 2 * LANES :] = side(beside, p)
        dst[ROWS:, 2 * LANES :] = side(corner, p)

    def target(p):
        if p < 2 * layers:
            return field_a.at[p // layers, p % layers]
        if p < 3 * layers:
            return eta_half.at[p - 2 * layers]
        return cover if p == 3 * layers else drag

    for q in range(strips // 2):
        first, second = pair_of(q, layers)
        for half in range(2):
            from_a, from_b = strip_a[2 * q + half], strip_b[2 * q + half]
            cut = slice(half * LANES, (half + 1) * LANES)
            target(first)[ROWS:, cut] = below_and_above(from_a, from_b)
            target(second)[ROWS:, cut] = pltpu.roll(above_and_below(from_a, from_b), HALO, 0)
        fill(first, target(first))
        fill(second, target(second))

    def row_next(v):
        return pltpu.roll(v, 2 * ROWS - 1, 0)

    def row_prev(v):
        return pltpu.roll(v, 1, 0)

    def col_next(v):
        return pltpu.roll(v, 3 * LANES - 1, 1)

    def col_prev(v):
        return pltpu.roll(v, 1, 1)

    for k in range(layers):
        e = eta_half[k]
        eta_row[k] = 2.0 * (e + row_next(e))
        eta_col[k] = 0.5 * (e + col_next(e))
        eta_up[k] = e + eta_half[k + 1] if k + 1 < layers else jnp.zeros_like(e)
        if k:
            eta_half[k - 1] = 0.5 * eta_half[k - 1]
    eta_half[layers - 1] = 0.5 * eta_half[layers - 1]

    own = (slice(0, ROWS), slice(0, 2 * LANES))
    bare = 1.0 - ice[...].astype(jnp.float32)

    def apply(t, src, dst):
        def layer(k, carry):
            below0, below1, odd, even = carry
            g0, g1 = src[0, k], src[1, k]
            after = jnp.minimum(k + 1, layers - 1)
            e_row, e_col, e_half, e_up = eta_row[k], eta_col[k], eta_half[k], eta_up[k]
            up0 = e_up * (g0 - src[0, after])
            up1 = e_up * (g1 - src[1, after])
            g0n, g1n = row_next(g0), col_next(g1)
            f = e_half * (g1n - col_prev(g1))
            h = e_half * (g0n - row_prev(g0))
            flux = e_row * (g0 - g0n)
            out0 = flux - row_next(f) - row_prev(flux - f)
            flux = e_col * (g0 - col_next(g0))
            out0 = out0 + (flux - col_prev(flux)) + (up0 - below0)
            flux = (4.0 * e_col) * (g1 - g1n)
            out1 = flux - col_next(h) - col_prev(flux - h)
            flux = (0.25 * e_row) * (g1 - row_next(g1))
            out1 = out1 + (flux - row_prev(flux)) + (up1 - below1)
            m = cover[...]
            out0, out1 = m * out0, m * out1
            if t < STEPS:
                dst[0, k], dst[1, k] = out0, out1
            for c, g, out in ((0, g0, out0), (1, g1, out1)):
                outside = rhs[c, k] * bare
                before = g[own] + outside
                now = out[own] + outside
                powers[t - 1, c, k] = now
                odd = odd + before * now
                even = even + now * now
            return up0, up1, odd, even

        zero = jnp.zeros((ROWS, 2 * LANES), jnp.float32)
        d = drag[...]
        start = (-d * src[0, 0], -d * src[1, 0], zero, zero)

        def block(b, carry):
            for i in range(UNROLL):
                carry = layer(b * UNROLL + i, carry)
            return carry

        return lax.fori_loop(0, layers // UNROLL, block, start)[2:]

    square = jnp.zeros((ROWS, 2 * LANES), jnp.float32)
    for c in range(2):
        for k in range(layers):
            square = square + rhs[c, k] * rhs[c, k]
    sums = [square]
    src, dst = field_a, field_b
    for t in range(1, STEPS + 1):
        sums.extend(apply(t, src, dst))
        src, dst = dst, src

    tall = lax.broadcasted_iota(jnp.int32, (2 * ROWS, LANES), 0)
    high = jnp.zeros((2 * ROWS, LANES), jnp.float32)
    low = jnp.zeros((2 * ROWS, LANES), jnp.float32)
    for j, total in enumerate(sums):
        pair = two_sum(total[:, :LANES], total[:, LANES:])
        for step in (4, 2, 1):
            pair = join(pair, tuple(pltpu.roll(v, step, 0) for v in pair))
        high = jnp.where(tall == j, jnp.concatenate([pair[0]] * 2, 0), high)
        low = jnp.where(tall == j, jnp.concatenate([pair[1]] * 2, 0), low)
    for copy in range(moments.shape[0]):
        moments[copy, 0] = high
        moments[copy, 1] = low


def solve(total):
    for step in (64, 32, 16, 8, 4, 2, 1):
        total = join(total, tuple(pltpu.roll(v, step, 1) for v in total))

    def spread(v, j):
        return jnp.broadcast_to(v[j : j + 1], (ROWS, LANES))

    centre = spread(total[0], 1) / spread(total[0], 0)
    wide = jnp.concatenate([centre, centre], 0)
    mu = [spread(total[0], 0)]
    for _ in range(2 * STEPS):
        step = times(wide, total)
        total = join(tuple(pltpu.roll(v, 2 * ROWS - 1, 0) for v in total), (-step[0], -step[1]))
        mu.append(spread(total[0], 0))

    def plus(a, b):
        n = max(len(a), len(b))
        return [a[i] + b[i] if i < min(len(a), len(b)) else (a[i] if i < len(a) else b[i]) for i in range(n)]

    def scaled(s, a):
        return [s * x for x in a]

    def operator(a):
        return plus([centre * x for x in a], [jnp.zeros_like(centre)] + a)

    def dot(a, b):
        square = [None] * (len(a) + len(b) - 1)
        for i, x in enumerate(a):
            for j, y in enumerate(b):
                z = x * y
                square[i + j] = z if square[i + j] is None else square[i + j] + z
        value = square[0] * mu[0]
        for n in range(1, len(square)):
            value = value + square[n] * mu[n]
        return value

    one = jnp.ones_like(centre)
    right = [one]
    quasi, search, update, iterate = right, right, [], []
    applied = operator(search)
    carried = applied
    rho = mu[0]
    tau_sq = rho
    alpha = theta_sq = eta = None
    for half in range(STEPS):
        if half % 2 == 0:
            alpha = rho / dot(carried, right)
            search_next = plus(search, scaled(-alpha, carried))
        quasi = plus(quasi, scaled(-alpha, applied))
        if half:
            update = plus(search, scaled(theta_sq / alpha * eta, update))
        else:
            update = search
        theta_sq = dot(quasi, quasi) / tau_sq
        cosine_sq = 1.0 / (1.0 + theta_sq)
        tau_sq = tau_sq * theta_sq * cosine_sq
        eta = cosine_sq * alpha
        iterate = plus(iterate, scaled(eta, update))
        if half % 2 == 0:
            search = search_next
            applied = operator(search)
        elif half < STEPS - 1:
            rho_next = dot(quasi, right)
            beta = rho_next / rho
            search = plus(quasi, scaled(beta, search))
            applied_next = operator(search)
            carried = plus(applied_next, scaled(beta, plus(applied, scaled(beta, carried))))
            applied, rho = applied_next, rho_next
    powers = [iterate[-1]]
    for c in iterate[-2::-1]:
        powers = plus([c] + powers, scaled(-centre, powers))
    return powers


def final_kernel(rhs, powers, friction, ice, grounded, speed, parts, iterate, residual, hessian):
    layers = rhs.shape[1]
    terms = [(parts[i, 0], parts[i, 1]) for i in range(parts.shape[0])]
    while len(terms) > 1:
        pairs = [join(x, y) for x, y in zip(terms[::2], terms[1::2])]
        terms = pairs + terms[2 * len(pairs) :]
    (total,) = terms
    factors = [jnp.concatenate([c, c], 1) for c in solve(total)]
    for c in range(2):
        for k in range(layers):
            r = rhs[c, k]
            vectors = [r] + [powers[t, c, k] for t in range(STEPS)]
            x = factors[0] * vectors[0]
            y = factors[0] * vectors[1]
            for t in range(1, STEPS):
                x = x + factors[t] * vectors[t]
                y = y + factors[t] * vectors[t + 1]
            iterate[c, k] = x
            residual[c, k] = r - y
    weight = ice[...].astype(jnp.float32) * (friction[...] * grounded[...].astype(jnp.float32))
    hessian[...] = weight * (speed[0] * iterate[0, 0] + speed[1] * iterate[1, 0])


def body(adjoint_rhs, viscosity, friction, ice_mask, grounded, basal_velocity):
    layers = viscosity.shape[0]
    inputs = (adjoint_rhs, viscosity, friction, ice_mask, grounded, basal_velocity)
    tile = (ROWS, LANES)
    strips = (2 * (layers + layers // 2 + 1),) + tile
    *held, column_a, column_b, strip_a, strip_b = call(
        pack_kernel,
        [jax.ShapeDtypeStruct(x.shape, x.dtype) for x in inputs] + [(2,) + tile, (2,) + tile, strips, strips],
        [pltpu.SemaphoreType.DMA((len(inputs),))],
        in_specs=[pl.BlockSpec(memory_space=pltpu.HBM)] * len(inputs),
    )(*[pltpu.with_memory_space_constraint(x, pltpu.HBM) for x in inputs])
    strip_a, strip_b = swapped(strip_a, "gx", 0), swapped(strip_b, "gx", 1)
    beside = ("gy", "gz")
    columns = jnp.concatenate([swapped(column_a, beside, 0), swapped(column_b, beside, 1)], axis=0)
    columns_a, columns_b = swapped(columns, "gx", 0), swapped(columns, "gx", 1)
    block = (layers, 2 * ROWS, 3 * LANES)
    powers, sums = call(
        power_kernel,
        [(STEPS,) + adjoint_rhs.shape, (lax.axis_size(GROUP), 2, 2 * ROWS, LANES)],
        [(2,) + block] * 2 + [block] * 4 + [block[1:]] * 2,
    )(*held[:5], strip_a, strip_b, columns, columns_a, columns_b)
    parts = lax.all_to_all(sums, GROUP, 0, 0)
    rhs, _, friction, ice_mask, grounded, speed = held
    return tuple(
        call(final_kernel, [adjoint_rhs.shape, adjoint_rhs.shape, friction.shape])(
            rhs, powers, friction, ice_mask, grounded, speed, parts
        )
    )


def solution(mesh):
    in_specs = (
        P(None, None, ("parts", "gx"), ("gy", "gz")),
        P(None, ("parts", "gx"), ("gy", "gz")),
        P(("parts", "gx"), ("gy", "gz")),
        P(("parts", "gx"), ("gy", "gz")),
        P(("parts", "gx"), ("gy", "gz")),
        P(None, ("parts", "gx"), ("gy", "gz")),
    )
    out_specs = (
        P(None, None, ("parts", "gx"), ("gy", "gz")),
        P(None, None, ("parts", "gx"), ("gy", "gz")),
        P(("parts", "gx"), ("gy", "gz")),
    )
    return jax.shard_map(body, mesh=mesh, in_specs=in_specs, out_specs=out_specs, check_vma=False)
```

```python
import functools

import jax
import jax.numpy as jnp
from jax import lax
from jax.experimental import pallas as pl
from jax.experimental.pallas import tpu as pltpu
from jax.sharding import PartitionSpec as P

STEPS = 4
HALO = 4
ROWS = 8
LANES = 128
UNROLL = 4
GROUP = ("gx", "gy", "gz")


def call(kernel, outs, scratch=(), **more):
    return pl.pallas_call(
        kernel,
        out_shape=[jax.ShapeDtypeStruct(s, jnp.float32) if isinstance(s, tuple) else s for s in outs],
        scratch_shapes=[pltpu.VMEM(s, jnp.float32) if isinstance(s, tuple) else s for s in scratch],
        compiler_params=pltpu.CompilerParams(vmem_limit_bytes=40 * 1024 * 1024),
        **more,
    )


def place_of(axis):
    place, count = lax.axis_index(axis), lax.axis_size(axis)
    even = place % 2 == 0
    has_a = jnp.logical_or(jnp.logical_not(even), place < count - 1)
    has_b = jnp.where(even, place > 0, place < count - 1)
    return even, has_a, has_b


def swapped(x, axis, first):
    count = lax.axis_size(axis)
    pairs = []
    for i in range(count):
        other = i + 1 if (i - first) % 2 == 0 else i - 1
        pairs.append((i, other if 0 <= other < count else i))
    return lax.ppermute(x, axis, pairs)


def own_planes(rhs, eta, friction, ice, grounded):
    layers = eta.shape[0]
    cover = ice[...].astype(jnp.float32)
    drag = friction[...] * grounded[...].astype(jnp.float32)

    def plane(p):
        if p < 2 * layers:
            return rhs[p // layers, p % layers] * cover
        if p < 3 * layers:
            return eta[p - 2 * layers]
        return cover if p == 3 * layers else drag

    return plane


def pair_of(q, layers):
    if q < layers:
        return q, q + layers
    if q < layers + layers // 2:
        return q + layers, q + layers + layers // 2
    return 3 * layers, 3 * layers + 1


def pack_kernel(*refs):
    sources, held, (column_a, column_b, strip_a, strip_b, arrived) = refs[:6], refs[6:12], refs[12:]
    copies = [pltpu.make_async_copy(a, b, arrived.at[i]) for i, (a, b) in enumerate(zip(sources, held))]
    for copy in copies:
        copy.start()
    for copy in copies:
        copy.wait()
    rhs, eta, friction, ice, grounded, _ = held
    layers = eta.shape[0]
    plane = own_planes(rhs, eta, friction, ice, grounded)
    lane = lax.broadcasted_iota(jnp.int32, (ROWS, LANES), 1)
    row = lax.broadcasted_iota(jnp.int32, (ROWS, LANES), 0)
    rows_even, _, _ = place_of("gx")
    columns_even, _, _ = place_of(("gy", "gz"))
    upper_a = (row < HALO) != rows_even
    width = strip_a.shape[0]
    left = [jnp.zeros((ROWS, LANES), jnp.float32) for _ in range(2)]
    right = [jnp.zeros((ROWS, LANES), jnp.float32) for _ in range(2)]
    for q in range(width // 2):
        first, second = pair_of(q, layers)
        x, y = plane(first), plane(second)
        for half in range(2):
            xs = x[:, half * LANES : (half + 1) * LANES]
            ys = y[:, half * LANES : (half + 1) * LANES]
            ys = pltpu.roll(ys, HALO, 0)
            strip_a[2 * q + half] = jnp.where(upper_a, xs, ys)
            strip_b[2 * q + half] = jnp.where(upper_a, ys, xs)
        for p, v in ((first, x), (second, y)):
            group, place = p // 32, HALO * (p % 32)
            mine = (lane >= place) & (lane < place + HALO)
            head, tail = v[:, :LANES], v[:, LANES:]
            shift = (place + HALO) % LANES
            left[group] = jnp.where(mine, pltpu.roll(head, place, 1) if place else head, left[group])
            right[group] = jnp.where(mine, pltpu.roll(tail, shift, 1) if shift else tail, right[group])
    for group in range(2):
        column_a[group] = jnp.where(columns_even, right[group], left[group])
        column_b[group] = jnp.where(columns_even, left[group], right[group])


def two_sum(a, b):
    s = a + b
    t = s - a
    return s, (a - (s - t)) + (b - t)


def join(x, y):
    s, e = two_sum(x[0], y[0])
    e = e + (x[1] + y[1])
    h = s + e
    return h, e - (h - s)


def times(scalar, x):
    def cut(v):
        t = v * 4097.0
        h = t - (t - v)
        return h, v - h

    p = scalar * x[0]
    sh, sl = cut(scalar)
    xh, xl = cut(x[0])
    e = ((sh * xh - p) + sh * xl + sl * xh) + sl * xl
    return p, e + scalar * x[1]


def power_kernel(
    rhs, eta, friction, ice, grounded, strip_a, strip_b, columns, columns_a, columns_b,
    powers, moments,
    field_a, field_b, eta_row, eta_col, eta_half, eta_up, cover, drag,
):
    layers = eta.shape[0]
    plane = own_planes(rhs, eta, friction, ice, grounded)
    lane = lax.broadcasted_iota(jnp.int32, (ROWS, LANES), 1)
    row = lax.broadcasted_iota(jnp.int32, (ROWS, LANES), 0)
    strips = strip_a.shape[0]
    even, has_a, has_b = place_of("gx")
    upper_a = (row < HALO) == even

    def below_and_above(from_a, from_b):
        return jnp.where(upper_a, jnp.where(has_a, from_a, 0.0), jnp.where(has_b, from_b, 0.0))

    def above_and_below(from_a, from_b):
        return jnp.where(upper_a, jnp.where(has_b, from_b, 0.0), jnp.where(has_a, from_a, 0.0))

    even, came_a, came_b = place_of(("gy", "gz"))

    def right_and_left(tiles):
        from_a = [jnp.where(came_a, tiles[t], 0.0) for t in (0, 1)]
        from_b = [jnp.where(came_b, tiles[t], 0.0) for t in (2, 3)]
        right = [jnp.where(even, x, y) for x, y in zip(from_a, from_b)]
        left = [jnp.where(even, y, x) for x, y in zip(from_a, from_b)]
        return right + left

    corner = right_and_left([below_and_above(columns_a[t], columns_b[t]) for t in range(4)])
    beside = right_and_left([columns[t] for t in range(4)])

    def side(tiles, p):
        group, place = p // 32, HALO * (p % 32)
        a, b = (LANES - place) % LANES, LANES - place - HALO
        right = pltpu.roll(tiles[group], a, 1) if a else tiles[group]
        left = pltpu.roll(tiles[2 + group], b, 1) if b else tiles[2 + group]
        return jnp.where(lane < HALO, right, jnp.where(lane >= LANES - HALO, left, 0.0))

    def fill(p, dst):
        dst[0:ROWS, 0 : 2 * LANES] = plane(p)
        dst[0:ROWS, 2 * LANES :] = side(beside, p)
        dst[ROWS:, 2 * LANES :] = side(corner, p)

    def target(p):
        if p < 2 * layers:
            return field_a.at[p // layers, p % layers]
        if p < 3 * layers:
            return eta_half.at[p - 2 * layers]
        return cover if p == 3 * layers else drag

    for q in range(strips // 2):
        first, second = pair_of(q, layers)
        for half in range(2):
            from_a, from_b = strip_a[2 * q + half], strip_b[2 * q + half]
            cut = slice(half * LANES, (half + 1) * LANES)
            target(first)[ROWS:, cut] = below_and_above(from_a, from_b)
            target(second)[ROWS:, cut] = pltpu.roll(above_and_below(from_a, from_b), HALO, 0)
        fill(first, target(first))
        fill(second, target(second))

    def row_next(v):
        return pltpu.roll(v, 2 * ROWS - 1, 0)

    def row_prev(v):
        return pltpu.roll(v, 1, 0)

    def col_next(v):
        return pltpu.roll(v, 3 * LANES - 1, 1)

    def col_prev(v):
        return pltpu.roll(v, 1, 1)

    for k in range(layers):
        e = eta_half[k]
        eta_row[k] = 2.0 * (e + row_next(e))
        eta_col[k] = 0.5 * (e + col_next(e))
        eta_up[k] = e + eta_half[k + 1] if k + 1 < layers else jnp.zeros_like(e)
        if k:
            eta_half[k - 1] = 0.5 * eta_half[k - 1]
    eta_half[layers - 1] = 0.5 * eta_half[layers - 1]

    own = (slice(0, ROWS), slice(0, 2 * LANES))
    bare = 1.0 - ice[...].astype(jnp.float32)

    def apply(t, src, dst):
        def layer(k, carry):
            below0, below1, odd, even = carry
            g0, g1 = src[0, k], src[1, k]
            after = jnp.minimum(k + 1, layers - 1)
            e_row, e_col, e_half, e_up = eta_row[k], eta_col[k], eta_half[k], eta_up[k]
            up0 = e_up * (g0 - src[0, after])
            up1 = e_up * (g1 - src[1, after])
            g0n, g1n = row_next(g0), col_next(g1)
            f = e_half * (g1n - col_prev(g1))
            h = e_half * (g0n - row_prev(g0))
            flux = e_row * (g0 - g0n)
            out0 = flux - row_next(f) - row_prev(flux - f)
            flux = e_col * (g0 - col_next(g0))
            out0 = out0 + (flux - col_prev(flux)) + (up0 - below0)
            flux = (4.0 * e_col) * (g1 - g1n)
            out1 = flux - col_next(h) - col_prev(flux - h)
            flux = (0.25 * e_row) * (g1 - row_next(g1))
            out1 = out1 + (flux - row_prev(flux)) + (up1 - below1)
            m = cover[...]
            out0, out1 = m * out0, m * out1
            if t < STEPS:
                dst[0, k], dst[1, k] = out0, out1
            for c, g, out in ((0, g0, out0), (1, g1, out1)):
                outside = rhs[c, k] * bare
                before = g[own] + outside
                now = out[own] + outside
                powers[t - 1, c, k] = now
                odd = odd + before * now
                even = even + now * now
            return up0, up1, odd, even

        zero = jnp.zeros((ROWS, 2 * LANES), jnp.float32)
        d = drag[...]
        start = (-d * src[0, 0], -d * src[1, 0], zero, zero)

        def block(b, carry):
            for i in range(UNROLL):
                carry = layer(b * UNROLL + i, carry)
            return carry

        return lax.fori_loop(0, layers // UNROLL, block, start)[2:]

    square = jnp.zeros((ROWS, 2 * LANES), jnp.float32)
    for c in range(2):
        for k in range(layers):
            square = square + rhs[c, k] * rhs[c, k]
    sums = [square]
    src, dst = field_a, field_b
    for t in range(1, STEPS + 1):
        sums.extend(apply(t, src, dst))
        src, dst = dst, src

    tall = lax.broadcasted_iota(jnp.int32, (2 * ROWS, LANES), 0)
    high = jnp.zeros((2 * ROWS, LANES), jnp.float32)
    low = jnp.zeros((2 * ROWS, LANES), jnp.float32)
    for j, total in enumerate(sums):
        pair = two_sum(total[:, :LANES], total[:, LANES:])
        for step in (4, 2, 1):
            pair = join(pair, tuple(pltpu.roll(v, step, 0) for v in pair))
        high = jnp.where(tall == j, jnp.concatenate([pair[0]] * 2, 0), high)
        low = jnp.where(tall == j, jnp.concatenate([pair[1]] * 2, 0), low)
    moments[0] = high
    moments[1] = low


def solve(total):
    for step in (64, 32, 16, 8, 4, 2, 1):
        total = join(total, tuple(pltpu.roll(v, step, 1) for v in total))

    def spread(v, j):
        return jnp.broadcast_to(v[j : j + 1], (ROWS, LANES))

    centre = spread(total[0], 1) / spread(total[0], 0)
    wide = jnp.concatenate([centre, centre], 0)
    mu = [spread(total[0], 0)]
    for _ in range(2 * STEPS):
        step = times(wide, total)
        total = join(tuple(pltpu.roll(v, 2 * ROWS - 1, 0) for v in total), (-step[0], -step[1]))
        mu.append(spread(total[0], 0))

    def plus(a, b):
        n = max(len(a), len(b))
        return [a[i] + b[i] if i < min(len(a), len(b)) else (a[i] if i < len(a) else b[i]) for i in range(n)]

    def scaled(s, a):
        return [s * x for x in a]

    def operator(a):
        return plus([centre * x for x in a], [jnp.zeros_like(centre)] + a)

    def dot(a, b):
        square = [None] * (len(a) + len(b) - 1)
        for i, x in enumerate(a):
            for j, y in enumerate(b):
                z = x * y
                square[i + j] = z if square[i + j] is None else square[i + j] + z
        value = square[0] * mu[0]
        for n in range(1, len(square)):
            value = value + square[n] * mu[n]
        return value

    one = jnp.ones_like(centre)
    right = [one]
    quasi, search, update, iterate = right, right, [], []
    applied = operator(search)
    carried = applied
    rho = mu[0]
    tau_sq = rho
    alpha = theta_sq = eta = None
    for half in range(STEPS):
        if half % 2 == 0:
            alpha = rho / dot(carried, right)
            search_next = plus(search, scaled(-alpha, carried))
        quasi = plus(quasi, scaled(-alpha, applied))
        if half:
            update = plus(search, scaled(theta_sq / alpha * eta, update))
        else:
            update = search
        theta_sq = dot(quasi, quasi) / tau_sq
        cosine_sq = 1.0 / (1.0 + theta_sq)
        tau_sq = tau_sq * theta_sq * cosine_sq
        eta = cosine_sq * alpha
        iterate = plus(iterate, scaled(eta, update))
        if half % 2 == 0:
            search = search_next
            applied = operator(search)
        elif half < STEPS - 1:
            rho_next = dot(quasi, right)
            beta = rho_next / rho
            search = plus(quasi, scaled(beta, search))
            applied_next = operator(search)
            carried = plus(applied_next, scaled(beta, plus(applied, scaled(beta, carried))))
            applied, rho = applied_next, rho_next
    powers = [iterate[-1]]
    for c in iterate[-2::-1]:
        powers = plus([c] + powers, scaled(-centre, powers))
    return powers


def final_kernel(rhs, powers, friction, ice, grounded, speed, parts, iterate, residual, hessian):
    layers = rhs.shape[1]
    terms = [(parts[i, 0], parts[i, 1]) for i in range(parts.shape[0])]
    while len(terms) > 1:
        pairs = [join(x, y) for x, y in zip(terms[::2], terms[1::2])]
        terms = pairs + terms[2 * len(pairs) :]
    (total,) = terms
    factors = [jnp.concatenate([c, c], 1) for c in solve(total)]
    for c in range(2):
        for k in range(layers):
            r = rhs[c, k]
            vectors = [r] + [powers[t, c, k] for t in range(STEPS)]
            x = factors[0] * vectors[0]
            y = factors[0] * vectors[1]
            for t in range(1, STEPS):
                x = x + factors[t] * vectors[t]
                y = y + factors[t] * vectors[t + 1]
            iterate[c, k] = x
            residual[c, k] = r - y
    weight = ice[...].astype(jnp.float32) * (friction[...] * grounded[...].astype(jnp.float32))
    hessian[...] = weight * (speed[0] * iterate[0, 0] + speed[1] * iterate[1, 0])


def body(adjoint_rhs, viscosity, friction, ice_mask, grounded, basal_velocity):
    layers = viscosity.shape[0]
    inputs = (adjoint_rhs, viscosity, friction, ice_mask, grounded, basal_velocity)
    tile = (ROWS, LANES)
    strips = (2 * (layers + layers // 2 + 1),) + tile
    *held, column_a, column_b, strip_a, strip_b = call(
        pack_kernel,
        [jax.ShapeDtypeStruct(x.shape, x.dtype) for x in inputs] + [(2,) + tile, (2,) + tile, strips, strips],
        [pltpu.SemaphoreType.DMA((len(inputs),))],
        in_specs=[pl.BlockSpec(memory_space=pltpu.HBM)] * len(inputs),
    )(*[pltpu.with_memory_space_constraint(x, pltpu.HBM) for x in inputs])
    strip_a, strip_b = swapped(strip_a, "gx", 0), swapped(strip_b, "gx", 1)
    beside = ("gy", "gz")
    columns = jnp.concatenate([swapped(column_a, beside, 0), swapped(column_b, beside, 1)], axis=0)
    columns_a, columns_b = swapped(columns, "gx", 0), swapped(columns, "gx", 1)
    block = (layers, 2 * ROWS, 3 * LANES)
    powers, sums = call(
        power_kernel,
        [(STEPS,) + adjoint_rhs.shape, (2, 2 * ROWS, LANES)],
        [(2,) + block] * 2 + [block] * 4 + [block[1:]] * 2,
    )(*held[:5], strip_a, strip_b, columns, columns_a, columns_b)
    parts = lax.all_gather(sums, GROUP)
    rhs, _, friction, ice_mask, grounded, speed = held
    return tuple(
        call(final_kernel, [adjoint_rhs.shape, adjoint_rhs.shape, friction.shape])(
            rhs, powers, friction, ice_mask, grounded, speed, parts
        )
    )


def solution(mesh):
    in_specs = (
        P(None, None, ("parts", "gx"), ("gy", "gz")),
        P(None, ("parts", "gx"), ("gy", "gz")),
        P(("parts", "gx"), ("gy", "gz")),
        P(("parts", "gx"), ("gy", "gz")),
        P(("parts", "gx"), ("gy", "gz")),
        P(None, ("parts", "gx"), ("gy", "gz")),
    )
    out_specs = (
        P(None, None, ("parts", "gx"), ("gy", "gz")),
        P(None, None, ("parts", "gx"), ("gy", "gz")),
        P(("parts", "gx"), ("gy", "gz")),
    )
    return jax.shard_map(body, mesh=mesh, in_specs=in_specs, out_specs=out_specs, check_vma=False)
```

```python
import functools

import jax
import jax.numpy as jnp
from jax import lax
from jax.experimental import pallas as pl
from jax.experimental.pallas import tpu as pltpu
from jax.sharding import PartitionSpec as P

STEPS = 4
HALO = 4
ROWS = 8
LANES = 128
UNROLL = 5
SLOT = 32


def call(kernel, outs, scratch=(), **more):
    return pl.pallas_call(
        kernel,
        out_shape=[jax.ShapeDtypeStruct(s, jnp.float32) if isinstance(s, tuple) else s for s in outs],
        scratch_shapes=[pltpu.VMEM(s, jnp.float32) if isinstance(s, tuple) else s for s in scratch],
        compiler_params=pltpu.CompilerParams(vmem_limit_bytes=40 * 1024 * 1024),
        **more,
    )


def place_of(axis):
    place, count = lax.axis_index(axis), lax.axis_size(axis)
    even = place % 2 == 0
    has_a = jnp.logical_or(jnp.logical_not(even), place < count - 1)
    has_b = jnp.where(even, place > 0, place < count - 1)
    return even, has_a, has_b


def swapped(x, axis, first):
    count = lax.axis_size(axis)
    pairs = []
    for i in range(count):
        other = i + 1 if (i - first) % 2 == 0 else i - 1
        pairs.append((i, other if 0 <= other < count else i))
    return lax.ppermute(x, axis, pairs)


def own_planes(rhs, eta, friction, ice, grounded):
    layers = eta.shape[0]
    cover = ice[...].astype(jnp.float32)
    drag = friction[...] * grounded[...].astype(jnp.float32)

    def plane(p):
        if p < 2 * layers:
            return rhs[p // layers, p % layers] * cover
        if p < 3 * layers:
            return eta[p - 2 * layers]
        return cover if p == 3 * layers else drag

    return plane


def pair_of(q, layers):
    if q < layers:
        return q, q + layers
    if q < layers + layers // 2:
        return q + layers, q + layers + layers // 2
    return 3 * layers, 3 * layers + 1


def ribbon_places(p, layers):
    tiles = layers // 4
    if p < 3 * layers:
        k = p % layers
        return p // layers * tiles + k % tiles, (k // tiles,)
    return (3 * tiles, (0, 1, 2, 3)) if p == 3 * layers else (3 * tiles + 1, (0,))


def ribbon_tiles(layers):
    return 3 * (layers // 4) + 2


def between(lane, first, width):
    return (lane >= first) & (lane < first + width)


def turned(v, shift):
    shift = shift % LANES
    return pltpu.roll(v, shift, 1) if shift else v


def pack_kernel(*refs):
    sources, held, (column_a, column_b, strip_a, strip_b, arrived) = refs[:6], refs[6:12], refs[12:]
    copies = [pltpu.make_async_copy(a, b, arrived.at[i]) for i, (a, b) in enumerate(zip(sources, held))]
    for copy in copies:
        copy.start()
    for copy in copies:
        copy.wait()
    rhs, eta, friction, ice, grounded, _ = held
    layers = eta.shape[0]
    plane = own_planes(rhs, eta, friction, ice, grounded)
    lane = lax.broadcasted_iota(jnp.int32, (ROWS, LANES), 1)
    row = lax.broadcasted_iota(jnp.int32, (ROWS, LANES), 0)
    rows_even, _, _ = place_of("gx")
    columns_even, _, _ = place_of(("gy", "gz"))
    upper_a = (row < HALO) != rows_even
    count = column_a.shape[0]
    left = [jnp.zeros((ROWS, LANES), jnp.float32) for _ in range(count)]
    right = [jnp.zeros((ROWS, LANES), jnp.float32) for _ in range(count)]
    for q in range(strip_a.shape[0] // 2):
        first, second = pair_of(q, layers)
        x, y = plane(first), plane(second)
        for half in range(2):
            xs = x[:, half * LANES : (half + 1) * LANES]
            ys = y[:, half * LANES : (half + 1) * LANES]
            ys = pltpu.roll(ys, HALO, 0)
            strip_a[2 * q + half] = jnp.where(upper_a, xs, ys)
            strip_b[2 * q + half] = jnp.where(upper_a, ys, xs)
        for p, v in ((first, x), (second, y)):
            tile, slots = ribbon_places(p, layers)
            for slot in slots:
                at = slot * SLOT
                left[tile] = jnp.where(between(lane, at + 8, 4), turned(v[:, :LANES], at + 8), left[tile])
                right[tile] = jnp.where(between(lane, at + 16, 4), turned(v[:, LANES:], at + 20), right[tile])
    for tile in range(count):
        column_a[tile] = jnp.where(columns_even, right[tile], left[tile])
        column_b[tile] = jnp.where(columns_even, left[tile], right[tile])


def beside_kernel(from_a, from_b, columns):
    _, has_a, has_b = place_of(("gy", "gz"))
    for tile in range(columns.shape[0]):
        columns[tile] = jnp.where(has_a, from_a[tile], 0.0) + jnp.where(has_b, from_b[tile], 0.0)


def two_sum(a, b):
    s = a + b
    t = s - a
    return s, (a - (s - t)) + (b - t)


def join(x, y):
    s, e = two_sum(x[0], y[0])
    e = e + (x[1] + y[1])
    h = s + e
    return h, e - (h - s)


def times(scalar, x):
    def cut(v):
        t = v * 4097.0
        h = t - (t - v)
        return h, v - h

    p = scalar * x[0]
    sh, sl = cut(scalar)
    xh, xl = cut(x[0])
    e = ((sh * xh - p) + sh * xl + sl * xh) + sl * xl
    return p, e + scalar * x[1]


def beyond():
    even, has_a, has_b = place_of("gx")
    upper_a = (lax.broadcasted_iota(jnp.int32, (ROWS, LANES), 0) < HALO) == even

    def below_and_above(from_a, from_b):
        return jnp.where(upper_a, jnp.where(has_a, from_a, 0.0), jnp.where(has_b, from_b, 0.0))

    def above_and_below(from_a, from_b):
        return jnp.where(upper_a, jnp.where(has_b, from_b, 0.0), jnp.where(has_a, from_a, 0.0))

    return below_and_above, above_and_below


def row_next(v):
    return pltpu.roll(v, 2 * ROWS - 1, 0)


def row_prev(v):
    return pltpu.roll(v, 1, 0)


def col_next(v):
    return pltpu.roll(v, v.shape[1] - 1, 1)


def col_prev(v):
    return pltpu.roll(v, 1, 1)


def horizontal(g0, g1, e_row, e_col, e_half):
    g0n, g1n = row_next(g0), col_next(g1)
    f = e_half * (g1n - col_prev(g1))
    h = e_half * (g0n - row_prev(g0))
    flux = e_row * (g0 - g0n)
    out0 = flux - row_next(f) - row_prev(flux - f)
    flux = e_col * (g0 - col_next(g0))
    out0 = out0 + (flux - col_prev(flux))
    flux = (4.0 * e_col) * (g1 - g1n)
    out1 = flux - col_next(h) - col_prev(flux - h)
    flux = (0.25 * e_row) * (g1 - row_next(g1))
    out1 = out1 + (flux - row_prev(flux))
    return out0, out1


def main_kernel(
    rhs, eta, friction, ice, grounded, strip_a, strip_b,
    powers, sums, ribbon,
    field_a, field_b, eta_row, eta_col, eta_half, eta_up, cover, drag,
):
    layers = eta.shape[0]
    plane = own_planes(rhs, eta, friction, ice, grounded)
    below_and_above, above_and_below = beyond()
    lane = lax.broadcasted_iota(jnp.int32, (2 * ROWS, LANES), 1)

    def target(p):
        if p < 2 * layers:
            return field_a.at[p // layers, p % layers]
        if p < 3 * layers:
            return eta_half.at[p - 2 * layers]
        return cover if p == 3 * layers else drag

    strips = [jnp.zeros((2 * ROWS, LANES), jnp.float32) for _ in range(ribbon.shape[0])]
    for q in range(strip_a.shape[0] // 2):
        first, second = pair_of(q, layers)
        halves = ([], [])
        for half in range(2):
            from_a, from_b = strip_a[2 * q + half], strip_b[2 * q + half]
            halves[0].append(below_and_above(from_a, from_b))
            halves[1].append(pltpu.roll(above_and_below(from_a, from_b), HALO, 0))
        for p, halo in zip((first, second), halves):
            v = plane(p)
            dst = target(p)
            dst[0:ROWS, :] = v
            dst[ROWS:, 0:LANES], dst[ROWS:, LANES:] = halo
            head = jnp.concatenate([v[:, :LANES], halo[0]], 0)
            tail = jnp.concatenate([v[:, LANES:], halo[1]], 0)
            tile, slots = ribbon_places(p, layers)
            for slot in slots:
                at = slot * SLOT
                strips[tile] = jnp.where(between(lane, at, 8), turned(tail, at + 8), strips[tile])
                strips[tile] = jnp.where(between(lane, at + 20, 8), turned(head, at + 20), strips[tile])
    for tile, v in enumerate(strips):
        ribbon[tile] = v

    for k in range(layers):
        e = eta_half[k]
        eta_row[k] = 2.0 * (e + row_next(e))
        eta_col[k] = 0.5 * (e + col_next(e))
        eta_up[k] = e + eta_half[k + 1] if k + 1 < layers else jnp.zeros_like(e)
        if k:
            eta_half[k - 1] = 0.5 * eta_half[k - 1]
    eta_half[layers - 1] = 0.5 * eta_half[layers - 1]

    def apply(t, src, dst):
        def layer(k, carry):
            below0, below1, odd, even = carry
            g0, g1 = src[0, k], src[1, k]
            after = jnp.minimum(k + 1, layers - 1)
            e_up = eta_up[k]
            up0 = e_up * (g0 - src[0, after])
            up1 = e_up * (g1 - src[1, after])
            out0, out1 = horizontal(g0, g1, eta_row[k], eta_col[k], eta_half[k])
            m = cover[...]
            out0, out1 = m * (out0 + (up0 - below0)), m * (out1 + (up1 - below1))
            if t < STEPS:
                dst[0, k], dst[1, k] = out0, out1
            for c, g, out in ((0, g0, out0), (1, g1, out1)):
                now = out[:ROWS]
                powers[t - 1, c, k] = now
                odd = odd + g[:ROWS] * now
                even = even + now * now
            return up0, up1, odd, even

        def block(b, carry):
            for i in range(UNROLL):
                carry = layer(b * UNROLL + i, carry)
            return carry

        zero = jnp.zeros((ROWS, 2 * LANES), jnp.float32)
        d = drag[...]
        start = (-d * src[0, 0], -d * src[1, 0], zero, zero)
        return lax.fori_loop(0, layers // UNROLL, block, start)[2:]

    bare = 1.0 - ice[...].astype(jnp.float32)
    whole = jnp.zeros((ROWS, 2 * LANES), jnp.float32)
    outside = jnp.zeros((ROWS, 2 * LANES), jnp.float32)
    for c in range(2):
        for k in range(layers):
            square = rhs[c, k] * rhs[c, k]
            whole = whole + square
            outside = outside + bare * square
    sums[0] = whole
    wide = lax.broadcasted_iota(jnp.int32, (ROWS, 2 * LANES), 1)
    inner = between(wide, HALO, 2 * LANES - 2 * HALO)
    src, dst = field_a, field_b
    for t in range(1, STEPS + 1):
        odd, even = apply(t, src, dst)
        sums[2 * t - 1] = jnp.where(inner, odd, 0.0) + outside
        sums[2 * t] = jnp.where(inner, even, 0.0) + outside
        src, dst = dst, src


def ribbon_kernel(ribbon, columns, columns_a, columns_b, sums, edges, moments):
    tiles = edges.shape[2]
    below_and_above, _ = beyond()
    lane = lax.broadcasted_iota(jnp.int32, (2 * ROWS, LANES), 1)

    def whole(tile):
        side = jnp.concatenate([columns[tile], below_and_above(columns_a[tile], columns_b[tile])], 0)
        return ribbon[tile] + side

    field = [[whole(c * tiles + n) for n in range(tiles)] for c in range(2)]
    eta = [whole(2 * tiles + n) for n in range(tiles)]
    cover, drag = whole(3 * tiles), whole(3 * tiles + 1)

    def after(v):
        return v[1:] + [turned(v[0], -SLOT)]

    eta_row = [2.0 * (e + row_next(e)) for e in eta]
    eta_col = [0.5 * (e + col_next(e)) for e in eta]
    eta_half = [0.5 * e for e in eta]
    eta_up = [e + n for e, n in zip(eta, after(eta))]
    eta_up[-1] = jnp.where(lane < LANES - SLOT, eta_up[-1], 0.0)
    place = lax.broadcasted_iota(jnp.int32, (ROWS, LANES), 1) % SLOT
    edge = between(place, 4, HALO) | between(place, 20, HALO)
    extra = [None]
    for t in range(1, STEPS + 1):
        ups = [[u * (g - n) for u, g, n in zip(eta_up, field[c], after(field[c]))] for c in range(2)]
        result = ([], [])
        odd = even = jnp.zeros((ROWS, LANES), jnp.float32)
        for n in range(tiles):
            outs = horizontal(field[0][n], field[1][n], eta_row[n], eta_col[n], eta_half[n])
            for c in range(2):
                below = ups[c][n - 1] if n else turned(ups[c][-1], SLOT) - drag * field[c][0]
                out = cover * (outs[c] + (ups[c][n] - below))
                result[c].append(out)
                now = out[:ROWS]
                edges[t - 1, c, n] = now
                odd = odd + field[c][n][:ROWS] * now
                even = even + now * now
        field = result
        extra.extend([jnp.where(edge, odd, 0.0), jnp.where(edge, even, 0.0)])

    tall = lax.broadcasted_iota(jnp.int32, (2 * ROWS, LANES), 0)
    high = jnp.zeros((2 * ROWS, LANES), jnp.float32)
    low = jnp.zeros((2 * ROWS, LANES), jnp.float32)
    for j, more in enumerate(extra):
        total = sums[j]
        pair = two_sum(total[:, :LANES], total[:, LANES:])
        if more is not None:
            pair = join(pair, (more, jnp.zeros_like(more)))
        for step in (4, 2, 1):
            pair = join(pair, tuple(pltpu.roll(v, step, 0) for v in pair))
        high = jnp.where(tall == j, jnp.concatenate([pair[0]] * 2, 0), high)
        low = jnp.where(tall == j, jnp.concatenate([pair[1]] * 2, 0), low)
    moments[0] = high
    moments[1] = low


def add_kernel(*refs):
    *ins, out = refs
    total = (ins[0][0], ins[0][1])
    for x in ins[1:]:
        total = join(total, (x[0], x[1]))
    out[0], out[1] = total


def solve(total):
    for step in (64, 32, 16, 8, 4, 2, 1):
        total = join(total, tuple(pltpu.roll(v, step, 1) for v in total))

    def spread(v, j):
        return jnp.broadcast_to(v[j : j + 1], (ROWS, LANES))

    centre = spread(total[0], 1) / spread(total[0], 0)
    wide = jnp.concatenate([centre, centre], 0)
    mu = [spread(total[0], 0)]
    for _ in range(2 * STEPS):
        step = times(wide, total)
        total = join(tuple(pltpu.roll(v, 2 * ROWS - 1, 0) for v in total), (-step[0], -step[1]))
        mu.append(spread(total[0], 0))

    def plus(a, b):
        n = max(len(a), len(b))
        return [a[i] + b[i] if i < min(len(a), len(b)) else (a[i] if i < len(a) else b[i]) for i in range(n)]

    def scaled(s, a):
        return [s * x for x in a]

    def operator(a):
        return plus([centre * x for x in a], [jnp.zeros_like(centre)] + a)

    def dot(a, b):
        square = [None] * (len(a) + len(b) - 1)
        for i, x in enumerate(a):
            for j, y in enumerate(b):
                z = x * y
                square[i + j] = z if square[i + j] is None else square[i + j] + z
        value = square[0] * mu[0]
        for n in range(1, len(square)):
            value = value + square[n] * mu[n]
        return value

    one = jnp.ones_like(centre)
    right = [one]
    quasi, search, update, iterate = right, right, [], []
    applied = operator(search)
    carried = applied
    rho = mu[0]
    tau_sq = rho
    alpha = theta_sq = eta = None
    for half in range(STEPS):
        if half % 2 == 0:
            alpha = rho / dot(carried, right)
            search_next = plus(search, scaled(-alpha, carried))
        quasi = plus(quasi, scaled(-alpha, applied))
        if half:
            update = plus(search, scaled(theta_sq / alpha * eta, update))
        else:
            update = search
        theta_sq = dot(quasi, quasi) / tau_sq
        cosine_sq = 1.0 / (1.0 + theta_sq)
        tau_sq = tau_sq * theta_sq * cosine_sq
        eta = cosine_sq * alpha
        iterate = plus(iterate, scaled(eta, update))
        if half % 2 == 0:
            search = search_next
            applied = operator(search)
        elif half < STEPS - 1:
            rho_next = dot(quasi, right)
            beta = rho_next / rho
            search = plus(quasi, scaled(beta, search))
            applied_next = operator(search)
            carried = plus(applied_next, scaled(beta, plus(applied, scaled(beta, carried))))
            applied, rho = applied_next, rho_next
    powers = [iterate[-1]]
    for c in iterate[-2::-1]:
        powers = plus([c] + powers, scaled(-centre, powers))
    return powers


def final_kernel(rhs, powers, edges, friction, ice, grounded, speed, *rest):
    *parts, iterate, residual, hessian = rest
    layers, tiles = rhs.shape[1], edges.shape[2]
    total = (parts[0][0], parts[0][1])
    for x in parts[1:]:
        total = join(total, (x[0], x[1]))
    factors = solve(total)
    wide = [jnp.concatenate([c, c], 1) for c in factors]
    rest = sum(wide[1:], wide[0])
    cover = ice[...].astype(jnp.float32)
    lane = lax.broadcasted_iota(jnp.int32, (ROWS, LANES), 1)

    def combined(vectors, weights):
        x = weights[1] * vectors[0]
        y = weights[0] * vectors[0]
        for t in range(1, STEPS):
            if t + 1 < STEPS:
                x = x + weights[t + 1] * vectors[t]
            y = y + weights[t] * vectors[t]
        return x, y

    for c in range(2):
        side = [combined([edges[t, c, n] for t in range(STEPS)], factors) for n in range(tiles)]
        for k in range(layers):
            at = k // tiles * SLOT
            inner = combined([powers[t, c, k] for t in range(STEPS)], wide)
            patched = []
            for v, e in zip(inner, side[k % tiles]):
                head = jnp.where(lane < HALO, turned(e, -at - 20), v[:, :LANES])
                tail = jnp.where(lane >= LANES - HALO, turned(e, 120 - at), v[:, LANES:])
                patched.append(jnp.concatenate([head, tail], 1))
            r = rhs[c, k]
            x, y = patched
            iterate[c, k] = jnp.where(cover > 0.0, wide[0] * r + x, rest * r)
            residual[c, k] = r - jnp.where(cover > 0.0, y, rest * r)
    weight = cover * (friction[...] * grounded[...].astype(jnp.float32))
    hessian[...] = weight * (speed[0] * iterate[0, 0] + speed[1] * iterate[1, 0])


def exchange(x, axis):
    count = lax.axis_size(axis)
    stride = 1
    rounds = []
    while stride < count:
        size = 4 if (count // stride) % 4 == 0 else 2
        rounds.append((stride, size))
        stride *= size
    for at, (stride, size) in enumerate(rounds):
        parts = [x]
        for turn in range(1, size):
            pairs = []
            for i in range(count):
                place = (i // stride) % size
                pairs.append((i, i + ((place ^ turn) - place) * stride))
            parts.append(lax.ppermute(x, axis, pairs))
        if at == len(rounds) - 1:
            return parts
        x = call(add_kernel, [x.shape])(*parts)[0]
    return [x]


def body(adjoint_rhs, viscosity, friction, ice_mask, grounded, basal_velocity):
    layers = viscosity.shape[0]
    inputs = (adjoint_rhs, viscosity, friction, ice_mask, grounded, basal_velocity)
    tile = (ROWS, LANES)
    strips = (2 * (layers + layers // 2 + 1),) + tile
    ribbons = (ribbon_tiles(layers),) + tile
    *held, column_a, column_b, strip_a, strip_b = call(
        pack_kernel,
        [jax.ShapeDtypeStruct(x.shape, x.dtype) for x in inputs] + [ribbons, ribbons, strips, strips],
        [pltpu.SemaphoreType.DMA((len(inputs),))],
        in_specs=[pl.BlockSpec(memory_space=pltpu.HBM)] * len(inputs),
    )(*[pltpu.with_memory_space_constraint(x, pltpu.HBM) for x in inputs])
    strip_a, strip_b = swapped(strip_a, "gx", 0), swapped(strip_b, "gx", 1)
    beside = ("gy", "gz")
    (columns,) = call(beside_kernel, [ribbons])(swapped(column_a, beside, 0), swapped(column_b, beside, 1))
    columns_a, columns_b = swapped(columns, "gx", 0), swapped(columns, "gx", 1)
    block = (layers, 2 * ROWS, 2 * LANES)
    powers, sums, ribbon = call(
        main_kernel,
        [(STEPS,) + adjoint_rhs.shape, (2 * STEPS + 1, ROWS, 2 * LANES), (ribbons[0], 2 * ROWS, LANES)],
        [(2,) + block] * 2 + [block] * 4 + [block[1:]] * 2,
        cost_estimate=pl.CostEstimate(flops=200_000_000, bytes_accessed=8_000_000, transcendentals=0),
    )(*held[:5], strip_a, strip_b)
    edges, sums = call(
        ribbon_kernel,
        [(STEPS, 2, layers // 4) + tile, (2, 2 * ROWS, LANES)],
    )(ribbon, columns, columns_a, columns_b, sums)
    parts = exchange(sums, ("gy", "gz"))
    if len(parts) > 1:
        sums = call(add_kernel, [sums.shape])(*parts)[0]
    parts = exchange(sums, "gx")
    rhs, _, friction, ice_mask, grounded, speed = held
    return tuple(
        call(final_kernel, [adjoint_rhs.shape, adjoint_rhs.shape, friction.shape])(
            rhs, powers, edges, friction, ice_mask, grounded, speed, *parts
        )
    )


def solution(mesh):
    in_specs = (
        P(None, None, ("parts", "gx"), ("gy", "gz")),
        P(None, ("parts", "gx"), ("gy", "gz")),
        P(("parts", "gx"), ("gy", "gz")),
        P(("parts", "gx"), ("gy", "gz")),
        P(("parts", "gx"), ("gy", "gz")),
        P(None, ("parts", "gx"), ("gy", "gz")),
    )
    out_specs = (
        P(None, None, ("parts", "gx"), ("gy", "gz")),
        P(None, None, ("parts", "gx"), ("gy", "gz")),
        P(("parts", "gx"), ("gy", "gz")),
    )
    return jax.shard_map(body, mesh=mesh, in_specs=in_specs, out_specs=out_specs, check_vma=False)
```

```python
import functools

import jax
import jax.numpy as jnp
from jax import lax
from jax.experimental import pallas as pl
from jax.experimental.pallas import tpu as pltpu
from jax.sharding import PartitionSpec as P

STEPS = 4
HALO = 4
ROWS = 8
LANES = 128
UNROLL = 10
SLOT = 32


def call(kernel, outs, scratch=(), **more):
    return pl.pallas_call(
        kernel,
        out_shape=[jax.ShapeDtypeStruct(s, jnp.float32) if isinstance(s, tuple) else s for s in outs],
        scratch_shapes=[pltpu.VMEM(s, jnp.float32) if isinstance(s, tuple) else s for s in scratch],
        compiler_params=pltpu.CompilerParams(vmem_limit_bytes=40 * 1024 * 1024),
        **more,
    )


def place_of(axis):
    place, count = lax.axis_index(axis), lax.axis_size(axis)
    even = place % 2 == 0
    has_a = jnp.logical_or(jnp.logical_not(even), place < count - 1)
    has_b = jnp.where(even, place > 0, place < count - 1)
    return even, has_a, has_b


def swapped(x, axis, first):
    count = lax.axis_size(axis)
    pairs = []
    for i in range(count):
        other = i + 1 if (i - first) % 2 == 0 else i - 1
        pairs.append((i, other if 0 <= other < count else i))
    return lax.ppermute(x, axis, pairs)


def own_planes(rhs, eta, friction, ice, grounded):
    layers = eta.shape[0]
    cover = ice[...].astype(jnp.float32)
    drag = friction[...] * grounded[...].astype(jnp.float32)

    def plane(p):
        if p < 2 * layers:
            return rhs[p // layers, p % layers] * cover
        if p < 3 * layers:
            return eta[p - 2 * layers]
        return cover if p == 3 * layers else drag

    return plane


def pair_of(q, layers):
    if q < layers:
        return q, q + layers
    if q < layers + layers // 2:
        return q + layers, q + layers + layers // 2
    return 3 * layers, 3 * layers + 1


def ribbon_places(p, layers):
    tiles = layers // 4
    if p < 3 * layers:
        k = p % layers
        return p // layers * tiles + k % tiles, (k // tiles,)
    return (3 * tiles, (0, 1, 2, 3)) if p == 3 * layers else (3 * tiles + 1, (0,))


def ribbon_tiles(layers):
    return 3 * (layers // 4) + 2


def between(lane, first, width):
    return (lane >= first) & (lane < first + width)


def turned(v, shift):
    shift = shift % LANES
    return pltpu.roll(v, shift, 1) if shift else v


def pack_kernel(*refs):
    sources, held, (strip_a, strip_b, arrived) = refs[:6], refs[6:12], refs[12:]
    copies = [pltpu.make_async_copy(a, b, arrived.at[i]) for i, (a, b) in enumerate(zip(sources, held))]
    for copy in copies:
        copy.start()
    for copy in copies:
        copy.wait()
    rhs, eta, friction, ice, grounded, _ = held
    layers = eta.shape[0]
    plane = own_planes(rhs, eta, friction, ice, grounded)
    row = lax.broadcasted_iota(jnp.int32, (ROWS, LANES), 0)
    rows_even, _, _ = place_of("gx")
    upper_a = (row < HALO) != rows_even
    for q in range(strip_a.shape[0] // 2):
        first, second = pair_of(q, layers)
        x, y = plane(first), plane(second)
        for half in range(2):
            xs = x[:, half * LANES : (half + 1) * LANES]
            ys = y[:, half * LANES : (half + 1) * LANES]
            ys = pltpu.roll(ys, HALO, 0)
            strip_a[2 * q + half] = jnp.where(upper_a, xs, ys)
            strip_b[2 * q + half] = jnp.where(upper_a, ys, xs)


def beyond(strip_a, strip_b):
    even, has_a, has_b = place_of("gx")
    upper_a = (lax.broadcasted_iota(jnp.int32, (ROWS, LANES), 0) < HALO) == even

    def halos(q):
        first, second = [], []
        for half in range(2):
            from_a = jnp.where(has_a, strip_a[2 * q + half], 0.0)
            from_b = jnp.where(has_b, strip_b[2 * q + half], 0.0)
            first.append(jnp.where(upper_a, from_a, from_b))
            second.append(pltpu.roll(jnp.where(upper_a, from_b, from_a), HALO, 0))
        return first, second

    return halos


def edge_kernel(rhs, eta, friction, ice, grounded, strip_a, strip_b, ribbon, column_a, column_b):
    layers = eta.shape[0]
    plane = own_planes(rhs, eta, friction, ice, grounded)
    halos = beyond(strip_a, strip_b)
    lane = lax.broadcasted_iota(jnp.int32, (2 * ROWS, LANES), 1)
    even, _, _ = place_of(("gy", "gz"))
    zero = jnp.zeros((2 * ROWS, LANES), jnp.float32)
    own = [zero] * ribbon.shape[0]
    left, right = list(own), list(own)
    for q in range(strip_a.shape[0] // 2):
        for p, halo in zip(pair_of(q, layers), halos(q)):
            v = plane(p)
            head = jnp.concatenate([v[:, :LANES], halo[0]], 0)
            tail = jnp.concatenate([v[:, LANES:], halo[1]], 0)
            tile, slots = ribbon_places(p, layers)
            for slot in slots:
                at = slot * SLOT
                own[tile] = jnp.where(between(lane, at, 8), turned(tail, at + 8), own[tile])
                own[tile] = jnp.where(between(lane, at + 20, 8), turned(head, at + 20), own[tile])
                left[tile] = jnp.where(between(lane, at + 8, 4), turned(head, at + 8), left[tile])
                right[tile] = jnp.where(between(lane, at + 16, 4), turned(tail, at + 20), right[tile])
    for tile in range(ribbon.shape[0]):
        ribbon[tile] = own[tile]
        column_a[tile] = jnp.where(even, right[tile], left[tile])
        column_b[tile] = jnp.where(even, left[tile], right[tile])


def two_sum(a, b):
    s = a + b
    t = s - a
    return s, (a - (s - t)) + (b - t)


def join(x, y):
    s, e = two_sum(x[0], y[0])
    e = e + (x[1] + y[1])
    h = s + e
    return h, e - (h - s)


def times(scalar, x):
    def cut(v):
        t = v * 4097.0
        h = t - (t - v)
        return h, v - h

    p = scalar * x[0]
    sh, sl = cut(scalar)
    xh, xl = cut(x[0])
    e = ((sh * xh - p) + sh * xl + sl * xh) + sl * xl
    return p, e + scalar * x[1]


def row_next(v):
    return pltpu.roll(v, 2 * ROWS - 1, 0)


def row_prev(v):
    return pltpu.roll(v, 1, 0)


def col_next(v):
    return pltpu.roll(v, v.shape[1] - 1, 1)


def col_prev(v):
    return pltpu.roll(v, 1, 1)


def horizontal(g0, g1, e_row, e_col, e_half):
    g0n, g1n = row_next(g0), col_next(g1)
    f = e_half * (g1n - col_prev(g1))
    h = e_half * (g0n - row_prev(g0))
    flux = e_row * (g0 - g0n)
    out0 = flux - row_next(f) - row_prev(flux - f)
    flux = e_col * (g0 - col_next(g0))
    out0 = out0 + (flux - col_prev(flux))
    flux = (4.0 * e_col) * (g1 - g1n)
    out1 = flux - col_next(h) - col_prev(flux - h)
    flux = (0.25 * e_row) * (g1 - row_next(g1))
    out1 = out1 + (flux - row_prev(flux))
    return out0, out1


def main_kernel(
    rhs, eta, friction, ice, grounded, strip_a, strip_b,
    powers, sums,
    field_a, field_b, eta_row, eta_col, eta_half, eta_up, cover, drag,
):
    layers = eta.shape[0]
    plane = own_planes(rhs, eta, friction, ice, grounded)
    halos = beyond(strip_a, strip_b)

    def target(p):
        if p < 2 * layers:
            return field_a.at[p // layers, p % layers]
        if p < 3 * layers:
            return eta_half.at[p - 2 * layers]
        return cover if p == 3 * layers else drag

    for q in range(strip_a.shape[0] // 2):
        for p, halo in zip(pair_of(q, layers), halos(q)):
            dst = target(p)
            dst[0:ROWS, :] = plane(p)
            dst[ROWS:, 0:LANES], dst[ROWS:, LANES:] = halo

    for k in range(layers):
        e = eta_half[k]
        eta_row[k] = 2.0 * (e + row_next(e))
        eta_col[k] = 0.5 * (e + col_next(e))
        eta_up[k] = e + eta_half[k + 1] if k + 1 < layers else jnp.zeros_like(e)
        if k:
            eta_half[k - 1] = 0.5 * eta_half[k - 1]
    eta_half[layers - 1] = 0.5 * eta_half[layers - 1]

    def apply(t, src, dst):
        def layer(k, carry):
            below0, below1, odd, even = carry
            g0, g1 = src[0, k], src[1, k]
            after = jnp.minimum(k + 1, layers - 1)
            e_up = eta_up[k]
            up0 = e_up * (g0 - src[0, after])
            up1 = e_up * (g1 - src[1, after])
            out0, out1 = horizontal(g0, g1, eta_row[k], eta_col[k], eta_half[k])
            m = cover[...]
            out0, out1 = m * (out0 + (up0 - below0)), m * (out1 + (up1 - below1))
            if t < STEPS:
                dst[0, k], dst[1, k] = out0, out1
            for c, g, out in ((0, g0, out0), (1, g1, out1)):
                now = out[:ROWS]
                powers[t - 1, c, k] = now
                odd = odd + g[:ROWS] * now
                even = even + now * now
            return up0, up1, odd, even

        def block(b, carry):
            for i in range(UNROLL):
                carry = layer(b * UNROLL + i, carry)
            return carry

        zero = jnp.zeros((ROWS, 2 * LANES), jnp.float32)
        d = drag[...]
        start = (-d * src[0, 0], -d * src[1, 0], zero, zero)
        return lax.fori_loop(0, layers // UNROLL, block, start)[2:]

    bare = 1.0 - ice[...].astype(jnp.float32)
    whole = jnp.zeros((ROWS, 2 * LANES), jnp.float32)
    outside = jnp.zeros((ROWS, 2 * LANES), jnp.float32)
    for c in range(2):
        for k in range(layers):
            square = rhs[c, k] * rhs[c, k]
            whole = whole + square
            outside = outside + bare * square
    sums[0] = whole
    wide = lax.broadcasted_iota(jnp.int32, (ROWS, 2 * LANES), 1)
    inner = between(wide, HALO, 2 * LANES - 2 * HALO)
    src, dst = field_a, field_b
    for t in range(1, STEPS + 1):
        odd, even = apply(t, src, dst)
        sums[2 * t - 1] = jnp.where(inner, odd, 0.0) + outside
        sums[2 * t] = jnp.where(inner, even, 0.0) + outside
        src, dst = dst, src


def ribbon_kernel(ribbon, column_a, column_b, sums, edges, moments):
    tiles = edges.shape[2]
    _, has_a, has_b = place_of(("gy", "gz"))
    lane = lax.broadcasted_iota(jnp.int32, (2 * ROWS, LANES), 1)

    def whole(tile):
        return ribbon[tile] + jnp.where(has_a, column_a[tile], 0.0) + jnp.where(has_b, column_b[tile], 0.0)

    field = [[whole(c * tiles + n) for n in range(tiles)] for c in range(2)]
    eta = [whole(2 * tiles + n) for n in range(tiles)]
    cover, drag = whole(3 * tiles), whole(3 * tiles + 1)

    def after(v):
        return v[1:] + [turned(v[0], -SLOT)]

    eta_row = [2.0 * (e + row_next(e)) for e in eta]
    eta_col = [0.5 * (e + col_next(e)) for e in eta]
    eta_half = [0.5 * e for e in eta]
    eta_up = [e + n for e, n in zip(eta, after(eta))]
    eta_up[-1] = jnp.where(lane < LANES - SLOT, eta_up[-1], 0.0)
    place = lax.broadcasted_iota(jnp.int32, (ROWS, LANES), 1) % SLOT
    edge = between(place, 4, HALO) | between(place, 20, HALO)
    extra = [None]
    for t in range(1, STEPS + 1):
        ups = [[u * (g - n) for u, g, n in zip(eta_up, field[c], after(field[c]))] for c in range(2)]
        result = ([], [])
        odd = even = jnp.zeros((ROWS, LANES), jnp.float32)
        for n in range(tiles):
            outs = horizontal(field[0][n], field[1][n], eta_row[n], eta_col[n], eta_half[n])
            for c in range(2):
                below = ups[c][n - 1] if n else turned(ups[c][-1], SLOT) - drag * field[c][0]
                out = cover * (outs[c] + (ups[c][n] - below))
                result[c].append(out)
                now = out[:ROWS]
                edges[t - 1, c, n] = now
                odd = odd + field[c][n][:ROWS] * now
                even = even + now * now
        field = result
        extra.extend([jnp.where(edge, odd, 0.0), jnp.where(edge, even, 0.0)])

    tall = lax.broadcasted_iota(jnp.int32, (2 * ROWS, LANES), 0)
    high = jnp.zeros((2 * ROWS, LANES), jnp.float32)
    low = jnp.zeros((2 * ROWS, LANES), jnp.float32)
    for j, more in enumerate(extra):
        total = sums[j]
        pair = two_sum(total[:, :LANES], total[:, LANES:])
        if more is not None:
            pair = join(pair, (more, jnp.zeros_like(more)))
        for step in (4, 2, 1):
            pair = join(pair, tuple(pltpu.roll(v, step, 0) for v in pair))
        high = jnp.where(tall == j, jnp.concatenate([pair[0]] * 2, 0), high)
        low = jnp.where(tall == j, jnp.concatenate([pair[1]] * 2, 0), low)
    moments[0] = high
    moments[1] = low


def add_kernel(*refs):
    *ins, out = refs
    total = (ins[0][0], ins[0][1])
    for x in ins[1:]:
        total = join(total, (x[0], x[1]))
    out[0], out[1] = total


def solve(total):
    for step in (64, 32, 16, 8, 4, 2, 1):
        total = join(total, tuple(pltpu.roll(v, step, 1) for v in total))

    def spread(v, j):
        return jnp.broadcast_to(v[j : j + 1], (ROWS, LANES))

    centre = spread(total[0], 1) / spread(total[0], 0)
    wide = jnp.concatenate([centre, centre], 0)
    mu = [spread(total[0], 0)]
    for _ in range(2 * STEPS):
        step = times(wide, total)
        total = join(tuple(pltpu.roll(v, 2 * ROWS - 1, 0) for v in total), (-step[0], -step[1]))
        mu.append(spread(total[0], 0))

    def plus(a, b):
        n = max(len(a), len(b))
        return [a[i] + b[i] if i < min(len(a), len(b)) else (a[i] if i < len(a) else b[i]) for i in range(n)]

    def scaled(s, a):
        return [s * x for x in a]

    def operator(a):
        return plus([centre * x for x in a], [jnp.zeros_like(centre)] + a)

    def dot(a, b):
        square = [None] * (len(a) + len(b) - 1)
        for i, x in enumerate(a):
            for j, y in enumerate(b):
                z = x * y
                square[i + j] = z if square[i + j] is None else square[i + j] + z
        value = square[0] * mu[0]
        for n in range(1, len(square)):
            value = value + square[n] * mu[n]
        return value

    one = jnp.ones_like(centre)
    right = [one]
    quasi, search, update, iterate = right, right, [], []
    applied = operator(search)
    carried = applied
    rho = mu[0]
    tau_sq = rho
    alpha = theta_sq = eta = None
    for half in range(STEPS):
        if half % 2 == 0:
            alpha = rho / dot(carried, right)
            search_next = plus(search, scaled(-alpha, carried))
        quasi = plus(quasi, scaled(-alpha, applied))
        if half:
            update = plus(search, scaled(theta_sq / alpha * eta, update))
        else:
            update = search
        theta_sq = dot(quasi, quasi) / tau_sq
        cosine_sq = 1.0 / (1.0 + theta_sq)
        tau_sq = tau_sq * theta_sq * cosine_sq
        eta = cosine_sq * alpha
        iterate = plus(iterate, scaled(eta, update))
        if half % 2 == 0:
            search = search_next
            applied = operator(search)
        elif half < STEPS - 1:
            rho_next = dot(quasi, right)
            beta = rho_next / rho
            search = plus(quasi, scaled(beta, search))
            applied_next = operator(search)
            carried = plus(applied_next, scaled(beta, plus(applied, scaled(beta, carried))))
            applied, rho = applied_next, rho_next
    powers = [iterate[-1]]
    for c in iterate[-2::-1]:
        powers = plus([c] + powers, scaled(-centre, powers))
    return powers


def final_kernel(rhs, powers, edges, friction, ice, grounded, speed, *rest):
    *parts, iterate, residual, hessian = rest
    layers, tiles = rhs.shape[1], edges.shape[2]
    total = (parts[0][0], parts[0][1])
    for x in parts[1:]:
        total = join(total, (x[0], x[1]))
    factors = solve(total)
    wide = [jnp.concatenate([c, c], 1) for c in factors]
    rest = sum(wide[1:], wide[0])
    cover = ice[...].astype(jnp.float32)
    lane = lax.broadcasted_iota(jnp.int32, (ROWS, LANES), 1)

    def combined(vectors, weights):
        x = weights[1] * vectors[0]
        y = weights[0] * vectors[0]
        for t in range(1, STEPS):
            if t + 1 < STEPS:
                x = x + weights[t + 1] * vectors[t]
            y = y + weights[t] * vectors[t]
        return x, y

    for c in range(2):
        side = [combined([edges[t, c, n] for t in range(STEPS)], factors) for n in range(tiles)]
        for k in range(layers):
            at = k // tiles * SLOT
            inner = combined([powers[t, c, k] for t in range(STEPS)], wide)
            patched = []
            for v, e in zip(inner, side[k % tiles]):
                head = jnp.where(lane < HALO, turned(e, -at - 20), v[:, :LANES])
                tail = jnp.where(lane >= LANES - HALO, turned(e, 120 - at), v[:, LANES:])
                patched.append(jnp.concatenate([head, tail], 1))
            r = rhs[c, k]
            x, y = patched
            iterate[c, k] = jnp.where(cover > 0.0, wide[0] * r + x, rest * r)
            residual[c, k] = r - jnp.where(cover > 0.0, y, rest * r)
    weight = cover * (friction[...] * grounded[...].astype(jnp.float32))
    hessian[...] = weight * (speed[0] * iterate[0, 0] + speed[1] * iterate[1, 0])


def exchange(x, axis):
    count = lax.axis_size(axis)
    stride = 1
    rounds = []
    while stride < count:
        size = 4 if (count // stride) % 4 == 0 else 2
        rounds.append((stride, size))
        stride *= size
    for at, (stride, size) in enumerate(rounds):
        parts = [x]
        for turn in range(1, size):
            pairs = []
            for i in range(count):
                place = (i // stride) % size
                pairs.append((i, i + ((place ^ turn) - place) * stride))
            parts.append(lax.ppermute(x, axis, pairs))
        if at == len(rounds) - 1:
            return parts
        x = call(add_kernel, [x.shape])(*parts)[0]
    return [x]


def body(adjoint_rhs, viscosity, friction, ice_mask, grounded, basal_velocity):
    layers = viscosity.shape[0]
    inputs = (adjoint_rhs, viscosity, friction, ice_mask, grounded, basal_velocity)
    tile = (ROWS, LANES)
    strips = (2 * (layers + layers // 2 + 1),) + tile
    ribbons = (ribbon_tiles(layers), 2 * ROWS, LANES)
    *held, strip_a, strip_b = call(
        pack_kernel,
        [jax.ShapeDtypeStruct(x.shape, x.dtype) for x in inputs] + [strips, strips],
        [pltpu.SemaphoreType.DMA((len(inputs),))],
        in_specs=[pl.BlockSpec(memory_space=pltpu.HBM)] * len(inputs),
    )(*[pltpu.with_memory_space_constraint(x, pltpu.HBM) for x in inputs])
    strip_a, strip_b = swapped(strip_a, "gx", 0), swapped(strip_b, "gx", 1)
    fields = (*held[:5], strip_a, strip_b)
    ribbon, column_a, column_b = call(edge_kernel, [ribbons] * 3)(*fields)
    column_a, column_b = swapped(column_a, ("gy", "gz"), 0), swapped(column_b, ("gy", "gz"), 1)
    block = (layers, 2 * ROWS, 2 * LANES)
    powers, sums = call(
        main_kernel,
        [(STEPS,) + adjoint_rhs.shape, (2 * STEPS + 1, ROWS, 2 * LANES)],
        [(2,) + block] * 2 + [block] * 4 + [block[1:]] * 2,
        cost_estimate=pl.CostEstimate(flops=200_000_000, bytes_accessed=8_000_000, transcendentals=0),
    )(*fields)
    edges, sums = call(
        ribbon_kernel,
        [(STEPS, 2, layers // 4) + tile, (2, 2 * ROWS, LANES)],
    )(ribbon, column_a, column_b, sums)
    parts = exchange(sums, ("gy", "gz"))
    if len(parts) > 1:
        sums = call(add_kernel, [sums.shape])(*parts)[0]
    parts = exchange(sums, "gx")
    rhs, _, friction, ice_mask, grounded, speed = held
    return tuple(
        call(final_kernel, [adjoint_rhs.shape, adjoint_rhs.shape, friction.shape])(
            rhs, powers, edges, friction, ice_mask, grounded, speed, *parts
        )
    )


def solution(mesh):
    in_specs = (
        P(None, None, ("parts", "gx"), ("gy", "gz")),
        P(None, ("parts", "gx"), ("gy", "gz")),
        P(("parts", "gx"), ("gy", "gz")),
        P(("parts", "gx"), ("gy", "gz")),
        P(("parts", "gx"), ("gy", "gz")),
        P(None, ("parts", "gx"), ("gy", "gz")),
    )
    out_specs = (
        P(None, None, ("parts", "gx"), ("gy", "gz")),
        P(None, None, ("parts", "gx"), ("gy", "gz")),
        P(("parts", "gx"), ("gy", "gz")),
    )
    return jax.shard_map(body, mesh=mesh, in_specs=in_specs, out_specs=out_specs, check_vma=False)
```

```python
import functools

import jax
import jax.numpy as jnp
from jax import lax
from jax.experimental import pallas as pl
from jax.experimental.pallas import tpu as pltpu
from jax.sharding import PartitionSpec as P

STEPS = 4
HALO = 4
ROWS = 8
LANES = 128
UNROLL = 5
SLOT = 32


def call(kernel, outs, scratch=(), **more):
    return pl.pallas_call(
        kernel,
        out_shape=[jax.ShapeDtypeStruct(s, jnp.float32) if isinstance(s, tuple) else s for s in outs],
        scratch_shapes=[pltpu.VMEM(s, jnp.float32) if isinstance(s, tuple) else s for s in scratch],
        compiler_params=pltpu.CompilerParams(vmem_limit_bytes=40 * 1024 * 1024),
        **more,
    )


def place_of(axis):
    place, count = lax.axis_index(axis), lax.axis_size(axis)
    even = place % 2 == 0
    has_a = jnp.logical_or(jnp.logical_not(even), place < count - 1)
    has_b = jnp.where(even, place > 0, place < count - 1)
    return even, has_a, has_b


def swapped(x, axis, first):
    count = lax.axis_size(axis)
    pairs = []
    for i in range(count):
        other = i + 1 if (i - first) % 2 == 0 else i - 1
        pairs.append((i, other if 0 <= other < count else i))
    return lax.ppermute(x, axis, pairs)


def own_planes(rhs, eta, friction, ice, grounded):
    layers = eta.shape[0]
    cover = ice[...].astype(jnp.float32)
    drag = friction[...] * grounded[...].astype(jnp.float32)

    def plane(p):
        if p < 2 * layers:
            return rhs[p // layers, p % layers] * cover
        if p < 3 * layers:
            return eta[p - 2 * layers]
        return cover if p == 3 * layers else drag

    return plane


def pair_of(q, layers):
    if q < layers:
        return q, q + layers
    if q < layers + layers // 2:
        return q + layers, q + layers + layers // 2
    return 3 * layers, 3 * layers + 1


def ribbon_places(p, layers):
    tiles = layers // 4
    if p < 3 * layers:
        k = p % layers
        return p // layers * tiles + k % tiles, (k // tiles,)
    return (3 * tiles, (0, 1, 2, 3)) if p == 3 * layers else (3 * tiles + 1, (0,))


def ribbon_tiles(layers):
    return 3 * (layers // 4) + 2


def between(lane, first, width):
    return (lane >= first) & (lane < first + width)


def turned(v, shift):
    shift = shift % LANES
    return pltpu.roll(v, shift, 1) if shift else v


def pack_kernel(*refs):
    sources, held, (column_a, column_b, strip_a, strip_b, arrived) = refs[:6], refs[6:12], refs[12:]
    copies = [pltpu.make_async_copy(a, b, arrived.at[i]) for i, (a, b) in enumerate(zip(sources, held))]
    for copy in copies:
        copy.start()
    for copy in copies:
        copy.wait()
    rhs, eta, friction, ice, grounded, _ = held
    layers = eta.shape[0]
    plane = own_planes(rhs, eta, friction, ice, grounded)
    lane = lax.broadcasted_iota(jnp.int32, (ROWS, LANES), 1)
    row = lax.broadcasted_iota(jnp.int32, (ROWS, LANES), 0)
    rows_even, _, _ = place_of("gx")
    columns_even, _, _ = place_of(("gy", "gz"))
    upper_a = (row < HALO) != rows_even
    count = column_a.shape[0]
    left = [jnp.zeros((ROWS, LANES), jnp.float32) for _ in range(count)]
    right = [jnp.zeros((ROWS, LANES), jnp.float32) for _ in range(count)]
    for q in range(strip_a.shape[0] // 2):
        first, second = pair_of(q, layers)
        x, y = plane(first), plane(second)
        for half in range(2):
            xs = x[:, half * LANES : (half + 1) * LANES]
            ys = y[:, half * LANES : (half + 1) * LANES]
            ys = pltpu.roll(ys, HALO, 0)
            strip_a[2 * q + half] = jnp.where(upper_a, xs, ys)
            strip_b[2 * q + half] = jnp.where(upper_a, ys, xs)
        for p, v in ((first, x), (second, y)):
            tile, slots = ribbon_places(p, layers)
            for slot in slots:
                at = slot * SLOT
                left[tile] = jnp.where(between(lane, at + 8, 4), turned(v[:, :LANES], at + 8), left[tile])
                right[tile] = jnp.where(between(lane, at + 16, 4), turned(v[:, LANES:], at + 20), right[tile])
    for tile in range(count):
        column_a[tile] = jnp.where(columns_even, right[tile], left[tile])
        column_b[tile] = jnp.where(columns_even, left[tile], right[tile])


def beside_kernel(from_a, from_b, columns):
    _, has_a, has_b = place_of(("gy", "gz"))
    for tile in range(columns.shape[0]):
        columns[tile] = jnp.where(has_a, from_a[tile], 0.0) + jnp.where(has_b, from_b[tile], 0.0)


def two_sum(a, b):
    s = a + b
    t = s - a
    return s, (a - (s - t)) + (b - t)


def join(x, y):
    s, e = two_sum(x[0], y[0])
    e = e + (x[1] + y[1])
    h = s + e
    return h, e - (h - s)


def times(scalar, x):
    def cut(v):
        t = v * 4097.0
        h = t - (t - v)
        return h, v - h

    p = scalar * x[0]
    sh, sl = cut(scalar)
    xh, xl = cut(x[0])
    e = ((sh * xh - p) + sh * xl + sl * xh) + sl * xl
    return p, e + scalar * x[1]


def beyond():
    even, has_a, has_b = place_of("gx")
    upper_a = (lax.broadcasted_iota(jnp.int32, (ROWS, LANES), 0) < HALO) == even

    def below_and_above(from_a, from_b):
        return jnp.where(upper_a, jnp.where(has_a, from_a, 0.0), jnp.where(has_b, from_b, 0.0))

    def above_and_below(from_a, from_b):
        return jnp.where(upper_a, jnp.where(has_b, from_b, 0.0), jnp.where(has_a, from_a, 0.0))

    return below_and_above, above_and_below


def row_next(v):
    return pltpu.roll(v, 2 * ROWS - 1, 0)


def row_prev(v):
    return pltpu.roll(v, 1, 0)


def col_next(v):
    return pltpu.roll(v, v.shape[1] - 1, 1)


def col_prev(v):
    return pltpu.roll(v, 1, 1)


def horizontal(g0, g1, e_row, e_col, e_half):
    g0n, g1n = row_next(g0), col_next(g1)
    f = e_half * (g1n - col_prev(g1))
    h = e_half * (g0n - row_prev(g0))
    flux = e_row * (g0 - g0n)
    out0 = flux - row_next(f) - row_prev(flux - f)
    flux = e_col * (g0 - col_next(g0))
    out0 = out0 + (flux - col_prev(flux))
    flux = (4.0 * e_col) * (g1 - g1n)
    out1 = flux - col_next(h) - col_prev(flux - h)
    flux = (0.25 * e_row) * (g1 - row_next(g1))
    out1 = out1 + (flux - row_prev(flux))
    return out0, out1


def main_kernel(
    rhs, eta, friction, ice, grounded, strip_a, strip_b,
    powers, sums, ribbon,
    fields, eta_row, eta_col, eta_half, eta_up, cover, drag,
):
    layers = eta.shape[0]
    plane = own_planes(rhs, eta, friction, ice, grounded)
    below_and_above, above_and_below = beyond()
    lane = lax.broadcasted_iota(jnp.int32, (2 * ROWS, LANES), 1)

    def target(p):
        if p < 2 * layers:
            return fields.at[0, p // layers, p % layers]
        if p < 3 * layers:
            return eta_half.at[p - 2 * layers]
        return cover if p == 3 * layers else drag

    strips = [jnp.zeros((2 * ROWS, LANES), jnp.float32) for _ in range(ribbon.shape[0])]
    for q in range(strip_a.shape[0] // 2):
        first, second = pair_of(q, layers)
        halves = ([], [])
        for half in range(2):
            from_a, from_b = strip_a[2 * q + half], strip_b[2 * q + half]
            halves[0].append(below_and_above(from_a, from_b))
            halves[1].append(pltpu.roll(above_and_below(from_a, from_b), HALO, 0))
        for p, halo in zip((first, second), halves):
            v = plane(p)
            dst = target(p)
            dst[0:ROWS, :] = v
            dst[ROWS:, 0:LANES], dst[ROWS:, LANES:] = halo
            head = jnp.concatenate([v[:, :LANES], halo[0]], 0)
            tail = jnp.concatenate([v[:, LANES:], halo[1]], 0)
            tile, slots = ribbon_places(p, layers)
            for slot in slots:
                at = slot * SLOT
                strips[tile] = jnp.where(between(lane, at, 8), turned(tail, at + 8), strips[tile])
                strips[tile] = jnp.where(between(lane, at + 20, 8), turned(head, at + 20), strips[tile])
    for tile, v in enumerate(strips):
        ribbon[tile] = v

    for k in range(layers):
        e = eta_half[k]
        eta_row[k] = 2.0 * (e + row_next(e))
        eta_col[k] = 0.5 * (e + col_next(e))
        eta_up[k] = e + eta_half[k + 1] if k + 1 < layers else jnp.zeros_like(e)
        if k:
            eta_half[k - 1] = 0.5 * eta_half[k - 1]
    eta_half[layers - 1] = 0.5 * eta_half[layers - 1]

    def apply(t, carry):
        src, dst = fields.at[t % 2], fields.at[1 - t % 2]

        def layer(k, carry):
            below0, below1, odd, even = carry
            g0, g1 = src[0, k], src[1, k]
            after = jnp.minimum(k + 1, layers - 1)
            e_up = eta_up[k]
            up0 = e_up * (g0 - src[0, after])
            up1 = e_up * (g1 - src[1, after])
            out0, out1 = horizontal(g0, g1, eta_row[k], eta_col[k], eta_half[k])
            m = cover[...]
            out0, out1 = m * (out0 + (up0 - below0)), m * (out1 + (up1 - below1))
            dst[0, k], dst[1, k] = out0, out1
            for c, g, out in ((0, g0, out0), (1, g1, out1)):
                now = out[:ROWS]
                powers[t, c, k] = now
                odd = odd + g[:ROWS] * now
                even = even + now * now
            return up0, up1, odd, even

        def block(b, carry):
            for i in range(UNROLL):
                carry = layer(b * UNROLL + i, carry)
            return carry

        zero = jnp.zeros((ROWS, 2 * LANES), jnp.float32)
        d = drag[...]
        start = (-d * src[0, 0], -d * src[1, 0], zero, zero)
        _, _, odd, even = lax.fori_loop(0, layers // UNROLL, block, start)
        sums[2 * t + 1] = jnp.where(inner, odd, 0.0) + outside
        sums[2 * t + 2] = jnp.where(inner, even, 0.0) + outside
        return carry

    bare = 1.0 - ice[...].astype(jnp.float32)
    whole = jnp.zeros((ROWS, 2 * LANES), jnp.float32)
    outside = jnp.zeros((ROWS, 2 * LANES), jnp.float32)
    for c in range(2):
        for k in range(layers):
            square = rhs[c, k] * rhs[c, k]
            whole = whole + square
            outside = outside + bare * square
    sums[0] = whole
    wide = lax.broadcasted_iota(jnp.int32, (ROWS, 2 * LANES), 1)
    inner = between(wide, HALO, 2 * LANES - 2 * HALO)
    lax.fori_loop(0, STEPS, apply, 0)


def ribbon_kernel(ribbon, columns, columns_a, columns_b, sums, edges, moments):
    tiles = edges.shape[2]
    below_and_above, _ = beyond()
    lane = lax.broadcasted_iota(jnp.int32, (2 * ROWS, LANES), 1)

    def whole(tile):
        side = jnp.concatenate([columns[tile], below_and_above(columns_a[tile], columns_b[tile])], 0)
        return ribbon[tile] + side

    field = [[whole(c * tiles + n) for n in range(tiles)] for c in range(2)]
    eta = [whole(2 * tiles + n) for n in range(tiles)]
    cover, drag = whole(3 * tiles), whole(3 * tiles + 1)

    def after(v):
        return v[1:] + [turned(v[0], -SLOT)]

    eta_row = [2.0 * (e + row_next(e)) for e in eta]
    eta_col = [0.5 * (e + col_next(e)) for e in eta]
    eta_half = [0.5 * e for e in eta]
    eta_up = [e + n for e, n in zip(eta, after(eta))]
    eta_up[-1] = jnp.where(lane < LANES - SLOT, eta_up[-1], 0.0)
    place = lax.broadcasted_iota(jnp.int32, (ROWS, LANES), 1) % SLOT
    edge = between(place, 4, HALO) | between(place, 20, HALO)
    extra = [None]
    for t in range(1, STEPS + 1):
        ups = [[u * (g - n) for u, g, n in zip(eta_up, field[c], after(field[c]))] for c in range(2)]
        result = ([], [])
        odd = even = jnp.zeros((ROWS, LANES), jnp.float32)
        for n in range(tiles):
            outs = horizontal(field[0][n], field[1][n], eta_row[n], eta_col[n], eta_half[n])
            for c in range(2):
                below = ups[c][n - 1] if n else turned(ups[c][-1], SLOT) - drag * field[c][0]
                out = cover * (outs[c] + (ups[c][n] - below))
                result[c].append(out)
                now = out[:ROWS]
                edges[t - 1, c, n] = now
                odd = odd + field[c][n][:ROWS] * now
                even = even + now * now
        field = result
        extra.extend([jnp.where(edge, odd, 0.0), jnp.where(edge, even, 0.0)])

    tall = lax.broadcasted_iota(jnp.int32, (2 * ROWS, LANES), 0)
    high = jnp.zeros((2 * ROWS, LANES), jnp.float32)
    low = jnp.zeros((2 * ROWS, LANES), jnp.float32)
    for j, more in enumerate(extra):
        total = sums[j]
        pair = two_sum(total[:, :LANES], total[:, LANES:])
        if more is not None:
            pair = join(pair, (more, jnp.zeros_like(more)))
        for step in (4, 2, 1):
            pair = join(pair, tuple(pltpu.roll(v, step, 0) for v in pair))
        high = jnp.where(tall == j, jnp.concatenate([pair[0]] * 2, 0), high)
        low = jnp.where(tall == j, jnp.concatenate([pair[1]] * 2, 0), low)
    moments[0] = high
    moments[1] = low


def add_kernel(*refs):
    *ins, out = refs
    total = (ins[0][0], ins[0][1])
    for x in ins[1:]:
        total = join(total, (x[0], x[1]))
    out[0], out[1] = total


def solve(total):
    for step in (64, 32, 16, 8, 4, 2, 1):
        total = join(total, tuple(pltpu.roll(v, step, 1) for v in total))

    def spread(v, j):
        return jnp.broadcast_to(v[j : j + 1], (ROWS, LANES))

    centre = spread(total[0], 1) / spread(total[0], 0)
    wide = jnp.concatenate([centre, centre], 0)
    mu = [spread(total[0], 0)]
    for _ in range(2 * STEPS):
        step = times(wide, total)
        total = join(tuple(pltpu.roll(v, 2 * ROWS - 1, 0) for v in total), (-step[0], -step[1]))
        mu.append(spread(total[0], 0))

    def plus(a, b):
        n = max(len(a), len(b))
        return [a[i] + b[i] if i < min(len(a), len(b)) else (a[i] if i < len(a) else b[i]) for i in range(n)]

    def scaled(s, a):
        return [s * x for x in a]

    def operator(a):
        return plus([centre * x for x in a], [jnp.zeros_like(centre)] + a)

    def dot(a, b):
        square = [None] * (len(a) + len(b) - 1)
        for i, x in enumerate(a):
            for j, y in enumerate(b):
                z = x * y
                square[i + j] = z if square[i + j] is None else square[i + j] + z
        value = square[0] * mu[0]
        for n in range(1, len(square)):
            value = value + square[n] * mu[n]
        return value

    one = jnp.ones_like(centre)
    right = [one]
    quasi, search, update, iterate = right, right, [], []
    applied = operator(search)
    carried = applied
    rho = mu[0]
    tau_sq = rho
    alpha = theta_sq = eta = None
    for half in range(STEPS):
        if half % 2 == 0:
            alpha = rho / dot(carried, right)
            search_next = plus(search, scaled(-alpha, carried))
        quasi = plus(quasi, scaled(-alpha, applied))
        if half:
            update = plus(search, scaled(theta_sq / alpha * eta, update))
        else:
            update = search
        theta_sq = dot(quasi, quasi) / tau_sq
        cosine_sq = 1.0 / (1.0 + theta_sq)
        tau_sq = tau_sq * theta_sq * cosine_sq
        eta = cosine_sq * alpha
        iterate = plus(iterate, scaled(eta, update))
        if half % 2 == 0:
            search = search_next
            applied = operator(search)
        elif half < STEPS - 1:
            rho_next = dot(quasi, right)
            beta = rho_next / rho
            search = plus(quasi, scaled(beta, search))
            applied_next = operator(search)
            carried = plus(applied_next, scaled(beta, plus(applied, scaled(beta, carried))))
            applied, rho = applied_next, rho_next
    powers = [iterate[-1]]
    for c in iterate[-2::-1]:
        powers = plus([c] + powers, scaled(-centre, powers))
    return powers


def final_kernel(rhs, powers, edges, friction, ice, grounded, speed, *rest):
    *parts, iterate, residual, hessian = rest
    layers, tiles = rhs.shape[1], edges.shape[2]
    total = (parts[0][0], parts[0][1])
    for x in parts[1:]:
        total = join(total, (x[0], x[1]))
    factors = solve(total)
    wide = [jnp.concatenate([c, c], 1) for c in factors]
    rest = sum(wide[1:], wide[0])
    cover = ice[...].astype(jnp.float32)
    lane = lax.broadcasted_iota(jnp.int32, (ROWS, LANES), 1)

    def combined(vectors, weights):
        x = weights[1] * vectors[0]
        y = weights[0] * vectors[0]
        for t in range(1, STEPS):
            if t + 1 < STEPS:
                x = x + weights[t + 1] * vectors[t]
            y = y + weights[t] * vectors[t]
        return x, y

    for c in range(2):
        side = [combined([edges[t, c, n] for t in range(STEPS)], factors) for n in range(tiles)]
        for k in range(layers):
            at = k // tiles * SLOT
            inner = combined([powers[t, c, k] for t in range(STEPS)], wide)
            patched = []
            for v, e in zip(inner, side[k % tiles]):
                head = jnp.where(lane < HALO, turned(e, -at - 20), v[:, :LANES])
                tail = jnp.where(lane >= LANES - HALO, turned(e, 120 - at), v[:, LANES:])
                patched.append(jnp.concatenate([head, tail], 1))
            r = rhs[c, k]
            x, y = patched
            iterate[c, k] = jnp.where(cover > 0.0, wide[0] * r + x, rest * r)
            residual[c, k] = r - jnp.where(cover > 0.0, y, rest * r)
    weight = cover * (friction[...] * grounded[...].astype(jnp.float32))
    hessian[...] = weight * (speed[0] * iterate[0, 0] + speed[1] * iterate[1, 0])


def exchange(x, axis):
    count = lax.axis_size(axis)
    stride = 1
    rounds = []
    while stride < count:
        size = 4 if (count // stride) % 4 == 0 else 2
        rounds.append((stride, size))
        stride *= size
    for at, (stride, size) in enumerate(rounds):
        parts = [x]
        for turn in range(1, size):
            pairs = []
            for i in range(count):
                place = (i // stride) % size
                pairs.append((i, i + ((place ^ turn) - place) * stride))
            parts.append(lax.ppermute(x, axis, pairs))
        if at == len(rounds) - 1:
            return parts
        x = call(add_kernel, [x.shape])(*parts)[0]
    return [x]


def body(adjoint_rhs, viscosity, friction, ice_mask, grounded, basal_velocity):
    layers = viscosity.shape[0]
    inputs = (adjoint_rhs, viscosity, friction, ice_mask, grounded, basal_velocity)
    tile = (ROWS, LANES)
    strips = (2 * (layers + layers // 2 + 1),) + tile
    ribbons = (ribbon_tiles(layers),) + tile
    *held, column_a, column_b, strip_a, strip_b = call(
        pack_kernel,
        [jax.ShapeDtypeStruct(x.shape, x.dtype) for x in inputs] + [ribbons, ribbons, strips, strips],
        [pltpu.SemaphoreType.DMA((len(inputs),))],
        in_specs=[pl.BlockSpec(memory_space=pltpu.HBM)] * len(inputs),
    )(*[pltpu.with_memory_space_constraint(x, pltpu.HBM) for x in inputs])
    beside = ("gy", "gz")
    column_a, column_b = swapped(column_a, beside, 0), swapped(column_b, beside, 1)
    strip_a, strip_b = swapped(strip_a, "gx", 0), swapped(strip_b, "gx", 1)
    (columns,) = call(
        beside_kernel,
        [ribbons],
        cost_estimate=pl.CostEstimate(flops=3_000_000_000, bytes_accessed=200_000, transcendentals=0),
    )(column_a, column_b)
    columns_a, columns_b = swapped(columns, "gx", 0), swapped(columns, "gx", 1)
    block = (layers, 2 * ROWS, 2 * LANES)
    powers, sums, ribbon = call(
        main_kernel,
        [(STEPS,) + adjoint_rhs.shape, (2 * STEPS + 1, ROWS, 2 * LANES), (ribbons[0], 2 * ROWS, LANES)],
        [(2, 2) + block] + [block] * 4 + [block[1:]] * 2,
        cost_estimate=pl.CostEstimate(flops=200_000_000, bytes_accessed=8_000_000, transcendentals=0),
    )(*held[:5], strip_a, strip_b)
    edges, sums = call(
        ribbon_kernel,
        [(STEPS, 2, layers // 4) + tile, (2, 2 * ROWS, LANES)],
    )(ribbon, columns, columns_a, columns_b, sums)
    parts = exchange(sums, ("gy", "gz"))
    if len(parts) > 1:
        sums = call(add_kernel, [sums.shape])(*parts)[0]
    parts = exchange(sums, "gx")
    rhs, _, friction, ice_mask, grounded, speed = held
    return tuple(
        call(final_kernel, [adjoint_rhs.shape, adjoint_rhs.shape, friction.shape])(
            rhs, powers, edges, friction, ice_mask, grounded, speed, *parts
        )
    )


def solution(mesh):
    in_specs = (
        P(None, None, ("parts", "gx"), ("gy", "gz")),
        P(None, ("parts", "gx"), ("gy", "gz")),
        P(("parts", "gx"), ("gy", "gz")),
        P(("parts", "gx"), ("gy", "gz")),
        P(("parts", "gx"), ("gy", "gz")),
        P(None, ("parts", "gx"), ("gy", "gz")),
    )
    out_specs = (
        P(None, None, ("parts", "gx"), ("gy", "gz")),
        P(None, None, ("parts", "gx"), ("gy", "gz")),
        P(("parts", "gx"), ("gy", "gz")),
    )
    return jax.shard_map(body, mesh=mesh, in_specs=in_specs, out_specs=out_specs, check_vma=False)
```

```python
import functools

import jax
import jax.numpy as jnp
from jax import lax
from jax.experimental import pallas as pl
from jax.experimental.pallas import tpu as pltpu
from jax.sharding import PartitionSpec as P

STEPS = 4
HALO = 4
ROWS = 8
LANES = 128
UNROLL = 5
PIECES = 2
SLOT = 32


def call(kernel, outs, scratch=(), **more):
    return pl.pallas_call(
        kernel,
        out_shape=[jax.ShapeDtypeStruct(s, jnp.float32) if isinstance(s, tuple) else s for s in outs],
        scratch_shapes=[pltpu.VMEM(s, jnp.float32) if isinstance(s, tuple) else s for s in scratch],
        compiler_params=pltpu.CompilerParams(vmem_limit_bytes=40 * 1024 * 1024),
        **more,
    )


def place_of(axis):
    place, count = lax.axis_index(axis), lax.axis_size(axis)
    even = place % 2 == 0
    has_a = jnp.logical_or(jnp.logical_not(even), place < count - 1)
    has_b = jnp.where(even, place > 0, place < count - 1)
    return even, has_a, has_b


def swapped(x, axis, first):
    count = lax.axis_size(axis)
    pairs = []
    for i in range(count):
        other = i + 1 if (i - first) % 2 == 0 else i - 1
        pairs.append((i, other if 0 <= other < count else i))
    return lax.ppermute(x, axis, pairs)


def own_planes(rhs, eta, friction, ice, grounded):
    layers = eta.shape[0]
    cover = ice[...].astype(jnp.float32)
    drag = friction[...] * grounded[...].astype(jnp.float32)

    def plane(p):
        if p < 2 * layers:
            return rhs[p // layers, p % layers] * cover
        if p < 3 * layers:
            return eta[p - 2 * layers]
        return cover if p == 3 * layers else drag

    return plane


def pair_of(q, layers):
    if q < layers:
        return q, q + layers
    if q < layers + layers // 2:
        return q + layers, q + layers + layers // 2
    return 3 * layers, 3 * layers + 1


def ribbon_places(p, layers):
    tiles = layers // 4
    if p < 3 * layers:
        k = p % layers
        return p // layers * tiles + k % tiles, (k // tiles,)
    return (3 * tiles, (0, 1, 2, 3)) if p == 3 * layers else (3 * tiles + 1, (0,))


def ribbon_tiles(layers):
    return 3 * (layers // 4) + 2


def packed_place(tile):
    return tile // 8, HALO * (tile % 8)


def between(lane, first, width):
    return (lane >= first) & (lane < first + width)


def turned(v, shift):
    shift = shift % LANES
    return pltpu.roll(v, shift, 1) if shift else v


def pack_kernel(*refs):
    sources, held, (column_a, column_b, strip_a, strip_b, arrived) = refs[:6], refs[6:12], refs[12:]
    copies = [pltpu.make_async_copy(a, b, arrived.at[i]) for i, (a, b) in enumerate(zip(sources, held))]
    for copy in copies:
        copy.start()
    for copy in copies:
        copy.wait()
    rhs, eta, friction, ice, grounded, _ = held
    layers = eta.shape[0]
    plane = own_planes(rhs, eta, friction, ice, grounded)
    lane = lax.broadcasted_iota(jnp.int32, (ROWS, LANES), 1)
    row = lax.broadcasted_iota(jnp.int32, (ROWS, LANES), 0)
    rows_even, _, _ = place_of("gx")
    columns_even, _, _ = place_of(("gy", "gz"))
    upper_a = (row < HALO) != rows_even
    count = ribbon_tiles(layers)
    zero = jnp.zeros((ROWS, LANES), jnp.float32)
    left, right = [zero] * count, [zero] * count
    for q in range(strip_a.shape[0] // 2):
        first, second = pair_of(q, layers)
        x, y = plane(first), plane(second)
        for half in range(2):
            xs = x[:, half * LANES : (half + 1) * LANES]
            ys = y[:, half * LANES : (half + 1) * LANES]
            ys = pltpu.roll(ys, HALO, 0)
            strip_a[2 * q + half] = jnp.where(upper_a, xs, ys)
            strip_b[2 * q + half] = jnp.where(upper_a, ys, xs)
        for p, v in ((first, x), (second, y)):
            tile, slots = ribbon_places(p, layers)
            for slot in slots:
                at = slot * SLOT
                left[tile] = jnp.where(between(lane, at + 8, 4), turned(v[:, :LANES], at + 8), left[tile])
                right[tile] = jnp.where(between(lane, at + 16, 4), turned(v[:, LANES:], at + 20), right[tile])
    to_left, to_right = [zero] * column_a.shape[0], [zero] * column_a.shape[0]
    for tile in range(count):
        group, at = packed_place(tile)
        here = between(lane % SLOT, at, HALO)
        to_left[group] = jnp.where(here, turned(left[tile], at - 8), to_left[group])
        to_right[group] = jnp.where(here, turned(right[tile], at - 16), to_right[group])
    for group in range(column_a.shape[0]):
        column_a[group] = jnp.where(columns_even, to_right[group], to_left[group])
        column_b[group] = jnp.where(columns_even, to_left[group], to_right[group])


def beside_kernel(from_a, from_b, columns):
    even, has_a, has_b = place_of(("gy", "gz"))
    count = from_a.shape[0]
    for group in range(count):
        a = jnp.where(has_a, from_a[group], 0.0)
        b = jnp.where(has_b, from_b[group], 0.0)
        columns[group] = jnp.where(even, a, b)
        columns[count + group] = jnp.where(even, b, a)


def two_sum(a, b):
    s = a + b
    t = s - a
    return s, (a - (s - t)) + (b - t)


def join(x, y):
    s, e = two_sum(x[0], y[0])
    e = e + (x[1] + y[1])
    h = s + e
    return h, e - (h - s)


def times(scalar, x):
    def cut(v):
        t = v * 4097.0
        h = t - (t - v)
        return h, v - h

    p = scalar * x[0]
    sh, sl = cut(scalar)
    xh, xl = cut(x[0])
    e = ((sh * xh - p) + sh * xl + sl * xh) + sl * xl
    return p, e + scalar * x[1]


def beyond():
    even, has_a, has_b = place_of("gx")
    upper_a = (lax.broadcasted_iota(jnp.int32, (ROWS, LANES), 0) < HALO) == even

    def below_and_above(from_a, from_b):
        return jnp.where(upper_a, jnp.where(has_a, from_a, 0.0), jnp.where(has_b, from_b, 0.0))

    def above_and_below(from_a, from_b):
        return jnp.where(upper_a, jnp.where(has_b, from_b, 0.0), jnp.where(has_a, from_a, 0.0))

    return below_and_above, above_and_below


def row_next(v):
    return pltpu.roll(v, 2 * ROWS - 1, 0)


def row_prev(v):
    return pltpu.roll(v, 1, 0)


def col_next(v):
    return pltpu.roll(v, v.shape[1] - 1, 1)


def col_prev(v):
    return pltpu.roll(v, 1, 1)


class Tiles:
    def __init__(self, tiles):
        self.tiles = tiles

    @staticmethod
    def load(ref):
        return Tiles([ref[r : r + ROWS, c : c + LANES] for r in (0, ROWS) for c in (0, LANES)])

    def store(self, ref):
        for v, (r, c) in zip(self.tiles, ((0, 0), (0, LANES), (ROWS, 0), (ROWS, LANES))):
            ref[r : r + ROWS, c : c + LANES] = v

    def both(self, other, op):
        if isinstance(other, Tiles):
            return Tiles([op(x, y) for x, y in zip(self.tiles, other.tiles)])
        return Tiles([op(x, other) for x in self.tiles])

    def __add__(self, other):
        return self.both(other, lambda x, y: x + y)

    def __sub__(self, other):
        return self.both(other, lambda x, y: x - y)

    def __mul__(self, other):
        return self.both(other, lambda x, y: x * y)

    __rmul__ = __mul__


class Moves:
    def __init__(self):
        row = lax.broadcasted_iota(jnp.int32, (ROWS, LANES), 0)
        lane = lax.broadcasted_iota(jnp.int32, (ROWS, LANES), 1)
        self.first_row, self.last_row = row == 0, row == ROWS - 1
        self.first_lane, self.last_lane = lane == 0, lane == LANES - 1

    def rows(self, v, shift, edge):
        own0, own1, halo0, halo1 = [pltpu.roll(x, shift, 0) for x in v.tiles]
        return Tiles(
            [
                jnp.where(edge, halo0, own0),
                jnp.where(edge, halo1, own1),
                jnp.where(edge, own0, halo0),
                jnp.where(edge, own1, halo1),
            ]
        )

    def row_next(self, v):
        return self.rows(v, ROWS - 1, self.last_row)

    def row_prev(self, v):
        return self.rows(v, 1, self.first_row)

    def col_next(self, v):
        own0, own1, halo0, halo1 = [pltpu.roll(x, LANES - 1, 1) for x in v.tiles]
        return Tiles([jnp.where(self.last_lane, own1, own0), own1, jnp.where(self.last_lane, halo1, halo0), halo1])

    def col_prev(self, v):
        own0, own1, halo0, halo1 = [pltpu.roll(x, 1, 1) for x in v.tiles]
        return Tiles([own0, jnp.where(self.first_lane, own0, own1), halo0, jnp.where(self.first_lane, halo0, halo1)])


class Turns:
    row_next = staticmethod(row_next)
    row_prev = staticmethod(row_prev)
    col_next = staticmethod(col_next)
    col_prev = staticmethod(col_prev)


def horizontal(g0, g1, e_row, e_col, e_half, moves):
    row_next, row_prev, col_next, col_prev = moves.row_next, moves.row_prev, moves.col_next, moves.col_prev
    g0n, g1n = row_next(g0), col_next(g1)
    f = e_half * (g1n - col_prev(g1))
    h = e_half * (g0n - row_prev(g0))
    flux = e_row * (g0 - g0n)
    out0 = flux - row_next(f) - row_prev(flux - f)
    flux = e_col * (g0 - col_next(g0))
    out0 = out0 + (flux - col_prev(flux))
    flux = (4.0 * e_col) * (g1 - g1n)
    out1 = flux - col_next(h) - col_prev(flux - h)
    flux = (0.25 * e_row) * (g1 - row_next(g1))
    out1 = out1 + (flux - row_prev(flux))
    return out0, out1


def main_kernel(
    rhs, eta, friction, ice, grounded, strip_a, strip_b,
    powers, sums, ribbon,
    field_a, field_b, eta_row, eta_col, eta_half, eta_up, cover, drag,
):
    layers = eta.shape[0]
    plane = own_planes(rhs, eta, friction, ice, grounded)
    below_and_above, above_and_below = beyond()
    lane = lax.broadcasted_iota(jnp.int32, (2 * ROWS, LANES), 1)

    def target(p):
        if p < 2 * layers:
            return field_a.at[p // layers, p % layers]
        if p < 3 * layers:
            return eta_half.at[p - 2 * layers]
        return cover if p == 3 * layers else drag

    strips = [jnp.zeros((2 * ROWS, LANES), jnp.float32) for _ in range(ribbon.shape[0])]
    for q in range(strip_a.shape[0] // 2):
        first, second = pair_of(q, layers)
        halves = ([], [])
        for half in range(2):
            from_a, from_b = strip_a[2 * q + half], strip_b[2 * q + half]
            halves[0].append(below_and_above(from_a, from_b))
            halves[1].append(pltpu.roll(above_and_below(from_a, from_b), HALO, 0))
        for p, halo in zip((first, second), halves):
            v = plane(p)
            dst = target(p)
            dst[0:ROWS, :] = v
            dst[ROWS:, 0:LANES], dst[ROWS:, LANES:] = halo
            head = jnp.concatenate([v[:, :LANES], halo[0]], 0)
            tail = jnp.concatenate([v[:, LANES:], halo[1]], 0)
            tile, slots = ribbon_places(p, layers)
            for slot in slots:
                at = slot * SLOT
                strips[tile] = jnp.where(between(lane, at, 8), turned(tail, at + 8), strips[tile])
                strips[tile] = jnp.where(between(lane, at + 20, 8), turned(head, at + 20), strips[tile])
    for tile, v in enumerate(strips):
        ribbon[tile] = v

    moves = Moves()
    load = Tiles.load
    for k in range(layers):
        e = load(eta_half.at[k])
        (2.0 * (e + moves.row_next(e))).store(eta_row.at[k])
        (0.5 * (e + moves.col_next(e))).store(eta_col.at[k])
        eta_up[k] = eta_half[k] + eta_half[k + 1] if k + 1 < layers else jnp.zeros_like(eta_up[k])
        if k:
            eta_half[k - 1] = 0.5 * eta_half[k - 1]
    eta_half[layers - 1] = 0.5 * eta_half[layers - 1]

    def apply(t, src, dst):
        def layer(k, carry):
            below0, below1, odd, even = carry
            g0, g1 = load(src.at[0, k]), load(src.at[1, k])
            after = jnp.minimum(k + 1, layers - 1)
            e_up = load(eta_up.at[k])
            up0 = e_up * (g0 - load(src.at[0, after]))
            up1 = e_up * (g1 - load(src.at[1, after]))
            out0, out1 = horizontal(g0, g1, load(eta_row.at[k]), load(eta_col.at[k]), load(eta_half.at[k]), moves)
            m = load(cover)
            out0, out1 = m * (out0 + (up0 - Tiles(below0))), m * (out1 + (up1 - Tiles(below1)))
            if t < STEPS:
                out0.store(dst.at[0, k])
                out1.store(dst.at[1, k])
            odd, even = list(odd), list(even)
            for c, g, out in ((0, g0, out0), (1, g1, out1)):
                for half in range(2):
                    now = out.tiles[half]
                    powers[t - 1, c, k, :, half * LANES : (half + 1) * LANES] = now
                    odd[half] = odd[half] + g.tiles[half] * now
                    even[half] = even[half] + now * now
            return up0.tiles, up1.tiles, odd, even

        def block(b, carry):
            for i in range(UNROLL):
                carry = layer(b * UNROLL + i, carry)
            return carry

        zero = [jnp.zeros((ROWS, LANES), jnp.float32)] * 2
        d = -1.0 * load(drag)
        start = ((d * load(src.at[0, 0])).tiles, (d * load(src.at[1, 0])).tiles, zero, zero)
        ends = lax.fori_loop(0, layers // UNROLL, block, start)[2:]
        return [jnp.concatenate(v, 1) for v in ends]

    bare = 1.0 - ice[...].astype(jnp.float32)
    whole = jnp.zeros((ROWS, 2 * LANES), jnp.float32)
    outside = jnp.zeros((ROWS, 2 * LANES), jnp.float32)
    for c in range(2):
        for k in range(layers):
            square = rhs[c, k] * rhs[c, k]
            whole = whole + square
            outside = outside + bare * square
    sums[0] = whole
    wide = lax.broadcasted_iota(jnp.int32, (ROWS, 2 * LANES), 1)
    inner = between(wide, HALO, 2 * LANES - 2 * HALO)
    src, dst = field_a, field_b
    for t in range(1, STEPS + 1):
        odd, even = apply(t, src, dst)
        sums[2 * t - 1] = jnp.where(inner, odd, 0.0) + outside
        sums[2 * t] = jnp.where(inner, even, 0.0) + outside
        src, dst = dst, src


def ribbon_kernel(ribbon, columns, columns_a, columns_b, sums, edges, moments):
    tiles = edges.shape[2]
    below_and_above, _ = beyond()
    lane = lax.broadcasted_iota(jnp.int32, (2 * ROWS, LANES), 1)

    count = columns.shape[0] // 2
    beside = [
        jnp.concatenate([columns[i], below_and_above(columns_a[i], columns_b[i])], 0) for i in range(2 * count)
    ]
    spot = lane % SLOT

    def whole(tile):
        group, at = packed_place(tile)
        right = jnp.where(between(spot, 8, HALO), turned(beside[group], 8 - at), ribbon[tile])
        return jnp.where(between(spot, 16, HALO), turned(beside[count + group], 16 - at), right)

    field = [[whole(c * tiles + n) for n in range(tiles)] for c in range(2)]
    eta = [whole(2 * tiles + n) for n in range(tiles)]
    cover, drag = whole(3 * tiles), whole(3 * tiles + 1)

    def after(v):
        return v[1:] + [turned(v[0], -SLOT)]

    eta_row = [2.0 * (e + row_next(e)) for e in eta]
    eta_col = [0.5 * (e + col_next(e)) for e in eta]
    eta_half = [0.5 * e for e in eta]
    eta_up = [e + n for e, n in zip(eta, after(eta))]
    eta_up[-1] = jnp.where(lane < LANES - SLOT, eta_up[-1], 0.0)
    place = lax.broadcasted_iota(jnp.int32, (ROWS, LANES), 1) % SLOT
    edge = between(place, 4, HALO) | between(place, 20, HALO)
    extra = [None]
    for t in range(1, STEPS + 1):
        ups = [[u * (g - n) for u, g, n in zip(eta_up, field[c], after(field[c]))] for c in range(2)]
        result = ([], [])
        odd = even = jnp.zeros((ROWS, LANES), jnp.float32)
        for n in range(tiles):
            outs = horizontal(field[0][n], field[1][n], eta_row[n], eta_col[n], eta_half[n], Turns)
            for c in range(2):
                below = ups[c][n - 1] if n else turned(ups[c][-1], SLOT) - drag * field[c][0]
                out = cover * (outs[c] + (ups[c][n] - below))
                result[c].append(out)
                now = out[:ROWS]
                edges[t - 1, c, n] = now
                odd = odd + field[c][n][:ROWS] * now
                even = even + now * now
        field = result
        extra.extend([jnp.where(edge, odd, 0.0), jnp.where(edge, even, 0.0)])

    tall = lax.broadcasted_iota(jnp.int32, (2 * ROWS, LANES), 0)
    high = jnp.zeros((2 * ROWS, LANES), jnp.float32)
    low = jnp.zeros((2 * ROWS, LANES), jnp.float32)
    for j, more in enumerate(extra):
        total = sums[j]
        pair = two_sum(total[:, :LANES], total[:, LANES:])
        if more is not None:
            pair = join(pair, (more, jnp.zeros_like(more)))
        for step in (4, 2, 1):
            pair = join(pair, tuple(pltpu.roll(v, step, 0) for v in pair))
        high = jnp.where(tall == j, jnp.concatenate([pair[0]] * 2, 0), high)
        low = jnp.where(tall == j, jnp.concatenate([pair[1]] * 2, 0), low)
    moments[0] = high
    moments[1] = low


def add_kernel(*refs):
    *ins, out = refs
    total = (ins[0][0], ins[0][1])
    for x in ins[1:]:
        total = join(total, (x[0], x[1]))
    out[0], out[1] = total


def solve(total):
    for step in (64, 32, 16, 8, 4, 2, 1):
        total = join(total, tuple(pltpu.roll(v, step, 1) for v in total))

    def spread(v, j):
        return jnp.broadcast_to(v[j : j + 1], (ROWS, LANES))

    centre = spread(total[0], 1) / spread(total[0], 0)
    wide = jnp.concatenate([centre, centre], 0)
    mu = [spread(total[0], 0)]
    for _ in range(2 * STEPS):
        step = times(wide, total)
        total = join(tuple(pltpu.roll(v, 2 * ROWS - 1, 0) for v in total), (-step[0], -step[1]))
        mu.append(spread(total[0], 0))

    def plus(a, b):
        n = max(len(a), len(b))
        return [a[i] + b[i] if i < min(len(a), len(b)) else (a[i] if i < len(a) else b[i]) for i in range(n)]

    def scaled(s, a):
        return [s * x for x in a]

    def operator(a):
        return plus([centre * x for x in a], [jnp.zeros_like(centre)] + a)

    def dot(a, b):
        square = [None] * (len(a) + len(b) - 1)
        for i, x in enumerate(a):
            for j, y in enumerate(b):
                z = x * y
                square[i + j] = z if square[i + j] is None else square[i + j] + z
        value = square[0] * mu[0]
        for n in range(1, len(square)):
            value = value + square[n] * mu[n]
        return value

    one = jnp.ones_like(centre)
    right = [one]
    quasi, search, update, iterate = right, right, [], []
    applied = operator(search)
    carried = applied
    rho = mu[0]
    tau_sq = rho
    alpha = theta_sq = eta = None
    for half in range(STEPS):
        if half % 2 == 0:
            alpha = rho / dot(carried, right)
            search_next = plus(search, scaled(-alpha, carried))
        quasi = plus(quasi, scaled(-alpha, applied))
        if half:
            update = plus(search, scaled(theta_sq / alpha * eta, update))
        else:
            update = search
        theta_sq = dot(quasi, quasi) / tau_sq
        cosine_sq = 1.0 / (1.0 + theta_sq)
        tau_sq = tau_sq * theta_sq * cosine_sq
        eta = cosine_sq * alpha
        iterate = plus(iterate, scaled(eta, update))
        if half % 2 == 0:
            search = search_next
            applied = operator(search)
        elif half < STEPS - 1:
            rho_next = dot(quasi, right)
            beta = rho_next / rho
            search = plus(quasi, scaled(beta, search))
            applied_next = operator(search)
            carried = plus(applied_next, scaled(beta, plus(applied, scaled(beta, carried))))
            applied, rho = applied_next, rho_next
    powers = [iterate[-1]]
    for c in iterate[-2::-1]:
        powers = plus([c] + powers, scaled(-centre, powers))
    return powers


def final_kernel(rhs, powers, edges, friction, ice, grounded, speed, *rest):
    *parts, iterate_out, residual_out, hessian, iterate, residual, gone = rest
    layers, tiles = rhs.shape[1], edges.shape[2]
    total = (parts[0][0], parts[0][1])
    for x in parts[1:]:
        total = join(total, (x[0], x[1]))
    factors = solve(total)
    wide = [jnp.concatenate([c, c], 1) for c in factors]
    rest = sum(wide[1:], wide[0])
    cover = ice[...].astype(jnp.float32)
    lane = lax.broadcasted_iota(jnp.int32, (ROWS, LANES), 1)

    def combined(vectors, weights):
        x = weights[1] * vectors[0]
        y = weights[0] * vectors[0]
        for t in range(1, STEPS):
            if t + 1 < STEPS:
                x = x + weights[t + 1] * vectors[t]
            y = y + weights[t] * vectors[t]
        return x, y

    piece = layers // PIECES
    copies = []
    for c in range(2):
        side = [combined([edges[t, c, n] for t in range(STEPS)], factors) for n in range(tiles)]
        for k in range(layers):
            at = k // tiles * SLOT
            inner = combined([powers[t, c, k] for t in range(STEPS)], wide)
            patched = []
            for v, e in zip(inner, side[k % tiles]):
                head = jnp.where(lane < HALO, turned(e, -at - 20), v[:, :LANES])
                tail = jnp.where(lane >= LANES - HALO, turned(e, 120 - at), v[:, LANES:])
                patched.append(jnp.concatenate([head, tail], 1))
            r = rhs[c, k]
            x, y = patched
            iterate[c, k] = jnp.where(cover > 0.0, wide[0] * r + x, rest * r)
            residual[c, k] = r - jnp.where(cover > 0.0, y, rest * r)
            if (k + 1) % piece == 0:
                for i, (src, dst) in enumerate(((iterate, iterate_out), (residual, residual_out))):
                    part = (c, pl.ds(k + 1 - piece, piece))
                    copies.append(pltpu.make_async_copy(src.at[part], dst.at[part], gone.at[len(copies)]))
                    copies[-1].start()
    weight = cover * (friction[...] * grounded[...].astype(jnp.float32))
    hessian[...] = weight * (speed[0] * iterate[0, 0] + speed[1] * iterate[1, 0])
    for copy in copies:
        copy.wait()


def exchange(x, axis):
    count = lax.axis_size(axis)
    stride = 1
    rounds = []
    while stride < count:
        size = 4 if (count // stride) % 4 == 0 else 2
        rounds.append((stride, size))
        stride *= size
    for at, (stride, size) in enumerate(rounds):
        parts = [x]
        for turn in range(1, size):
            pairs = []
            for i in range(count):
                place = (i // stride) % size
                pairs.append((i, i + ((place ^ turn) - place) * stride))
            parts.append(lax.ppermute(x, axis, pairs))
        if at == len(rounds) - 1:
            return parts
        x = call(add_kernel, [x.shape])(*parts)[0]
    return [x]


def body(adjoint_rhs, viscosity, friction, ice_mask, grounded, basal_velocity):
    layers = viscosity.shape[0]
    inputs = (adjoint_rhs, viscosity, friction, ice_mask, grounded, basal_velocity)
    tile = (ROWS, LANES)
    strips = (2 * (layers + layers // 2 + 1),) + tile
    ribbons = ribbon_tiles(layers)
    packed = ((ribbons + 7) // 8,) + tile
    both = (2 * packed[0],) + tile
    *held, column_a, column_b, strip_a, strip_b = call(
        pack_kernel,
        [jax.ShapeDtypeStruct(x.shape, x.dtype) for x in inputs] + [packed, packed, strips, strips],
        [pltpu.SemaphoreType.DMA((len(inputs),))],
        in_specs=[pl.BlockSpec(memory_space=pltpu.HBM)] * len(inputs),
    )(*[pltpu.with_memory_space_constraint(x, pltpu.HBM) for x in inputs])
    strip_a, strip_b = swapped(strip_a, "gx", 0), swapped(strip_b, "gx", 1)
    beside = ("gy", "gz")
    (columns,) = call(beside_kernel, [both])(swapped(column_a, beside, 0), swapped(column_b, beside, 1))
    columns_a, columns_b = swapped(columns, "gx", 0), swapped(columns, "gx", 1)
    block = (layers, 2 * ROWS, 2 * LANES)
    powers, sums, ribbon = call(
        main_kernel,
        [(STEPS,) + adjoint_rhs.shape, (2 * STEPS + 1, ROWS, 2 * LANES), (ribbons, 2 * ROWS, LANES)],
        [(2,) + block] * 2 + [block] * 4 + [block[1:]] * 2,
        cost_estimate=pl.CostEstimate(flops=200_000_000, bytes_accessed=8_000_000, transcendentals=0),
    )(*held[:5], strip_a, strip_b)
    edges, sums = call(
        ribbon_kernel,
        [(STEPS, 2, layers // 4) + tile, (2, 2 * ROWS, LANES)],
    )(ribbon, columns, columns_a, columns_b, sums)
    parts = exchange(sums, ("gy", "gz"))
    if len(parts) > 1:
        sums = call(add_kernel, [sums.shape])(*parts)[0]
    parts = exchange(sums, "gx")
    rhs, _, friction, ice_mask, grounded, speed = held
    return tuple(
        call(
            final_kernel,
            [adjoint_rhs.shape, adjoint_rhs.shape, friction.shape],
            [adjoint_rhs.shape] * 2 + [pltpu.SemaphoreType.DMA((4 * PIECES,))],
            out_specs=[pl.BlockSpec(memory_space=pltpu.HBM)] * 2 + [pl.BlockSpec(memory_space=pltpu.VMEM)],
        )(
            rhs, powers, edges, friction, ice_mask, grounded, speed, *parts
        )
    )


def solution(mesh):
    in_specs = (
        P(None, None, ("parts", "gx"), ("gy", "gz")),
        P(None, ("parts", "gx"), ("gy", "gz")),
        P(("parts", "gx"), ("gy", "gz")),
        P(("parts", "gx"), ("gy", "gz")),
        P(("parts", "gx"), ("gy", "gz")),
        P(None, ("parts", "gx"), ("gy", "gz")),
    )
    out_specs = (
        P(None, None, ("parts", "gx"), ("gy", "gz")),
        P(None, None, ("parts", "gx"), ("gy", "gz")),
        P(("parts", "gx"), ("gy", "gz")),
    )
    return jax.shard_map(body, mesh=mesh, in_specs=in_specs, out_specs=out_specs, check_vma=False)
```

```python
import functools

import jax
import jax.numpy as jnp
from jax import lax
from jax.experimental import pallas as pl
from jax.experimental.pallas import tpu as pltpu
from jax.sharding import PartitionSpec as P

STEPS = 4
HALO = 4
ROWS = 8
LANES = 128
UNROLL = 5
FIRST = 4
SLOT = 32


def call(kernel, outs, scratch=(), **more):
    return pl.pallas_call(
        kernel,
        out_shape=[jax.ShapeDtypeStruct(s, jnp.float32) if isinstance(s, tuple) else s for s in outs],
        scratch_shapes=[pltpu.VMEM(s, jnp.float32) if isinstance(s, tuple) else s for s in scratch],
        compiler_params=pltpu.CompilerParams(vmem_limit_bytes=40 * 1024 * 1024),
        **more,
    )


def place_of(axis):
    place, count = lax.axis_index(axis), lax.axis_size(axis)
    even = place % 2 == 0
    has_a = jnp.logical_or(jnp.logical_not(even), place < count - 1)
    has_b = jnp.where(even, place > 0, place < count - 1)
    return even, has_a, has_b


def swapped(x, axis, first):
    count = lax.axis_size(axis)
    pairs = []
    for i in range(count):
        other = i + 1 if (i - first) % 2 == 0 else i - 1
        pairs.append((i, other if 0 <= other < count else i))
    return lax.ppermute(x, axis, pairs)


def own_planes(rhs, eta, friction, ice, grounded):
    layers = eta.shape[0]
    cover = ice[...].astype(jnp.float32)
    drag = friction[...] * grounded[...].astype(jnp.float32)

    def plane(p):
        if p < 2 * layers:
            return rhs[p // layers, p % layers] * cover
        if p < 3 * layers:
            return eta[p - 2 * layers]
        return cover if p == 3 * layers else drag

    return plane


def pair_of(q, layers):
    if q < layers:
        return q, q + layers
    if q < layers + layers // 2:
        return q + layers, q + layers + layers // 2
    return 3 * layers, 3 * layers + 1


def ribbon_places(p, layers):
    tiles = layers // 4
    if p < 3 * layers:
        k = p % layers
        return p // layers * tiles + k % tiles, (k // tiles,)
    return (3 * tiles, (0, 1, 2, 3)) if p == 3 * layers else (3 * tiles + 1, (0,))


def ribbon_tiles(layers):
    return 3 * (layers // 4) + 2


def packed_place(tile):
    return tile // 8, HALO * (tile % 8)


def between(lane, first, width):
    return (lane >= first) & (lane < first + width)


def turned(v, shift):
    shift = shift % LANES
    return pltpu.roll(v, shift, 1) if shift else v


def pack_kernel(*refs):
    sources, held, (column_a, column_b, strip_a, strip_b, arrived) = refs[:6], refs[6:12], refs[12:]
    copies = [pltpu.make_async_copy(a, b, arrived.at[i]) for i, (a, b) in enumerate(zip(sources, held))]
    for copy in copies:
        copy.start()
    for copy in copies:
        copy.wait()
    rhs, eta, friction, ice, grounded, _ = held
    layers = eta.shape[0]
    plane = own_planes(rhs, eta, friction, ice, grounded)
    lane = lax.broadcasted_iota(jnp.int32, (ROWS, LANES), 1)
    row = lax.broadcasted_iota(jnp.int32, (ROWS, LANES), 0)
    rows_even, _, _ = place_of("gx")
    columns_even, _, _ = place_of(("gy", "gz"))
    upper_a = (row < HALO) != rows_even
    count = ribbon_tiles(layers)
    zero = jnp.zeros((ROWS, LANES), jnp.float32)
    left, right = [zero] * count, [zero] * count
    for q in range(strip_a.shape[0] // 2):
        first, second = pair_of(q, layers)
        x, y = plane(first), plane(second)
        for half in range(2):
            xs = x[:, half * LANES : (half + 1) * LANES]
            ys = y[:, half * LANES : (half + 1) * LANES]
            ys = pltpu.roll(ys, HALO, 0)
            strip_a[2 * q + half] = jnp.where(upper_a, xs, ys)
            strip_b[2 * q + half] = jnp.where(upper_a, ys, xs)
        for p, v in ((first, x), (second, y)):
            tile, slots = ribbon_places(p, layers)
            for slot in slots:
                at = slot * SLOT
                left[tile] = jnp.where(between(lane, at + 8, 4), turned(v[:, :LANES], at + 8), left[tile])
                right[tile] = jnp.where(between(lane, at + 16, 4), turned(v[:, LANES:], at + 20), right[tile])
    to_left, to_right = [zero] * column_a.shape[0], [zero] * column_a.shape[0]
    for tile in range(count):
        group, at = packed_place(tile)
        here = between(lane % SLOT, at, HALO)
        to_left[group] = jnp.where(here, turned(left[tile], at - 8), to_left[group])
        to_right[group] = jnp.where(here, turned(right[tile], at - 16), to_right[group])
    for group in range(column_a.shape[0]):
        column_a[group] = jnp.where(columns_even, to_right[group], to_left[group])
        column_b[group] = jnp.where(columns_even, to_left[group], to_right[group])


def beside_kernel(from_a, from_b, columns):
    even, has_a, has_b = place_of(("gy", "gz"))
    count = from_a.shape[0]
    for group in range(count):
        a = jnp.where(has_a, from_a[group], 0.0)
        b = jnp.where(has_b, from_b[group], 0.0)
        columns[group] = jnp.where(even, a, b)
        columns[count + group] = jnp.where(even, b, a)


def two_sum(a, b):
    s = a + b
    t = s - a
    return s, (a - (s - t)) + (b - t)


def join(x, y):
    s, e = two_sum(x[0], y[0])
    e = e + (x[1] + y[1])
    h = s + e
    return h, e - (h - s)


def times(scalar, x):
    def cut(v):
        t = v * 4097.0
        h = t - (t - v)
        return h, v - h

    p = scalar * x[0]
    sh, sl = cut(scalar)
    xh, xl = cut(x[0])
    e = ((sh * xh - p) + sh * xl + sl * xh) + sl * xl
    return p, e + scalar * x[1]


def beyond():
    even, has_a, has_b = place_of("gx")
    upper_a = (lax.broadcasted_iota(jnp.int32, (ROWS, LANES), 0) < HALO) == even

    def below_and_above(from_a, from_b):
        return jnp.where(upper_a, jnp.where(has_a, from_a, 0.0), jnp.where(has_b, from_b, 0.0))

    def above_and_below(from_a, from_b):
        return jnp.where(upper_a, jnp.where(has_b, from_b, 0.0), jnp.where(has_a, from_a, 0.0))

    return below_and_above, above_and_below


def row_next(v):
    return pltpu.roll(v, 2 * ROWS - 1, 0)


def row_prev(v):
    return pltpu.roll(v, 1, 0)


def col_next(v):
    return pltpu.roll(v, v.shape[1] - 1, 1)


def col_prev(v):
    return pltpu.roll(v, 1, 1)


class Tiles:
    def __init__(self, tiles):
        self.tiles = tiles

    @staticmethod
    def load(ref, *place, shift=0):
        at = FIRST + shift
        return Tiles([ref[(half, *place, pl.ds(at + r, ROWS))] for r in (0, ROWS) for half in (0, 1)])

    def store(self, ref, *place):
        for i, v in enumerate(self.tiles):
            ref[(i % 2, *place, pl.ds(FIRST + i // 2 * ROWS, ROWS))] = v

    def both(self, other, op):
        if isinstance(other, Tiles):
            return Tiles([op(x, y) for x, y in zip(self.tiles, other.tiles)])
        return Tiles([op(x, other) for x in self.tiles])

    def __add__(self, other):
        return self.both(other, lambda x, y: x + y)

    def __sub__(self, other):
        return self.both(other, lambda x, y: x - y)

    def __mul__(self, other):
        return self.both(other, lambda x, y: x * y)

    __rmul__ = __mul__


class Moves:
    def __init__(self):
        row = lax.broadcasted_iota(jnp.int32, (ROWS, LANES), 0)
        lane = lax.broadcasted_iota(jnp.int32, (ROWS, LANES), 1)
        self.first_row, self.last_row = row == 0, row == ROWS - 1
        self.first_lane, self.last_lane = lane == 0, lane == LANES - 1

    def row_next(self, v):
        top0, top1, low0, low1 = [pltpu.roll(x, ROWS - 1, 0) for x in v.tiles]
        return Tiles([jnp.where(self.last_row, low0, top0), jnp.where(self.last_row, low1, top1), low0, low1])

    def row_prev(self, v):
        top0, top1, low0, low1 = [pltpu.roll(x, 1, 0) for x in v.tiles]
        return Tiles([top0, top1, jnp.where(self.first_row, top0, low0), jnp.where(self.first_row, top1, low1)])

    def col_next(self, v):
        own0, own1, halo0, halo1 = [pltpu.roll(x, LANES - 1, 1) for x in v.tiles]
        return Tiles([jnp.where(self.last_lane, own1, own0), own1, jnp.where(self.last_lane, halo1, halo0), halo1])

    def col_prev(self, v):
        own0, own1, halo0, halo1 = [pltpu.roll(x, 1, 1) for x in v.tiles]
        return Tiles([own0, jnp.where(self.first_lane, own0, own1), halo0, jnp.where(self.first_lane, halo0, halo1)])


class Turns:
    row_next = staticmethod(row_next)
    row_prev = staticmethod(row_prev)
    col_next = staticmethod(col_next)
    col_prev = staticmethod(col_prev)


def horizontal(g0, g1, e_row, e_row_prev, e_col, e_half, moves, rows=None):
    row_next, row_prev, col_next, col_prev = moves.row_next, moves.row_prev, moves.col_next, moves.col_prev
    g0n, g0p, g1n, g1p = rows or (row_next(g0), row_prev(g0), row_next(g1), row_prev(g1))
    g1c = col_next(g1)
    f = e_half * (g1c - col_prev(g1))
    h = e_half * (g0n - g0p)
    out0 = e_row * (g0 - g0n) + e_row_prev * (g0 - g0p) - row_next(f) + row_prev(f)
    flux = e_col * (g0 - col_next(g0))
    out0 = out0 + (flux - col_prev(flux))
    flux = (4.0 * e_col) * (g1 - g1c)
    out1 = flux - col_next(h) - col_prev(flux - h)
    out1 = out1 + 0.25 * (e_row * (g1 - g1n) + e_row_prev * (g1 - g1p))
    return out0, out1


def main_kernel(
    rhs, eta, friction, ice, grounded, strip_a, strip_b,
    power_1, power_2, power_3, power_4, sums, ribbon,
    masked, eta_row, eta_col, eta_half, eta_up, cover, drag,
):
    layers = eta.shape[0]
    plane = own_planes(rhs, eta, friction, ice, grounded)
    below_and_above, above_and_below = beyond()
    lane = lax.broadcasted_iota(jnp.int32, (2 * ROWS, LANES), 1)

    def target(p):
        if p < 2 * layers:
            return masked, (p // layers, p % layers)
        if p < 3 * layers:
            return eta_half, (p - 2 * layers,)
        return (cover if p == 3 * layers else drag), ()

    strips = [jnp.zeros((2 * ROWS, LANES), jnp.float32) for _ in range(ribbon.shape[0])]
    for q in range(strip_a.shape[0] // 2):
        first, second = pair_of(q, layers)
        halves = ([], [])
        for half in range(2):
            from_a, from_b = strip_a[2 * q + half], strip_b[2 * q + half]
            halves[0].append(below_and_above(from_a, from_b))
            halves[1].append(pltpu.roll(above_and_below(from_a, from_b), HALO, 0))
        for p, halo in zip((first, second), halves):
            v = plane(p)
            ref, at = target(p)
            for half in range(2):
                ref[(half, *at, pl.ds(FIRST + HALO, ROWS))] = v[:, half * LANES : (half + 1) * LANES]
                ref[(half, *at, pl.ds(FIRST, HALO))] = halo[half][HALO:]
                ref[(half, *at, pl.ds(FIRST + HALO + ROWS, HALO))] = halo[half][:HALO]
            head = jnp.concatenate([v[:, :LANES], halo[0]], 0)
            tail = jnp.concatenate([v[:, LANES:], halo[1]], 0)
            tile, slots = ribbon_places(p, layers)
            for slot in slots:
                at = slot * SLOT
                strips[tile] = jnp.where(between(lane, at, 8), turned(tail, at + 8), strips[tile])
                strips[tile] = jnp.where(between(lane, at + 20, 8), turned(head, at + 20), strips[tile])
    for tile, v in enumerate(strips):
        ribbon[tile] = v

    moves = Moves()
    load = Tiles.load
    before = None
    for k in range(layers):
        e = load(eta_half, k)
        (2.0 * (e + load(eta_half, k, shift=1))).store(eta_row, k)
        (0.5 * (e + moves.col_next(e))).store(eta_col, k)
        if k:
            (before + e).store(eta_up, k - 1)
        before = e
    (0.0 * before).store(eta_up, layers - 1)
    for k in range(layers):
        (0.5 * load(eta_half, k)).store(eta_half, k)

    def apply(src, dst):
        def layer(k, carry):
            below0, below1, odd, even = carry
            g0, g1 = load(src, 0, k), load(src, 1, k)
            after = jnp.minimum(k + 1, layers - 1)
            e_up = load(eta_up, k)
            up0 = e_up * (g0 - load(src, 0, after))
            up1 = e_up * (g1 - load(src, 1, after))
            rows = [load(src, c, k, shift=d) for c in (0, 1) for d in (1, -1)]
            coefficients = (load(eta_row, k), load(eta_row, k, shift=-1), load(eta_col, k), load(eta_half, k))
            out0, out1 = horizontal(g0, g1, *coefficients, moves, rows)
            m = load(cover)
            out0, out1 = m * (out0 + (up0 - Tiles(below0))), m * (out1 + (up1 - Tiles(below1)))
            out0.store(dst, 0, k)
            out1.store(dst, 1, k)
            odd = Tiles(odd) + (g0 * out0 + g1 * out1)
            even = Tiles(even) + (out0 * out0 + out1 * out1)
            return up0.tiles, up1.tiles, odd.tiles, even.tiles

        def block(b, carry):
            for i in range(UNROLL):
                carry = layer(b * UNROLL + i, carry)
            return carry

        zero = [jnp.zeros((ROWS, LANES), jnp.float32)] * 4
        d = -1.0 * load(drag)
        start = ((d * load(src, 0, 0)).tiles, (d * load(src, 1, 0)).tiles, zero, zero)
        ends = lax.fori_loop(0, layers // UNROLL, block, start)[2:]
        halo = lax.broadcasted_iota(jnp.int32, (ROWS, LANES), 0) < HALO
        return [jnp.concatenate([jnp.where(halo, v[2 + i], v[i]) for i in (0, 1)], 1) for v in ends]

    bare = 1.0 - ice[...].astype(jnp.float32)
    whole = jnp.zeros((ROWS, 2 * LANES), jnp.float32)
    outside = jnp.zeros((ROWS, 2 * LANES), jnp.float32)
    for c in range(2):
        for k in range(layers):
            square = rhs[c, k] * rhs[c, k]
            whole = whole + square
            outside = outside + bare * square
    sums[0] = whole
    wide = lax.broadcasted_iota(jnp.int32, (ROWS, 2 * LANES), 1)
    inner = between(wide, HALO, 2 * LANES - 2 * HALO)
    fields = (masked, power_1, power_2, power_3, power_4)
    for t in range(1, STEPS + 1):
        odd, even = apply(fields[t - 1], fields[t])
        sums[2 * t - 1] = jnp.where(inner, odd, 0.0) + outside
        sums[2 * t] = jnp.where(inner, even, 0.0) + outside


def ribbon_kernel(ribbon, columns, columns_a, columns_b, sums, edges, moments):
    tiles = edges.shape[2]
    below_and_above, _ = beyond()
    lane = lax.broadcasted_iota(jnp.int32, (2 * ROWS, LANES), 1)

    count = columns.shape[0] // 2
    beside = [
        jnp.concatenate([columns[i], below_and_above(columns_a[i], columns_b[i])], 0) for i in range(2 * count)
    ]
    spot = lane % SLOT

    def whole(tile):
        group, at = packed_place(tile)
        right = jnp.where(between(spot, 8, HALO), turned(beside[group], 8 - at), ribbon[tile])
        return jnp.where(between(spot, 16, HALO), turned(beside[count + group], 16 - at), right)

    field = [[whole(c * tiles + n) for n in range(tiles)] for c in range(2)]
    eta = [whole(2 * tiles + n) for n in range(tiles)]
    cover, drag = whole(3 * tiles), whole(3 * tiles + 1)

    def after(v):
        return v[1:] + [turned(v[0], -SLOT)]

    eta_row = [2.0 * (e + row_next(e)) for e in eta]
    eta_row_prev = [row_prev(e) for e in eta_row]
    eta_col = [0.5 * (e + col_next(e)) for e in eta]
    eta_half = [0.5 * e for e in eta]
    eta_up = [e + n for e, n in zip(eta, after(eta))]
    eta_up[-1] = jnp.where(lane < LANES - SLOT, eta_up[-1], 0.0)
    place = lax.broadcasted_iota(jnp.int32, (ROWS, LANES), 1) % SLOT
    edge = between(place, 4, HALO) | between(place, 20, HALO)
    extra = [None]
    for t in range(1, STEPS + 1):
        ups = [[u * (g - n) for u, g, n in zip(eta_up, field[c], after(field[c]))] for c in range(2)]
        result = ([], [])
        odd = even = jnp.zeros((ROWS, LANES), jnp.float32)
        for n in range(tiles):
            coefficients = (eta_row[n], eta_row_prev[n], eta_col[n], eta_half[n])
            outs = horizontal(field[0][n], field[1][n], *coefficients, Turns)
            for c in range(2):
                below = ups[c][n - 1] if n else turned(ups[c][-1], SLOT) - drag * field[c][0]
                out = cover * (outs[c] + (ups[c][n] - below))
                result[c].append(out)
                now = out[:ROWS]
                edges[t - 1, c, n] = now
                odd = odd + field[c][n][:ROWS] * now
                even = even + now * now
        field = result
        extra.extend([jnp.where(edge, odd, 0.0), jnp.where(edge, even, 0.0)])

    tall = lax.broadcasted_iota(jnp.int32, (2 * ROWS, LANES), 0)
    high = jnp.zeros((2 * ROWS, LANES), jnp.float32)
    low = jnp.zeros((2 * ROWS, LANES), jnp.float32)
    for j, more in enumerate(extra):
        total = sums[j]
        pair = two_sum(total[:, :LANES], total[:, LANES:])
        if more is not None:
            pair = join(pair, (more, jnp.zeros_like(more)))
        for step in (4, 2, 1):
            pair = join(pair, tuple(pltpu.roll(v, step, 0) for v in pair))
        high = jnp.where(tall == j, jnp.concatenate([pair[0]] * 2, 0), high)
        low = jnp.where(tall == j, jnp.concatenate([pair[1]] * 2, 0), low)
    moments[0] = high
    moments[1] = low


def add_kernel(*refs):
    *ins, out = refs
    total = (ins[0][0], ins[0][1])
    for x in ins[1:]:
        total = join(total, (x[0], x[1]))
    out[0], out[1] = total


def solve(total):
    for step in (64, 32, 16, 8, 4, 2, 1):
        total = join(total, tuple(pltpu.roll(v, step, 1) for v in total))

    def spread(v, j):
        return jnp.broadcast_to(v[j : j + 1], (ROWS, LANES))

    centre = spread(total[0], 1) / spread(total[0], 0)
    wide = jnp.concatenate([centre, centre], 0)
    mu = [spread(total[0], 0)]
    for _ in range(2 * STEPS):
        step = times(wide, total)
        total = join(tuple(pltpu.roll(v, 2 * ROWS - 1, 0) for v in total), (-step[0], -step[1]))
        mu.append(spread(total[0], 0))

    def plus(a, b):
        n = max(len(a), len(b))
        return [a[i] + b[i] if i < min(len(a), len(b)) else (a[i] if i < len(a) else b[i]) for i in range(n)]

    def scaled(s, a):
        return [s * x for x in a]

    def operator(a):
        return plus([centre * x for x in a], [jnp.zeros_like(centre)] + a)

    def dot(a, b):
        square = [None] * (len(a) + len(b) - 1)
        for i, x in enumerate(a):
            for j, y in enumerate(b):
                z = x * y
                square[i + j] = z if square[i + j] is None else square[i + j] + z
        value = square[0] * mu[0]
        for n in range(1, len(square)):
            value = value + square[n] * mu[n]
        return value

    one = jnp.ones_like(centre)
    right = [one]
    quasi, search, update, iterate = right, right, [], []
    applied = operator(search)
    carried = applied
    rho = mu[0]
    tau_sq = rho
    alpha = theta_sq = eta = None
    for half in range(STEPS):
        if half % 2 == 0:
            alpha = rho / dot(carried, right)
            search_next = plus(search, scaled(-alpha, carried))
        quasi = plus(quasi, scaled(-alpha, applied))
        if half:
            update = plus(search, scaled(theta_sq / alpha * eta, update))
        else:
            update = search
        theta_sq = dot(quasi, quasi) / tau_sq
        cosine_sq = 1.0 / (1.0 + theta_sq)
        tau_sq = tau_sq * theta_sq * cosine_sq
        eta = cosine_sq * alpha
        iterate = plus(iterate, scaled(eta, update))
        if half % 2 == 0:
            search = search_next
            applied = operator(search)
        elif half < STEPS - 1:
            rho_next = dot(quasi, right)
            beta = rho_next / rho
            search = plus(quasi, scaled(beta, search))
            applied_next = operator(search)
            carried = plus(applied_next, scaled(beta, plus(applied, scaled(beta, carried))))
            applied, rho = applied_next, rho_next
    powers = [iterate[-1]]
    for c in iterate[-2::-1]:
        powers = plus([c] + powers, scaled(-centre, powers))
    return powers


def final_kernel(rhs, power_1, power_2, power_3, power_4, edges, friction, ice, grounded, speed, *rest):
    *parts, iterate, residual, hessian = rest
    layers, tiles = rhs.shape[1], edges.shape[2]
    total = (parts[0][0], parts[0][1])
    for x in parts[1:]:
        total = join(total, (x[0], x[1]))
    factors = solve(total)
    powers = (power_1, power_2, power_3, power_4)
    wide = [jnp.concatenate([c, c], 1) for c in factors]
    rest = sum(wide[1:], wide[0])
    cover = ice[...].astype(jnp.float32)
    lane = lax.broadcasted_iota(jnp.int32, (ROWS, LANES), 1)

    def combined(vectors, weights):
        x = weights[1] * vectors[0]
        y = weights[0] * vectors[0]
        for t in range(1, STEPS):
            if t + 1 < STEPS:
                x = x + weights[t + 1] * vectors[t]
            y = y + weights[t] * vectors[t]
        return x, y

    for c in range(2):
        side = [combined([edges[t, c, n] for t in range(STEPS)], factors) for n in range(tiles)]
        for k in range(layers):
            at = k // tiles * SLOT
            halves = [
                combined([p[half, c, k, FIRST + HALO : FIRST + HALO + ROWS] for p in powers], factors)
                for half in (0, 1)
            ]
            inner = zip(*halves)
            patched = []
            for (head, tail), e in zip(inner, side[k % tiles]):
                head = jnp.where(lane < HALO, turned(e, -at - 20), head)
                tail = jnp.where(lane >= LANES - HALO, turned(e, 120 - at), tail)
                patched.append(jnp.concatenate([head, tail], 1))
            r = rhs[c, k]
            x, y = patched
            iterate[c, k] = jnp.where(cover > 0.0, wide[0] * r + x, rest * r)
            residual[c, k] = r - jnp.where(cover > 0.0, y, rest * r)
    weight = cover * (friction[...] * grounded[...].astype(jnp.float32))
    hessian[...] = weight * (speed[0] * iterate[0, 0] + speed[1] * iterate[1, 0])


def exchange(x, axis):
    count = lax.axis_size(axis)
    stride = 1
    rounds = []
    while stride < count:
        size = 4 if (count // stride) % 4 == 0 else 2
        rounds.append((stride, size))
        stride *= size
    for at, (stride, size) in enumerate(rounds):
        parts = [x]
        for turn in range(1, size):
            pairs = []
            for i in range(count):
                place = (i // stride) % size
                pairs.append((i, i + ((place ^ turn) - place) * stride))
            parts.append(lax.ppermute(x, axis, pairs))
        if at == len(rounds) - 1:
            return parts
        x = call(add_kernel, [x.shape])(*parts)[0]
    return [x]


def body(adjoint_rhs, viscosity, friction, ice_mask, grounded, basal_velocity):
    layers = viscosity.shape[0]
    inputs = (adjoint_rhs, viscosity, friction, ice_mask, grounded, basal_velocity)
    tile = (ROWS, LANES)
    strips = (2 * (layers + layers // 2 + 1),) + tile
    ribbons = ribbon_tiles(layers)
    packed = ((ribbons + 7) // 8,) + tile
    both = (2 * packed[0],) + tile
    *held, column_a, column_b, strip_a, strip_b = call(
        pack_kernel,
        [jax.ShapeDtypeStruct(x.shape, x.dtype) for x in inputs] + [packed, packed, strips, strips],
        [pltpu.SemaphoreType.DMA((len(inputs),))],
        in_specs=[pl.BlockSpec(memory_space=pltpu.HBM)] * len(inputs),
    )(*[pltpu.with_memory_space_constraint(x, pltpu.HBM) for x in inputs])
    strip_a, strip_b = swapped(strip_a, "gx", 0), swapped(strip_b, "gx", 1)
    beside = ("gy", "gz")
    (columns,) = call(beside_kernel, [both])(swapped(column_a, beside, 0), swapped(column_b, beside, 1))
    columns_a, columns_b = swapped(columns, "gx", 0), swapped(columns, "gx", 1)
    block = (layers, 3 * ROWS, LANES)
    *powers, sums, ribbon = call(
        main_kernel,
        [(2, 2) + block] * STEPS + [(2 * STEPS + 1, ROWS, 2 * LANES), (ribbons, 2 * ROWS, LANES)],
        [(2, 2) + block] + [(2,) + block] * 4 + [(2,) + block[1:]] * 2,
        cost_estimate=pl.CostEstimate(flops=200_000_000, bytes_accessed=8_000_000, transcendentals=0),
    )(*held[:5], strip_a, strip_b)
    edges, sums = call(
        ribbon_kernel,
        [(STEPS, 2, layers // 4) + tile, (2, 2 * ROWS, LANES)],
    )(ribbon, columns, columns_a, columns_b, sums)
    parts = exchange(sums, ("gy", "gz"))
    if len(parts) > 1:
        sums = call(add_kernel, [sums.shape])(*parts)[0]
    parts = exchange(sums, "gx")
    rhs, _, friction, ice_mask, grounded, speed = held
    return tuple(
        call(final_kernel, [adjoint_rhs.shape, adjoint_rhs.shape, friction.shape])(
            rhs, *powers, edges, friction, ice_mask, grounded, speed, *parts
        )
    )


def solution(mesh):
    in_specs = (
        P(None, None, ("parts", "gx"), ("gy", "gz")),
        P(None, ("parts", "gx"), ("gy", "gz")),
        P(("parts", "gx"), ("gy", "gz")),
        P(("parts", "gx"), ("gy", "gz")),
        P(("parts", "gx"), ("gy", "gz")),
        P(None, ("parts", "gx"), ("gy", "gz")),
    )
    out_specs = (
        P(None, None, ("parts", "gx"), ("gy", "gz")),
        P(None, None, ("parts", "gx"), ("gy", "gz")),
        P(("parts", "gx"), ("gy", "gz")),
    )
    return jax.shard_map(body, mesh=mesh, in_specs=in_specs, out_specs=out_specs, check_vma=False)
```

```python
import functools

import jax
import jax.numpy as jnp
from jax import lax
from jax.experimental import pallas as pl
from jax.experimental.pallas import tpu as pltpu
from jax.sharding import PartitionSpec as P

STEPS = 4
HALO = 4
ROWS = 8
LANES = 128
UNROLL = 5
SLOT = 32


def call(kernel, outs, scratch=(), **more):
    return pl.pallas_call(
        kernel,
        out_shape=[jax.ShapeDtypeStruct(s, jnp.float32) if isinstance(s, tuple) else s for s in outs],
        scratch_shapes=[pltpu.VMEM(s, jnp.float32) if isinstance(s, tuple) else s for s in scratch],
        compiler_params=pltpu.CompilerParams(vmem_limit_bytes=40 * 1024 * 1024),
        **more,
    )


def place_of(axis):
    place, count = lax.axis_index(axis), lax.axis_size(axis)
    even = place % 2 == 0
    has_a = jnp.logical_or(jnp.logical_not(even), place < count - 1)
    has_b = jnp.where(even, place > 0, place < count - 1)
    return even, has_a, has_b


def swapped(x, axis, first):
    count = lax.axis_size(axis)
    pairs = []
    for i in range(count):
        other = i + 1 if (i - first) % 2 == 0 else i - 1
        pairs.append((i, other if 0 <= other < count else i))
    return lax.ppermute(x, axis, pairs)


def own_planes(rhs, eta, friction, ice, grounded):
    layers = eta.shape[0]
    cover = ice[...].astype(jnp.float32)
    drag = friction[...] * grounded[...].astype(jnp.float32)

    def plane(p):
        if p < 2 * layers:
            return rhs[p // layers, p % layers] * cover
        if p < 3 * layers:
            return eta[p - 2 * layers]
        return cover if p == 3 * layers else drag

    return plane


def pair_of(q, layers):
    if q < layers:
        return q, q + layers
    if q < layers + layers // 2:
        return q + layers, q + layers + layers // 2
    return 3 * layers, 3 * layers + 1


def ribbon_places(p, layers):
    tiles = layers // 4
    if p < 3 * layers:
        k = p % layers
        return p // layers * tiles + k % tiles, (k // tiles,)
    return (3 * tiles, (0, 1, 2, 3)) if p == 3 * layers else (3 * tiles + 1, (0,))


def ribbon_tiles(layers):
    return 3 * (layers // 4) + 2


def packed_place(tile):
    return tile // 8, HALO * (tile % 8)


def between(lane, first, width):
    return (lane >= first) & (lane < first + width)


def turned(v, shift):
    shift = shift % LANES
    return pltpu.roll(v, shift, 1) if shift else v


def pack_kernel(*refs):
    sources, held, (column_a, column_b, strip_a, strip_b, arrived) = refs[:6], refs[6:12], refs[12:]
    copies = [pltpu.make_async_copy(a, b, arrived.at[i]) for i, (a, b) in enumerate(zip(sources, held))]
    for copy in copies:
        copy.start()
    for copy in copies:
        copy.wait()
    rhs, eta, friction, ice, grounded, _ = held
    layers = eta.shape[0]
    plane = own_planes(rhs, eta, friction, ice, grounded)
    lane = lax.broadcasted_iota(jnp.int32, (ROWS, LANES), 1)
    row = lax.broadcasted_iota(jnp.int32, (ROWS, LANES), 0)
    rows_even, _, _ = place_of("gx")
    columns_even, _, _ = place_of(("gy", "gz"))
    upper_a = (row < HALO) != rows_even
    count = ribbon_tiles(layers)
    zero = jnp.zeros((ROWS, LANES), jnp.float32)
    left, right = [zero] * count, [zero] * count
    for q in range(strip_a.shape[0] // 2):
        first, second = pair_of(q, layers)
        x, y = plane(first), plane(second)
        for half in range(2):
            xs = x[:, half * LANES : (half + 1) * LANES]
            ys = y[:, half * LANES : (half + 1) * LANES]
            ys = pltpu.roll(ys, HALO, 0)
            strip_a[2 * q + half] = jnp.where(upper_a, xs, ys)
            strip_b[2 * q + half] = jnp.where(upper_a, ys, xs)
        for p, v in ((first, x), (second, y)):
            tile, slots = ribbon_places(p, layers)
            for slot in slots:
                at = slot * SLOT
                left[tile] = jnp.where(between(lane, at + 8, 4), turned(v[:, :LANES], at + 8), left[tile])
                right[tile] = jnp.where(between(lane, at + 16, 4), turned(v[:, LANES:], at + 20), right[tile])
    to_left, to_right = [zero] * column_a.shape[0], [zero] * column_a.shape[0]
    for tile in range(count):
        group, at = packed_place(tile)
        here = between(lane % SLOT, at, HALO)
        to_left[group] = jnp.where(here, turned(left[tile], at - 8), to_left[group])
        to_right[group] = jnp.where(here, turned(right[tile], at - 16), to_right[group])
    for group in range(column_a.shape[0]):
        column_a[group] = jnp.where(columns_even, to_right[group], to_left[group])
        column_b[group] = jnp.where(columns_even, to_left[group], to_right[group])


def beside_kernel(from_a, from_b, columns):
    even, has_a, has_b = place_of(("gy", "gz"))
    count = from_a.shape[0]
    for group in range(count):
        a = jnp.where(has_a, from_a[group], 0.0)
        b = jnp.where(has_b, from_b[group], 0.0)
        columns[group] = jnp.where(even, a, b)
        columns[count + group] = jnp.where(even, b, a)


def two_sum(a, b):
    s = a + b
    t = s - a
    return s, (a - (s - t)) + (b - t)


def join(x, y):
    s, e = two_sum(x[0], y[0])
    e = e + (x[1] + y[1])
    h = s + e
    return h, e - (h - s)


def times(scalar, x):
    def cut(v):
        t = v * 4097.0
        h = t - (t - v)
        return h, v - h

    p = scalar * x[0]
    sh, sl = cut(scalar)
    xh, xl = cut(x[0])
    e = ((sh * xh - p) + sh * xl + sl * xh) + sl * xl
    return p, e + scalar * x[1]


def beyond():
    even, has_a, has_b = place_of("gx")
    upper_a = (lax.broadcasted_iota(jnp.int32, (ROWS, LANES), 0) < HALO) == even

    def below_and_above(from_a, from_b):
        return jnp.where(upper_a, jnp.where(has_a, from_a, 0.0), jnp.where(has_b, from_b, 0.0))

    def above_and_below(from_a, from_b):
        return jnp.where(upper_a, jnp.where(has_b, from_b, 0.0), jnp.where(has_a, from_a, 0.0))

    return below_and_above, above_and_below


def row_next(v):
    return pltpu.roll(v, 2 * ROWS - 1, 0)


def row_prev(v):
    return pltpu.roll(v, 1, 0)


def col_next(v):
    return pltpu.roll(v, v.shape[1] - 1, 1)


def col_prev(v):
    return pltpu.roll(v, 1, 1)


class Tiles:
    def __init__(self, tiles):
        self.tiles = tiles

    @staticmethod
    def load(ref):
        return Tiles([ref[r : r + ROWS, c : c + LANES] for r in (0, ROWS) for c in (0, LANES)])

    def store(self, ref):
        for v, (r, c) in zip(self.tiles, ((0, 0), (0, LANES), (ROWS, 0), (ROWS, LANES))):
            ref[r : r + ROWS, c : c + LANES] = v

    def both(self, other, op):
        if isinstance(other, Tiles):
            return Tiles([op(x, y) for x, y in zip(self.tiles, other.tiles)])
        return Tiles([op(x, other) for x in self.tiles])

    def __add__(self, other):
        return self.both(other, lambda x, y: x + y)

    def __sub__(self, other):
        return self.both(other, lambda x, y: x - y)

    def __mul__(self, other):
        return self.both(other, lambda x, y: x * y)

    __rmul__ = __mul__


class Moves:
    def __init__(self):
        row = lax.broadcasted_iota(jnp.int32, (ROWS, LANES), 0)
        lane = lax.broadcasted_iota(jnp.int32, (ROWS, LANES), 1)
        self.first_row, self.last_row = row == 0, row == ROWS - 1
        self.first_lane, self.last_lane = lane == 0, lane == LANES - 1

    def rows(self, v, shift, edge):
        own0, own1, halo0, halo1 = [pltpu.roll(x, shift, 0) for x in v.tiles]
        return Tiles(
            [
                jnp.where(edge, halo0, own0),
                jnp.where(edge, halo1, own1),
                jnp.where(edge, own0, halo0),
                jnp.where(edge, own1, halo1),
            ]
        )

    def row_next(self, v):
        return self.rows(v, ROWS - 1, self.last_row)

    def row_prev(self, v):
        return self.rows(v, 1, self.first_row)

    def col_next(self, v):
        own0, own1, halo0, halo1 = [pltpu.roll(x, LANES - 1, 1) for x in v.tiles]
        return Tiles([jnp.where(self.last_lane, own1, own0), own1, jnp.where(self.last_lane, halo1, halo0), halo1])

    def col_prev(self, v):
        own0, own1, halo0, halo1 = [pltpu.roll(x, 1, 1) for x in v.tiles]
        return Tiles([own0, jnp.where(self.first_lane, own0, own1), halo0, jnp.where(self.first_lane, halo0, halo1)])


class Turns:
    row_next = staticmethod(row_next)
    row_prev = staticmethod(row_prev)
    col_next = staticmethod(col_next)
    col_prev = staticmethod(col_prev)


def horizontal(g0, g1, e_row, e_col, e_half, moves):
    row_next, row_prev, col_next, col_prev = moves.row_next, moves.row_prev, moves.col_next, moves.col_prev
    g0n, g1n = row_next(g0), col_next(g1)
    f = e_half * (g1n - col_prev(g1))
    h = e_half * (g0n - row_prev(g0))
    flux = e_row * (g0 - g0n)
    out0 = flux - row_next(f) - row_prev(flux - f)
    flux = e_col * (g0 - col_next(g0))
    out0 = out0 + (flux - col_prev(flux))
    flux = (4.0 * e_col) * (g1 - g1n)
    out1 = flux - col_next(h) - col_prev(flux - h)
    flux = (0.25 * e_row) * (g1 - row_next(g1))
    out1 = out1 + (flux - row_prev(flux))
    return out0, out1


def main_kernel(
    rhs, eta, friction, ice, grounded, strip_b, strip_a,
    powers, sums, ribbon,
    field_a, field_b, eta_row, eta_col, eta_half, eta_up, cover, drag,
):
    layers = eta.shape[0]
    plane = own_planes(rhs, eta, friction, ice, grounded)
    below_and_above, above_and_below = beyond()
    lane = lax.broadcasted_iota(jnp.int32, (2 * ROWS, LANES), 1)

    def target(p):
        if p < 2 * layers:
            return field_a.at[p // layers, p % layers]
        if p < 3 * layers:
            return eta_half.at[p - 2 * layers]
        return cover if p == 3 * layers else drag

    strips = [jnp.zeros((2 * ROWS, LANES), jnp.float32) for _ in range(ribbon.shape[0])]
    for q in range(strip_a.shape[0] // 2):
        first, second = pair_of(q, layers)
        halves = ([], [])
        for half in range(2):
            from_a, from_b = strip_a[2 * q + half], strip_b[2 * q + half]
            halves[0].append(below_and_above(from_a, from_b))
            halves[1].append(pltpu.roll(above_and_below(from_a, from_b), HALO, 0))
        for p, halo in zip((first, second), halves):
            v = plane(p)
            dst = target(p)
            dst[0:ROWS, :] = v
            dst[ROWS:, 0:LANES], dst[ROWS:, LANES:] = halo
            head = jnp.concatenate([v[:, :LANES], halo[0]], 0)
            tail = jnp.concatenate([v[:, LANES:], halo[1]], 0)
            tile, slots = ribbon_places(p, layers)
            for slot in slots:
                at = slot * SLOT
                strips[tile] = jnp.where(between(lane, at, 8), turned(tail, at + 8), strips[tile])
                strips[tile] = jnp.where(between(lane, at + 20, 8), turned(head, at + 20), strips[tile])
    for tile, v in enumerate(strips):
        ribbon[tile] = v

    moves = Moves()
    load = Tiles.load
    for k in range(layers):
        e = load(eta_half.at[k])
        (2.0 * (e + moves.row_next(e))).store(eta_row.at[k])
        (0.5 * (e + moves.col_next(e))).store(eta_col.at[k])
        eta_up[k] = eta_half[k] + eta_half[k + 1] if k + 1 < layers else jnp.zeros_like(eta_up[k])
        if k:
            eta_half[k - 1] = 0.5 * eta_half[k - 1]
    eta_half[layers - 1] = 0.5 * eta_half[layers - 1]

    def apply(t, src, dst):
        def layer(k, carry):
            below0, below1, odd, even = carry
            g0, g1 = load(src.at[0, k]), load(src.at[1, k])
            after = jnp.minimum(k + 1, layers - 1)
            e_up = load(eta_up.at[k])
            up0 = e_up * (g0 - load(src.at[0, after]))
            up1 = e_up * (g1 - load(src.at[1, after]))
            out0, out1 = horizontal(g0, g1, load(eta_row.at[k]), load(eta_col.at[k]), load(eta_half.at[k]), moves)
            m = load(cover)
            out0, out1 = m * (out0 + (up0 - Tiles(below0))), m * (out1 + (up1 - Tiles(below1)))
            if t < STEPS:
                out0.store(dst.at[0, k])
                out1.store(dst.at[1, k])
            odd, even = list(odd), list(even)
            for c, g, out in ((0, g0, out0), (1, g1, out1)):
                for half in range(2):
                    now = out.tiles[half]
                    powers[t - 1, c, k, :, half * LANES : (half + 1) * LANES] = now
                    odd[half] = odd[half] + g.tiles[half] * now
                    even[half] = even[half] + now * now
            return up0.tiles, up1.tiles, odd, even

        def block(b, carry):
            for i in range(UNROLL):
                carry = layer(b * UNROLL + i, carry)
            return carry

        zero = [jnp.zeros((ROWS, LANES), jnp.float32)] * 2
        d = -1.0 * load(drag)
        start = ((d * load(src.at[0, 0])).tiles, (d * load(src.at[1, 0])).tiles, zero, zero)
        ends = lax.fori_loop(0, layers // UNROLL, block, start)[2:]
        return [jnp.concatenate(v, 1) for v in ends]

    bare = 1.0 - ice[...].astype(jnp.float32)
    whole = jnp.zeros((ROWS, 2 * LANES), jnp.float32)
    outside = jnp.zeros((ROWS, 2 * LANES), jnp.float32)
    for c in range(2):
        for k in range(layers):
            square = rhs[c, k] * rhs[c, k]
            whole = whole + square
            outside = outside + bare * square
    sums[0] = whole
    wide = lax.broadcasted_iota(jnp.int32, (ROWS, 2 * LANES), 1)
    inner = between(wide, HALO, 2 * LANES - 2 * HALO)
    src, dst = field_a, field_b
    for t in range(1, STEPS + 1):
        odd, even = apply(t, src, dst)
        sums[2 * t - 1] = jnp.where(inner, odd, 0.0) + outside
        sums[2 * t] = jnp.where(inner, even, 0.0) + outside
        src, dst = dst, src


def ribbon_kernel(ribbon, columns, columns_a, columns_b, sums, edges, moments):
    tiles = edges.shape[2]
    below_and_above, _ = beyond()
    lane = lax.broadcasted_iota(jnp.int32, (2 * ROWS, LANES), 1)

    count = columns.shape[0] // 2
    beside = [
        jnp.concatenate([columns[i], below_and_above(columns_a[i], columns_b[i])], 0) for i in range(2 * count)
    ]
    spot = lane % SLOT

    def whole(tile):
        group, at = packed_place(tile)
        right = jnp.where(between(spot, 8, HALO), turned(beside[group], 8 - at), ribbon[tile])
        return jnp.where(between(spot, 16, HALO), turned(beside[count + group], 16 - at), right)

    field = [[whole(c * tiles + n) for n in range(tiles)] for c in range(2)]
    eta = [whole(2 * tiles + n) for n in range(tiles)]
    cover, drag = whole(3 * tiles), whole(3 * tiles + 1)

    def after(v):
        return v[1:] + [turned(v[0], -SLOT)]

    eta_row = [2.0 * (e + row_next(e)) for e in eta]
    eta_col = [0.5 * (e + col_next(e)) for e in eta]
    eta_half = [0.5 * e for e in eta]
    eta_up = [e + n for e, n in zip(eta, after(eta))]
    eta_up[-1] = jnp.where(lane < LANES - SLOT, eta_up[-1], 0.0)
    place = lax.broadcasted_iota(jnp.int32, (ROWS, LANES), 1) % SLOT
    edge = between(place, 4, HALO) | between(place, 20, HALO)
    extra = [None]
    for t in range(1, STEPS + 1):
        ups = [[u * (g - n) for u, g, n in zip(eta_up, field[c], after(field[c]))] for c in range(2)]
        result = ([], [])
        odd = even = jnp.zeros((ROWS, LANES), jnp.float32)
        for n in range(tiles):
            outs = horizontal(field[0][n], field[1][n], eta_row[n], eta_col[n], eta_half[n], Turns)
            for c in range(2):
                below = ups[c][n - 1] if n else turned(ups[c][-1], SLOT) - drag * field[c][0]
                out = cover * (outs[c] + (ups[c][n] - below))
                result[c].append(out)
                now = out[:ROWS]
                edges[t - 1, c, n] = now
                odd = odd + field[c][n][:ROWS] * now
                even = even + now * now
        field = result
        extra.extend([jnp.where(edge, odd, 0.0), jnp.where(edge, even, 0.0)])

    tall = lax.broadcasted_iota(jnp.int32, (2 * ROWS, LANES), 0)
    high = jnp.zeros((2 * ROWS, LANES), jnp.float32)
    low = jnp.zeros((2 * ROWS, LANES), jnp.float32)
    for j, more in enumerate(extra):
        total = sums[j]
        pair = two_sum(total[:, :LANES], total[:, LANES:])
        if more is not None:
            pair = join(pair, (more, jnp.zeros_like(more)))
        for step in (4, 2, 1):
            pair = join(pair, tuple(pltpu.roll(v, step, 0) for v in pair))
        high = jnp.where(tall == j, jnp.concatenate([pair[0]] * 2, 0), high)
        low = jnp.where(tall == j, jnp.concatenate([pair[1]] * 2, 0), low)
    moments[0] = high
    moments[1] = low


def add_kernel(*refs):
    *ins, out = refs
    total = (ins[0][0], ins[0][1])
    for x in ins[1:]:
        total = join(total, (x[0], x[1]))
    out[0], out[1] = total


def solve(total):
    for step in (64, 32, 16, 8, 4, 2, 1):
        total = join(total, tuple(pltpu.roll(v, step, 1) for v in total))

    def spread(v, j):
        return jnp.broadcast_to(v[j : j + 1], (ROWS, LANES))

    centre = spread(total[0], 1) / spread(total[0], 0)
    wide = jnp.concatenate([centre, centre], 0)
    mu = [spread(total[0], 0)]
    for _ in range(2 * STEPS):
        step = times(wide, total)
        total = join(tuple(pltpu.roll(v, 2 * ROWS - 1, 0) for v in total), (-step[0], -step[1]))
        mu.append(spread(total[0], 0))

    def plus(a, b):
        n = max(len(a), len(b))
        return [a[i] + b[i] if i < min(len(a), len(b)) else (a[i] if i < len(a) else b[i]) for i in range(n)]

    def scaled(s, a):
        return [s * x for x in a]

    def operator(a):
        return plus([centre * x for x in a], [jnp.zeros_like(centre)] + a)

    def dot(a, b):
        square = [None] * (len(a) + len(b) - 1)
        for i, x in enumerate(a):
            for j, y in enumerate(b):
                z = x * y
                square[i + j] = z if square[i + j] is None else square[i + j] + z
        value = square[0] * mu[0]
        for n in range(1, len(square)):
            value = value + square[n] * mu[n]
        return value

    one = jnp.ones_like(centre)
    right = [one]
    quasi, search, update, iterate = right, right, [], []
    applied = operator(search)
    carried = applied
    rho = mu[0]
    tau_sq = rho
    alpha = theta_sq = eta = None
    for half in range(STEPS):
        if half % 2 == 0:
            alpha = rho / dot(carried, right)
            search_next = plus(search, scaled(-alpha, carried))
        quasi = plus(quasi, scaled(-alpha, applied))
        if half:
            update = plus(search, scaled(theta_sq / alpha * eta, update))
        else:
            update = search
        theta_sq = dot(quasi, quasi) / tau_sq
        cosine_sq = 1.0 / (1.0 + theta_sq)
        tau_sq = tau_sq * theta_sq * cosine_sq
        eta = cosine_sq * alpha
        iterate = plus(iterate, scaled(eta, update))
        if half % 2 == 0:
            search = search_next
            applied = operator(search)
        elif half < STEPS - 1:
            rho_next = dot(quasi, right)
            beta = rho_next / rho
            search = plus(quasi, scaled(beta, search))
            applied_next = operator(search)
            carried = plus(applied_next, scaled(beta, plus(applied, scaled(beta, carried))))
            applied, rho = applied_next, rho_next
    powers = [iterate[-1]]
    for c in iterate[-2::-1]:
        powers = plus([c] + powers, scaled(-centre, powers))
    return powers


def final_kernel(rhs, powers, edges, friction, ice, grounded, speed, *rest):
    *parts, iterate, residual, hessian = rest
    layers, tiles = rhs.shape[1], edges.shape[2]
    total = (parts[0][0], parts[0][1])
    for x in parts[1:]:
        total = join(total, (x[0], x[1]))
    factors = solve(total)
    wide = [jnp.concatenate([c, c], 1) for c in factors]
    rest = sum(wide[1:], wide[0])
    cover = ice[...].astype(jnp.float32)
    lane = lax.broadcasted_iota(jnp.int32, (ROWS, LANES), 1)

    def combined(vectors, weights):
        x = weights[1] * vectors[0]
        y = weights[0] * vectors[0]
        for t in range(1, STEPS):
            if t + 1 < STEPS:
                x = x + weights[t + 1] * vectors[t]
            y = y + weights[t] * vectors[t]
        return x, y

    for c in range(2):
        side = [combined([edges[t, c, n] for t in range(STEPS)], factors) for n in range(tiles)]
        for k in range(layers):
            at = k // tiles * SLOT
            inner = combined([powers[t, c, k] for t in range(STEPS)], wide)
            patched = []
            for v, e in zip(inner, side[k % tiles]):
                head = jnp.where(lane < HALO, turned(e, -at - 20), v[:, :LANES])
                tail = jnp.where(lane >= LANES - HALO, turned(e, 120 - at), v[:, LANES:])
                patched.append(jnp.concatenate([head, tail], 1))
            r = rhs[c, k]
            x, y = patched
            iterate[c, k] = jnp.where(cover > 0.0, wide[0] * r + x, rest * r)
            residual[c, k] = r - jnp.where(cover > 0.0, y, rest * r)
    weight = cover * (friction[...] * grounded[...].astype(jnp.float32))
    hessian[...] = weight * (speed[0] * iterate[0, 0] + speed[1] * iterate[1, 0])


def exchange(x, axis):
    count = lax.axis_size(axis)
    stride = 1
    rounds = []
    while stride < count:
        size = 4 if (count // stride) % 4 == 0 else 2
        rounds.append((stride, size))
        stride *= size
    for at, (stride, size) in enumerate(rounds):
        parts = [x]
        for turn in range(1, size):
            pairs = []
            for i in range(count):
                place = (i // stride) % size
                pairs.append((i, i + ((place ^ turn) - place) * stride))
            parts.append(lax.ppermute(x, axis, pairs))
        if at == len(rounds) - 1:
            return parts
        x = call(add_kernel, [x.shape])(*parts)[0]
    return [x]


def body(adjoint_rhs, viscosity, friction, ice_mask, grounded, basal_velocity):
    layers = viscosity.shape[0]
    inputs = (adjoint_rhs, viscosity, friction, ice_mask, grounded, basal_velocity)
    tile = (ROWS, LANES)
    strips = (2 * (layers + layers // 2 + 1),) + tile
    ribbons = ribbon_tiles(layers)
    packed = ((ribbons + 7) // 8,) + tile
    both = (2 * packed[0],) + tile
    *held, column_a, column_b, strip_a, strip_b = call(
        pack_kernel,
        [jax.ShapeDtypeStruct(x.shape, x.dtype) for x in inputs] + [packed, packed, strips, strips],
        [pltpu.SemaphoreType.DMA((len(inputs),))],
        in_specs=[pl.BlockSpec(memory_space=pltpu.HBM)] * len(inputs),
    )(*[pltpu.with_memory_space_constraint(x, pltpu.HBM) for x in inputs])
    strip_b, strip_a = swapped(strip_b, "gx", 1), swapped(strip_a, "gx", 0)
    beside = ("gy", "gz")
    (columns,) = call(beside_kernel, [both])(swapped(column_a, beside, 0), swapped(column_b, beside, 1))
    columns_a, columns_b = swapped(columns, "gx", 0), swapped(columns, "gx", 1)
    block = (layers, 2 * ROWS, 2 * LANES)
    powers, sums, ribbon = call(
        main_kernel,
        [(STEPS,) + adjoint_rhs.shape, (2 * STEPS + 1, ROWS, 2 * LANES), (ribbons, 2 * ROWS, LANES)],
        [(2,) + block] * 2 + [block] * 4 + [block[1:]] * 2,
        cost_estimate=pl.CostEstimate(flops=200_000_000, bytes_accessed=8_000_000, transcendentals=0),
    )(*held[:5], strip_b, strip_a)
    edges, sums = call(
        ribbon_kernel,
        [(STEPS, 2, layers // 4) + tile, (2, 2 * ROWS, LANES)],
    )(ribbon, columns, columns_a, columns_b, sums)
    parts = exchange(sums, ("gy", "gz"))
    if len(parts) > 1:
        sums = call(add_kernel, [sums.shape])(*parts)[0]
    parts = exchange(sums, "gx")
    rhs, _, friction, ice_mask, grounded, speed = held
    return tuple(
        call(final_kernel, [adjoint_rhs.shape, adjoint_rhs.shape, friction.shape])(
            rhs, powers, edges, friction, ice_mask, grounded, speed, *parts
        )
    )


def solution(mesh):
    in_specs = (
        P(None, None, ("parts", "gx"), ("gy", "gz")),
        P(None, ("parts", "gx"), ("gy", "gz")),
        P(("parts", "gx"), ("gy", "gz")),
        P(("parts", "gx"), ("gy", "gz")),
        P(("parts", "gx"), ("gy", "gz")),
        P(None, ("parts", "gx"), ("gy", "gz")),
    )
    out_specs = (
        P(None, None, ("parts", "gx"), ("gy", "gz")),
        P(None, None, ("parts", "gx"), ("gy", "gz")),
        P(("parts", "gx"), ("gy", "gz")),
    )
    return jax.shard_map(body, mesh=mesh, in_specs=in_specs, out_specs=out_specs, check_vma=False)
```

```python
import functools

import jax
import jax.numpy as jnp
from jax import lax
from jax.experimental import pallas as pl
from jax.experimental.pallas import tpu as pltpu
from jax.sharding import PartitionSpec as P

STEPS = 4
HALO = 4
ROWS = 8
LANES = 128
UNROLL = 5
SLOT = 32


def call(kernel, outs, scratch=(), **more):
    return pl.pallas_call(
        kernel,
        out_shape=[jax.ShapeDtypeStruct(s, jnp.float32) if isinstance(s, tuple) else s for s in outs],
        scratch_shapes=[pltpu.VMEM(s, jnp.float32) if isinstance(s, tuple) else s for s in scratch],
        compiler_params=pltpu.CompilerParams(vmem_limit_bytes=40 * 1024 * 1024),
        **more,
    )


def place_of(axis):
    place, count = lax.axis_index(axis), lax.axis_size(axis)
    even = place % 2 == 0
    has_a = jnp.logical_or(jnp.logical_not(even), place < count - 1)
    has_b = jnp.where(even, place > 0, place < count - 1)
    return even, has_a, has_b


def swapped(x, axis, first):
    count = lax.axis_size(axis)
    pairs = []
    for i in range(count):
        other = i + 1 if (i - first) % 2 == 0 else i - 1
        pairs.append((i, other if 0 <= other < count else i))
    return lax.ppermute(x, axis, pairs)


def own_planes(rhs, eta, friction, ice, grounded):
    layers = eta.shape[0]
    cover = ice[...].astype(jnp.float32)
    drag = friction[...] * grounded[...].astype(jnp.float32)

    def plane(p):
        if p < 2 * layers:
            return rhs[p // layers, p % layers] * cover
        if p < 3 * layers:
            return eta[p - 2 * layers]
        return cover if p == 3 * layers else drag

    return plane


def pair_of(q, layers):
    if q < layers:
        return q, q + layers
    if q < layers + layers // 2:
        return q + layers, q + layers + layers // 2
    return 3 * layers, 3 * layers + 1


def ribbon_places(p, layers):
    tiles = layers // 4
    if p < 3 * layers:
        k = p % layers
        return p // layers * tiles + k % tiles, (k // tiles,)
    return (3 * tiles, (0, 1, 2, 3)) if p == 3 * layers else (3 * tiles + 1, (0,))


def ribbon_tiles(layers):
    return 3 * (layers // 4) + 2


def packed_place(tile):
    return tile // 8, HALO * (tile % 8)


def between(lane, first, width):
    return (lane >= first) & (lane < first + width)


def turned(v, shift):
    shift = shift % LANES
    return pltpu.roll(v, shift, 1) if shift else v


def pack_kernel(*refs):
    sources, held, (packs, strip_a, strip_b, arrived) = refs[:6], refs[6:12], refs[12:]
    copies = [pltpu.make_async_copy(a, b, arrived.at[i]) for i, (a, b) in enumerate(zip(sources, held))]
    for copy in copies:
        copy.start()
    for copy in copies:
        copy.wait()
    rhs, eta, friction, ice, grounded, _ = held
    layers = eta.shape[0]
    plane = own_planes(rhs, eta, friction, ice, grounded)
    lane = lax.broadcasted_iota(jnp.int32, (ROWS, LANES), 1)
    row = lax.broadcasted_iota(jnp.int32, (ROWS, LANES), 0)
    rows_even, _, _ = place_of("gx")
    upper_a = (row < HALO) != rows_even
    count = ribbon_tiles(layers)
    zero = jnp.zeros((ROWS, LANES), jnp.float32)
    left, right = [zero] * count, [zero] * count
    for q in range(strip_a.shape[0] // 2):
        first, second = pair_of(q, layers)
        x, y = plane(first), plane(second)
        for half in range(2):
            xs = x[:, half * LANES : (half + 1) * LANES]
            ys = y[:, half * LANES : (half + 1) * LANES]
            ys = pltpu.roll(ys, HALO, 0)
            strip_a[2 * q + half] = jnp.where(upper_a, xs, ys)
            strip_b[2 * q + half] = jnp.where(upper_a, ys, xs)
        for p, v in ((first, x), (second, y)):
            tile, slots = ribbon_places(p, layers)
            for slot in slots:
                at = slot * SLOT
                left[tile] = jnp.where(between(lane, at + 8, 4), turned(v[:, :LANES], at + 8), left[tile])
                right[tile] = jnp.where(between(lane, at + 16, 4), turned(v[:, LANES:], at + 20), right[tile])
    groups = packs.shape[0] // 2
    packed = [zero] * packs.shape[0]
    for tile in range(count):
        group, at = packed_place(tile)
        here = between(lane % SLOT, at, HALO)
        packed[group] = jnp.where(here, turned(left[tile], at - 8), packed[group])
        packed[groups + group] = jnp.where(here, turned(right[tile], at - 16), packed[groups + group])
    for group, v in enumerate(packed):
        packs[group] = v


def column_kernel(packs, packs_b, packs_a, column_a, column_b):
    below_and_above, _ = beyond()
    even, _, _ = place_of(("gy", "gz"))
    groups = packs.shape[0] // 2
    for group in range(groups):
        to_left, to_right = [
            jnp.concatenate([packs[i], below_and_above(packs_a[i], packs_b[i])], 0) for i in (group, groups + group)
        ]
        column_a[group] = jnp.where(even, to_right, to_left)
        column_b[group] = jnp.where(even, to_left, to_right)


def two_sum(a, b):
    s = a + b
    t = s - a
    return s, (a - (s - t)) + (b - t)


def join(x, y):
    s, e = two_sum(x[0], y[0])
    e = e + (x[1] + y[1])
    h = s + e
    return h, e - (h - s)


def times(scalar, x):
    def cut(v):
        t = v * 4097.0
        h = t - (t - v)
        return h, v - h

    p = scalar * x[0]
    sh, sl = cut(scalar)
    xh, xl = cut(x[0])
    e = ((sh * xh - p) + sh * xl + sl * xh) + sl * xl
    return p, e + scalar * x[1]


def beyond():
    even, has_a, has_b = place_of("gx")
    upper_a = (lax.broadcasted_iota(jnp.int32, (ROWS, LANES), 0) < HALO) == even

    def below_and_above(from_a, from_b):
        return jnp.where(upper_a, jnp.where(has_a, from_a, 0.0), jnp.where(has_b, from_b, 0.0))

    def above_and_below(from_a, from_b):
        return jnp.where(upper_a, jnp.where(has_b, from_b, 0.0), jnp.where(has_a, from_a, 0.0))

    return below_and_above, above_and_below


def row_next(v):
    return pltpu.roll(v, 2 * ROWS - 1, 0)


def row_prev(v):
    return pltpu.roll(v, 1, 0)


def col_next(v):
    return pltpu.roll(v, v.shape[1] - 1, 1)


def col_prev(v):
    return pltpu.roll(v, 1, 1)


class Tiles:
    def __init__(self, tiles):
        self.tiles = tiles

    @staticmethod
    def load(ref):
        return Tiles([ref[r : r + ROWS, c : c + LANES] for r in (0, ROWS) for c in (0, LANES)])

    def store(self, ref):
        for v, (r, c) in zip(self.tiles, ((0, 0), (0, LANES), (ROWS, 0), (ROWS, LANES))):
            ref[r : r + ROWS, c : c + LANES] = v

    def both(self, other, op):
        if isinstance(other, Tiles):
            return Tiles([op(x, y) for x, y in zip(self.tiles, other.tiles)])
        return Tiles([op(x, other) for x in self.tiles])

    def __add__(self, other):
        return self.both(other, lambda x, y: x + y)

    def __sub__(self, other):
        return self.both(other, lambda x, y: x - y)

    def __mul__(self, other):
        return self.both(other, lambda x, y: x * y)

    __rmul__ = __mul__


class Moves:
    def __init__(self):
        row = lax.broadcasted_iota(jnp.int32, (ROWS, LANES), 0)
        lane = lax.broadcasted_iota(jnp.int32, (ROWS, LANES), 1)
        self.first_row, self.last_row = row == 0, row == ROWS - 1
        self.first_lane, self.last_lane = lane == 0, lane == LANES - 1

    def rows(self, v, shift, edge):
        own0, own1, halo0, halo1 = [pltpu.roll(x, shift, 0) for x in v.tiles]
        return Tiles(
            [
                jnp.where(edge, halo0, own0),
                jnp.where(edge, halo1, own1),
                jnp.where(edge, own0, halo0),
                jnp.where(edge, own1, halo1),
            ]
        )

    def row_next(self, v):
        return self.rows(v, ROWS - 1, self.last_row)

    def row_prev(self, v):
        return self.rows(v, 1, self.first_row)

    def col_next(self, v):
        own0, own1, halo0, halo1 = [pltpu.roll(x, LANES - 1, 1) for x in v.tiles]
        return Tiles([jnp.where(self.last_lane, own1, own0), own1, jnp.where(self.last_lane, halo1, halo0), halo1])

    def col_prev(self, v):
        own0, own1, halo0, halo1 = [pltpu.roll(x, 1, 1) for x in v.tiles]
        return Tiles([own0, jnp.where(self.first_lane, own0, own1), halo0, jnp.where(self.first_lane, halo0, halo1)])


class Turns:
    row_next = staticmethod(row_next)
    row_prev = staticmethod(row_prev)
    col_next = staticmethod(col_next)
    col_prev = staticmethod(col_prev)


def horizontal(g0, g1, e_row, e_col, e_half, moves):
    row_next, row_prev, col_next, col_prev = moves.row_next, moves.row_prev, moves.col_next, moves.col_prev
    g0n, g1n = row_next(g0), col_next(g1)
    f = e_half * (g1n - col_prev(g1))
    h = e_half * (g0n - row_prev(g0))
    flux = e_row * (g0 - g0n)
    out0 = flux - row_next(f) - row_prev(flux - f)
    flux = e_col * (g0 - col_next(g0))
    out0 = out0 + (flux - col_prev(flux))
    flux = (4.0 * e_col) * (g1 - g1n)
    out1 = flux - col_next(h) - col_prev(flux - h)
    flux = (0.25 * e_row) * (g1 - row_next(g1))
    out1 = out1 + (flux - row_prev(flux))
    return out0, out1


def main_kernel(
    rhs, eta, friction, ice, grounded, strip_b, strip_a,
    powers, sums, ribbon,
    field_a, field_b, eta_row, eta_col, eta_half, eta_up, cover, drag,
):
    layers = eta.shape[0]
    plane = own_planes(rhs, eta, friction, ice, grounded)
    below_and_above, above_and_below = beyond()
    lane = lax.broadcasted_iota(jnp.int32, (2 * ROWS, LANES), 1)

    def target(p):
        if p < 2 * layers:
            return field_a.at[p // layers, p % layers]
        if p < 3 * layers:
            return eta_half.at[p - 2 * layers]
        return cover if p == 3 * layers else drag

    strips = [jnp.zeros((2 * ROWS, LANES), jnp.float32) for _ in range(ribbon.shape[0])]
    for q in range(strip_a.shape[0] // 2):
        first, second = pair_of(q, layers)
        halves = ([], [])
        for half in range(2):
            from_a, from_b = strip_a[2 * q + half], strip_b[2 * q + half]
            halves[0].append(below_and_above(from_a, from_b))
            halves[1].append(pltpu.roll(above_and_below(from_a, from_b), HALO, 0))
        for p, halo in zip((first, second), halves):
            v = plane(p)
            dst = target(p)
            dst[0:ROWS, :] = v
            dst[ROWS:, 0:LANES], dst[ROWS:, LANES:] = halo
            head = jnp.concatenate([v[:, :LANES], halo[0]], 0)
            tail = jnp.concatenate([v[:, LANES:], halo[1]], 0)
            tile, slots = ribbon_places(p, layers)
            for slot in slots:
                at = slot * SLOT
                strips[tile] = jnp.where(between(lane, at, 8), turned(tail, at + 8), strips[tile])
                strips[tile] = jnp.where(between(lane, at + 20, 8), turned(head, at + 20), strips[tile])
    for tile, v in enumerate(strips):
        ribbon[tile] = v

    moves = Moves()
    load = Tiles.load
    for k in range(layers):
        e = load(eta_half.at[k])
        (2.0 * (e + moves.row_next(e))).store(eta_row.at[k])
        (0.5 * (e + moves.col_next(e))).store(eta_col.at[k])
        eta_up[k] = eta_half[k] + eta_half[k + 1] if k + 1 < layers else jnp.zeros_like(eta_up[k])
        if k:
            eta_half[k - 1] = 0.5 * eta_half[k - 1]
    eta_half[layers - 1] = 0.5 * eta_half[layers - 1]

    def apply(t, src, dst):
        def layer(k, carry):
            below0, below1, odd, even = carry
            g0, g1 = load(src.at[0, k]), load(src.at[1, k])
            after = jnp.minimum(k + 1, layers - 1)
            e_up = load(eta_up.at[k])
            up0 = e_up * (g0 - load(src.at[0, after]))
            up1 = e_up * (g1 - load(src.at[1, after]))
            out0, out1 = horizontal(g0, g1, load(eta_row.at[k]), load(eta_col.at[k]), load(eta_half.at[k]), moves)
            m = load(cover)
            out0, out1 = m * (out0 + (up0 - Tiles(below0))), m * (out1 + (up1 - Tiles(below1)))
            if t < STEPS:
                out0.store(dst.at[0, k])
                out1.store(dst.at[1, k])
            odd, even = list(odd), list(even)
            for c, g, out in ((0, g0, out0), (1, g1, out1)):
                for half in range(2):
                    now = out.tiles[half]
                    powers[t - 1, c, k, :, half * LANES : (half + 1) * LANES] = now
                    odd[half] = odd[half] + g.tiles[half] * now
                    even[half] = even[half] + now * now
            return up0.tiles, up1.tiles, odd, even

        def block(b, carry):
            for i in range(UNROLL):
                carry = layer(b * UNROLL + i, carry)
            return carry

        zero = [jnp.zeros((ROWS, LANES), jnp.float32)] * 2
        d = -1.0 * load(drag)
        start = ((d * load(src.at[0, 0])).tiles, (d * load(src.at[1, 0])).tiles, zero, zero)
        ends = lax.fori_loop(0, layers // UNROLL, block, start)[2:]
        return [jnp.concatenate(v, 1) for v in ends]

    bare = 1.0 - ice[...].astype(jnp.float32)
    whole = jnp.zeros((ROWS, 2 * LANES), jnp.float32)
    outside = jnp.zeros((ROWS, 2 * LANES), jnp.float32)
    for c in range(2):
        for k in range(layers):
            square = rhs[c, k] * rhs[c, k]
            whole = whole + square
            outside = outside + bare * square
    sums[0] = whole
    wide = lax.broadcasted_iota(jnp.int32, (ROWS, 2 * LANES), 1)
    inner = between(wide, HALO, 2 * LANES - 2 * HALO)
    src, dst = field_a, field_b
    for t in range(1, STEPS + 1):
        odd, even = apply(t, src, dst)
        sums[2 * t - 1] = jnp.where(inner, odd, 0.0) + outside
        sums[2 * t] = jnp.where(inner, even, 0.0) + outside
        src, dst = dst, src


def ribbon_kernel(ribbon, column_a, column_b, sums, edges, moments):
    tiles = edges.shape[2]
    lane = lax.broadcasted_iota(jnp.int32, (2 * ROWS, LANES), 1)
    even, has_a, has_b = place_of(("gy", "gz"))
    came = [
        (jnp.where(has_a, column_a[i], 0.0), jnp.where(has_b, column_b[i], 0.0)) for i in range(column_a.shape[0])
    ]
    from_right = [jnp.where(even, a, b) for a, b in came]
    from_left = [jnp.where(even, b, a) for a, b in came]
    spot = lane % SLOT

    def whole(tile):
        group, at = packed_place(tile)
        right = jnp.where(between(spot, 8, HALO), turned(from_right[group], 8 - at), ribbon[tile])
        return jnp.where(between(spot, 16, HALO), turned(from_left[group], 16 - at), right)

    field = [[whole(c * tiles + n) for n in range(tiles)] for c in range(2)]
    eta = [whole(2 * tiles + n) for n in range(tiles)]
    cover, drag = whole(3 * tiles), whole(3 * tiles + 1)

    def after(v):
        return v[1:] + [turned(v[0], -SLOT)]

    eta_row = [2.0 * (e + row_next(e)) for e in eta]
    eta_col = [0.5 * (e + col_next(e)) for e in eta]
    eta_half = [0.5 * e for e in eta]
    eta_up = [e + n for e, n in zip(eta, after(eta))]
    eta_up[-1] = jnp.where(lane < LANES - SLOT, eta_up[-1], 0.0)
    place = lax.broadcasted_iota(jnp.int32, (ROWS, LANES), 1) % SLOT
    edge = between(place, 4, HALO) | between(place, 20, HALO)
    extra = [None]
    for t in range(1, STEPS + 1):
        ups = [[u * (g - n) for u, g, n in zip(eta_up, field[c], after(field[c]))] for c in range(2)]
        result = ([], [])
        odd = even = jnp.zeros((ROWS, LANES), jnp.float32)
        for n in range(tiles):
            outs = horizontal(field[0][n], field[1][n], eta_row[n], eta_col[n], eta_half[n], Turns)
            for c in range(2):
                below = ups[c][n - 1] if n else turned(ups[c][-1], SLOT) - drag * field[c][0]
                out = cover * (outs[c] + (ups[c][n] - below))
                result[c].append(out)
                now = out[:ROWS]
                edges[t - 1, c, n] = now
                odd = odd + field[c][n][:ROWS] * now
                even = even + now * now
        field = result
        extra.extend([jnp.where(edge, odd, 0.0), jnp.where(edge, even, 0.0)])

    tall = lax.broadcasted_iota(jnp.int32, (2 * ROWS, LANES), 0)
    high = jnp.zeros((2 * ROWS, LANES), jnp.float32)
    low = jnp.zeros((2 * ROWS, LANES), jnp.float32)
    for j, more in enumerate(extra):
        total = sums[j]
        pair = two_sum(total[:, :LANES], total[:, LANES:])
        if more is not None:
            pair = join(pair, (more, jnp.zeros_like(more)))
        for step in (4, 2, 1):
            pair = join(pair, tuple(pltpu.roll(v, step, 0) for v in pair))
        high = jnp.where(tall == j, jnp.concatenate([pair[0]] * 2, 0), high)
        low = jnp.where(tall == j, jnp.concatenate([pair[1]] * 2, 0), low)
    moments[0] = high
    moments[1] = low


def add_kernel(*refs):
    *ins, out = refs
    total = (ins[0][0], ins[0][1])
    for x in ins[1:]:
        total = join(total, (x[0], x[1]))
    out[0], out[1] = total


def solve(total):
    for step in (64, 32, 16, 8, 4, 2, 1):
        total = join(total, tuple(pltpu.roll(v, step, 1) for v in total))

    def spread(v, j):
        return jnp.broadcast_to(v[j : j + 1], (ROWS, LANES))

    centre = spread(total[0], 1) / spread(total[0], 0)
    wide = jnp.concatenate([centre, centre], 0)
    mu = [spread(total[0], 0)]
    for _ in range(2 * STEPS):
        step = times(wide, total)
        total = join(tuple(pltpu.roll(v, 2 * ROWS - 1, 0) for v in total), (-step[0], -step[1]))
        mu.append(spread(total[0], 0))

    def plus(a, b):
        n = max(len(a), len(b))
        return [a[i] + b[i] if i < min(len(a), len(b)) else (a[i] if i < len(a) else b[i]) for i in range(n)]

    def scaled(s, a):
        return [s * x for x in a]

    def operator(a):
        return plus([centre * x for x in a], [jnp.zeros_like(centre)] + a)

    def dot(a, b):
        square = [None] * (len(a) + len(b) - 1)
        for i, x in enumerate(a):
            for j, y in enumerate(b):
                z = x * y
                square[i + j] = z if square[i + j] is None else square[i + j] + z
        value = square[0] * mu[0]
        for n in range(1, len(square)):
            value = value + square[n] * mu[n]
        return value

    one = jnp.ones_like(centre)
    right = [one]
    quasi, search, update, iterate = right, right, [], []
    applied = operator(search)
    carried = applied
    rho = mu[0]
    tau_sq = rho
    alpha = theta_sq = eta = None
    for half in range(STEPS):
        if half % 2 == 0:
            alpha = rho / dot(carried, right)
            search_next = plus(search, scaled(-alpha, carried))
        quasi = plus(quasi, scaled(-alpha, applied))
        if half:
            update = plus(search, scaled(theta_sq / alpha * eta, update))
        else:
            update = search
        theta_sq = dot(quasi, quasi) / tau_sq
        cosine_sq = 1.0 / (1.0 + theta_sq)
        tau_sq = tau_sq * theta_sq * cosine_sq
        eta = cosine_sq * alpha
        iterate = plus(iterate, scaled(eta, update))
        if half % 2 == 0:
            search = search_next
            applied = operator(search)
        elif half < STEPS - 1:
            rho_next = dot(quasi, right)
            beta = rho_next / rho
            search = plus(quasi, scaled(beta, search))
            applied_next = operator(search)
            carried = plus(applied_next, scaled(beta, plus(applied, scaled(beta, carried))))
            applied, rho = applied_next, rho_next
    powers = [iterate[-1]]
    for c in iterate[-2::-1]:
        powers = plus([c] + powers, scaled(-centre, powers))
    return powers


def final_kernel(rhs, powers, edges, friction, ice, grounded, speed, *rest):
    *parts, iterate, residual, hessian = rest
    layers, tiles = rhs.shape[1], edges.shape[2]
    total = (parts[0][0], parts[0][1])
    for x in parts[1:]:
        total = join(total, (x[0], x[1]))
    factors = solve(total)
    wide = [jnp.concatenate([c, c], 1) for c in factors]
    rest = sum(wide[1:], wide[0])
    cover = ice[...].astype(jnp.float32)
    lane = lax.broadcasted_iota(jnp.int32, (ROWS, LANES), 1)

    def combined(vectors, weights):
        x = weights[1] * vectors[0]
        y = weights[0] * vectors[0]
        for t in range(1, STEPS):
            if t + 1 < STEPS:
                x = x + weights[t + 1] * vectors[t]
            y = y + weights[t] * vectors[t]
        return x, y

    for c in range(2):
        side = [combined([edges[t, c, n] for t in range(STEPS)], factors) for n in range(tiles)]
        for k in range(layers):
            at = k // tiles * SLOT
            inner = combined([powers[t, c, k] for t in range(STEPS)], wide)
            patched = []
            for v, e in zip(inner, side[k % tiles]):
                head = jnp.where(lane < HALO, turned(e, -at - 20), v[:, :LANES])
                tail = jnp.where(lane >= LANES - HALO, turned(e, 120 - at), v[:, LANES:])
                patched.append(jnp.concatenate([head, tail], 1))
            r = rhs[c, k]
            x, y = patched
            iterate[c, k] = jnp.where(cover > 0.0, wide[0] * r + x, rest * r)
            residual[c, k] = r - jnp.where(cover > 0.0, y, rest * r)
    weight = cover * (friction[...] * grounded[...].astype(jnp.float32))
    hessian[...] = weight * (speed[0] * iterate[0, 0] + speed[1] * iterate[1, 0])


def exchange(x, axis):
    count = lax.axis_size(axis)
    stride = 1
    rounds = []
    while stride < count:
        size = 4 if (count // stride) % 4 == 0 else 2
        rounds.append((stride, size))
        stride *= size
    for at, (stride, size) in enumerate(rounds):
        parts = [x]
        for turn in range(1, size):
            pairs = []
            for i in range(count):
                place = (i // stride) % size
                pairs.append((i, i + ((place ^ turn) - place) * stride))
            parts.append(lax.ppermute(x, axis, pairs))
        if at == len(rounds) - 1:
            return parts
        x = call(add_kernel, [x.shape])(*parts)[0]
    return [x]


def body(adjoint_rhs, viscosity, friction, ice_mask, grounded, basal_velocity):
    layers = viscosity.shape[0]
    inputs = (adjoint_rhs, viscosity, friction, ice_mask, grounded, basal_velocity)
    tile = (ROWS, LANES)
    strips = (2 * (layers + layers // 2 + 1),) + tile
    ribbons = ribbon_tiles(layers)
    groups = (ribbons + 7) // 8
    *held, packs, strip_a, strip_b = call(
        pack_kernel,
        [jax.ShapeDtypeStruct(x.shape, x.dtype) for x in inputs] + [(2 * groups,) + tile, strips, strips],
        [pltpu.SemaphoreType.DMA((len(inputs),))],
        in_specs=[pl.BlockSpec(memory_space=pltpu.HBM)] * len(inputs),
    )(*[pltpu.with_memory_space_constraint(x, pltpu.HBM) for x in inputs])
    packs_b, packs_a = swapped(packs, "gx", 1), swapped(packs, "gx", 0)
    strip_b, strip_a = swapped(strip_b, "gx", 1), swapped(strip_a, "gx", 0)
    column_a, column_b = call(
        column_kernel,
        [(groups, 2 * ROWS, LANES)] * 2,
        cost_estimate=pl.CostEstimate(flops=3_000_000_000, bytes_accessed=200_000, transcendentals=0),
    )(packs, packs_b, packs_a)
    column_a, column_b = swapped(column_a, ("gy", "gz"), 0), swapped(column_b, ("gy", "gz"), 1)
    block = (layers, 2 * ROWS, 2 * LANES)
    powers, sums, ribbon = call(
        main_kernel,
        [(STEPS,) + adjoint_rhs.shape, (2 * STEPS + 1, ROWS, 2 * LANES), (ribbons, 2 * ROWS, LANES)],
        [(2,) + block] * 2 + [block] * 4 + [block[1:]] * 2,
        cost_estimate=pl.CostEstimate(flops=200_000_000, bytes_accessed=8_000_000, transcendentals=0),
    )(*held[:5], strip_b, strip_a)
    edges, sums = call(
        ribbon_kernel,
        [(STEPS, 2, layers // 4) + tile, (2, 2 * ROWS, LANES)],
    )(ribbon, column_a, column_b, sums)
    parts = exchange(sums, ("gy", "gz"))
    if len(parts) > 1:
        sums = call(add_kernel, [sums.shape])(*parts)[0]
    parts = exchange(sums, "gx")
    rhs, _, friction, ice_mask, grounded, speed = held
    return tuple(
        call(final_kernel, [adjoint_rhs.shape, adjoint_rhs.shape, friction.shape])(
            rhs, powers, edges, friction, ice_mask, grounded, speed, *parts
        )
    )


def solution(mesh):
    in_specs = (
        P(None, None, ("parts", "gx"), ("gy", "gz")),
        P(None, ("parts", "gx"), ("gy", "gz")),
        P(("parts", "gx"), ("gy", "gz")),
        P(("parts", "gx"), ("gy", "gz")),
        P(("parts", "gx"), ("gy", "gz")),
        P(None, ("parts", "gx"), ("gy", "gz")),
    )
    out_specs = (
        P(None, None, ("parts", "gx"), ("gy", "gz")),
        P(None, None, ("parts", "gx"), ("gy", "gz")),
        P(("parts", "gx"), ("gy", "gz")),
    )
    return jax.shard_map(body, mesh=mesh, in_specs=in_specs, out_specs=out_specs, check_vma=False)
```

```python
import functools

import jax
import jax.numpy as jnp
from jax import lax
from jax.experimental import pallas as pl
from jax.experimental.pallas import tpu as pltpu
from jax.sharding import PartitionSpec as P

STEPS = 4
HALO = 4
ROWS = 8
LANES = 128
UNROLL = 5
SLOT = 32


def call(kernel, outs, scratch=(), **more):
    return pl.pallas_call(
        kernel,
        out_shape=[jax.ShapeDtypeStruct(s, jnp.float32) if isinstance(s, tuple) else s for s in outs],
        scratch_shapes=[pltpu.VMEM(s, jnp.float32) if isinstance(s, tuple) else s for s in scratch],
        compiler_params=pltpu.CompilerParams(vmem_limit_bytes=40 * 1024 * 1024),
        **more,
    )


def place_of(axis):
    place, count = lax.axis_index(axis), lax.axis_size(axis)
    even = place % 2 == 0
    has_a = jnp.logical_or(jnp.logical_not(even), place < count - 1)
    has_b = jnp.where(even, place > 0, place < count - 1)
    return even, has_a, has_b


def swapped(x, axes, first):
    count, parts = lax.axis_size(axes), lax.axis_size("parts")
    pairs = []
    for part in range(parts):
        for i in range(count):
            other = i + 1 if (i - first) % 2 == 0 else i - 1
            at = part
            if not 0 <= other < count:
                other, at = i, part ^ 1 if part ^ 1 < parts else part
            pairs.append((part * count + i, at * count + other))
    return lax.ppermute(x, ("parts", *axes), pairs)


def own_planes(rhs, eta, friction, ice, grounded):
    layers = eta.shape[0]
    cover = ice[...].astype(jnp.float32)
    drag = friction[...] * grounded[...].astype(jnp.float32)

    def plane(p):
        if p < 2 * layers:
            return rhs[p // layers, p % layers] * cover
        if p < 3 * layers:
            return eta[p - 2 * layers]
        return cover if p == 3 * layers else drag

    return plane


def pair_of(q, layers):
    if q < layers:
        return q, q + layers
    if q < layers + layers // 2:
        return q + layers, q + layers + layers // 2
    return 3 * layers, 3 * layers + 1


def ribbon_places(p, layers):
    tiles = layers // 4
    if p < 3 * layers:
        k = p % layers
        return p // layers * tiles + k % tiles, (k // tiles,)
    return (3 * tiles, (0, 1, 2, 3)) if p == 3 * layers else (3 * tiles + 1, (0,))


def ribbon_tiles(layers):
    return 3 * (layers // 4) + 2


def packed_place(tile):
    return tile // 8, HALO * (tile % 8)


def between(lane, first, width):
    return (lane >= first) & (lane < first + width)


def turned(v, shift):
    shift = shift % LANES
    return pltpu.roll(v, shift, 1) if shift else v


def pack_kernel(*refs):
    sources, held, (column_a, column_b, strip_a, strip_b, arrived) = refs[:6], refs[6:12], refs[12:]
    copies = [pltpu.make_async_copy(a, b, arrived.at[i]) for i, (a, b) in enumerate(zip(sources, held))]
    for copy in copies:
        copy.start()
    for copy in copies:
        copy.wait()
    rhs, eta, friction, ice, grounded, _ = held
    layers = eta.shape[0]
    plane = own_planes(rhs, eta, friction, ice, grounded)
    lane = lax.broadcasted_iota(jnp.int32, (ROWS, LANES), 1)
    row = lax.broadcasted_iota(jnp.int32, (ROWS, LANES), 0)
    rows_even, _, _ = place_of("gx")
    columns_even, _, _ = place_of(("gy", "gz"))
    upper_a = (row < HALO) != rows_even
    count = ribbon_tiles(layers)
    zero = jnp.zeros((ROWS, LANES), jnp.float32)
    left, right = [zero] * count, [zero] * count
    for q in range(strip_a.shape[0] // 2):
        first, second = pair_of(q, layers)
        x, y = plane(first), plane(second)
        for half in range(2):
            xs = x[:, half * LANES : (half + 1) * LANES]
            ys = y[:, half * LANES : (half + 1) * LANES]
            ys = pltpu.roll(ys, HALO, 0)
            strip_a[2 * q + half] = jnp.where(upper_a, xs, ys)
            strip_b[2 * q + half] = jnp.where(upper_a, ys, xs)
        for p, v in ((first, x), (second, y)):
            tile, slots = ribbon_places(p, layers)
            for slot in slots:
                at = slot * SLOT
                left[tile] = jnp.where(between(lane, at + 8, 4), turned(v[:, :LANES], at + 8), left[tile])
                right[tile] = jnp.where(between(lane, at + 16, 4), turned(v[:, LANES:], at + 20), right[tile])
    to_left, to_right = [zero] * column_a.shape[0], [zero] * column_a.shape[0]
    for tile in range(count):
        group, at = packed_place(tile)
        here = between(lane % SLOT, at, HALO)
        to_left[group] = jnp.where(here, turned(left[tile], at - 8), to_left[group])
        to_right[group] = jnp.where(here, turned(right[tile], at - 16), to_right[group])
    for group in range(column_a.shape[0]):
        column_a[group] = jnp.where(columns_even, to_right[group], to_left[group])
        column_b[group] = jnp.where(columns_even, to_left[group], to_right[group])


def beside_kernel(from_a, from_b, columns):
    even, has_a, has_b = place_of(("gy", "gz"))
    count = from_a.shape[0]
    for group in range(count):
        a = jnp.where(has_a, from_a[group], 0.0)
        b = jnp.where(has_b, from_b[group], 0.0)
        columns[group] = jnp.where(even, a, b)
        columns[count + group] = jnp.where(even, b, a)


def two_sum(a, b):
    s = a + b
    t = s - a
    return s, (a - (s - t)) + (b - t)


def join(x, y):
    s, e = two_sum(x[0], y[0])
    e = e + (x[1] + y[1])
    h = s + e
    return h, e - (h - s)


def times(scalar, x):
    def cut(v):
        t = v * 4097.0
        h = t - (t - v)
        return h, v - h

    p = scalar * x[0]
    sh, sl = cut(scalar)
    xh, xl = cut(x[0])
    e = ((sh * xh - p) + sh * xl + sl * xh) + sl * xl
    return p, e + scalar * x[1]


def beyond():
    even, has_a, has_b = place_of("gx")
    upper_a = (lax.broadcasted_iota(jnp.int32, (ROWS, LANES), 0) < HALO) == even

    def below_and_above(from_a, from_b):
        return jnp.where(upper_a, jnp.where(has_a, from_a, 0.0), jnp.where(has_b, from_b, 0.0))

    def above_and_below(from_a, from_b):
        return jnp.where(upper_a, jnp.where(has_b, from_b, 0.0), jnp.where(has_a, from_a, 0.0))

    return below_and_above, above_and_below


def row_next(v):
    return pltpu.roll(v, 2 * ROWS - 1, 0)


def row_prev(v):
    return pltpu.roll(v, 1, 0)


def col_next(v):
    return pltpu.roll(v, v.shape[1] - 1, 1)


def col_prev(v):
    return pltpu.roll(v, 1, 1)


class Tiles:
    def __init__(self, tiles):
        self.tiles = tiles

    @staticmethod
    def load(ref):
        return Tiles([ref[r : r + ROWS, c : c + LANES] for r in (0, ROWS) for c in (0, LANES)])

    def store(self, ref):
        for v, (r, c) in zip(self.tiles, ((0, 0), (0, LANES), (ROWS, 0), (ROWS, LANES))):
            ref[r : r + ROWS, c : c + LANES] = v

    def both(self, other, op):
        if isinstance(other, Tiles):
            return Tiles([op(x, y) for x, y in zip(self.tiles, other.tiles)])
        return Tiles([op(x, other) for x in self.tiles])

    def __add__(self, other):
        return self.both(other, lambda x, y: x + y)

    def __sub__(self, other):
        return self.both(other, lambda x, y: x - y)

    def __mul__(self, other):
        return self.both(other, lambda x, y: x * y)

    __rmul__ = __mul__


class Moves:
    def __init__(self):
        row = lax.broadcasted_iota(jnp.int32, (ROWS, LANES), 0)
        lane = lax.broadcasted_iota(jnp.int32, (ROWS, LANES), 1)
        self.first_row, self.last_row = row == 0, row == ROWS - 1
        self.first_lane, self.last_lane = lane == 0, lane == LANES - 1

    def rows(self, v, shift, edge):
        own0, own1, halo0, halo1 = [pltpu.roll(x, shift, 0) for x in v.tiles]
        return Tiles(
            [
                jnp.where(edge, halo0, own0),
                jnp.where(edge, halo1, own1),
                jnp.where(edge, own0, halo0),
                jnp.where(edge, own1, halo1),
            ]
        )

    def row_next(self, v):
        return self.rows(v, ROWS - 1, self.last_row)

    def row_prev(self, v):
        return self.rows(v, 1, self.first_row)

    def col_next(self, v):
        own0, own1, halo0, halo1 = [pltpu.roll(x, LANES - 1, 1) for x in v.tiles]
        return Tiles([jnp.where(self.last_lane, own1, own0), own1, jnp.where(self.last_lane, halo1, halo0), halo1])

    def col_prev(self, v):
        own0, own1, halo0, halo1 = [pltpu.roll(x, 1, 1) for x in v.tiles]
        return Tiles([own0, jnp.where(self.first_lane, own0, own1), halo0, jnp.where(self.first_lane, halo0, halo1)])


class Turns:
    row_next = staticmethod(row_next)
    row_prev = staticmethod(row_prev)
    col_next = staticmethod(col_next)
    col_prev = staticmethod(col_prev)


def horizontal(g0, g1, e_row, e_col, e_half, moves):
    row_next, row_prev, col_next, col_prev = moves.row_next, moves.row_prev, moves.col_next, moves.col_prev
    g0n, g1n = row_next(g0), col_next(g1)
    f = e_half * (g1n - col_prev(g1))
    h = e_half * (g0n - row_prev(g0))
    flux = e_row * (g0 - g0n)
    out0 = flux - row_next(f) - row_prev(flux - f)
    flux = e_col * (g0 - col_next(g0))
    out0 = out0 + (flux - col_prev(flux))
    flux = (4.0 * e_col) * (g1 - g1n)
    out1 = flux - col_next(h) - col_prev(flux - h)
    flux = (0.25 * e_row) * (g1 - row_next(g1))
    out1 = out1 + (flux - row_prev(flux))
    return out0, out1


def main_kernel(
    rhs, eta, friction, ice, grounded, strip_b, strip_a,
    powers, sums, ribbon,
    field_a, field_b, eta_row, eta_col, eta_half, eta_up, cover, drag,
):
    layers = eta.shape[0]
    plane = own_planes(rhs, eta, friction, ice, grounded)
    below_and_above, above_and_below = beyond()
    lane = lax.broadcasted_iota(jnp.int32, (2 * ROWS, LANES), 1)

    def target(p):
        if p < 2 * layers:
            return field_a.at[p // layers, p % layers]
        if p < 3 * layers:
            return eta_half.at[p - 2 * layers]
        return cover if p == 3 * layers else drag

    strips = [jnp.zeros((2 * ROWS, LANES), jnp.float32) for _ in range(ribbon.shape[0])]
    for q in range(strip_a.shape[0] // 2):
        first, second = pair_of(q, layers)
        halves = ([], [])
        for half in range(2):
            from_a, from_b = strip_a[2 * q + half], strip_b[2 * q + half]
            halves[0].append(below_and_above(from_a, from_b))
            halves[1].append(pltpu.roll(above_and_below(from_a, from_b), HALO, 0))
        for p, halo in zip((first, second), halves):
            v = plane(p)
            dst = target(p)
            dst[0:ROWS, :] = v
            dst[ROWS:, 0:LANES], dst[ROWS:, LANES:] = halo
            head = jnp.concatenate([v[:, :LANES], halo[0]], 0)
            tail = jnp.concatenate([v[:, LANES:], halo[1]], 0)
            tile, slots = ribbon_places(p, layers)
            for slot in slots:
                at = slot * SLOT
                strips[tile] = jnp.where(between(lane, at, 8), turned(tail, at + 8), strips[tile])
                strips[tile] = jnp.where(between(lane, at + 20, 8), turned(head, at + 20), strips[tile])
    for tile, v in enumerate(strips):
        ribbon[tile] = v

    moves = Moves()
    load = Tiles.load
    for k in range(layers):
        e = load(eta_half.at[k])
        (2.0 * (e + moves.row_next(e))).store(eta_row.at[k])
        (0.5 * (e + moves.col_next(e))).store(eta_col.at[k])
        eta_up[k] = eta_half[k] + eta_half[k + 1] if k + 1 < layers else jnp.zeros_like(eta_up[k])
        if k:
            eta_half[k - 1] = 0.5 * eta_half[k - 1]
    eta_half[layers - 1] = 0.5 * eta_half[layers - 1]

    def apply(t, src, dst):
        def layer(k, carry):
            below0, below1, odd, even = carry
            g0, g1 = load(src.at[0, k]), load(src.at[1, k])
            after = jnp.minimum(k + 1, layers - 1)
            e_up = load(eta_up.at[k])
            up0 = e_up * (g0 - load(src.at[0, after]))
            up1 = e_up * (g1 - load(src.at[1, after]))
            out0, out1 = horizontal(g0, g1, load(eta_row.at[k]), load(eta_col.at[k]), load(eta_half.at[k]), moves)
            m = load(cover)
            out0, out1 = m * (out0 + (up0 - Tiles(below0))), m * (out1 + (up1 - Tiles(below1)))
            if t < STEPS:
                out0.store(dst.at[0, k])
                out1.store(dst.at[1, k])
            odd, even = list(odd), list(even)
            for c, g, out in ((0, g0, out0), (1, g1, out1)):
                for half in range(2):
                    now = out.tiles[half]
                    powers[t - 1, c, k, :, half * LANES : (half + 1) * LANES] = now
                    odd[half] = odd[half] + g.tiles[half] * now
                    even[half] = even[half] + now * now
            return up0.tiles, up1.tiles, odd, even

        def block(b, carry):
            for i in range(UNROLL):
                carry = layer(b * UNROLL + i, carry)
            return carry

        zero = [jnp.zeros((ROWS, LANES), jnp.float32)] * 2
        d = -1.0 * load(drag)
        start = ((d * load(src.at[0, 0])).tiles, (d * load(src.at[1, 0])).tiles, zero, zero)
        ends = lax.fori_loop(0, layers // UNROLL, block, start)[2:]
        return [jnp.concatenate(v, 1) for v in ends]

    bare = 1.0 - ice[...].astype(jnp.float32)
    whole = jnp.zeros((ROWS, 2 * LANES), jnp.float32)
    outside = jnp.zeros((ROWS, 2 * LANES), jnp.float32)
    for c in range(2):
        for k in range(layers):
            square = rhs[c, k] * rhs[c, k]
            whole = whole + square
            outside = outside + bare * square
    sums[0] = whole
    wide = lax.broadcasted_iota(jnp.int32, (ROWS, 2 * LANES), 1)
    inner = between(wide, HALO, 2 * LANES - 2 * HALO)
    src, dst = field_a, field_b
    for t in range(1, STEPS + 1):
        odd, even = apply(t, src, dst)
        sums[2 * t - 1] = jnp.where(inner, odd, 0.0) + outside
        sums[2 * t] = jnp.where(inner, even, 0.0) + outside
        src, dst = dst, src


def ribbon_kernel(ribbon, columns, columns_b, columns_a, sums, edges, moments):
    tiles = edges.shape[2]
    below_and_above, _ = beyond()
    lane = lax.broadcasted_iota(jnp.int32, (2 * ROWS, LANES), 1)

    count = columns.shape[0] // 2
    beside = [
        jnp.concatenate([columns[i], below_and_above(columns_a[i], columns_b[i])], 0) for i in range(2 * count)
    ]
    spot = lane % SLOT

    def whole(tile):
        group, at = packed_place(tile)
        right = jnp.where(between(spot, 8, HALO), turned(beside[group], 8 - at), ribbon[tile])
        return jnp.where(between(spot, 16, HALO), turned(beside[count + group], 16 - at), right)

    field = [[whole(c * tiles + n) for n in range(tiles)] for c in range(2)]
    eta = [whole(2 * tiles + n) for n in range(tiles)]
    cover, drag = whole(3 * tiles), whole(3 * tiles + 1)

    def after(v):
        return v[1:] + [turned(v[0], -SLOT)]

    eta_row = [2.0 * (e + row_next(e)) for e in eta]
    eta_col = [0.5 * (e + col_next(e)) for e in eta]
    eta_half = [0.5 * e for e in eta]
    eta_up = [e + n for e, n in zip(eta, after(eta))]
    eta_up[-1] = jnp.where(lane < LANES - SLOT, eta_up[-1], 0.0)
    place = lax.broadcasted_iota(jnp.int32, (ROWS, LANES), 1) % SLOT
    edge = between(place, 4, HALO) | between(place, 20, HALO)
    extra = [None]
    for t in range(1, STEPS + 1):
        ups = [[u * (g - n) for u, g, n in zip(eta_up, field[c], after(field[c]))] for c in range(2)]
        result = ([], [])
        odd = even = jnp.zeros((ROWS, LANES), jnp.float32)
        for n in range(tiles):
            outs = horizontal(field[0][n], field[1][n], eta_row[n], eta_col[n], eta_half[n], Turns)
            for c in range(2):
                below = ups[c][n - 1] if n else turned(ups[c][-1], SLOT) - drag * field[c][0]
                out = cover * (outs[c] + (ups[c][n] - below))
                result[c].append(out)
                now = out[:ROWS]
                edges[t - 1, c, n] = now
                odd = odd + field[c][n][:ROWS] * now
                even = even + now * now
        field = result
        extra.extend([jnp.where(edge, odd, 0.0), jnp.where(edge, even, 0.0)])

    tall = lax.broadcasted_iota(jnp.int32, (2 * ROWS, LANES), 0)
    high = jnp.zeros((2 * ROWS, LANES), jnp.float32)
    low = jnp.zeros((2 * ROWS, LANES), jnp.float32)
    for j, more in enumerate(extra):
        total = sums[j]
        pair = two_sum(total[:, :LANES], total[:, LANES:])
        if more is not None:
            pair = join(pair, (more, jnp.zeros_like(more)))
        for step in (4, 2, 1):
            pair = join(pair, tuple(pltpu.roll(v, step, 0) for v in pair))
        high = jnp.where(tall == j, jnp.concatenate([pair[0]] * 2, 0), high)
        low = jnp.where(tall == j, jnp.concatenate([pair[1]] * 2, 0), low)
    moments[0] = high
    moments[1] = low


def add_kernel(*refs):
    *ins, out = refs
    total = (ins[0][0], ins[0][1])
    for x in ins[1:]:
        total = join(total, (x[0], x[1]))
    out[0], out[1] = total


def solve(total):
    for step in (64, 32, 16, 8, 4, 2, 1):
        total = join(total, tuple(pltpu.roll(v, step, 1) for v in total))

    def spread(v, j):
        return jnp.broadcast_to(v[j : j + 1], (ROWS, LANES))

    centre = spread(total[0], 1) / spread(total[0], 0)
    wide = jnp.concatenate([centre, centre], 0)
    mu = [spread(total[0], 0)]
    for _ in range(2 * STEPS):
        step = times(wide, total)
        total = join(tuple(pltpu.roll(v, 2 * ROWS - 1, 0) for v in total), (-step[0], -step[1]))
        mu.append(spread(total[0], 0))

    def plus(a, b):
        n = max(len(a), len(b))
        return [a[i] + b[i] if i < min(len(a), len(b)) else (a[i] if i < len(a) else b[i]) for i in range(n)]

    def scaled(s, a):
        return [s * x for x in a]

    def operator(a):
        return plus([centre * x for x in a], [jnp.zeros_like(centre)] + a)

    def dot(a, b):
        square = [None] * (len(a) + len(b) - 1)
        for i, x in enumerate(a):
            for j, y in enumerate(b):
                z = x * y
                square[i + j] = z if square[i + j] is None else square[i + j] + z
        value = square[0] * mu[0]
        for n in range(1, len(square)):
            value = value + square[n] * mu[n]
        return value

    one = jnp.ones_like(centre)
    right = [one]
    quasi, search, update, iterate = right, right, [], []
    applied = operator(search)
    carried = applied
    rho = mu[0]
    tau_sq = rho
    alpha = theta_sq = eta = None
    for half in range(STEPS):
        if half % 2 == 0:
            alpha = rho / dot(carried, right)
            search_next = plus(search, scaled(-alpha, carried))
        quasi = plus(quasi, scaled(-alpha, applied))
        if half:
            update = plus(search, scaled(theta_sq / alpha * eta, update))
        else:
            update = search
        theta_sq = dot(quasi, quasi) / tau_sq
        cosine_sq = 1.0 / (1.0 + theta_sq)
        tau_sq = tau_sq * theta_sq * cosine_sq
        eta = cosine_sq * alpha
        iterate = plus(iterate, scaled(eta, update))
        if half % 2 == 0:
            search = search_next
            applied = operator(search)
        elif half < STEPS - 1:
            rho_next = dot(quasi, right)
            beta = rho_next / rho
            search = plus(quasi, scaled(beta, search))
            applied_next = operator(search)
            carried = plus(applied_next, scaled(beta, plus(applied, scaled(beta, carried))))
            applied, rho = applied_next, rho_next
    powers = [iterate[-1]]
    for c in iterate[-2::-1]:
        powers = plus([c] + powers, scaled(-centre, powers))
    return powers


def final_kernel(rhs, powers, edges, friction, ice, grounded, speed, *rest):
    *parts, iterate, residual, hessian = rest
    layers, tiles = rhs.shape[1], edges.shape[2]
    total = (parts[0][0], parts[0][1])
    for x in parts[1:]:
        total = join(total, (x[0], x[1]))
    factors = solve(total)
    wide = [jnp.concatenate([c, c], 1) for c in factors]
    rest = sum(wide[1:], wide[0])
    cover = ice[...].astype(jnp.float32)
    lane = lax.broadcasted_iota(jnp.int32, (ROWS, LANES), 1)

    def combined(vectors, weights):
        x = weights[1] * vectors[0]
        y = weights[0] * vectors[0]
        for t in range(1, STEPS):
            if t + 1 < STEPS:
                x = x + weights[t + 1] * vectors[t]
            y = y + weights[t] * vectors[t]
        return x, y

    for c in range(2):
        side = [combined([edges[t, c, n] for t in range(STEPS)], factors) for n in range(tiles)]
        for k in range(layers):
            at = k // tiles * SLOT
            inner = combined([powers[t, c, k] for t in range(STEPS)], wide)
            patched = []
            for v, e in zip(inner, side[k % tiles]):
                head = jnp.where(lane < HALO, turned(e, -at - 20), v[:, :LANES])
                tail = jnp.where(lane >= LANES - HALO, turned(e, 120 - at), v[:, LANES:])
                patched.append(jnp.concatenate([head, tail], 1))
            r = rhs[c, k]
            x, y = patched
            iterate[c, k] = jnp.where(cover > 0.0, wide[0] * r + x, rest * r)
            residual[c, k] = r - jnp.where(cover > 0.0, y, rest * r)
    weight = cover * (friction[...] * grounded[...].astype(jnp.float32))
    hessian[...] = weight * (speed[0] * iterate[0, 0] + speed[1] * iterate[1, 0])


def exchange(x, axis):
    count = lax.axis_size(axis)
    stride = 1
    rounds = []
    while stride < count:
        size = 4 if (count // stride) % 4 == 0 else 2
        rounds.append((stride, size))
        stride *= size
    for at, (stride, size) in enumerate(rounds):
        parts = [x]
        for turn in range(1, size):
            pairs = []
            for i in range(count):
                place = (i // stride) % size
                pairs.append((i, i + ((place ^ turn) - place) * stride))
            parts.append(lax.ppermute(x, axis, pairs))
        if at == len(rounds) - 1:
            return parts
        x = call(add_kernel, [x.shape])(*parts)[0]
    return [x]


def body(adjoint_rhs, viscosity, friction, ice_mask, grounded, basal_velocity):
    layers = viscosity.shape[0]
    inputs = (adjoint_rhs, viscosity, friction, ice_mask, grounded, basal_velocity)
    tile = (ROWS, LANES)
    strips = (2 * (layers + layers // 2 + 1),) + tile
    ribbons = ribbon_tiles(layers)
    packed = ((ribbons + 7) // 8,) + tile
    both = (2 * packed[0],) + tile
    *held, column_a, column_b, strip_a, strip_b = call(
        pack_kernel,
        [jax.ShapeDtypeStruct(x.shape, x.dtype) for x in inputs] + [packed, packed, strips, strips],
        [pltpu.SemaphoreType.DMA((len(inputs),))],
        in_specs=[pl.BlockSpec(memory_space=pltpu.HBM)] * len(inputs),
    )(*[pltpu.with_memory_space_constraint(x, pltpu.HBM) for x in inputs])
    strip_b, strip_a = swapped(strip_b, ("gx",), 1), swapped(strip_a, ("gx",), 0)
    beside = ("gy", "gz")
    (columns,) = call(beside_kernel, [both])(swapped(column_a, beside, 0), swapped(column_b, beside, 1))
    columns_b, columns_a = swapped(columns, ("gx",), 1), swapped(columns, ("gx",), 0)
    block = (layers, 2 * ROWS, 2 * LANES)
    powers, sums, ribbon = call(
        main_kernel,
        [(STEPS,) + adjoint_rhs.shape, (2 * STEPS + 1, ROWS, 2 * LANES), (ribbons, 2 * ROWS, LANES)],
        [(2,) + block] * 2 + [block] * 4 + [block[1:]] * 2,
        cost_estimate=pl.CostEstimate(flops=200_000_000, bytes_accessed=8_000_000, transcendentals=0),
    )(*held[:5], strip_b, strip_a)
    edges, sums = call(
        ribbon_kernel,
        [(STEPS, 2, layers // 4) + tile, (2, 2 * ROWS, LANES)],
    )(ribbon, columns, columns_b, columns_a, sums)
    parts = exchange(sums, ("gy", "gz"))
    if len(parts) > 1:
        sums = call(add_kernel, [sums.shape])(*parts)[0]
    parts = exchange(sums, "gx")
    rhs, _, friction, ice_mask, grounded, speed = held
    return tuple(
        call(final_kernel, [adjoint_rhs.shape, adjoint_rhs.shape, friction.shape])(
            rhs, powers, edges, friction, ice_mask, grounded, speed, *parts
        )
    )


def solution(mesh):
    in_specs = (
        P(None, None, ("parts", "gx"), ("gy", "gz")),
        P(None, ("parts", "gx"), ("gy", "gz")),
        P(("parts", "gx"), ("gy", "gz")),
        P(("parts", "gx"), ("gy", "gz")),
        P(("parts", "gx"), ("gy", "gz")),
        P(None, ("parts", "gx"), ("gy", "gz")),
    )
    out_specs = (
        P(None, None, ("parts", "gx"), ("gy", "gz")),
        P(None, None, ("parts", "gx"), ("gy", "gz")),
        P(("parts", "gx"), ("gy", "gz")),
    )
    return jax.shard_map(body, mesh=mesh, in_specs=in_specs, out_specs=out_specs, check_vma=False)
```

```python
import functools

import jax
import jax.numpy as jnp
from jax import lax
from jax.experimental import pallas as pl
from jax.experimental.pallas import tpu as pltpu
from jax.sharding import PartitionSpec as P

STEPS = 4
HALO = 4
ROWS = 8
LANES = 128
UNROLL = 5
SLOT = 32


def call(kernel, outs, scratch=(), **more):
    return pl.pallas_call(
        kernel,
        out_shape=[jax.ShapeDtypeStruct(s, jnp.float32) if isinstance(s, tuple) else s for s in outs],
        scratch_shapes=[pltpu.VMEM(s, jnp.float32) if isinstance(s, tuple) else s for s in scratch],
        compiler_params=pltpu.CompilerParams(vmem_limit_bytes=40 * 1024 * 1024),
        **more,
    )


def place_of(axis):
    place, count = lax.axis_index(axis), lax.axis_size(axis)
    even = place % 2 == 0
    has_a = jnp.logical_or(jnp.logical_not(even), place < count - 1)
    has_b = jnp.where(even, place > 0, place < count - 1)
    return even, has_a, has_b


def swapped(x, axes, first, spare=None):
    count, others = lax.axis_size(axes), lax.axis_size(spare) if spare else 1
    pairs = []
    for at in range(others):
        for i in range(count):
            other, to = (i + 1 if (i - first) % 2 == 0 else i - 1), at
            if not 0 <= other < count:
                other, to = (i, at ^ 1) if spare else (count - 1 - i, at)
                if to >= others or count % 2:
                    other, to = i, at
            if spare == "parts":
                pairs.append((at * count + i, to * count + other))
            else:
                pairs.append((i * others + at, other * others + to))
    names = axes if not spare else ("parts", *axes) if spare == "parts" else (*axes, spare)
    return lax.ppermute(x, names, pairs)


def own_planes(rhs, eta, friction, ice, grounded):
    layers = eta.shape[0]
    cover = ice[...].astype(jnp.float32)
    drag = friction[...] * grounded[...].astype(jnp.float32)

    def plane(p):
        if p < 2 * layers:
            return rhs[p // layers, p % layers] * cover
        if p < 3 * layers:
            return eta[p - 2 * layers]
        return cover if p == 3 * layers else drag

    return plane


def pair_of(q, layers):
    if q < layers:
        return q, q + layers
    if q < layers + layers // 2:
        return q + layers, q + layers + layers // 2
    return 3 * layers, 3 * layers + 1


def ribbon_places(p, layers):
    tiles = layers // 4
    if p < 3 * layers:
        k = p % layers
        return p // layers * tiles + k % tiles, (k // tiles,)
    return (3 * tiles, (0, 1, 2, 3)) if p == 3 * layers else (3 * tiles + 1, (0,))


def ribbon_tiles(layers):
    return 3 * (layers // 4) + 2


def packed_place(tile):
    return tile // 8, HALO * (tile % 8)


def between(lane, first, width):
    return (lane >= first) & (lane < first + width)


def turned(v, shift):
    shift = shift % LANES
    return pltpu.roll(v, shift, 1) if shift else v


def pack_kernel(*refs):
    sources, held, (column_a, column_b, strip_a, strip_b, arrived) = refs[:6], refs[6:12], refs[12:]
    copies = [pltpu.make_async_copy(a, b, arrived.at[i]) for i, (a, b) in enumerate(zip(sources, held))]
    for copy in copies:
        copy.start()
    for copy in copies:
        copy.wait()
    rhs, eta, friction, ice, grounded, _ = held
    layers = eta.shape[0]
    plane = own_planes(rhs, eta, friction, ice, grounded)
    lane = lax.broadcasted_iota(jnp.int32, (ROWS, LANES), 1)
    row = lax.broadcasted_iota(jnp.int32, (ROWS, LANES), 0)
    rows_even, _, _ = place_of("gx")
    columns_even, _, _ = place_of(("gy", "gz"))
    upper_a = (row < HALO) != rows_even
    count = ribbon_tiles(layers)
    zero = jnp.zeros((ROWS, LANES), jnp.float32)
    left, right = [zero] * count, [zero] * count
    for q in range(strip_a.shape[0] // 2):
        first, second = pair_of(q, layers)
        x, y = plane(first), plane(second)
        for half in range(2):
            xs = x[:, half * LANES : (half + 1) * LANES]
            ys = y[:, half * LANES : (half + 1) * LANES]
            ys = pltpu.roll(ys, HALO, 0)
            strip_a[2 * q + half] = jnp.where(upper_a, xs, ys)
            strip_b[2 * q + half] = jnp.where(upper_a, ys, xs)
        for p, v in ((first, x), (second, y)):
            tile, slots = ribbon_places(p, layers)
            for slot in slots:
                at = slot * SLOT
                left[tile] = jnp.where(between(lane, at + 8, 4), turned(v[:, :LANES], at + 8), left[tile])
                right[tile] = jnp.where(between(lane, at + 16, 4), turned(v[:, LANES:], at + 20), right[tile])
    to_left, to_right = [zero] * column_a.shape[0], [zero] * column_a.shape[0]
    for tile in range(count):
        group, at = packed_place(tile)
        here = between(lane % SLOT, at, HALO)
        to_left[group] = jnp.where(here, turned(left[tile], at - 8), to_left[group])
        to_right[group] = jnp.where(here, turned(right[tile], at - 16), to_right[group])
    for group in range(column_a.shape[0]):
        column_a[group] = jnp.where(columns_even, to_right[group], to_left[group])
        column_b[group] = jnp.where(columns_even, to_left[group], to_right[group])


def beside_kernel(from_a, from_b, columns):
    even, has_a, has_b = place_of(("gy", "gz"))
    count = from_a.shape[0]
    for group in range(count):
        a = jnp.where(has_a, from_a[group], 0.0)
        b = jnp.where(has_b, from_b[group], 0.0)
        columns[group] = jnp.where(even, a, b)
        columns[count + group] = jnp.where(even, b, a)


def two_sum(a, b):
    s = a + b
    t = s - a
    return s, (a - (s - t)) + (b - t)


def join(x, y):
    s, e = two_sum(x[0], y[0])
    e = e + (x[1] + y[1])
    h = s + e
    return h, e - (h - s)


def times(scalar, x):
    def cut(v):
        t = v * 4097.0
        h = t - (t - v)
        return h, v - h

    p = scalar * x[0]
    sh, sl = cut(scalar)
    xh, xl = cut(x[0])
    e = ((sh * xh - p) + sh * xl + sl * xh) + sl * xl
    return p, e + scalar * x[1]


def beyond():
    even, has_a, has_b = place_of("gx")
    upper_a = (lax.broadcasted_iota(jnp.int32, (ROWS, LANES), 0) < HALO) == even

    def below_and_above(from_a, from_b):
        return jnp.where(upper_a, jnp.where(has_a, from_a, 0.0), jnp.where(has_b, from_b, 0.0))

    def above_and_below(from_a, from_b):
        return jnp.where(upper_a, jnp.where(has_b, from_b, 0.0), jnp.where(has_a, from_a, 0.0))

    return below_and_above, above_and_below


def row_next(v):
    return pltpu.roll(v, 2 * ROWS - 1, 0)


def row_prev(v):
    return pltpu.roll(v, 1, 0)


def col_next(v):
    return pltpu.roll(v, v.shape[1] - 1, 1)


def col_prev(v):
    return pltpu.roll(v, 1, 1)


class Tiles:
    def __init__(self, tiles):
        self.tiles = tiles

    @staticmethod
    def load(ref):
        return Tiles([ref[r : r + ROWS, c : c + LANES] for r in (0, ROWS) for c in (0, LANES)])

    def store(self, ref):
        for v, (r, c) in zip(self.tiles, ((0, 0), (0, LANES), (ROWS, 0), (ROWS, LANES))):
            ref[r : r + ROWS, c : c + LANES] = v

    def both(self, other, op):
        if isinstance(other, Tiles):
            return Tiles([op(x, y) for x, y in zip(self.tiles, other.tiles)])
        return Tiles([op(x, other) for x in self.tiles])

    def __add__(self, other):
        return self.both(other, lambda x, y: x + y)

    def __sub__(self, other):
        return self.both(other, lambda x, y: x - y)

    def __mul__(self, other):
        return self.both(other, lambda x, y: x * y)

    __rmul__ = __mul__


class Moves:
    def __init__(self):
        row = lax.broadcasted_iota(jnp.int32, (ROWS, LANES), 0)
        lane = lax.broadcasted_iota(jnp.int32, (ROWS, LANES), 1)
        self.first_row, self.last_row = row == 0, row == ROWS - 1
        self.first_lane, self.last_lane = lane == 0, lane == LANES - 1

    def rows(self, v, shift, edge):
        own0, own1, halo0, halo1 = [pltpu.roll(x, shift, 0) for x in v.tiles]
        return Tiles(
            [
                jnp.where(edge, halo0, own0),
                jnp.where(edge, halo1, own1),
                jnp.where(edge, own0, halo0),
                jnp.where(edge, own1, halo1),
            ]
        )

    def row_next(self, v):
        return self.rows(v, ROWS - 1, self.last_row)

    def row_prev(self, v):
        return self.rows(v, 1, self.first_row)

    def col_next(self, v):
        own0, own1, halo0, halo1 = [pltpu.roll(x, LANES - 1, 1) for x in v.tiles]
        return Tiles([jnp.where(self.last_lane, own1, own0), own1, jnp.where(self.last_lane, halo1, halo0), halo1])

    def col_prev(self, v):
        own0, own1, halo0, halo1 = [pltpu.roll(x, 1, 1) for x in v.tiles]
        return Tiles([own0, jnp.where(self.first_lane, own0, own1), halo0, jnp.where(self.first_lane, halo0, halo1)])


class Turns:
    row_next = staticmethod(row_next)
    row_prev = staticmethod(row_prev)
    col_next = staticmethod(col_next)
    col_prev = staticmethod(col_prev)


def horizontal(g0, g1, e_row, e_col, e_half, moves):
    row_next, row_prev, col_next, col_prev = moves.row_next, moves.row_prev, moves.col_next, moves.col_prev
    g0n, g1n = row_next(g0), col_next(g1)
    f = e_half * (g1n - col_prev(g1))
    h = e_half * (g0n - row_prev(g0))
    flux = e_row * (g0 - g0n)
    out0 = flux - row_next(f) - row_prev(flux - f)
    flux = e_col * (g0 - col_next(g0))
    out0 = out0 + (flux - col_prev(flux))
    flux = (4.0 * e_col) * (g1 - g1n)
    out1 = flux - col_next(h) - col_prev(flux - h)
    flux = (0.25 * e_row) * (g1 - row_next(g1))
    out1 = out1 + (flux - row_prev(flux))
    return out0, out1


def main_kernel(
    rhs, eta, friction, ice, grounded, strip_b, strip_a,
    power_1, power_2, power_3, power_4, sums, ribbon,
    masked, eta_row, eta_col, eta_half, eta_up, cover, drag,
):
    layers = eta.shape[0]
    plane = own_planes(rhs, eta, friction, ice, grounded)
    below_and_above, above_and_below = beyond()
    lane = lax.broadcasted_iota(jnp.int32, (2 * ROWS, LANES), 1)

    def target(p):
        if p < 2 * layers:
            return masked.at[p // layers, p % layers]
        if p < 3 * layers:
            return eta_half.at[p - 2 * layers]
        return cover if p == 3 * layers else drag

    strips = [jnp.zeros((2 * ROWS, LANES), jnp.float32) for _ in range(ribbon.shape[0])]
    for q in range(strip_a.shape[0] // 2):
        first, second = pair_of(q, layers)
        halves = ([], [])
        for half in range(2):
            from_a, from_b = strip_a[2 * q + half], strip_b[2 * q + half]
            halves[0].append(below_and_above(from_a, from_b))
            halves[1].append(pltpu.roll(above_and_below(from_a, from_b), HALO, 0))
        for p, halo in zip((first, second), halves):
            v = plane(p)
            dst = target(p)
            dst[0:ROWS, :] = v
            dst[ROWS:, 0:LANES], dst[ROWS:, LANES:] = halo
            head = jnp.concatenate([v[:, :LANES], halo[0]], 0)
            tail = jnp.concatenate([v[:, LANES:], halo[1]], 0)
            tile, slots = ribbon_places(p, layers)
            for slot in slots:
                at = slot * SLOT
                strips[tile] = jnp.where(between(lane, at, 8), turned(tail, at + 8), strips[tile])
                strips[tile] = jnp.where(between(lane, at + 20, 8), turned(head, at + 20), strips[tile])
    for tile, v in enumerate(strips):
        ribbon[tile] = v

    moves = Moves()
    load = Tiles.load
    for k in range(layers):
        e = load(eta_half.at[k])
        (2.0 * (e + moves.row_next(e))).store(eta_row.at[k])
        (0.5 * (e + moves.col_next(e))).store(eta_col.at[k])
        eta_up[k] = eta_half[k] + eta_half[k + 1] if k + 1 < layers else jnp.zeros_like(eta_up[k])
        if k:
            eta_half[k - 1] = 0.5 * eta_half[k - 1]
    eta_half[layers - 1] = 0.5 * eta_half[layers - 1]

    def apply(t, src, dst):
        def block(b, carry):
            g0, g1, below0, below1, odd, even = carry
            g0, g1, below0, below1 = Tiles(g0), Tiles(g1), Tiles(below0), Tiles(below1)
            odd, even = list(odd), list(even)
            m = load(cover)
            for i in range(UNROLL):
                k = b * UNROLL + i
                after = k + 1 if i + 1 < UNROLL else jnp.minimum(k + 1, layers - 1)
                next0, next1 = load(src.at[0, after]), load(src.at[1, after])
                e_up = load(eta_up.at[k])
                up0, up1 = e_up * (g0 - next0), e_up * (g1 - next1)
                out0, out1 = horizontal(g0, g1, load(eta_row.at[k]), load(eta_col.at[k]), load(eta_half.at[k]), moves)
                out0, out1 = m * (out0 + (up0 - below0)), m * (out1 + (up1 - below1))
                for c, g, out in ((0, g0, out0), (1, g1, out1)):
                    if t < STEPS:
                        out.store(dst.at[c, k])
                    for half in range(2):
                        now = out.tiles[half]
                        if t == STEPS:
                            dst[c, k, :, half * LANES : (half + 1) * LANES] = now
                        odd[half] = odd[half] + g.tiles[half] * now
                        even[half] = even[half] + now * now
                g0, g1, below0, below1 = next0, next1, up0, up1
            return g0.tiles, g1.tiles, below0.tiles, below1.tiles, odd, even

        zero = [jnp.zeros((ROWS, LANES), jnp.float32)] * 2
        d = -1.0 * load(drag)
        g0, g1 = load(src.at[0, 0]), load(src.at[1, 0])
        start = (g0.tiles, g1.tiles, (d * g0).tiles, (d * g1).tiles, zero, zero)
        ends = lax.fori_loop(0, layers // UNROLL, block, start)[4:]
        return [jnp.concatenate(v, 1) for v in ends]

    bare = 1.0 - ice[...].astype(jnp.float32)
    whole = jnp.zeros((ROWS, 2 * LANES), jnp.float32)
    outside = jnp.zeros((ROWS, 2 * LANES), jnp.float32)
    for c in range(2):
        for k in range(layers):
            square = rhs[c, k] * rhs[c, k]
            whole = whole + square
            outside = outside + bare * square
    sums[0] = whole
    wide = lax.broadcasted_iota(jnp.int32, (ROWS, 2 * LANES), 1)
    inner = between(wide, HALO, 2 * LANES - 2 * HALO)
    fields = (masked, power_1, power_2, power_3, power_4)
    for t in range(1, STEPS + 1):
        odd, even = apply(t, fields[t - 1], fields[t])
        sums[2 * t - 1] = jnp.where(inner, odd, 0.0) + outside
        sums[2 * t] = jnp.where(inner, even, 0.0) + outside


def ribbon_kernel(ribbon, columns, columns_b, columns_a, sums, edges, moments):
    tiles = edges.shape[2]
    below_and_above, _ = beyond()
    lane = lax.broadcasted_iota(jnp.int32, (2 * ROWS, LANES), 1)

    count = columns.shape[0] // 2
    beside = [
        jnp.concatenate([columns[i], below_and_above(columns_a[i], columns_b[i])], 0) for i in range(2 * count)
    ]
    spot = lane % SLOT

    def whole(tile):
        group, at = packed_place(tile)
        right = jnp.where(between(spot, 8, HALO), turned(beside[group], 8 - at), ribbon[tile])
        return jnp.where(between(spot, 16, HALO), turned(beside[count + group], 16 - at), right)

    field = [[whole(c * tiles + n) for n in range(tiles)] for c in range(2)]
    eta = [whole(2 * tiles + n) for n in range(tiles)]
    cover, drag = whole(3 * tiles), whole(3 * tiles + 1)

    def after(v):
        return v[1:] + [turned(v[0], -SLOT)]

    eta_row = [2.0 * (e + row_next(e)) for e in eta]
    eta_col = [0.5 * (e + col_next(e)) for e in eta]
    eta_half = [0.5 * e for e in eta]
    eta_up = [e + n for e, n in zip(eta, after(eta))]
    eta_up[-1] = jnp.where(lane < LANES - SLOT, eta_up[-1], 0.0)
    place = lax.broadcasted_iota(jnp.int32, (ROWS, LANES), 1) % SLOT
    edge = between(place, 4, HALO) | between(place, 20, HALO)
    extra = [None]
    for t in range(1, STEPS + 1):
        ups = [[u * (g - n) for u, g, n in zip(eta_up, field[c], after(field[c]))] for c in range(2)]
        result = ([], [])
        odd = even = jnp.zeros((ROWS, LANES), jnp.float32)
        for n in range(tiles):
            outs = horizontal(field[0][n], field[1][n], eta_row[n], eta_col[n], eta_half[n], Turns)
            for c in range(2):
                below = ups[c][n - 1] if n else turned(ups[c][-1], SLOT) - drag * field[c][0]
                out = cover * (outs[c] + (ups[c][n] - below))
                result[c].append(out)
                now = out[:ROWS]
                edges[t - 1, c, n] = now
                odd = odd + field[c][n][:ROWS] * now
                even = even + now * now
        field = result
        extra.extend([jnp.where(edge, odd, 0.0), jnp.where(edge, even, 0.0)])

    tall = lax.broadcasted_iota(jnp.int32, (2 * ROWS, LANES), 0)
    high = jnp.zeros((2 * ROWS, LANES), jnp.float32)
    low = jnp.zeros((2 * ROWS, LANES), jnp.float32)
    for j, more in enumerate(extra):
        total = sums[j]
        pair = two_sum(total[:, :LANES], total[:, LANES:])
        if more is not None:
            pair = join(pair, (more, jnp.zeros_like(more)))
        for step in (4, 2, 1):
            pair = join(pair, tuple(pltpu.roll(v, step, 0) for v in pair))
        high = jnp.where(tall == j, jnp.concatenate([pair[0]] * 2, 0), high)
        low = jnp.where(tall == j, jnp.concatenate([pair[1]] * 2, 0), low)
    moments[0] = high
    moments[1] = low


def add_kernel(*refs):
    *ins, out = refs
    total = (ins[0][0], ins[0][1])
    for x in ins[1:]:
        total = join(total, (x[0], x[1]))
    out[0], out[1] = total


def solve(total):
    for step in (64, 32, 16, 8, 4, 2, 1):
        total = join(total, tuple(pltpu.roll(v, step, 1) for v in total))

    def spread(v, j):
        return jnp.broadcast_to(v[j : j + 1], (ROWS, LANES))

    centre = spread(total[0], 1) / spread(total[0], 0)
    wide = jnp.concatenate([centre, centre], 0)
    mu = [spread(total[0], 0)]
    for _ in range(2 * STEPS):
        step = times(wide, total)
        total = join(tuple(pltpu.roll(v, 2 * ROWS - 1, 0) for v in total), (-step[0], -step[1]))
        mu.append(spread(total[0], 0))

    def plus(a, b):
        n = max(len(a), len(b))
        return [a[i] + b[i] if i < min(len(a), len(b)) else (a[i] if i < len(a) else b[i]) for i in range(n)]

    def scaled(s, a):
        return [s * x for x in a]

    def operator(a):
        return plus([centre * x for x in a], [jnp.zeros_like(centre)] + a)

    def dot(a, b):
        square = [None] * (len(a) + len(b) - 1)
        for i, x in enumerate(a):
            for j, y in enumerate(b):
                z = x * y
                square[i + j] = z if square[i + j] is None else square[i + j] + z
        value = square[0] * mu[0]
        for n in range(1, len(square)):
            value = value + square[n] * mu[n]
        return value

    one = jnp.ones_like(centre)
    right = [one]
    quasi, search, update, iterate = right, right, [], []
    applied = operator(search)
    carried = applied
    rho = mu[0]
    tau_sq = rho
    alpha = theta_sq = eta = None
    for half in range(STEPS):
        if half % 2 == 0:
            alpha = rho / dot(carried, right)
            search_next = plus(search, scaled(-alpha, carried))
        quasi = plus(quasi, scaled(-alpha, applied))
        if half:
            update = plus(search, scaled(theta_sq / alpha * eta, update))
        else:
            update = search
        theta_sq = dot(quasi, quasi) / tau_sq
        cosine_sq = 1.0 / (1.0 + theta_sq)
        tau_sq = tau_sq * theta_sq * cosine_sq
        eta = cosine_sq * alpha
        iterate = plus(iterate, scaled(eta, update))
        if half % 2 == 0:
            search = search_next
            applied = operator(search)
        elif half < STEPS - 1:
            rho_next = dot(quasi, right)
            beta = rho_next / rho
            search = plus(quasi, scaled(beta, search))
            applied_next = operator(search)
            carried = plus(applied_next, scaled(beta, plus(applied, scaled(beta, carried))))
            applied, rho = applied_next, rho_next
    powers = [iterate[-1]]
    for c in iterate[-2::-1]:
        powers = plus([c] + powers, scaled(-centre, powers))
    return powers


def final_kernel(rhs, power_1, power_2, power_3, power_4, edges, friction, ice, grounded, speed, *rest):
    *parts, iterate, residual, hessian = rest
    layers, tiles = rhs.shape[1], edges.shape[2]
    total = (parts[0][0], parts[0][1])
    for x in parts[1:]:
        total = join(total, (x[0], x[1]))
    factors = solve(total)
    powers = (power_1, power_2, power_3, power_4)
    wide = [jnp.concatenate([c, c], 1) for c in factors]
    rest = sum(wide[1:], wide[0])
    cover = ice[...].astype(jnp.float32)
    lane = lax.broadcasted_iota(jnp.int32, (ROWS, LANES), 1)

    def combined(vectors, weights):
        x = weights[1] * vectors[0]
        y = weights[0] * vectors[0]
        for t in range(1, STEPS):
            if t + 1 < STEPS:
                x = x + weights[t + 1] * vectors[t]
            y = y + weights[t] * vectors[t]
        return x, y

    for c in range(2):
        side = [combined([edges[t, c, n] for t in range(STEPS)], factors) for n in range(tiles)]
        for k in range(layers):
            at = k // tiles * SLOT
            inner = combined([p[c, k, :ROWS] for p in powers], wide)
            patched = []
            for v, e in zip(inner, side[k % tiles]):
                head = jnp.where(lane < HALO, turned(e, -at - 20), v[:, :LANES])
                tail = jnp.where(lane >= LANES - HALO, turned(e, 120 - at), v[:, LANES:])
                patched.append(jnp.concatenate([head, tail], 1))
            r = rhs[c, k]
            x, y = patched
            iterate[c, k] = jnp.where(cover > 0.0, wide[0] * r + x, rest * r)
            residual[c, k] = r - jnp.where(cover > 0.0, y, rest * r)
    weight = cover * (friction[...] * grounded[...].astype(jnp.float32))
    hessian[...] = weight * (speed[0] * iterate[0, 0] + speed[1] * iterate[1, 0])


def exchange(x, axis):
    count = lax.axis_size(axis)
    stride = 1
    rounds = []
    while stride < count:
        size = 4 if (count // stride) % 4 == 0 else 2
        rounds.append((stride, size))
        stride *= size
    for at, (stride, size) in enumerate(rounds):
        parts = [x]
        for turn in range(1, size):
            pairs = []
            for i in range(count):
                place = (i // stride) % size
                pairs.append((i, i + ((place ^ turn) - place) * stride))
            parts.append(lax.ppermute(x, axis, pairs))
        if at == len(rounds) - 1:
            return parts
        x = call(add_kernel, [x.shape])(*parts)[0]
    return [x]


def body(adjoint_rhs, viscosity, friction, ice_mask, grounded, basal_velocity):
    layers = viscosity.shape[0]
    inputs = (adjoint_rhs, viscosity, friction, ice_mask, grounded, basal_velocity)
    tile = (ROWS, LANES)
    strips = (2 * (layers + layers // 2 + 1),) + tile
    ribbons = ribbon_tiles(layers)
    packed = ((ribbons + 7) // 8,) + tile
    both = (2 * packed[0],) + tile
    *held, column_a, column_b, strip_a, strip_b = call(
        pack_kernel,
        [jax.ShapeDtypeStruct(x.shape, x.dtype) for x in inputs] + [packed, packed, strips, strips],
        [pltpu.SemaphoreType.DMA((len(inputs),))],
        in_specs=[pl.BlockSpec(memory_space=pltpu.HBM)] * len(inputs),
    )(*[pltpu.with_memory_space_constraint(x, pltpu.HBM) for x in inputs])
    strip_b, strip_a = swapped(strip_b, ("gx",), 1, "parts"), swapped(strip_a, ("gx",), 0)
    beside = ("gy", "gz")
    (columns,) = call(beside_kernel, [both])(swapped(column_a, beside, 0), swapped(column_b, beside, 1))
    columns_b, columns_a = swapped(columns, ("gx",), 1, "gy"), swapped(columns, ("gx",), 0)
    block = (layers, 2 * ROWS, 2 * LANES)
    *powers, sums, ribbon = call(
        main_kernel,
        [(2,) + block] * (STEPS - 1) + [adjoint_rhs.shape, (2 * STEPS + 1, ROWS, 2 * LANES), (ribbons, 2 * ROWS, LANES)],
        [(2,) + block] + [block] * 4 + [block[1:]] * 2,
        cost_estimate=pl.CostEstimate(flops=200_000_000, bytes_accessed=8_000_000, transcendentals=0),
    )(*held[:5], strip_b, strip_a)
    edges, sums = call(
        ribbon_kernel,
        [(STEPS, 2, layers // 4) + tile, (2, 2 * ROWS, LANES)],
    )(ribbon, columns, columns_b, columns_a, sums)
    parts = exchange(sums, ("gy", "gz"))
    if len(parts) > 1:
        sums = call(add_kernel, [sums.shape])(*parts)[0]
    parts = exchange(sums, "gx")
    rhs, _, friction, ice_mask, grounded, speed = held
    return tuple(
        call(final_kernel, [adjoint_rhs.shape, adjoint_rhs.shape, friction.shape])(
            rhs, *powers, edges, friction, ice_mask, grounded, speed, *parts
        )
    )


def solution(mesh):
    in_specs = (
        P(None, None, ("parts", "gx"), ("gy", "gz")),
        P(None, ("parts", "gx"), ("gy", "gz")),
        P(("parts", "gx"), ("gy", "gz")),
        P(("parts", "gx"), ("gy", "gz")),
        P(("parts", "gx"), ("gy", "gz")),
        P(None, ("parts", "gx"), ("gy", "gz")),
    )
    out_specs = (
        P(None, None, ("parts", "gx"), ("gy", "gz")),
        P(None, None, ("parts", "gx"), ("gy", "gz")),
        P(("parts", "gx"), ("gy", "gz")),
    )
    return jax.shard_map(body, mesh=mesh, in_specs=in_specs, out_specs=out_specs, check_vma=False)
```

```python
import functools

import jax
import jax.numpy as jnp
from jax import lax
from jax.experimental import pallas as pl
from jax.experimental.pallas import tpu as pltpu
from jax.sharding import PartitionSpec as P

STEPS = 4
HALO = 4
ROWS = 8
LANES = 128
UNROLL = 5
FIRST = 4
SLOT = 32


def call(kernel, outs, scratch=(), **more):
    return pl.pallas_call(
        kernel,
        out_shape=[jax.ShapeDtypeStruct(s, jnp.float32) if isinstance(s, tuple) else s for s in outs],
        scratch_shapes=[pltpu.VMEM(s, jnp.float32) if isinstance(s, tuple) else s for s in scratch],
        compiler_params=pltpu.CompilerParams(vmem_limit_bytes=40 * 1024 * 1024),
        **more,
    )


def place_of(axis):
    place, count = lax.axis_index(axis), lax.axis_size(axis)
    even = place % 2 == 0
    has_a = jnp.logical_or(jnp.logical_not(even), place < count - 1)
    has_b = jnp.where(even, place > 0, place < count - 1)
    return even, has_a, has_b


def swapped(x, axes, first, spare=None):
    count, others = lax.axis_size(axes), lax.axis_size(spare) if spare else 1
    pairs = []
    for at in range(others):
        for i in range(count):
            other, to = (i + 1 if (i - first) % 2 == 0 else i - 1), at
            if not 0 <= other < count:
                other, to = (i, at ^ 1) if spare else (count - 1 - i, at)
                if to >= others or count % 2:
                    other, to = i, at
            if spare == "parts":
                pairs.append((at * count + i, to * count + other))
            else:
                pairs.append((i * others + at, other * others + to))
    names = axes if not spare else ("parts", *axes) if spare == "parts" else (*axes, spare)
    return lax.ppermute(x, names, pairs)


def own_planes(rhs, eta, friction, ice, grounded):
    layers = eta.shape[0]
    cover = ice[...].astype(jnp.float32)
    drag = friction[...] * grounded[...].astype(jnp.float32)

    def plane(p):
        if p < 2 * layers:
            return rhs[p // layers, p % layers] * cover
        if p < 3 * layers:
            return eta[p - 2 * layers]
        return cover if p == 3 * layers else drag

    return plane


def pair_of(q, layers):
    if q < layers:
        return q, q + layers
    if q < layers + layers // 2:
        return q + layers, q + layers + layers // 2
    return 3 * layers, 3 * layers + 1


def ribbon_places(p, layers):
    tiles = layers // 4
    if p < 3 * layers:
        k = p % layers
        return p // layers * tiles + k % tiles, (k // tiles,)
    return (3 * tiles, (0, 1, 2, 3)) if p == 3 * layers else (3 * tiles + 1, (0,))


def ribbon_tiles(layers):
    return 3 * (layers // 4) + 2


def packed_place(tile):
    return tile // 8, HALO * (tile % 8)


def between(lane, first, width):
    return (lane >= first) & (lane < first + width)


def turned(v, shift):
    shift = shift % LANES
    return pltpu.roll(v, shift, 1) if shift else v


def pack_kernel(*refs):
    sources, held, (column_a, column_b, strip_a, strip_b, arrived) = refs[:6], refs[6:12], refs[12:]
    copies = [pltpu.make_async_copy(a, b, arrived.at[i]) for i, (a, b) in enumerate(zip(sources, held))]
    for copy in copies:
        copy.start()
    for copy in copies:
        copy.wait()
    rhs, eta, friction, ice, grounded, _ = held
    layers = eta.shape[0]
    plane = own_planes(rhs, eta, friction, ice, grounded)
    lane = lax.broadcasted_iota(jnp.int32, (ROWS, LANES), 1)
    row = lax.broadcasted_iota(jnp.int32, (ROWS, LANES), 0)
    rows_even, _, _ = place_of("gx")
    columns_even, _, _ = place_of(("gy", "gz"))
    upper_a = (row < HALO) != rows_even
    count = ribbon_tiles(layers)
    zero = jnp.zeros((ROWS, LANES), jnp.float32)
    left, right = [zero] * count, [zero] * count
    for q in range(strip_a.shape[0] // 2):
        first, second = pair_of(q, layers)
        x, y = plane(first), plane(second)
        for half in range(2):
            xs = x[:, half * LANES : (half + 1) * LANES]
            ys = y[:, half * LANES : (half + 1) * LANES]
            ys = pltpu.roll(ys, HALO, 0)
            strip_a[2 * q + half] = jnp.where(upper_a, xs, ys)
            strip_b[2 * q + half] = jnp.where(upper_a, ys, xs)
        for p, v in ((first, x), (second, y)):
            tile, slots = ribbon_places(p, layers)
            for slot in slots:
                at = slot * SLOT
                left[tile] = jnp.where(between(lane, at + 8, 4), turned(v[:, :LANES], at + 8), left[tile])
                right[tile] = jnp.where(between(lane, at + 16, 4), turned(v[:, LANES:], at + 20), right[tile])
    to_left, to_right = [zero] * column_a.shape[0], [zero] * column_a.shape[0]
    for tile in range(count):
        group, at = packed_place(tile)
        here = between(lane % SLOT, at, HALO)
        to_left[group] = jnp.where(here, turned(left[tile], at - 8), to_left[group])
        to_right[group] = jnp.where(here, turned(right[tile], at - 16), to_right[group])
    for group in range(column_a.shape[0]):
        column_a[group] = jnp.where(columns_even, to_right[group], to_left[group])
        column_b[group] = jnp.where(columns_even, to_left[group], to_right[group])


def beside_kernel(from_a, from_b, columns):
    even, has_a, has_b = place_of(("gy", "gz"))
    count = from_a.shape[0]
    for group in range(count):
        a = jnp.where(has_a, from_a[group], 0.0)
        b = jnp.where(has_b, from_b[group], 0.0)
        columns[group] = jnp.where(even, a, b)
        columns[count + group] = jnp.where(even, b, a)


def two_sum(a, b):
    s = a + b
    t = s - a
    return s, (a - (s - t)) + (b - t)


def join(x, y):
    s, e = two_sum(x[0], y[0])
    e = e + (x[1] + y[1])
    h = s + e
    return h, e - (h - s)


def times(scalar, x):
    def cut(v):
        t = v * 4097.0
        h = t - (t - v)
        return h, v - h

    p = scalar * x[0]
    sh, sl = cut(scalar)
    xh, xl = cut(x[0])
    e = ((sh * xh - p) + sh * xl + sl * xh) + sl * xl
    return p, e + scalar * x[1]


def beyond():
    even, has_a, has_b = place_of("gx")
    upper_a = (lax.broadcasted_iota(jnp.int32, (ROWS, LANES), 0) < HALO) == even

    def below_and_above(from_a, from_b):
        return jnp.where(upper_a, jnp.where(has_a, from_a, 0.0), jnp.where(has_b, from_b, 0.0))

    def above_and_below(from_a, from_b):
        return jnp.where(upper_a, jnp.where(has_b, from_b, 0.0), jnp.where(has_a, from_a, 0.0))

    return below_and_above, above_and_below


def row_next(v):
    return pltpu.roll(v, 2 * ROWS - 1, 0)


def row_prev(v):
    return pltpu.roll(v, 1, 0)


def col_next(v):
    return pltpu.roll(v, v.shape[1] - 1, 1)


def col_prev(v):
    return pltpu.roll(v, 1, 1)


class Tiles:
    def __init__(self, tiles):
        self.tiles = tiles

    @staticmethod
    def load(ref, *place):
        return Tiles([ref[(half, *place, pl.ds(r, ROWS))] for r in (0, ROWS) for half in (0, 1)])

    def store(self, ref, *place):
        for i, v in enumerate(self.tiles):
            ref[(i % 2, *place, pl.ds(i // 2 * ROWS, ROWS))] = v

    @staticmethod
    def gather(ref, *place):
        return Tiles([ref[(half, *place, pl.ds(FIRST + r, ROWS, stride=2))] for r in (0, 1) for half in (0, 1)])

    def spread(self, ref, *place):
        for i, v in enumerate(self.tiles):
            ref[(i % 2, *place, pl.ds(FIRST + i // 2, ROWS, stride=2))] = v

    def both(self, other, op):
        if isinstance(other, Tiles):
            return Tiles([op(x, y) for x, y in zip(self.tiles, other.tiles)])
        return Tiles([op(x, other) for x in self.tiles])

    def __add__(self, other):
        return self.both(other, lambda x, y: x + y)

    def __sub__(self, other):
        return self.both(other, lambda x, y: x - y)

    def __mul__(self, other):
        return self.both(other, lambda x, y: x * y)

    __rmul__ = __mul__


class Moves:
    def __init__(self):
        lane = lax.broadcasted_iota(jnp.int32, (ROWS, LANES), 1)
        self.first_lane, self.last_lane = lane == 0, lane == LANES - 1

    def row_next(self, v):
        even0, even1, odd0, odd1 = v.tiles
        return Tiles([odd0, odd1, pltpu.roll(even0, ROWS - 1, 0), pltpu.roll(even1, ROWS - 1, 0)])

    def row_prev(self, v):
        even0, even1, odd0, odd1 = v.tiles
        return Tiles([pltpu.roll(odd0, 1, 0), pltpu.roll(odd1, 1, 0), even0, even1])

    def col_next(self, v):
        own0, own1, halo0, halo1 = [pltpu.roll(x, LANES - 1, 1) for x in v.tiles]
        return Tiles([jnp.where(self.last_lane, own1, own0), own1, jnp.where(self.last_lane, halo1, halo0), halo1])

    def col_prev(self, v):
        own0, own1, halo0, halo1 = [pltpu.roll(x, 1, 1) for x in v.tiles]
        return Tiles([own0, jnp.where(self.first_lane, own0, own1), halo0, jnp.where(self.first_lane, halo0, halo1)])


class Turns:
    row_next = staticmethod(row_next)
    row_prev = staticmethod(row_prev)
    col_next = staticmethod(col_next)
    col_prev = staticmethod(col_prev)


def horizontal(g0, g1, e_row, e_col, e_half, moves):
    row_next, row_prev, col_next, col_prev = moves.row_next, moves.row_prev, moves.col_next, moves.col_prev
    g0n, g1n = row_next(g0), col_next(g1)
    f = e_half * (g1n - col_prev(g1))
    h = e_half * (g0n - row_prev(g0))
    flux = e_row * (g0 - g0n)
    out0 = flux - row_next(f) - row_prev(flux - f)
    flux = e_col * (g0 - col_next(g0))
    out0 = out0 + (flux - col_prev(flux))
    flux = (4.0 * e_col) * (g1 - g1n)
    out1 = flux - col_next(h) - col_prev(flux - h)
    flux = (0.25 * e_row) * (g1 - row_next(g1))
    out1 = out1 + (flux - row_prev(flux))
    return out0, out1


def main_kernel(
    rhs, eta, friction, ice, grounded, strip_b, strip_a,
    power_1, power_2, power_3, power_4, sums, ribbon,
    rows, field_a, field_b, eta_row, eta_col, eta_half, eta_up, cover,
):
    layers = eta.shape[0]
    plane = own_planes(rhs, eta, friction, ice, grounded)
    below_and_above, above_and_below = beyond()
    lane = lax.broadcasted_iota(jnp.int32, (2 * ROWS, LANES), 1)

    strips = [jnp.zeros((2 * ROWS, LANES), jnp.float32) for _ in range(ribbon.shape[0])]
    for q in range(strip_a.shape[0] // 2):
        first, second = pair_of(q, layers)
        halves = ([], [])
        for half in range(2):
            from_a, from_b = strip_a[2 * q + half], strip_b[2 * q + half]
            halves[0].append(below_and_above(from_a, from_b))
            halves[1].append(pltpu.roll(above_and_below(from_a, from_b), HALO, 0))
        for p, halo in zip((first, second), halves):
            v = plane(p)
            for half in range(2):
                rows[half, p, FIRST + HALO : FIRST + HALO + ROWS] = v[:, half * LANES : (half + 1) * LANES]
                rows[half, p, FIRST : FIRST + HALO] = halo[half][HALO:]
                rows[half, p, FIRST + HALO + ROWS : FIRST + 2 * ROWS] = halo[half][:HALO]
            head = jnp.concatenate([v[:, :LANES], halo[0]], 0)
            tail = jnp.concatenate([v[:, LANES:], halo[1]], 0)
            tile, slots = ribbon_places(p, layers)
            for slot in slots:
                at = slot * SLOT
                strips[tile] = jnp.where(between(lane, at, 8), turned(tail, at + 8), strips[tile])
                strips[tile] = jnp.where(between(lane, at + 20, 8), turned(head, at + 20), strips[tile])
    for tile, v in enumerate(strips):
        ribbon[tile] = v

    moves = Moves()
    load = Tiles.load
    before = None
    for k in range(layers):
        for c in range(2):
            Tiles.gather(rows, c * layers + k).store(field_a, c, k)
        e = Tiles.gather(rows, 2 * layers + k)
        (2.0 * (e + moves.row_next(e))).store(eta_row, k)
        (0.5 * (e + moves.col_next(e))).store(eta_col, k)
        (0.5 * e).store(eta_half, k)
        if k:
            (before + e).store(eta_up, k - 1)
        before = e
    (0.0 * before).store(eta_up, layers - 1)
    Tiles.gather(rows, 3 * layers).store(cover)
    drag = Tiles.gather(rows, 3 * layers + 1)

    def apply(src, dst, power):
        def block(b, carry):
            g0, g1, below0, below1, odd, even = [Tiles(v) for v in carry]
            m = load(cover)
            for i in range(UNROLL):
                k = b * UNROLL + i
                after = k + 1 if i + 1 < UNROLL else jnp.minimum(k + 1, layers - 1)
                next0, next1 = load(src, 0, after), load(src, 1, after)
                e_up = load(eta_up, k)
                up0, up1 = e_up * (g0 - next0), e_up * (g1 - next1)
                out0, out1 = horizontal(g0, g1, load(eta_row, k), load(eta_col, k), load(eta_half, k), moves)
                out0, out1 = m * (out0 + (up0 - below0)), m * (out1 + (up1 - below1))
                for c, out in ((0, out0), (1, out1)):
                    if dst is not None:
                        out.store(dst, c, k)
                    out.spread(power, c, k)
                odd = odd + (g0 * out0 + g1 * out1)
                even = even + (out0 * out0 + out1 * out1)
                g0, g1, below0, below1 = next0, next1, up0, up1
            return [v.tiles for v in (g0, g1, below0, below1, odd, even)]

        zero = [jnp.zeros((ROWS, LANES), jnp.float32)] * 4
        g0, g1 = load(src, 0, 0), load(src, 1, 0)
        start = [g0.tiles, g1.tiles, (-1.0 * drag * g0).tiles, (-1.0 * drag * g1).tiles, zero, zero]
        ends = lax.fori_loop(0, layers // UNROLL, block, start)[4:]
        mine = between(lax.broadcasted_iota(jnp.int32, (ROWS, LANES), 0), HALO // 2, ROWS // 2)
        return [
            jnp.concatenate([jnp.where(mine, v[i], 0.0) + jnp.where(mine, v[2 + i], 0.0) for i in (0, 1)], 1) for v in ends
        ]

    bare = 1.0 - ice[...].astype(jnp.float32)
    whole = jnp.zeros((ROWS, 2 * LANES), jnp.float32)
    outside = jnp.zeros((ROWS, 2 * LANES), jnp.float32)
    for c in range(2):
        for k in range(layers):
            square = rhs[c, k] * rhs[c, k]
            whole = whole + square
            outside = outside + bare * square
    sums[0] = whole
    wide = lax.broadcasted_iota(jnp.int32, (ROWS, 2 * LANES), 1)
    inner = between(wide, HALO, 2 * LANES - 2 * HALO)
    fields = (field_a, field_b, field_a, field_b, None)
    for t, power in enumerate((power_1, power_2, power_3, power_4), 1):
        odd, even = apply(fields[t - 1], fields[t], power)
        sums[2 * t - 1] = jnp.where(inner, odd, 0.0) + outside
        sums[2 * t] = jnp.where(inner, even, 0.0) + outside


def ribbon_kernel(ribbon, columns, columns_b, columns_a, sums, edges, moments):
    tiles = edges.shape[2]
    below_and_above, _ = beyond()
    lane = lax.broadcasted_iota(jnp.int32, (2 * ROWS, LANES), 1)

    count = columns.shape[0] // 2
    beside = [
        jnp.concatenate([columns[i], below_and_above(columns_a[i], columns_b[i])], 0) for i in range(2 * count)
    ]
    spot = lane % SLOT

    def whole(tile):
        group, at = packed_place(tile)
        right = jnp.where(between(spot, 8, HALO), turned(beside[group], 8 - at), ribbon[tile])
        return jnp.where(between(spot, 16, HALO), turned(beside[count + group], 16 - at), right)

    field = [[whole(c * tiles + n) for n in range(tiles)] for c in range(2)]
    eta = [whole(2 * tiles + n) for n in range(tiles)]
    cover, drag = whole(3 * tiles), whole(3 * tiles + 1)

    def after(v):
        return v[1:] + [turned(v[0], -SLOT)]

    eta_row = [2.0 * (e + row_next(e)) for e in eta]
    eta_col = [0.5 * (e + col_next(e)) for e in eta]
    eta_half = [0.5 * e for e in eta]
    eta_up = [e + n for e, n in zip(eta, after(eta))]
    eta_up[-1] = jnp.where(lane < LANES - SLOT, eta_up[-1], 0.0)
    place = lax.broadcasted_iota(jnp.int32, (ROWS, LANES), 1) % SLOT
    edge = between(place, 4, HALO) | between(place, 20, HALO)
    extra = [None]
    for t in range(1, STEPS + 1):
        ups = [[u * (g - n) for u, g, n in zip(eta_up, field[c], after(field[c]))] for c in range(2)]
        result = ([], [])
        odd = even = jnp.zeros((ROWS, LANES), jnp.float32)
        for n in range(tiles):
            outs = horizontal(field[0][n], field[1][n], eta_row[n], eta_col[n], eta_half[n], Turns)
            for c in range(2):
                below = ups[c][n - 1] if n else turned(ups[c][-1], SLOT) - drag * field[c][0]
                out = cover * (outs[c] + (ups[c][n] - below))
                result[c].append(out)
                now = out[:ROWS]
                edges[t - 1, c, n] = now
                odd = odd + field[c][n][:ROWS] * now
                even = even + now * now
        field = result
        extra.extend([jnp.where(edge, odd, 0.0), jnp.where(edge, even, 0.0)])

    tall = lax.broadcasted_iota(jnp.int32, (2 * ROWS, LANES), 0)
    high = jnp.zeros((2 * ROWS, LANES), jnp.float32)
    low = jnp.zeros((2 * ROWS, LANES), jnp.float32)
    for j, more in enumerate(extra):
        total = sums[j]
        pair = two_sum(total[:, :LANES], total[:, LANES:])
        if more is not None:
            pair = join(pair, (more, jnp.zeros_like(more)))
        for step in (4, 2, 1):
            pair = join(pair, tuple(pltpu.roll(v, step, 0) for v in pair))
        high = jnp.where(tall == j, jnp.concatenate([pair[0]] * 2, 0), high)
        low = jnp.where(tall == j, jnp.concatenate([pair[1]] * 2, 0), low)
    moments[0] = high
    moments[1] = low


def add_kernel(*refs):
    *ins, out = refs
    total = (ins[0][0], ins[0][1])
    for x in ins[1:]:
        total = join(total, (x[0], x[1]))
    out[0], out[1] = total


def solve(total):
    for step in (64, 32, 16, 8, 4, 2, 1):
        total = join(total, tuple(pltpu.roll(v, step, 1) for v in total))

    def spread(v, j):
        return jnp.broadcast_to(v[j : j + 1], (ROWS, LANES))

    centre = spread(total[0], 1) / spread(total[0], 0)
    wide = jnp.concatenate([centre, centre], 0)
    mu = [spread(total[0], 0)]
    for _ in range(2 * STEPS):
        step = times(wide, total)
        total = join(tuple(pltpu.roll(v, 2 * ROWS - 1, 0) for v in total), (-step[0], -step[1]))
        mu.append(spread(total[0], 0))

    def plus(a, b):
        n = max(len(a), len(b))
        return [a[i] + b[i] if i < min(len(a), len(b)) else (a[i] if i < len(a) else b[i]) for i in range(n)]

    def scaled(s, a):
        return [s * x for x in a]

    def operator(a):
        return plus([centre * x for x in a], [jnp.zeros_like(centre)] + a)

    def dot(a, b):
        square = [None] * (len(a) + len(b) - 1)
        for i, x in enumerate(a):
            for j, y in enumerate(b):
                z = x * y
                square[i + j] = z if square[i + j] is None else square[i + j] + z
        value = square[0] * mu[0]
        for n in range(1, len(square)):
            value = value + square[n] * mu[n]
        return value

    one = jnp.ones_like(centre)
    right = [one]
    quasi, search, update, iterate = right, right, [], []
    applied = operator(search)
    carried = applied
    rho = mu[0]
    tau_sq = rho
    alpha = theta_sq = eta = None
    for half in range(STEPS):
        if half % 2 == 0:
            alpha = rho / dot(carried, right)
            search_next = plus(search, scaled(-alpha, carried))
        quasi = plus(quasi, scaled(-alpha, applied))
        if half:
            update = plus(search, scaled(theta_sq / alpha * eta, update))
        else:
            update = search
        theta_sq = dot(quasi, quasi) / tau_sq
        cosine_sq = 1.0 / (1.0 + theta_sq)
        tau_sq = tau_sq * theta_sq * cosine_sq
        eta = cosine_sq * alpha
        iterate = plus(iterate, scaled(eta, update))
        if half % 2 == 0:
            search = search_next
            applied = operator(search)
        elif half < STEPS - 1:
            rho_next = dot(quasi, right)
            beta = rho_next / rho
            search = plus(quasi, scaled(beta, search))
            applied_next = operator(search)
            carried = plus(applied_next, scaled(beta, plus(applied, scaled(beta, carried))))
            applied, rho = applied_next, rho_next
    powers = [iterate[-1]]
    for c in iterate[-2::-1]:
        powers = plus([c] + powers, scaled(-centre, powers))
    return powers


def final_kernel(rhs, power_1, power_2, power_3, power_4, edges, friction, ice, grounded, speed, *rest):
    *parts, iterate, residual, hessian = rest
    layers, tiles = rhs.shape[1], edges.shape[2]
    total = (parts[0][0], parts[0][1])
    for x in parts[1:]:
        total = join(total, (x[0], x[1]))
    factors = solve(total)
    powers = (power_1, power_2, power_3, power_4)
    wide = [jnp.concatenate([c, c], 1) for c in factors]
    rest = sum(wide[1:], wide[0])
    cover = ice[...].astype(jnp.float32)
    lane = lax.broadcasted_iota(jnp.int32, (ROWS, LANES), 1)

    def combined(vectors, weights):
        x = weights[1] * vectors[0]
        y = weights[0] * vectors[0]
        for t in range(1, STEPS):
            if t + 1 < STEPS:
                x = x + weights[t + 1] * vectors[t]
            y = y + weights[t] * vectors[t]
        return x, y

    for c in range(2):
        side = [combined([edges[t, c, n] for t in range(STEPS)], factors) for n in range(tiles)]
        for k in range(layers):
            at = k // tiles * SLOT
            halves = [
                combined([p[half, c, k, FIRST + HALO : FIRST + HALO + ROWS] for p in powers], factors)
                for half in (0, 1)
            ]
            inner = zip(*halves)
            patched = []
            for (head, tail), e in zip(inner, side[k % tiles]):
                head = jnp.where(lane < HALO, turned(e, -at - 20), head)
                tail = jnp.where(lane >= LANES - HALO, turned(e, 120 - at), tail)
                patched.append(jnp.concatenate([head, tail], 1))
            r = rhs[c, k]
            x, y = patched
            iterate[c, k] = jnp.where(cover > 0.0, wide[0] * r + x, rest * r)
            residual[c, k] = r - jnp.where(cover > 0.0, y, rest * r)
    weight = cover * (friction[...] * grounded[...].astype(jnp.float32))
    hessian[...] = weight * (speed[0] * iterate[0, 0] + speed[1] * iterate[1, 0])


def exchange(x, axis):
    count = lax.axis_size(axis)
    stride = 1
    rounds = []
    while stride < count:
        size = 4 if (count // stride) % 4 == 0 else 2
        rounds.append((stride, size))
        stride *= size
    for at, (stride, size) in enumerate(rounds):
        parts = [x]
        for turn in range(1, size):
            pairs = []
            for i in range(count):
                place = (i // stride) % size
                pairs.append((i, i + ((place ^ turn) - place) * stride))
            parts.append(lax.ppermute(x, axis, pairs))
        if at == len(rounds) - 1:
            return parts
        x = call(add_kernel, [x.shape])(*parts)[0]
    return [x]


def body(adjoint_rhs, viscosity, friction, ice_mask, grounded, basal_velocity):
    layers = viscosity.shape[0]
    inputs = (adjoint_rhs, viscosity, friction, ice_mask, grounded, basal_velocity)
    tile = (ROWS, LANES)
    strips = (2 * (layers + layers // 2 + 1),) + tile
    ribbons = ribbon_tiles(layers)
    packed = ((ribbons + 7) // 8,) + tile
    both = (2 * packed[0],) + tile
    *held, column_a, column_b, strip_a, strip_b = call(
        pack_kernel,
        [jax.ShapeDtypeStruct(x.shape, x.dtype) for x in inputs] + [packed, packed, strips, strips],
        [pltpu.SemaphoreType.DMA((len(inputs),))],
        in_specs=[pl.BlockSpec(memory_space=pltpu.HBM)] * len(inputs),
    )(*[pltpu.with_memory_space_constraint(x, pltpu.HBM) for x in inputs])
    strip_b, strip_a = swapped(strip_b, ("gx",), 1, "parts"), swapped(strip_a, ("gx",), 0)
    beside = ("gy", "gz")
    (columns,) = call(beside_kernel, [both])(swapped(column_a, beside, 0), swapped(column_b, beside, 1))
    columns_b, columns_a = swapped(columns, ("gx",), 1, "gy"), swapped(columns, ("gx",), 0)
    block = (layers, 2 * ROWS, LANES)
    inorder = (2, 2, layers, 3 * ROWS, LANES)
    *powers, sums, ribbon = call(
        main_kernel,
        [inorder] * STEPS + [(2 * STEPS + 1, ROWS, 2 * LANES), (ribbons, 2 * ROWS, LANES)],
        [(2, 3 * layers + 2, 3 * ROWS, LANES)] + [(2, 2) + block] * 2 + [(2,) + block] * 4 + [(2,) + block[1:]],
        cost_estimate=pl.CostEstimate(flops=200_000_000, bytes_accessed=8_000_000, transcendentals=0),
    )(*held[:5], strip_b, strip_a)
    edges, sums = call(
        ribbon_kernel,
        [(STEPS, 2, layers // 4) + tile, (2, 2 * ROWS, LANES)],
    )(ribbon, columns, columns_b, columns_a, sums)
    parts = exchange(sums, ("gy", "gz"))
    if len(parts) > 1:
        sums = call(add_kernel, [sums.shape])(*parts)[0]
    parts = exchange(sums, "gx")
    rhs, _, friction, ice_mask, grounded, speed = held
    return tuple(
        call(final_kernel, [adjoint_rhs.shape, adjoint_rhs.shape, friction.shape])(
            rhs, *powers, edges, friction, ice_mask, grounded, speed, *parts
        )
    )


def solution(mesh):
    in_specs = (
        P(None, None, ("parts", "gx"), ("gy", "gz")),
        P(None, ("parts", "gx"), ("gy", "gz")),
        P(("parts", "gx"), ("gy", "gz")),
        P(("parts", "gx"), ("gy", "gz")),
        P(("parts", "gx"), ("gy", "gz")),
        P(None, ("parts", "gx"), ("gy", "gz")),
    )
    out_specs = (
        P(None, None, ("parts", "gx"), ("gy", "gz")),
        P(None, None, ("parts", "gx"), ("gy", "gz")),
        P(("parts", "gx"), ("gy", "gz")),
    )
    return jax.shard_map(body, mesh=mesh, in_specs=in_specs, out_specs=out_specs, check_vma=False)
```

```python
import functools

import jax
import jax.numpy as jnp
from jax import lax
from jax.experimental import pallas as pl
from jax.experimental.pallas import tpu as pltpu
from jax.sharding import PartitionSpec as P

STEPS = 4
HALO = 4
ROWS = 8
LANES = 128
UNROLL = 5
SLOT = 32


def call(kernel, outs, scratch=(), **more):
    return pl.pallas_call(
        kernel,
        out_shape=[jax.ShapeDtypeStruct(s, jnp.float32) if isinstance(s, tuple) else s for s in outs],
        scratch_shapes=[pltpu.VMEM(s, jnp.float32) if isinstance(s, tuple) else s for s in scratch],
        compiler_params=pltpu.CompilerParams(vmem_limit_bytes=40 * 1024 * 1024),
        **more,
    )


def place_of(axis):
    place, count = lax.axis_index(axis), lax.axis_size(axis)
    even = place % 2 == 0
    has_a = jnp.logical_or(jnp.logical_not(even), place < count - 1)
    has_b = jnp.where(even, place > 0, place < count - 1)
    return even, has_a, has_b


def swapped(x, axes, first, spare=None):
    count, others = lax.axis_size(axes), lax.axis_size(spare) if spare else 1
    pairs = []
    for at in range(others):
        for i in range(count):
            other, to = (i + 1 if (i - first) % 2 == 0 else i - 1), at
            if not 0 <= other < count:
                other, to = (i, at ^ 1) if spare else (count - 1 - i, at)
                if to >= others or count % 2:
                    other, to = i, at
            if spare == "parts":
                pairs.append((at * count + i, to * count + other))
            else:
                pairs.append((i * others + at, other * others + to))
    names = axes if not spare else ("parts", *axes) if spare == "parts" else (*axes, spare)
    return lax.ppermute(x, names, pairs)


def own_planes(rhs, eta, friction, ice, grounded):
    layers = eta.shape[0]
    cover = ice[...].astype(jnp.float32)
    drag = friction[...] * grounded[...].astype(jnp.float32)

    def plane(p):
        if p < 2 * layers:
            return rhs[p // layers, p % layers] * cover
        if p < 3 * layers:
            return eta[p - 2 * layers]
        return cover if p == 3 * layers else drag

    return plane


def pair_of(q, layers):
    if q < layers:
        return q, q + layers
    if q < layers + layers // 2:
        return q + layers, q + layers + layers // 2
    return 3 * layers, 3 * layers + 1


def ribbon_places(p, layers):
    tiles = layers // 4
    if p < 3 * layers:
        k = p % layers
        return p // layers * tiles + k % tiles, (k // tiles,)
    return (3 * tiles, (0, 1, 2, 3)) if p == 3 * layers else (3 * tiles + 1, (0,))


def ribbon_tiles(layers):
    return 3 * (layers // 4) + 2


def packed_place(tile):
    return tile // 8, HALO * (tile % 8)


def between(lane, first, width):
    return (lane >= first) & (lane < first + width)


def turned(v, shift):
    shift = shift % LANES
    return pltpu.roll(v, shift, 1) if shift else v


def strip_kernel(*refs):
    sources, held, (strip_a, strip_b, arrived) = refs[:6], refs[6:12], refs[12:]
    copies = [pltpu.make_async_copy(a, b, arrived.at[i]) for i, (a, b) in enumerate(zip(sources, held))]
    for copy in copies:
        copy.start()
    for copy in copies:
        copy.wait()
    rhs, eta, friction, ice, grounded, _ = held
    layers = eta.shape[0]
    plane = own_planes(rhs, eta, friction, ice, grounded)
    even, _, _ = place_of("gx")
    upper_a = (lax.broadcasted_iota(jnp.int32, (ROWS, LANES), 0) < HALO) != even
    for q in range(strip_a.shape[0] // 2):
        first, second = pair_of(q, layers)
        x, y = plane(first), plane(second)
        for half in range(2):
            xs = x[:, half * LANES : (half + 1) * LANES]
            ys = y[:, half * LANES : (half + 1) * LANES]
            ys = pltpu.roll(ys, HALO, 0)
            strip_a[2 * q + half] = jnp.where(upper_a, xs, ys)
            strip_b[2 * q + half] = jnp.where(upper_a, ys, xs)


def column_kernel(rhs, eta, friction, ice, grounded, column_a, column_b):
    layers = eta.shape[0]
    plane = own_planes(rhs, eta, friction, ice, grounded)
    lane = lax.broadcasted_iota(jnp.int32, (ROWS, LANES), 1)
    even, _, _ = place_of(("gy", "gz"))
    zero = jnp.zeros((ROWS, LANES), jnp.float32)
    to_left, to_right = [zero] * column_a.shape[0], [zero] * column_a.shape[0]
    for p in range(3 * layers + 2):
        v = plane(p)
        tile, slots = ribbon_places(p, layers)
        group, at = packed_place(tile)
        for slot in slots:
            here = between(lane, slot * SLOT + at, HALO)
            to_left[group] = jnp.where(here, turned(v[:, :LANES], slot * SLOT + at), to_left[group])
            to_right[group] = jnp.where(here, turned(v[:, LANES:], slot * SLOT + at + HALO), to_right[group])
    for group in range(column_a.shape[0]):
        column_a[group] = jnp.where(even, to_right[group], to_left[group])
        column_b[group] = jnp.where(even, to_left[group], to_right[group])


def beside_kernel(from_a, from_b, columns):
    even, has_a, has_b = place_of(("gy", "gz"))
    count = from_a.shape[0]
    for group in range(count):
        a = jnp.where(has_a, from_a[group], 0.0)
        b = jnp.where(has_b, from_b[group], 0.0)
        columns[group] = jnp.where(even, a, b)
        columns[count + group] = jnp.where(even, b, a)


def two_sum(a, b):
    s = a + b
    t = s - a
    return s, (a - (s - t)) + (b - t)


def join(x, y):
    s, e = two_sum(x[0], y[0])
    return s, e + (x[1] + y[1])


def cut(v, bits):
    t = v * (2.0**bits + 1.0)
    h = t - (t - v)
    return h, v - h


def times(scalar, x):
    high, low = cut(x[0], 12)
    return scalar * high, scalar * low + scalar * x[1]


def beyond():
    even, has_a, has_b = place_of("gx")
    upper_a = (lax.broadcasted_iota(jnp.int32, (ROWS, LANES), 0) < HALO) == even

    def below_and_above(from_a, from_b):
        return jnp.where(upper_a, jnp.where(has_a, from_a, 0.0), jnp.where(has_b, from_b, 0.0))

    def above_and_below(from_a, from_b):
        return jnp.where(upper_a, jnp.where(has_b, from_b, 0.0), jnp.where(has_a, from_a, 0.0))

    return below_and_above, above_and_below


def row_next(v):
    return pltpu.roll(v, 2 * ROWS - 1, 0)


def row_prev(v):
    return pltpu.roll(v, 1, 0)


def col_next(v):
    return pltpu.roll(v, v.shape[1] - 1, 1)


def col_prev(v):
    return pltpu.roll(v, 1, 1)


class Tiles:
    def __init__(self, tiles):
        self.tiles = tiles

    @staticmethod
    def load(ref):
        return Tiles([ref[r : r + ROWS, c : c + LANES] for r in (0, ROWS) for c in (0, LANES)])

    def store(self, ref):
        for v, (r, c) in zip(self.tiles, ((0, 0), (0, LANES), (ROWS, 0), (ROWS, LANES))):
            ref[r : r + ROWS, c : c + LANES] = v

    def both(self, other, op):
        if isinstance(other, Tiles):
            return Tiles([op(x, y) for x, y in zip(self.tiles, other.tiles)])
        return Tiles([op(x, other) for x in self.tiles])

    def __add__(self, other):
        return self.both(other, lambda x, y: x + y)

    def __sub__(self, other):
        return self.both(other, lambda x, y: x - y)

    def __mul__(self, other):
        return self.both(other, lambda x, y: x * y)

    __rmul__ = __mul__


class Moves:
    def __init__(self):
        row = lax.broadcasted_iota(jnp.int32, (ROWS, LANES), 0)
        lane = lax.broadcasted_iota(jnp.int32, (ROWS, LANES), 1)
        self.first_row, self.last_row = row == 0, row == ROWS - 1
        self.first_lane, self.last_lane = lane == 0, lane == LANES - 1

    def rows(self, v, shift, edge):
        own0, own1, halo0, halo1 = [pltpu.roll(x, shift, 0) for x in v.tiles]
        return Tiles(
            [
                jnp.where(edge, halo0, own0),
                jnp.where(edge, halo1, own1),
                jnp.where(edge, own0, halo0),
                jnp.where(edge, own1, halo1),
            ]
        )

    def row_next(self, v):
        return self.rows(v, ROWS - 1, self.last_row)

    def row_prev(self, v):
        return self.rows(v, 1, self.first_row)

    def col_next(self, v):
        own0, own1, halo0, halo1 = [pltpu.roll(x, LANES - 1, 1) for x in v.tiles]
        return Tiles([jnp.where(self.last_lane, own1, own0), own1, jnp.where(self.last_lane, halo1, halo0), halo1])

    def col_prev(self, v):
        own0, own1, halo0, halo1 = [pltpu.roll(x, 1, 1) for x in v.tiles]
        return Tiles([own0, jnp.where(self.first_lane, own0, own1), halo0, jnp.where(self.first_lane, halo0, halo1)])


class Turns:
    row_next = staticmethod(row_next)
    row_prev = staticmethod(row_prev)
    col_next = staticmethod(col_next)
    col_prev = staticmethod(col_prev)


def horizontal(g0, g1, e_row, e_row_1, e_col, e_col_1, e_half, moves):
    row_next, row_prev, col_next, col_prev = moves.row_next, moves.row_prev, moves.col_next, moves.col_prev
    g0n, g1n = row_next(g0), col_next(g1)
    f = e_half * (g1n - col_prev(g1))
    h = e_half * (g0n - row_prev(g0))
    flux = e_row * (g0 - g0n)
    out0 = flux - row_next(f) - row_prev(flux - f)
    flux = e_col * (g0 - col_next(g0))
    out0 = out0 + (flux - col_prev(flux))
    flux = e_col_1 * (g1 - g1n)
    out1 = flux - col_next(h) - col_prev(flux - h)
    flux = e_row_1 * (g1 - row_next(g1))
    out1 = out1 + (flux - row_prev(flux))
    return out0, out1


def main_kernel(
    rhs, eta, friction, ice, grounded, strip_a, strip_b,
    power_1, power_2, power_3, power_4, sums, ribbon,
    masked, eta_row, eta_col, eta_half, eta_up, cover, drag,
):
    layers = eta.shape[0]
    plane = own_planes(rhs, eta, friction, ice, grounded)
    below_and_above, above_and_below = beyond()
    lane = lax.broadcasted_iota(jnp.int32, (2 * ROWS, LANES), 1)

    def target(p):
        if p < 2 * layers:
            return masked.at[p // layers, p % layers]
        if p < 3 * layers:
            return eta_half.at[p - 2 * layers]
        return cover if p == 3 * layers else drag

    strips = [jnp.zeros((2 * ROWS, LANES), jnp.float32) for _ in range(ribbon.shape[0])]
    for q in range(strip_a.shape[0] // 2):
        first, second = pair_of(q, layers)
        halves = ([], [])
        for half in range(2):
            from_a, from_b = strip_a[2 * q + half], strip_b[2 * q + half]
            halves[0].append(below_and_above(from_a, from_b))
            halves[1].append(pltpu.roll(above_and_below(from_a, from_b), HALO, 0))
        for p, halo in zip((first, second), halves):
            v = plane(p)
            dst = target(p)
            dst[0:ROWS, :] = v
            dst[ROWS:, 0:LANES], dst[ROWS:, LANES:] = halo
            head = jnp.concatenate([v[:, :LANES], halo[0]], 0)
            tail = jnp.concatenate([v[:, LANES:], halo[1]], 0)
            tile, slots = ribbon_places(p, layers)
            for slot in slots:
                at = slot * SLOT
                strips[tile] = jnp.where(between(lane, at, 8), turned(tail, at + 8), strips[tile])
                strips[tile] = jnp.where(between(lane, at + 20, 8), turned(head, at + 20), strips[tile])
    for tile, v in enumerate(strips):
        ribbon[tile] = v

    moves = Moves()
    load = Tiles.load
    for k in range(layers):
        e = load(eta_half.at[k])
        pair = e + moves.row_next(e)
        (2.0 * pair).store(eta_row.at[0, k])
        (0.5 * pair).store(eta_row.at[1, k])
        pair = e + moves.col_next(e)
        (0.5 * pair).store(eta_col.at[0, k])
        (2.0 * pair).store(eta_col.at[1, k])
        eta_up[k] = eta_half[k] + eta_half[k + 1] if k + 1 < layers else jnp.zeros_like(eta_up[k])
        if k:
            eta_half[k - 1] = 0.5 * eta_half[k - 1]
    eta_half[layers - 1] = 0.5 * eta_half[layers - 1]

    def apply(t, src, dst):
        def block(b, carry):
            g0, g1, below0, below1, odd, even = carry
            g0, g1, below0, below1 = Tiles(g0), Tiles(g1), Tiles(below0), Tiles(below1)
            odd, even = list(odd), list(even)
            m = load(cover)
            for i in range(UNROLL):
                k = b * UNROLL + i
                after = k + 1 if i + 1 < UNROLL else jnp.minimum(k + 1, layers - 1)
                next0, next1 = load(src.at[0, after]), load(src.at[1, after])
                e_up = load(eta_up.at[k])
                up0, up1 = e_up * (g0 - next0), e_up * (g1 - next1)
                pairs = [load(ref.at[c, k]) for ref in (eta_row, eta_col) for c in range(2)]
                out0, out1 = horizontal(g0, g1, *pairs, load(eta_half.at[k]), moves)
                out0, out1 = m * (out0 + (up0 - below0)), m * (out1 + (up1 - below1))
                for c, g, out in ((0, g0, out0), (1, g1, out1)):
                    if t < STEPS:
                        out.store(dst.at[c, k])
                    for half in range(2):
                        now = out.tiles[half]
                        if t == STEPS:
                            dst[c, k, :, half * LANES : (half + 1) * LANES] = now
                        odd[half] = odd[half] + g.tiles[half] * now
                        even[half] = even[half] + now * now
                g0, g1, below0, below1 = next0, next1, up0, up1
            return g0.tiles, g1.tiles, below0.tiles, below1.tiles, odd, even

        zero = [jnp.zeros((ROWS, LANES), jnp.float32)] * 2
        d = -1.0 * load(drag)
        g0, g1 = load(src.at[0, 0]), load(src.at[1, 0])
        start = (g0.tiles, g1.tiles, (d * g0).tiles, (d * g1).tiles, zero, zero)
        ends = lax.fori_loop(0, layers // UNROLL, block, start)[4:]
        return [jnp.concatenate(v, 1) for v in ends]

    bare = 1.0 - ice[...].astype(jnp.float32)
    whole = jnp.zeros((ROWS, 2 * LANES), jnp.float32)
    outside = jnp.zeros((ROWS, 2 * LANES), jnp.float32)
    for c in range(2):
        for k in range(layers):
            square = rhs[c, k] * rhs[c, k]
            whole = whole + square
            outside = outside + bare * square
    sums[0] = whole
    wide = lax.broadcasted_iota(jnp.int32, (ROWS, 2 * LANES), 1)
    inner = between(wide, HALO, 2 * LANES - 2 * HALO)
    fields = (masked, power_1, power_2, power_3, power_4)
    for t in range(1, STEPS + 1):
        odd, even = apply(t, fields[t - 1], fields[t])
        sums[2 * t - 1] = jnp.where(inner, odd, 0.0) + outside
        sums[2 * t] = jnp.where(inner, even, 0.0) + outside


def ribbon_kernel(ribbon, columns, columns_b, columns_a, sums, edges, moments):
    tiles = edges.shape[2]
    below_and_above, _ = beyond()
    lane = lax.broadcasted_iota(jnp.int32, (2 * ROWS, LANES), 1)

    count = columns.shape[0] // 2
    beside = [
        jnp.concatenate([columns[i], below_and_above(columns_a[i], columns_b[i])], 0) for i in range(2 * count)
    ]
    spot = lane % SLOT

    def whole(tile):
        group, at = packed_place(tile)
        right = jnp.where(between(spot, 8, HALO), turned(beside[group], 8 - at), ribbon[tile])
        return jnp.where(between(spot, 16, HALO), turned(beside[count + group], 16 - at), right)

    field = [[whole(c * tiles + n) for n in range(tiles)] for c in range(2)]
    eta = [whole(2 * tiles + n) for n in range(tiles)]
    cover, drag = whole(3 * tiles), whole(3 * tiles + 1)

    def after(v):
        return v[1:] + [turned(v[0], -SLOT)]

    eta_row = [2.0 * (e + row_next(e)) for e in eta]
    eta_col = [0.5 * (e + col_next(e)) for e in eta]
    eta_row_1, eta_col_1 = [0.25 * e for e in eta_row], [4.0 * e for e in eta_col]
    eta_half = [0.5 * e for e in eta]
    eta_up = [e + n for e, n in zip(eta, after(eta))]
    eta_up[-1] = jnp.where(lane < LANES - SLOT, eta_up[-1], 0.0)
    place = lax.broadcasted_iota(jnp.int32, (ROWS, LANES), 1) % SLOT
    edge = between(place, 4, HALO) | between(place, 20, HALO)
    extra = [None]
    for t in range(1, STEPS + 1):
        ups = [[u * (g - n) for u, g, n in zip(eta_up, field[c], after(field[c]))] for c in range(2)]
        result = ([], [])
        odd = even = jnp.zeros((ROWS, LANES), jnp.float32)
        for n in range(tiles):
            coefficients = (eta_row[n], eta_row_1[n], eta_col[n], eta_col_1[n], eta_half[n])
            outs = horizontal(field[0][n], field[1][n], *coefficients, Turns)
            for c in range(2):
                below = ups[c][n - 1] if n else turned(ups[c][-1], SLOT) - drag * field[c][0]
                out = cover * (outs[c] + (ups[c][n] - below))
                result[c].append(out)
                now = out[:ROWS]
                edges[t - 1, c, n] = now
                odd = odd + field[c][n][:ROWS] * now
                even = even + now * now
        field = result
        extra.extend([jnp.where(edge, odd, 0.0), jnp.where(edge, even, 0.0)])

    tall = lax.broadcasted_iota(jnp.int32, (2 * ROWS, LANES), 0)
    high = jnp.zeros((2 * ROWS, LANES), jnp.float32)
    low = jnp.zeros((2 * ROWS, LANES), jnp.float32)
    for j, more in enumerate(extra):
        total = sums[j]
        pair = two_sum(total[:, :LANES], total[:, LANES:])
        if more is not None:
            pair = join(pair, (more, jnp.zeros_like(more)))
        for step in (4, 2, 1):
            pair = join(pair, tuple(pltpu.roll(v, step, 0) for v in pair))
        high = jnp.where(tall == j, jnp.concatenate([pair[0]] * 2, 0), high)
        low = jnp.where(tall == j, jnp.concatenate([pair[1]] * 2, 0), low)
    moments[0] = high
    moments[1] = low


def add_kernel(*refs):
    *ins, out = refs
    total = (ins[0][0], ins[0][1])
    for x in ins[1:]:
        total = join(total, (x[0], x[1]))
    out[0], out[1] = total


def solve(total):
    for step in (64, 32, 16, 8, 4, 2, 1):
        total = join(total, tuple(pltpu.roll(v, step, 1) for v in total))

    def spread(v, j):
        return jnp.broadcast_to(v[j : j + 1], (ROWS, LANES))

    centre, _ = cut(spread(total[0], 1) / spread(total[0], 0), 13)
    wide = jnp.concatenate([centre, centre], 0)
    mu = [spread(total[0] + total[1], 0)]
    for _ in range(2 * STEPS):
        step = times(wide, total)
        total = join(tuple(pltpu.roll(v, 2 * ROWS - 1, 0) for v in total), (-step[0], -step[1]))
        mu.append(spread(total[0] + total[1], 0))

    def plus(a, b):
        n = max(len(a), len(b))
        return [a[i] + b[i] if i < min(len(a), len(b)) else (a[i] if i < len(a) else b[i]) for i in range(n)]

    def scaled(s, a):
        return [s * x for x in a]

    def operator(a):
        return plus([centre * x for x in a], [jnp.zeros_like(centre)] + a)

    def dot(a, b):
        square = [None] * (len(a) + len(b) - 1)
        for i, x in enumerate(a):
            for j, y in enumerate(b):
                z = x * y
                square[i + j] = z if square[i + j] is None else square[i + j] + z
        value = square[0] * mu[0]
        for n in range(1, len(square)):
            value = value + square[n] * mu[n]
        return value

    one = jnp.ones_like(centre)
    right = [one]
    quasi, search, update, iterate = right, right, [], []
    applied = operator(search)
    carried = applied
    rho = mu[0]
    tau_sq = rho
    alpha = theta_sq = eta = None
    for half in range(STEPS):
        if half % 2 == 0:
            alpha = rho / dot(carried, right)
            search_next = plus(search, scaled(-alpha, carried))
        quasi = plus(quasi, scaled(-alpha, applied))
        if half:
            update = plus(search, scaled(theta_sq / alpha * eta, update))
        else:
            update = search
        theta_sq = dot(quasi, quasi) / tau_sq
        cosine_sq = 1.0 / (1.0 + theta_sq)
        tau_sq = tau_sq * theta_sq * cosine_sq
        eta = cosine_sq * alpha
        iterate = plus(iterate, scaled(eta, update))
        if half % 2 == 0:
            search = search_next
            applied = operator(search)
        elif half < STEPS - 1:
            rho_next = dot(quasi, right)
            beta = rho_next / rho
            search = plus(quasi, scaled(beta, search))
            applied_next = operator(search)
            carried = plus(applied_next, scaled(beta, plus(applied, scaled(beta, carried))))
            applied, rho = applied_next, rho_next
    powers = [iterate[-1]]
    for c in iterate[-2::-1]:
        powers = plus([c] + powers, scaled(-centre, powers))
    return powers


def final_kernel(rhs, power_1, power_2, power_3, power_4, edges, friction, ice, grounded, speed, *rest):
    *parts, iterate, residual, hessian = rest
    layers, tiles = rhs.shape[1], edges.shape[2]
    total = (parts[0][0], parts[0][1])
    for x in parts[1:]:
        total = join(total, (x[0], x[1]))
    factors = solve(total)
    powers = (power_1, power_2, power_3, power_4)
    wide = [jnp.concatenate([c, c], 1) for c in factors]
    rest = sum(wide[1:], wide[0])
    cover = ice[...].astype(jnp.float32)
    lane = lax.broadcasted_iota(jnp.int32, (ROWS, LANES), 1)

    def combined(vectors, weights):
        x = weights[1] * vectors[0]
        y = weights[0] * vectors[0]
        for t in range(1, STEPS):
            if t + 1 < STEPS:
                x = x + weights[t + 1] * vectors[t]
            y = y + weights[t] * vectors[t]
        return x, y

    for c in range(2):
        side = [combined([edges[t, c, n] for t in range(STEPS)], factors) for n in range(tiles)]
        for k in range(layers):
            at = k // tiles * SLOT
            inner = combined([p[c, k, :ROWS] for p in powers], wide)
            patched = []
            for v, e in zip(inner, side[k % tiles]):
                head = jnp.where(lane < HALO, turned(e, -at - 20), v[:, :LANES])
                tail = jnp.where(lane >= LANES - HALO, turned(e, 120 - at), v[:, LANES:])
                patched.append(jnp.concatenate([head, tail], 1))
            r = rhs[c, k]
            x, y = patched
            iterate[c, k] = jnp.where(cover > 0.0, wide[0] * r + x, rest * r)
            residual[c, k] = r - jnp.where(cover > 0.0, y, rest * r)
    weight = cover * (friction[...] * grounded[...].astype(jnp.float32))
    hessian[...] = weight * (speed[0] * iterate[0, 0] + speed[1] * iterate[1, 0])


def exchange(x, axis):
    count = lax.axis_size(axis)
    stride = 1
    rounds = []
    while stride < count:
        size = 4 if (count // stride) % 4 == 0 else 2
        rounds.append((stride, size))
        stride *= size
    for at, (stride, size) in enumerate(rounds):
        parts = [x]
        for turn in range(1, size):
            pairs = []
            for i in range(count):
                place = (i // stride) % size
                pairs.append((i, i + ((place ^ turn) - place) * stride))
            parts.append(lax.ppermute(x, axis, pairs))
        if at == len(rounds) - 1:
            return parts
        x = call(add_kernel, [x.shape])(*parts)[0]
    return [x]


def body(adjoint_rhs, viscosity, friction, ice_mask, grounded, basal_velocity):
    layers = viscosity.shape[0]
    inputs = (adjoint_rhs, viscosity, friction, ice_mask, grounded, basal_velocity)
    tile = (ROWS, LANES)
    strips = (2 * (layers + layers // 2 + 1),) + tile
    ribbons = ribbon_tiles(layers)
    packed = ((ribbons + 7) // 8,) + tile
    both = (2 * packed[0],) + tile
    *held, strip_a, strip_b = call(
        strip_kernel,
        [jax.ShapeDtypeStruct(x.shape, x.dtype) for x in inputs] + [strips, strips],
        [pltpu.SemaphoreType.DMA((len(inputs),))],
        in_specs=[pl.BlockSpec(memory_space=pltpu.HBM)] * len(inputs),
    )(*[pltpu.with_memory_space_constraint(x, pltpu.HBM) for x in inputs])
    strip_a, strip_b = swapped(strip_a, ("gx",), 0), swapped(strip_b, ("gx",), 1, "parts")
    column_a, column_b = call(column_kernel, [packed, packed])(*held[:5])
    beside = ("gy", "gz")
    (columns,) = call(beside_kernel, [both])(swapped(column_a, beside, 0), swapped(column_b, beside, 1))
    columns_b, columns_a = swapped(columns, ("gx",), 1, "gy"), swapped(columns, ("gx",), 0)
    block = (layers, 2 * ROWS, 2 * LANES)
    *powers, sums, ribbon = call(
        main_kernel,
        [(2,) + block] * (STEPS - 1) + [adjoint_rhs.shape, (2 * STEPS + 1, ROWS, 2 * LANES), (ribbons, 2 * ROWS, LANES)],
        [(2,) + block] * 3 + [block] * 2 + [block[1:]] * 2,
        cost_estimate=pl.CostEstimate(flops=200_000_000, bytes_accessed=8_000_000, transcendentals=0),
    )(*held[:5], strip_a, strip_b)
    edges, sums = call(
        ribbon_kernel,
        [(STEPS, 2, layers // 4) + tile, (2, 2 * ROWS, LANES)],
    )(ribbon, columns, columns_b, columns_a, sums)
    parts = exchange(sums, ("gy", "gz"))
    if len(parts) > 1:
        sums = call(add_kernel, [sums.shape])(*parts)[0]
    parts = exchange(sums, "gx")
    rhs, _, friction, ice_mask, grounded, speed = held
    return tuple(
        call(final_kernel, [adjoint_rhs.shape, adjoint_rhs.shape, friction.shape])(
            rhs, *powers, edges, friction, ice_mask, grounded, speed, *parts
        )
    )


def solution(mesh):
    in_specs = (
        P(None, None, ("parts", "gx"), ("gy", "gz")),
        P(None, ("parts", "gx"), ("gy", "gz")),
        P(("parts", "gx"), ("gy", "gz")),
        P(("parts", "gx"), ("gy", "gz")),
        P(("parts", "gx"), ("gy", "gz")),
        P(None, ("parts", "gx"), ("gy", "gz")),
    )
    out_specs = (
        P(None, None, ("parts", "gx"), ("gy", "gz")),
        P(None, None, ("parts", "gx"), ("gy", "gz")),
        P(("parts", "gx"), ("gy", "gz")),
    )
    return jax.shard_map(body, mesh=mesh, in_specs=in_specs, out_specs=out_specs, check_vma=False)
```

```python
import functools

import jax
import jax.numpy as jnp
from jax import lax
from jax.experimental import pallas as pl
from jax.experimental.pallas import tpu as pltpu
from jax.sharding import PartitionSpec as P

STEPS = 4
HALO = 4
ROWS = 8
LANES = 128
UNROLL = 5
SLOT = 32


def call(kernel, outs, scratch=(), **more):
    return pl.pallas_call(
        kernel,
        out_shape=[jax.ShapeDtypeStruct(s, jnp.float32) if isinstance(s, tuple) else s for s in outs],
        scratch_shapes=[pltpu.VMEM(s, jnp.float32) if isinstance(s, tuple) else s for s in scratch],
        compiler_params=pltpu.CompilerParams(vmem_limit_bytes=40 * 1024 * 1024),
        **more,
    )


def place_of(axis):
    place, count = lax.axis_index(axis), lax.axis_size(axis)
    even = place % 2 == 0
    has_a = jnp.logical_or(jnp.logical_not(even), place < count - 1)
    has_b = jnp.where(even, place > 0, place < count - 1)
    return even, has_a, has_b


def swapped(x, axes, first, spare=None):
    count, others = lax.axis_size(axes), lax.axis_size(spare) if spare else 1
    pairs = []
    for at in range(others):
        for i in range(count):
            other, to = (i + 1 if (i - first) % 2 == 0 else i - 1), at
            if not 0 <= other < count:
                other, to = (i, at ^ 1) if spare else (count - 1 - i, at)
                if to >= others or count % 2:
                    other, to = i, at
            pairs.append((i * others + at, other * others + to))
    return lax.ppermute(x, (*axes, spare) if spare else axes, pairs)


def own_planes(rhs, eta, friction, ice, grounded):
    layers = eta.shape[0]
    cover = ice[...].astype(jnp.float32)
    drag = friction[...] * grounded[...].astype(jnp.float32)

    def plane(p):
        if p < 2 * layers:
            return rhs[p // layers, p % layers] * cover
        if p < 3 * layers:
            return eta[p - 2 * layers]
        return cover if p == 3 * layers else drag

    return plane


def pair_of(q, layers):
    if q < layers:
        return q, q + layers
    if q < layers + layers // 2:
        return q + layers, q + layers + layers // 2
    return 3 * layers, 3 * layers + 1


def ribbon_places(p, layers):
    tiles = layers // 4
    if p < 3 * layers:
        k = p % layers
        return p // layers * tiles + k % tiles, (k // tiles,)
    return (3 * tiles, (0, 1, 2, 3)) if p == 3 * layers else (3 * tiles + 1, (0,))


def ribbon_tiles(layers):
    return 3 * (layers // 4) + 2


def packed_place(tile):
    return tile // 8, HALO * (tile % 8)


def between(lane, first, width):
    return (lane >= first) & (lane < first + width)


def turned(v, shift):
    shift = shift % LANES
    return pltpu.roll(v, shift, 1) if shift else v


def strip_kernel(*refs):
    sources, held, (strip_a, strip_b, arrived) = refs[:6], refs[6:12], refs[12:]
    copies = [pltpu.make_async_copy(a, b, arrived.at[i]) for i, (a, b) in enumerate(zip(sources, held))]
    for copy in copies:
        copy.start()
    for copy in copies:
        copy.wait()
    rhs, eta, friction, ice, grounded, _ = held
    layers = eta.shape[0]
    plane = own_planes(rhs, eta, friction, ice, grounded)
    even, _, _ = place_of("gx")
    upper_a = (lax.broadcasted_iota(jnp.int32, (ROWS, LANES), 0) < HALO) != even
    for q in range(strip_a.shape[0] // 2):
        first, second = pair_of(q, layers)
        x, y = plane(first), plane(second)
        for half in range(2):
            xs = x[:, half * LANES : (half + 1) * LANES]
            ys = y[:, half * LANES : (half + 1) * LANES]
            ys = pltpu.roll(ys, HALO, 0)
            strip_a[2 * q + half] = jnp.where(upper_a, xs, ys)
            strip_b[2 * q + half] = jnp.where(upper_a, ys, xs)


def column_kernel(rhs, eta, friction, ice, grounded, column_a, column_b):
    layers = eta.shape[0]
    plane = own_planes(rhs, eta, friction, ice, grounded)
    lane = lax.broadcasted_iota(jnp.int32, (ROWS, LANES), 1)
    even, _, _ = place_of(("gy", "gz"))
    zero = jnp.zeros((ROWS, LANES), jnp.float32)
    to_left, to_right = [zero] * column_a.shape[0], [zero] * column_a.shape[0]
    for p in range(3 * layers + 2):
        v = plane(p)
        tile, slots = ribbon_places(p, layers)
        group, at = packed_place(tile)
        for slot in slots:
            here = between(lane, slot * SLOT + at, HALO)
            to_left[group] = jnp.where(here, turned(v[:, :LANES], slot * SLOT + at), to_left[group])
            to_right[group] = jnp.where(here, turned(v[:, LANES:], slot * SLOT + at + HALO), to_right[group])
    for group in range(column_a.shape[0]):
        column_a[group] = jnp.where(even, to_right[group], to_left[group])
        column_b[group] = jnp.where(even, to_left[group], to_right[group])


def beside_kernel(from_a, from_b, columns):
    even, has_a, has_b = place_of(("gy", "gz"))
    count = from_a.shape[0]
    for group in range(count):
        a = jnp.where(has_a, from_a[group], 0.0)
        b = jnp.where(has_b, from_b[group], 0.0)
        columns[group] = jnp.where(even, a, b)
        columns[count + group] = jnp.where(even, b, a)


def two_sum(a, b):
    s = a + b
    t = s - a
    return s, (a - (s - t)) + (b - t)


def join(x, y):
    s, e = two_sum(x[0], y[0])
    return s, e + (x[1] + y[1])


def cut(v, bits):
    t = v * (2.0**bits + 1.0)
    h = t - (t - v)
    return h, v - h


def times(scalar, x):
    high, low = cut(x[0], 12)
    return scalar * high, scalar * low + scalar * x[1]


def beyond():
    even, has_a, has_b = place_of("gx")
    upper_a = (lax.broadcasted_iota(jnp.int32, (ROWS, LANES), 0) < HALO) == even

    def below_and_above(from_a, from_b):
        return jnp.where(upper_a, jnp.where(has_a, from_a, 0.0), jnp.where(has_b, from_b, 0.0))

    def above_and_below(from_a, from_b):
        return jnp.where(upper_a, jnp.where(has_b, from_b, 0.0), jnp.where(has_a, from_a, 0.0))

    return below_and_above, above_and_below


def row_next(v):
    return pltpu.roll(v, 2 * ROWS - 1, 0)


def row_prev(v):
    return pltpu.roll(v, 1, 0)


def col_next(v):
    return pltpu.roll(v, v.shape[1] - 1, 1)


def col_prev(v):
    return pltpu.roll(v, 1, 1)


class Tiles:
    def __init__(self, tiles):
        self.tiles = tiles

    @staticmethod
    def load(ref):
        return Tiles([ref[r : r + ROWS, c : c + LANES] for r in (0, ROWS) for c in (0, LANES)])

    def store(self, ref):
        for v, (r, c) in zip(self.tiles, ((0, 0), (0, LANES), (ROWS, 0), (ROWS, LANES))):
            ref[r : r + ROWS, c : c + LANES] = v

    def both(self, other, op):
        if isinstance(other, Tiles):
            return Tiles([op(x, y) for x, y in zip(self.tiles, other.tiles)])
        return Tiles([op(x, other) for x in self.tiles])

    def __add__(self, other):
        return self.both(other, lambda x, y: x + y)

    def __sub__(self, other):
        return self.both(other, lambda x, y: x - y)

    def __mul__(self, other):
        return self.both(other, lambda x, y: x * y)

    __rmul__ = __mul__


class Moves:
    def __init__(self):
        row = lax.broadcasted_iota(jnp.int32, (ROWS, LANES), 0)
        lane = lax.broadcasted_iota(jnp.int32, (ROWS, LANES), 1)
        self.first_row, self.last_row = row == 0, row == ROWS - 1
        self.first_lane, self.last_lane = lane == 0, lane == LANES - 1

    def rows(self, v, shift, edge):
        own0, own1, halo0, halo1 = [pltpu.roll(x, shift, 0) for x in v.tiles]
        return Tiles(
            [
                jnp.where(edge, halo0, own0),
                jnp.where(edge, halo1, own1),
                jnp.where(edge, own0, halo0),
                jnp.where(edge, own1, halo1),
            ]
        )

    def row_next(self, v):
        return self.rows(v, ROWS - 1, self.last_row)

    def row_prev(self, v):
        return self.rows(v, 1, self.first_row)

    def col_next(self, v):
        own0, own1, halo0, halo1 = [pltpu.roll(x, LANES - 1, 1) for x in v.tiles]
        return Tiles([jnp.where(self.last_lane, own1, own0), own1, jnp.where(self.last_lane, halo1, halo0), halo1])

    def col_prev(self, v):
        own0, own1, halo0, halo1 = [pltpu.roll(x, 1, 1) for x in v.tiles]
        return Tiles([own0, jnp.where(self.first_lane, own0, own1), halo0, jnp.where(self.first_lane, halo0, halo1)])


class Turns:
    row_next = staticmethod(row_next)
    row_prev = staticmethod(row_prev)
    col_next = staticmethod(col_next)
    col_prev = staticmethod(col_prev)


def horizontal(g0, g1, e_row, e_row_1, e_col, e_col_1, e_half, moves):
    row_next, row_prev, col_next, col_prev = moves.row_next, moves.row_prev, moves.col_next, moves.col_prev
    g0n, g1n = row_next(g0), col_next(g1)
    f = e_half * (g1n - col_prev(g1))
    h = e_half * (g0n - row_prev(g0))
    flux = e_row * (g0 - g0n)
    out0 = flux - row_next(f) - row_prev(flux - f)
    flux = e_col * (g0 - col_next(g0))
    out0 = out0 + (flux - col_prev(flux))
    flux = e_col_1 * (g1 - g1n)
    out1 = flux - col_next(h) - col_prev(flux - h)
    flux = e_row_1 * (g1 - row_next(g1))
    out1 = out1 + (flux - row_prev(flux))
    return out0, out1


def main_kernel(
    rhs, eta, friction, ice, grounded, strip_b, strip_a,
    power_1, power_2, power_3, power_4, sums, ribbon,
    masked, eta_row, eta_col, eta_half, eta_up, cover, drag,
):
    layers = eta.shape[0]
    plane = own_planes(rhs, eta, friction, ice, grounded)
    below_and_above, above_and_below = beyond()
    lane = lax.broadcasted_iota(jnp.int32, (2 * ROWS, LANES), 1)

    def target(p):
        if p < 2 * layers:
            return masked.at[p // layers, p % layers]
        if p < 3 * layers:
            return eta_half.at[p - 2 * layers]
        return cover if p == 3 * layers else drag

    strips = [jnp.zeros((2 * ROWS, LANES), jnp.float32) for _ in range(ribbon.shape[0])]
    for q in range(strip_a.shape[0] // 2):
        first, second = pair_of(q, layers)
        halves = ([], [])
        for half in range(2):
            from_a, from_b = strip_a[2 * q + half], strip_b[2 * q + half]
            halves[0].append(below_and_above(from_a, from_b))
            halves[1].append(pltpu.roll(above_and_below(from_a, from_b), HALO, 0))
        for p, halo in zip((first, second), halves):
            v = plane(p)
            dst = target(p)
            dst[0:ROWS, :] = v
            dst[ROWS:, 0:LANES], dst[ROWS:, LANES:] = halo
            head = jnp.concatenate([v[:, :LANES], halo[0]], 0)
            tail = jnp.concatenate([v[:, LANES:], halo[1]], 0)
            tile, slots = ribbon_places(p, layers)
            for slot in slots:
                at = slot * SLOT
                strips[tile] = jnp.where(between(lane, at, 8), turned(tail, at + 8), strips[tile])
                strips[tile] = jnp.where(between(lane, at + 20, 8), turned(head, at + 20), strips[tile])
    for tile, v in enumerate(strips):
        ribbon[tile] = v

    moves = Moves()
    load = Tiles.load
    for k in range(layers):
        e = load(eta_half.at[k])
        pair = e + moves.row_next(e)
        (2.0 * pair).store(eta_row.at[0, k])
        (0.5 * pair).store(eta_row.at[1, k])
        pair = e + moves.col_next(e)
        (0.5 * pair).store(eta_col.at[0, k])
        (2.0 * pair).store(eta_col.at[1, k])
        eta_up[k] = eta_half[k] + eta_half[k + 1] if k + 1 < layers else jnp.zeros_like(eta_up[k])
        if k:
            eta_half[k - 1] = 0.5 * eta_half[k - 1]
    eta_half[layers - 1] = 0.5 * eta_half[layers - 1]

    def apply(t, src, dst):
        def block(b, carry):
            g0, g1, below0, below1, odd, even = carry
            g0, g1, below0, below1 = Tiles(g0), Tiles(g1), Tiles(below0), Tiles(below1)
            odd, even = list(odd), list(even)
            m = load(cover)
            for i in range(UNROLL):
                k = b * UNROLL + i
                after = k + 1 if i + 1 < UNROLL else jnp.minimum(k + 1, layers - 1)
                next0, next1 = load(src.at[0, after]), load(src.at[1, after])
                e_up = load(eta_up.at[k])
                up0, up1 = e_up * (g0 - next0), e_up * (g1 - next1)
                pairs = [load(ref.at[c, k]) for ref in (eta_row, eta_col) for c in range(2)]
                out0, out1 = horizontal(g0, g1, *pairs, load(eta_half.at[k]), moves)
                out0, out1 = m * (out0 + (up0 - below0)), m * (out1 + (up1 - below1))
                for c, g, out in ((0, g0, out0), (1, g1, out1)):
                    if t < STEPS:
                        out.store(dst.at[c, k])
                    for half in range(2):
                        now = out.tiles[half]
                        if t == STEPS:
                            dst[c, k, :, half * LANES : (half + 1) * LANES] = now
                        odd[half] = odd[half] + g.tiles[half] * now
                        even[half] = even[half] + now * now
                g0, g1, below0, below1 = next0, next1, up0, up1
            return g0.tiles, g1.tiles, below0.tiles, below1.tiles, odd, even

        zero = [jnp.zeros((ROWS, LANES), jnp.float32)] * 2
        d = -1.0 * load(drag)
        g0, g1 = load(src.at[0, 0]), load(src.at[1, 0])
        start = (g0.tiles, g1.tiles, (d * g0).tiles, (d * g1).tiles, zero, zero)
        ends = lax.fori_loop(0, layers // UNROLL, block, start)[4:]
        return [jnp.concatenate(v, 1) for v in ends]

    bare = 1.0 - ice[...].astype(jnp.float32)
    whole = jnp.zeros((ROWS, 2 * LANES), jnp.float32)
    outside = jnp.zeros((ROWS, 2 * LANES), jnp.float32)
    for c in range(2):
        for k in range(layers):
            square = rhs[c, k] * rhs[c, k]
            whole = whole + square
            outside = outside + bare * square
    sums[0] = whole
    wide = lax.broadcasted_iota(jnp.int32, (ROWS, 2 * LANES), 1)
    inner = between(wide, HALO, 2 * LANES - 2 * HALO)
    fields = (masked, power_1, power_2, power_3, power_4)
    for t in range(1, STEPS + 1):
        odd, even = apply(t, fields[t - 1], fields[t])
        sums[2 * t - 1] = jnp.where(inner, odd, 0.0) + outside
        sums[2 * t] = jnp.where(inner, even, 0.0) + outside


def ribbon_kernel(ribbon, columns, columns_b, columns_a, sums, edges, moments):
    tiles = edges.shape[2]
    below_and_above, _ = beyond()
    lane = lax.broadcasted_iota(jnp.int32, (2 * ROWS, LANES), 1)

    count = columns.shape[0] // 2
    beside = [
        jnp.concatenate([columns[i], below_and_above(columns_a[i], columns_b[i])], 0) for i in range(2 * count)
    ]
    spot = lane % SLOT

    def whole(tile):
        group, at = packed_place(tile)
        right = jnp.where(between(spot, 8, HALO), turned(beside[group], 8 - at), ribbon[tile])
        return jnp.where(between(spot, 16, HALO), turned(beside[count + group], 16 - at), right)

    field = [[whole(c * tiles + n) for n in range(tiles)] for c in range(2)]
    eta = [whole(2 * tiles + n) for n in range(tiles)]
    cover, drag = whole(3 * tiles), whole(3 * tiles + 1)

    def after(v):
        return v[1:] + [turned(v[0], -SLOT)]

    eta_row = [2.0 * (e + row_next(e)) for e in eta]
    eta_col = [0.5 * (e + col_next(e)) for e in eta]
    eta_row_1, eta_col_1 = [0.25 * e for e in eta_row], [4.0 * e for e in eta_col]
    eta_half = [0.5 * e for e in eta]
    eta_up = [e + n for e, n in zip(eta, after(eta))]
    eta_up[-1] = jnp.where(lane < LANES - SLOT, eta_up[-1], 0.0)
    place = lax.broadcasted_iota(jnp.int32, (ROWS, LANES), 1) % SLOT
    edge = between(place, 4, HALO) | between(place, 20, HALO)
    extra = [None]
    for t in range(1, STEPS + 1):
        ups = [[u * (g - n) for u, g, n in zip(eta_up, field[c], after(field[c]))] for c in range(2)]
        result = ([], [])
        odd = even = jnp.zeros((ROWS, LANES), jnp.float32)
        for n in range(tiles):
            coefficients = (eta_row[n], eta_row_1[n], eta_col[n], eta_col_1[n], eta_half[n])
            outs = horizontal(field[0][n], field[1][n], *coefficients, Turns)
            for c in range(2):
                below = ups[c][n - 1] if n else turned(ups[c][-1], SLOT) - drag * field[c][0]
                out = cover * (outs[c] + (ups[c][n] - below))
                result[c].append(out)
                now = out[:ROWS]
                edges[t - 1, c, n] = now
                odd = odd + field[c][n][:ROWS] * now
                even = even + now * now
        field = result
        extra.extend([jnp.where(edge, odd, 0.0), jnp.where(edge, even, 0.0)])

    tall = lax.broadcasted_iota(jnp.int32, (2 * ROWS, LANES), 0)
    high = jnp.zeros((2 * ROWS, LANES), jnp.float32)
    low = jnp.zeros((2 * ROWS, LANES), jnp.float32)
    for j, more in enumerate(extra):
        total = sums[j]
        pair = two_sum(total[:, :LANES], total[:, LANES:])
        if more is not None:
            pair = join(pair, (more, jnp.zeros_like(more)))
        for step in (4, 2, 1):
            pair = join(pair, tuple(pltpu.roll(v, step, 0) for v in pair))
        high = jnp.where(tall == j, jnp.concatenate([pair[0]] * 2, 0), high)
        low = jnp.where(tall == j, jnp.concatenate([pair[1]] * 2, 0), low)
    moments[0] = high
    moments[1] = low


def add_kernel(*refs):
    *ins, out = refs
    total = (ins[0][0], ins[0][1])
    for x in ins[1:]:
        total = join(total, (x[0], x[1]))
    out[0], out[1] = total


def solve(total):
    for step in (64, 32, 16, 8, 4, 2, 1):
        total = join(total, tuple(pltpu.roll(v, step, 1) for v in total))

    def spread(v, j):
        return jnp.broadcast_to(v[j : j + 1], (ROWS, LANES))

    centre, _ = cut(spread(total[0], 1) / spread(total[0], 0), 13)
    wide = jnp.concatenate([centre, centre], 0)
    mu = [spread(total[0] + total[1], 0)]
    for _ in range(2 * STEPS):
        step = times(wide, total)
        total = join(tuple(pltpu.roll(v, 2 * ROWS - 1, 0) for v in total), (-step[0], -step[1]))
        mu.append(spread(total[0] + total[1], 0))

    def plus(a, b):
        n = max(len(a), len(b))
        return [a[i] + b[i] if i < min(len(a), len(b)) else (a[i] if i < len(a) else b[i]) for i in range(n)]

    def scaled(s, a):
        return [s * x for x in a]

    def operator(a):
        return plus([centre * x for x in a], [jnp.zeros_like(centre)] + a)

    def dot(a, b):
        square = [None] * (len(a) + len(b) - 1)
        for i, x in enumerate(a):
            for j, y in enumerate(b):
                z = x * y
                square[i + j] = z if square[i + j] is None else square[i + j] + z
        value = square[0] * mu[0]
        for n in range(1, len(square)):
            value = value + square[n] * mu[n]
        return value

    one = jnp.ones_like(centre)
    right = [one]
    quasi, search, update, iterate = right, right, [], []
    applied = operator(search)
    carried = applied
    rho = mu[0]
    tau_sq = rho
    alpha = theta_sq = eta = None
    for half in range(STEPS):
        if half % 2 == 0:
            alpha = rho / dot(carried, right)
            search_next = plus(search, scaled(-alpha, carried))
        quasi = plus(quasi, scaled(-alpha, applied))
        if half:
            update = plus(search, scaled(theta_sq / alpha * eta, update))
        else:
            update = search
        theta_sq = dot(quasi, quasi) / tau_sq
        cosine_sq = 1.0 / (1.0 + theta_sq)
        tau_sq = tau_sq * theta_sq * cosine_sq
        eta = cosine_sq * alpha
        iterate = plus(iterate, scaled(eta, update))
        if half % 2 == 0:
            search = search_next
            applied = operator(search)
        elif half < STEPS - 1:
            rho_next = dot(quasi, right)
            beta = rho_next / rho
            search = plus(quasi, scaled(beta, search))
            applied_next = operator(search)
            carried = plus(applied_next, scaled(beta, plus(applied, scaled(beta, carried))))
            applied, rho = applied_next, rho_next
    powers = [iterate[-1]]
    for c in iterate[-2::-1]:
        powers = plus([c] + powers, scaled(-centre, powers))
    return powers


def final_kernel(rhs, power_1, power_2, power_3, power_4, edges, friction, ice, grounded, speed, *rest):
    *parts, iterate, residual, hessian = rest
    layers, tiles = rhs.shape[1], edges.shape[2]
    total = (parts[0][0], parts[0][1])
    for x in parts[1:]:
        total = join(total, (x[0], x[1]))
    factors = solve(total)
    powers = (power_1, power_2, power_3, power_4)
    wide = [jnp.concatenate([c, c], 1) for c in factors]
    rest = sum(wide[1:], wide[0])
    cover = ice[...].astype(jnp.float32)
    lane = lax.broadcasted_iota(jnp.int32, (ROWS, LANES), 1)

    def combined(vectors, weights):
        x = weights[1] * vectors[0]
        y = weights[0] * vectors[0]
        for t in range(1, STEPS):
            if t + 1 < STEPS:
                x = x + weights[t + 1] * vectors[t]
            y = y + weights[t] * vectors[t]
        return x, y

    for c in range(2):
        side = [combined([edges[t, c, n] for t in range(STEPS)], factors) for n in range(tiles)]
        for k in range(layers):
            at = k // tiles * SLOT
            inner = combined([p[c, k, :ROWS] for p in powers], wide)
            patched = []
            for v, e in zip(inner, side[k % tiles]):
                head = jnp.where(lane < HALO, turned(e, -at - 20), v[:, :LANES])
                tail = jnp.where(lane >= LANES - HALO, turned(e, 120 - at), v[:, LANES:])
                patched.append(jnp.concatenate([head, tail], 1))
            r = rhs[c, k]
            x, y = patched
            iterate[c, k] = jnp.where(cover > 0.0, wide[0] * r + x, rest * r)
            residual[c, k] = r - jnp.where(cover > 0.0, y, rest * r)
    weight = cover * (friction[...] * grounded[...].astype(jnp.float32))
    hessian[...] = weight * (speed[0] * iterate[0, 0] + speed[1] * iterate[1, 0])


def exchange(x, axis):
    count = lax.axis_size(axis)
    stride = 1
    rounds = []
    while stride < count:
        size = 4 if (count // stride) % 4 == 0 else 2
        rounds.append((stride, size))
        stride *= size
    for at, (stride, size) in enumerate(rounds):
        parts = [x]
        for turn in range(size - 1, 0, -1):
            pairs = []
            for i in range(count):
                place = (i // stride) % size
                pairs.append((i, i + ((place ^ turn) - place) * stride))
            parts.append(lax.ppermute(x, axis, pairs))
        if at == len(rounds) - 1:
            return parts
        x = call(add_kernel, [x.shape])(*parts)[0]
    return [x]


def body(adjoint_rhs, viscosity, friction, ice_mask, grounded, basal_velocity):
    layers = viscosity.shape[0]
    inputs = (adjoint_rhs, viscosity, friction, ice_mask, grounded, basal_velocity)
    tile = (ROWS, LANES)
    strips = (2 * (layers + layers // 2 + 1),) + tile
    ribbons = ribbon_tiles(layers)
    packed = ((ribbons + 7) // 8,) + tile
    both = (2 * packed[0],) + tile
    *held, strip_a, strip_b = call(
        strip_kernel,
        [jax.ShapeDtypeStruct(x.shape, x.dtype) for x in inputs] + [strips, strips],
        [pltpu.SemaphoreType.DMA((len(inputs),))],
        in_specs=[pl.BlockSpec(memory_space=pltpu.HBM)] * len(inputs),
    )(*[pltpu.with_memory_space_constraint(x, pltpu.HBM) for x in inputs])
    strip_b, strip_a = swapped(strip_b, ("gx",), 1, "gz"), swapped(strip_a, ("gx",), 0)
    column_a, column_b = call(column_kernel, [packed, packed])(*held[:5])
    beside = ("gy", "gz")
    (columns,) = call(beside_kernel, [both])(swapped(column_a, beside, 0), swapped(column_b, beside, 1))
    columns_b, columns_a = swapped(columns, ("gx",), 1, "gz"), swapped(columns, ("gx",), 0)
    block = (layers, 2 * ROWS, 2 * LANES)
    *powers, sums, ribbon = call(
        main_kernel,
        [(2,) + block] * (STEPS - 1) + [adjoint_rhs.shape, (2 * STEPS + 1, ROWS, 2 * LANES), (ribbons, 2 * ROWS, LANES)],
        [(2,) + block] * 3 + [block] * 2 + [block[1:]] * 2,
        cost_estimate=pl.CostEstimate(flops=200_000_000, bytes_accessed=8_000_000, transcendentals=0),
    )(*held[:5], strip_b, strip_a)
    edges, sums = call(
        ribbon_kernel,
        [(STEPS, 2, layers // 4) + tile, (2, 2 * ROWS, LANES)],
    )(ribbon, columns, columns_b, columns_a, sums)
    parts = exchange(sums, ("gy", "gz"))
    if len(parts) > 1:
        sums = call(add_kernel, [sums.shape])(*parts)[0]
    parts = exchange(sums, "gx")
    rhs, _, friction, ice_mask, grounded, speed = held
    return tuple(
        call(final_kernel, [adjoint_rhs.shape, adjoint_rhs.shape, friction.shape])(
            rhs, *powers, edges, friction, ice_mask, grounded, speed, *parts
        )
    )


def solution(mesh):
    in_specs = (
        P(None, None, ("parts", "gx"), ("gy", "gz")),
        P(None, ("parts", "gx"), ("gy", "gz")),
        P(("parts", "gx"), ("gy", "gz")),
        P(("parts", "gx"), ("gy", "gz")),
        P(("parts", "gx"), ("gy", "gz")),
        P(None, ("parts", "gx"), ("gy", "gz")),
    )
    out_specs = (
        P(None, None, ("parts", "gx"), ("gy", "gz")),
        P(None, None, ("parts", "gx"), ("gy", "gz")),
        P(("parts", "gx"), ("gy", "gz")),
    )
    return jax.shard_map(body, mesh=mesh, in_specs=in_specs, out_specs=out_specs, check_vma=False)
```

```python
import functools

import jax
import jax.numpy as jnp
from jax import lax
from jax.experimental import pallas as pl
from jax.experimental.pallas import tpu as pltpu
from jax.sharding import PartitionSpec as P

STEPS = 4
HALO = 4
ROWS = 8
LANES = 128
UNROLL = 5
SLOT = 32


def call(kernel, outs, scratch=(), **more):
    return pl.pallas_call(
        kernel,
        out_shape=[jax.ShapeDtypeStruct(s, jnp.float32) if isinstance(s, tuple) else s for s in outs],
        scratch_shapes=[pltpu.VMEM(s, jnp.float32) if isinstance(s, tuple) else s for s in scratch],
        compiler_params=pltpu.CompilerParams(vmem_limit_bytes=40 * 1024 * 1024),
        **more,
    )


def place_of(axis):
    place, count = lax.axis_index(axis), lax.axis_size(axis)
    even = place % 2 == 0
    has_a = jnp.logical_or(jnp.logical_not(even), place < count - 1)
    has_b = jnp.where(even, place > 0, place < count - 1)
    return even, has_a, has_b


def swapped(x, axes, first, spare=None):
    count, others = lax.axis_size(axes), lax.axis_size(spare) if spare else 1
    pairs = []
    for at in range(others):
        for i in range(count):
            other, to = (i + 1 if (i - first) % 2 == 0 else i - 1), at
            if not 0 <= other < count:
                other, to = (i, at ^ 1) if spare else (count - 1 - i, at)
                if to >= others or count % 2:
                    other, to = i, at
            pairs.append((i * others + at, other * others + to))
    return lax.ppermute(x, (*axes, spare) if spare else axes, pairs)


def own_planes(rhs, eta, friction, ice, grounded):
    layers = eta.shape[0]
    cover = ice[...].astype(jnp.float32)
    drag = friction[...] * grounded[...].astype(jnp.float32)

    def plane(p):
        if p < 2 * layers:
            return rhs[p // layers, p % layers] * cover
        if p < 3 * layers:
            return eta[p - 2 * layers]
        return cover if p == 3 * layers else drag

    return plane


def pair_of(q, layers):
    if q < layers:
        return q, q + layers
    if q < layers + layers // 2:
        return q + layers, q + layers + layers // 2
    return 3 * layers, 3 * layers + 1


def ribbon_places(p, layers):
    tiles = layers // 4
    if p < 3 * layers:
        k = p % layers
        return p // layers * tiles + k % tiles, (k // tiles,)
    return (3 * tiles, (0, 1, 2, 3)) if p == 3 * layers else (3 * tiles + 1, (0,))


def ribbon_tiles(layers):
    return 3 * (layers // 4) + 2


def packed_place(tile):
    return tile // 8, HALO * (tile % 8)


def between(lane, first, width):
    return (lane >= first) & (lane < first + width)


def turned(v, shift):
    shift = shift % LANES
    return pltpu.roll(v, shift, 1) if shift else v


def strip_kernel(*refs):
    sources, held, (strip_a, strip_b, arrived) = refs[:6], refs[6:12], refs[12:]
    copies = [pltpu.make_async_copy(a, b, arrived.at[i]) for i, (a, b) in enumerate(zip(sources, held))]
    for copy in copies:
        copy.start()
    for copy in copies:
        copy.wait()
    rhs, eta, friction, ice, grounded, _ = held
    layers = eta.shape[0]
    plane = own_planes(rhs, eta, friction, ice, grounded)
    even, _, _ = place_of("gx")
    upper_a = (lax.broadcasted_iota(jnp.int32, (ROWS, LANES), 0) < HALO) != even
    for q in range(strip_a.shape[0] // 2):
        first, second = pair_of(q, layers)
        x, y = plane(first), plane(second)
        for half in range(2):
            xs = x[:, half * LANES : (half + 1) * LANES]
            ys = y[:, half * LANES : (half + 1) * LANES]
            ys = pltpu.roll(ys, HALO, 0)
            strip_a[2 * q + half] = jnp.where(upper_a, xs, ys)
            strip_b[2 * q + half] = jnp.where(upper_a, ys, xs)


def column_kernel(rhs, eta, friction, ice, grounded, column_a, column_b):
    layers = eta.shape[0]
    plane = own_planes(rhs, eta, friction, ice, grounded)
    lane = lax.broadcasted_iota(jnp.int32, (ROWS, LANES), 1)
    even, _, _ = place_of(("gy", "gz"))
    zero = jnp.zeros((ROWS, LANES), jnp.float32)
    to_left, to_right = [zero] * column_a.shape[0], [zero] * column_a.shape[0]
    for p in range(3 * layers + 2):
        v = plane(p)
        tile, slots = ribbon_places(p, layers)
        group, at = packed_place(tile)
        for slot in slots:
            here = between(lane, slot * SLOT + at, HALO)
            to_left[group] = jnp.where(here, turned(v[:, :LANES], slot * SLOT + at), to_left[group])
            to_right[group] = jnp.where(here, turned(v[:, LANES:], slot * SLOT + at + HALO), to_right[group])
    for group in range(column_a.shape[0]):
        column_a[group] = jnp.where(even, to_right[group], to_left[group])
        column_b[group] = jnp.where(even, to_left[group], to_right[group])


def beside_kernel(from_a, from_b, columns):
    even, has_a, has_b = place_of(("gy", "gz"))
    count = from_a.shape[0]
    for group in range(count):
        a = jnp.where(has_a, from_a[group], 0.0)
        b = jnp.where(has_b, from_b[group], 0.0)
        columns[group] = jnp.where(even, a, b)
        columns[count + group] = jnp.where(even, b, a)


def two_sum(a, b):
    s = a + b
    t = s - a
    return s, (a - (s - t)) + (b - t)


def join(x, y):
    s, e = two_sum(x[0], y[0])
    return s, e + (x[1] + y[1])


def cut(v, bits):
    t = v * (2.0**bits + 1.0)
    h = t - (t - v)
    return h, v - h


def times(scalar, x):
    high, low = cut(x[0], 12)
    return scalar * high, scalar * low + scalar * x[1]


def beyond():
    even, has_a, has_b = place_of("gx")
    upper_a = (lax.broadcasted_iota(jnp.int32, (ROWS, LANES), 0) < HALO) == even
    lower_a = jnp.logical_not(upper_a)

    def below_and_above(from_a, from_b):
        return jnp.where(upper_a & has_a, from_a, jnp.where(lower_a & has_b, from_b, 0.0))

    def above_and_below(from_a, from_b):
        return jnp.where(lower_a & has_a, from_a, jnp.where(upper_a & has_b, from_b, 0.0))

    return below_and_above, above_and_below


def row_next(v):
    return pltpu.roll(v, 2 * ROWS - 1, 0)


def row_prev(v):
    return pltpu.roll(v, 1, 0)


def col_next(v):
    return pltpu.roll(v, v.shape[1] - 1, 1)


def col_prev(v):
    return pltpu.roll(v, 1, 1)


def ribbon_of(p, layers, head, tail, lane, strips):
    tile, slots = ribbon_places(p, layers)
    for slot in slots:
        at = slot * SLOT
        strips[tile] = jnp.where(between(lane, at, 8), turned(tail, at + 8), strips[tile])
        strips[tile] = jnp.where(between(lane, at + 20, 8), turned(head, at + 20), strips[tile])


def own_kernel(_, rhs, eta, friction, ice, grounded, ribbon, squares):
    layers = eta.shape[0]
    plane = own_planes(rhs, eta, friction, ice, grounded)
    lane = lax.broadcasted_iota(jnp.int32, (ROWS, LANES), 1)
    strips = [jnp.zeros((ROWS, LANES), jnp.float32)] * ribbon.shape[0]
    for p in range(3 * layers + 2):
        v = plane(p)
        ribbon_of(p, layers, v[:, :LANES], v[:, LANES:], lane, strips)
    for tile, v in enumerate(strips):
        ribbon[tile] = v
    bare = 1.0 - ice[...].astype(jnp.float32)
    whole = jnp.zeros((ROWS, 2 * LANES), jnp.float32)
    outside = jnp.zeros((ROWS, 2 * LANES), jnp.float32)
    for c in range(2):
        for k in range(layers):
            square = rhs[c, k] * rhs[c, k]
            whole = whole + square
            outside = outside + bare * square
    squares[0], squares[1] = whole, outside


class Tiles:
    def __init__(self, tiles):
        self.tiles = tiles

    @staticmethod
    def load(ref):
        return Tiles([ref[r : r + ROWS, c : c + LANES] for r in (0, ROWS) for c in (0, LANES)])

    def store(self, ref):
        for v, (r, c) in zip(self.tiles, ((0, 0), (0, LANES), (ROWS, 0), (ROWS, LANES))):
            ref[r : r + ROWS, c : c + LANES] = v

    def both(self, other, op):
        if isinstance(other, Tiles):
            return Tiles([op(x, y) for x, y in zip(self.tiles, other.tiles)])
        return Tiles([op(x, other) for x in self.tiles])

    def __add__(self, other):
        return self.both(other, lambda x, y: x + y)

    def __sub__(self, other):
        return self.both(other, lambda x, y: x - y)

    def __mul__(self, other):
        return self.both(other, lambda x, y: x * y)

    __rmul__ = __mul__


class Moves:
    def __init__(self):
        row = lax.broadcasted_iota(jnp.int32, (ROWS, LANES), 0)
        lane = lax.broadcasted_iota(jnp.int32, (ROWS, LANES), 1)
        self.first_row, self.last_row = row == 0, row == ROWS - 1
        self.first_lane, self.last_lane = lane == 0, lane == LANES - 1

    def rows(self, v, shift, edge):
        own0, own1, halo0, halo1 = [pltpu.roll(x, shift, 0) for x in v.tiles]
        return Tiles(
            [
                jnp.where(edge, halo0, own0),
                jnp.where(edge, halo1, own1),
                jnp.where(edge, own0, halo0),
                jnp.where(edge, own1, halo1),
            ]
        )

    def row_next(self, v):
        return self.rows(v, ROWS - 1, self.last_row)

    def row_prev(self, v):
        return self.rows(v, 1, self.first_row)

    def col_next(self, v):
        own0, own1, halo0, halo1 = [pltpu.roll(x, LANES - 1, 1) for x in v.tiles]
        return Tiles([jnp.where(self.last_lane, own1, own0), own1, jnp.where(self.last_lane, halo1, halo0), halo1])

    def col_prev(self, v):
        own0, own1, halo0, halo1 = [pltpu.roll(x, 1, 1) for x in v.tiles]
        return Tiles([own0, jnp.where(self.first_lane, own0, own1), halo0, jnp.where(self.first_lane, halo0, halo1)])


class Turns:
    row_next = staticmethod(row_next)
    row_prev = staticmethod(row_prev)
    col_next = staticmethod(col_next)
    col_prev = staticmethod(col_prev)


def horizontal(g0, g1, e_row, e_row_1, e_col, e_col_1, e_half, moves):
    row_next, row_prev, col_next, col_prev = moves.row_next, moves.row_prev, moves.col_next, moves.col_prev
    g0n, g1n = row_next(g0), col_next(g1)
    f = e_half * (g1n - col_prev(g1))
    h = e_half * (g0n - row_prev(g0))
    flux = e_row * (g0 - g0n)
    out0 = flux - row_next(f) - row_prev(flux - f)
    flux = e_col * (g0 - col_next(g0))
    out0 = out0 + (flux - col_prev(flux))
    flux = e_col_1 * (g1 - g1n)
    out1 = flux - col_next(h) - col_prev(flux - h)
    flux = e_row_1 * (g1 - row_next(g1))
    out1 = out1 + (flux - row_prev(flux))
    return out0, out1


def main_kernel(
    rhs, eta, friction, ice, grounded, squares, strip_b, strip_a,
    power_1, power_2, power_3, power_4, sums, ribbon,
    masked, eta_row, eta_col, eta_half, eta_up, cover, drag,
):
    layers = eta.shape[0]
    plane = own_planes(rhs, eta, friction, ice, grounded)
    below_and_above, above_and_below = beyond()
    lane = lax.broadcasted_iota(jnp.int32, (ROWS, LANES), 1)

    def target(p):
        if p < 2 * layers:
            return masked.at[p // layers, p % layers]
        if p < 3 * layers:
            return eta_up.at[p - 2 * layers]
        return cover if p == 3 * layers else drag

    strips = [jnp.zeros((ROWS, LANES), jnp.float32)] * ribbon.shape[0]
    for q in range(strip_a.shape[0] // 2):
        first, second = pair_of(q, layers)
        halves = ([], [])
        for half in range(2):
            from_a, from_b = strip_a[2 * q + half], strip_b[2 * q + half]
            halves[0].append(below_and_above(from_a, from_b))
            halves[1].append(pltpu.roll(above_and_below(from_a, from_b), HALO, 0))
        for p, halo in zip((first, second), halves):
            v = plane(p)
            dst = target(p)
            dst[0:ROWS, :] = v
            dst[ROWS:, 0:LANES], dst[ROWS:, LANES:] = halo
            ribbon_of(p, layers, *halo, lane, strips)
    for tile, v in enumerate(strips):
        ribbon[tile] = v

    moves = Moves()
    load = Tiles.load
    e = load(eta_up.at[0])
    for k in range(layers):
        pair = e + moves.row_next(e)
        (2.0 * pair).store(eta_row.at[0, k])
        (0.5 * pair).store(eta_row.at[1, k])
        pair = e + moves.col_next(e)
        (0.5 * pair).store(eta_col.at[0, k])
        (2.0 * pair).store(eta_col.at[1, k])
        (0.5 * e).store(eta_half.at[k])
        after = load(eta_up.at[k + 1]) if k + 1 < layers else None
        (e + after if k + 1 < layers else 0.0 * e).store(eta_up.at[k])
        e = after

    def apply(t, src, dst):
        def block(b, carry):
            g0, g1, below0, below1, odd, even = carry
            g0, g1, below0, below1 = Tiles(g0), Tiles(g1), Tiles(below0), Tiles(below1)
            odd, even = list(odd), list(even)
            m = load(cover)
            for i in range(UNROLL):
                k = b * UNROLL + i
                after = k + 1 if i + 1 < UNROLL else jnp.minimum(k + 1, layers - 1)
                next0, next1 = load(src.at[0, after]), load(src.at[1, after])
                e_up = load(eta_up.at[k])
                up0, up1 = e_up * (g0 - next0), e_up * (g1 - next1)
                pairs = [load(ref.at[c, k]) for ref in (eta_row, eta_col) for c in range(2)]
                out0, out1 = horizontal(g0, g1, *pairs, load(eta_half.at[k]), moves)
                out0, out1 = m * (out0 + (up0 - below0)), m * (out1 + (up1 - below1))
                for c, g, out in ((0, g0, out0), (1, g1, out1)):
                    if t < STEPS:
                        out.store(dst.at[c, k])
                    for half in range(2):
                        now = out.tiles[half]
                        if t == STEPS:
                            dst[c, k, :, half * LANES : (half + 1) * LANES] = now
                        odd[half] = odd[half] + g.tiles[half] * now
                        even[half] = even[half] + now * now
                g0, g1, below0, below1 = next0, next1, up0, up1
            return g0.tiles, g1.tiles, below0.tiles, below1.tiles, odd, even

        zero = [jnp.zeros((ROWS, LANES), jnp.float32)] * 2
        d = -1.0 * load(drag)
        g0, g1 = load(src.at[0, 0]), load(src.at[1, 0])
        start = (g0.tiles, g1.tiles, (d * g0).tiles, (d * g1).tiles, zero, zero)
        ends = lax.fori_loop(0, layers // UNROLL, block, start)[4:]
        return [jnp.concatenate(v, 1) for v in ends]

    outside = squares[1]
    sums[0] = squares[0]
    wide = lax.broadcasted_iota(jnp.int32, (ROWS, 2 * LANES), 1)
    inner = between(wide, HALO, 2 * LANES - 2 * HALO)
    fields = (masked, power_1, power_2, power_3, power_4)
    for t in range(1, STEPS + 1):
        odd, even = apply(t, fields[t - 1], fields[t])
        sums[2 * t - 1] = jnp.where(inner, odd, 0.0) + outside
        sums[2 * t] = jnp.where(inner, even, 0.0) + outside


def ribbon_kernel(own, halo, columns, columns_b, columns_a, sums, edges, moments):
    tiles = edges.shape[2]
    below_and_above, _ = beyond()
    lane = lax.broadcasted_iota(jnp.int32, (2 * ROWS, LANES), 1)

    count = columns.shape[0] // 2
    beside = [
        jnp.concatenate([columns[i], below_and_above(columns_a[i], columns_b[i])], 0) for i in range(2 * count)
    ]
    spot = lane % SLOT

    def whole(tile):
        group, at = packed_place(tile)
        right = jnp.where(between(spot, 8, HALO), turned(beside[group], 8 - at), jnp.concatenate([own[tile], halo[tile]], 0))
        return jnp.where(between(spot, 16, HALO), turned(beside[count + group], 16 - at), right)

    field = [[whole(c * tiles + n) for n in range(tiles)] for c in range(2)]
    eta = [whole(2 * tiles + n) for n in range(tiles)]
    cover, drag = whole(3 * tiles), whole(3 * tiles + 1)

    def after(v):
        return v[1:] + [turned(v[0], -SLOT)]

    eta_row = [2.0 * (e + row_next(e)) for e in eta]
    eta_col = [0.5 * (e + col_next(e)) for e in eta]
    eta_row_1, eta_col_1 = [0.25 * e for e in eta_row], [4.0 * e for e in eta_col]
    eta_half = [0.5 * e for e in eta]
    eta_up = [e + n for e, n in zip(eta, after(eta))]
    eta_up[-1] = jnp.where(lane < LANES - SLOT, eta_up[-1], 0.0)
    place = lax.broadcasted_iota(jnp.int32, (ROWS, LANES), 1) % SLOT
    edge = between(place, 4, HALO) | between(place, 20, HALO)
    extra = [None]
    for t in range(1, STEPS + 1):
        ups = [[u * (g - n) for u, g, n in zip(eta_up, field[c], after(field[c]))] for c in range(2)]
        result = ([], [])
        odd = even = jnp.zeros((ROWS, LANES), jnp.float32)
        for n in range(tiles):
            coefficients = (eta_row[n], eta_row_1[n], eta_col[n], eta_col_1[n], eta_half[n])
            outs = horizontal(field[0][n], field[1][n], *coefficients, Turns)
            for c in range(2):
                below = ups[c][n - 1] if n else turned(ups[c][-1], SLOT) - drag * field[c][0]
                out = cover * (outs[c] + (ups[c][n] - below))
                result[c].append(out)
                now = out[:ROWS]
                edges[t - 1, c, n] = now
                odd = odd + field[c][n][:ROWS] * now
                even = even + now * now
        field = result
        extra.extend([jnp.where(edge, odd, 0.0), jnp.where(edge, even, 0.0)])

    tall = lax.broadcasted_iota(jnp.int32, (2 * ROWS, LANES), 0)
    high = jnp.zeros((2 * ROWS, LANES), jnp.float32)
    low = jnp.zeros((2 * ROWS, LANES), jnp.float32)
    for j, more in enumerate(extra):
        total = sums[j]
        pair = two_sum(total[:, :LANES], total[:, LANES:])
        if more is not None:
            pair = join(pair, (more, jnp.zeros_like(more)))
        for step in (4, 2, 1):
            pair = join(pair, tuple(pltpu.roll(v, step, 0) for v in pair))
        high = jnp.where(tall == j, jnp.concatenate([pair[0]] * 2, 0), high)
        low = jnp.where(tall == j, jnp.concatenate([pair[1]] * 2, 0), low)
    moments[0] = high
    moments[1] = low


def add_kernel(*refs):
    *ins, out = refs
    total = (ins[0][0], ins[0][1])
    for x in ins[1:]:
        total = join(total, (x[0], x[1]))
    out[0], out[1] = total


def solve(total):
    for step in (64, 32, 16, 8, 4, 2, 1):
        total = join(total, tuple(pltpu.roll(v, step, 1) for v in total))

    def spread(v, j):
        return jnp.broadcast_to(v[j : j + 1], (ROWS, LANES))

    centre, _ = cut(spread(total[0], 1) / spread(total[0], 0), 13)
    wide = jnp.concatenate([centre, centre], 0)
    mu = [spread(total[0] + total[1], 0)]
    for _ in range(2 * STEPS):
        step = times(wide, total)
        total = join(tuple(pltpu.roll(v, 2 * ROWS - 1, 0) for v in total), (-step[0], -step[1]))
        mu.append(spread(total[0] + total[1], 0))

    def plus(a, b):
        n = max(len(a), len(b))
        return [a[i] + b[i] if i < min(len(a), len(b)) else (a[i] if i < len(a) else b[i]) for i in range(n)]

    def scaled(s, a):
        return [s * x for x in a]

    def operator(a):
        return plus([centre * x for x in a], [jnp.zeros_like(centre)] + a)

    def dot(a, b):
        square = [None] * (len(a) + len(b) - 1)
        for i, x in enumerate(a):
            for j, y in enumerate(b):
                z = x * y
                square[i + j] = z if square[i + j] is None else square[i + j] + z
        value = square[0] * mu[0]
        for n in range(1, len(square)):
            value = value + square[n] * mu[n]
        return value

    one = jnp.ones_like(centre)
    right = [one]
    quasi, search, update, iterate = right, right, [], []
    applied = operator(search)
    carried = applied
    rho = mu[0]
    tau_sq = rho
    alpha = theta_sq = eta = None
    for half in range(STEPS):
        if half % 2 == 0:
            alpha = rho / dot(carried, right)
            search_next = plus(search, scaled(-alpha, carried))
        quasi = plus(quasi, scaled(-alpha, applied))
        if half:
            update = plus(search, scaled(theta_sq / alpha * eta, update))
        else:
            update = search
        theta_sq = dot(quasi, quasi) / tau_sq
        cosine_sq = 1.0 / (1.0 + theta_sq)
        tau_sq = tau_sq * theta_sq * cosine_sq
        eta = cosine_sq * alpha
        iterate = plus(iterate, scaled(eta, update))
        if half % 2 == 0:
            search = search_next
            applied = operator(search)
        elif half < STEPS - 1:
            rho_next = dot(quasi, right)
            beta = rho_next / rho
            search = plus(quasi, scaled(beta, search))
            applied_next = operator(search)
            carried = plus(applied_next, scaled(beta, plus(applied, scaled(beta, carried))))
            applied, rho = applied_next, rho_next
    powers = [iterate[-1]]
    for c in iterate[-2::-1]:
        powers = plus([c] + powers, scaled(-centre, powers))
    return powers


def final_kernel(rhs, power_1, power_2, power_3, power_4, edges, friction, ice, grounded, speed, *rest):
    *parts, iterate, residual, hessian = rest
    layers, tiles = rhs.shape[1], edges.shape[2]
    total = (parts[0][0], parts[0][1])
    for x in parts[1:]:
        total = join(total, (x[0], x[1]))
    factors = solve(total)
    powers = (power_1, power_2, power_3, power_4)
    wide = [jnp.concatenate([c, c], 1) for c in factors]
    rest = sum(wide[1:], wide[0])
    cover = ice[...].astype(jnp.float32)
    lane = lax.broadcasted_iota(jnp.int32, (ROWS, LANES), 1)

    def combined(vectors, weights):
        x = weights[1] * vectors[0]
        y = weights[0] * vectors[0]
        for t in range(1, STEPS):
            if t + 1 < STEPS:
                x = x + weights[t + 1] * vectors[t]
            y = y + weights[t] * vectors[t]
        return x, y

    for c in range(2):
        side = [combined([edges[t, c, n] for t in range(STEPS)], factors) for n in range(tiles)]
        for k in range(layers):
            at = k // tiles * SLOT
            inner = combined([p[c, k, :ROWS] for p in powers], wide)
            patched = []
            for v, e in zip(inner, side[k % tiles]):
                head = jnp.where(lane < HALO, turned(e, -at - 20), v[:, :LANES])
                tail = jnp.where(lane >= LANES - HALO, turned(e, 120 - at), v[:, LANES:])
                patched.append(jnp.concatenate([head, tail], 1))
            r = rhs[c, k]
            x, y = patched
            iterate[c, k] = jnp.where(cover > 0.0, wide[0] * r + x, rest * r)
            residual[c, k] = r - jnp.where(cover > 0.0, y, rest * r)
    weight = cover * (friction[...] * grounded[...].astype(jnp.float32))
    hessian[...] = weight * (speed[0] * iterate[0, 0] + speed[1] * iterate[1, 0])


def exchange(x, axis, order):
    count = lax.axis_size(axis)
    stride = 1
    rounds = []
    while stride < count:
        size = 4 if (count // stride) % 4 == 0 else 2
        rounds.append((stride, size))
        stride *= size
    for at, (stride, size) in enumerate(rounds):
        parts = [x]
        for turn in order if size == 4 else (1,):
            pairs = []
            for i in range(count):
                place = (i // stride) % size
                pairs.append((i, i + ((place ^ turn) - place) * stride))
            parts.append(lax.ppermute(x, axis, pairs))
        if at == len(rounds) - 1:
            return parts
        x = call(add_kernel, [x.shape])(*parts)[0]
    return [x]


def body(adjoint_rhs, viscosity, friction, ice_mask, grounded, basal_velocity):
    layers = viscosity.shape[0]
    inputs = (adjoint_rhs, viscosity, friction, ice_mask, grounded, basal_velocity)
    tile = (ROWS, LANES)
    strips = (2 * (layers + layers // 2 + 1),) + tile
    ribbons = ribbon_tiles(layers)
    packed = ((ribbons + 7) // 8,) + tile
    both = (2 * packed[0],) + tile
    *held, strip_a, strip_b = call(
        strip_kernel,
        [jax.ShapeDtypeStruct(x.shape, x.dtype) for x in inputs] + [strips, strips],
        [pltpu.SemaphoreType.DMA((len(inputs),))],
        in_specs=[pl.BlockSpec(memory_space=pltpu.HBM)] * len(inputs),
    )(*[pltpu.with_memory_space_constraint(x, pltpu.HBM) for x in inputs])
    strip_b, strip_a = swapped(strip_b, ("gx",), 1, "gz"), swapped(strip_a, ("gx",), 0)
    column_a, column_b = call(column_kernel, [packed, packed])(*held[:5])
    beside = ("gy", "gz")
    (columns,) = call(beside_kernel, [both])(swapped(column_a, beside, 0), swapped(column_b, beside, 1))
    columns_b, columns_a = swapped(columns, ("gx",), 1, "gz"), swapped(columns, ("gx",), 0)
    block = (layers, 2 * ROWS, 2 * LANES)
    own, squares = call(
        own_kernel,
        [(ribbons,) + tile, (2, ROWS, 2 * LANES)],
        in_specs=[pl.BlockSpec(memory_space=pl.ANY)] + [pl.BlockSpec(memory_space=pltpu.VMEM)] * 5,
    )(columns, *held[:5])
    *powers, sums, halo = call(
        main_kernel,
        [(2,) + block] * (STEPS - 1) + [adjoint_rhs.shape, (2 * STEPS + 1, ROWS, 2 * LANES), (ribbons,) + tile],
        [(2,) + block] * 3 + [block] * 2 + [block[1:]] * 2,
        cost_estimate=pl.CostEstimate(flops=200_000_000, bytes_accessed=8_000_000, transcendentals=0),
    )(*held[:5], squares, strip_b, strip_a)
    edges, sums = call(
        ribbon_kernel,
        [(STEPS, 2, layers // 4) + tile, (2, 2 * ROWS, LANES)],
    )(own, halo, columns, columns_b, columns_a, sums)
    parts = exchange(sums, ("gy", "gz"), (3, 2, 1))
    if len(parts) > 1:
        sums = call(add_kernel, [sums.shape])(*parts)[0]
    parts = exchange(sums, "gx", (1, 2, 3))
    rhs, _, friction, ice_mask, grounded, speed = held
    return tuple(
        call(final_kernel, [adjoint_rhs.shape, adjoint_rhs.shape, friction.shape])(
            rhs, *powers, edges, friction, ice_mask, grounded, speed, *parts
        )
    )


def solution(mesh):
    in_specs = (
        P(None, None, ("parts", "gx"), ("gy", "gz")),
        P(None, ("parts", "gx"), ("gy", "gz")),
        P(("parts", "gx"), ("gy", "gz")),
        P(("parts", "gx"), ("gy", "gz")),
        P(("parts", "gx"), ("gy", "gz")),
        P(None, ("parts", "gx"), ("gy", "gz")),
    )
    out_specs = (
        P(None, None, ("parts", "gx"), ("gy", "gz")),
        P(None, None, ("parts", "gx"), ("gy", "gz")),
        P(("parts", "gx"), ("gy", "gz")),
    )
    return jax.shard_map(body, mesh=mesh, in_specs=in_specs, out_specs=out_specs, check_vma=False)
```

```python
import functools

import jax
import jax.numpy as jnp
from jax import lax
from jax.experimental import pallas as pl
from jax.experimental.pallas import tpu as pltpu
from jax.sharding import PartitionSpec as P

STEPS = 4
HALO = 4
ROWS = 8
LANES = 128
UNROLL = 5
SLOT = 32


def call(kernel, outs, scratch=(), **more):
    return pl.pallas_call(
        kernel,
        out_shape=[jax.ShapeDtypeStruct(s, jnp.float32) if isinstance(s, tuple) else s for s in outs],
        scratch_shapes=[pltpu.VMEM(s, jnp.float32) if isinstance(s, tuple) else s for s in scratch],
        compiler_params=pltpu.CompilerParams(vmem_limit_bytes=40 * 1024 * 1024),
        **more,
    )


def place_of(axis):
    place, count = lax.axis_index(axis), lax.axis_size(axis)
    even = place % 2 == 0
    has_a = jnp.logical_or(jnp.logical_not(even), place < count - 1)
    has_b = jnp.where(even, place > 0, place < count - 1)
    return even, has_a, has_b


def swapped(x, axes, first, spare=None):
    count, others = lax.axis_size(axes), lax.axis_size(spare) if spare else 1
    pairs = []
    for at in range(others):
        for i in range(count):
            other, to = (i + 1 if (i - first) % 2 == 0 else i - 1), at
            if not 0 <= other < count:
                other, to = (i, at ^ 1) if spare else (count - 1 - i, at)
                if to >= others or count % 2:
                    other, to = i, at
            pairs.append((i * others + at, other * others + to))
    return lax.ppermute(x, (*axes, spare) if spare else axes, pairs)


def own_planes(rhs, eta, friction, ice, grounded):
    layers = eta.shape[0]
    cover = ice[...].astype(jnp.float32)
    drag = friction[...] * grounded[...].astype(jnp.float32)

    def plane(p):
        if p < 2 * layers:
            return rhs[p // layers, p % layers] * cover
        if p < 3 * layers:
            return eta[p - 2 * layers]
        return cover if p == 3 * layers else drag

    return plane


def pair_of(q, layers):
    if q < layers:
        return q, q + layers
    if q < layers + layers // 2:
        return q + layers, q + layers + layers // 2
    return 3 * layers, 3 * layers + 1


def ribbon_places(p, layers):
    tiles = layers // 4
    if p < 3 * layers:
        k = p % layers
        return p // layers * tiles + k % tiles, (k // tiles,)
    return (3 * tiles, (0, 1, 2, 3)) if p == 3 * layers else (3 * tiles + 1, (0,))


def ribbon_tiles(layers):
    return 3 * (layers // 4) + 2


def packed_place(tile):
    return tile // 8, HALO * (tile % 8)


def between(lane, first, width):
    return (lane >= first) & (lane < first + width)


def turned(v, shift):
    shift = shift % LANES
    return pltpu.roll(v, shift, 1) if shift else v


def strip_kernel(*refs):
    sources, held, (strip_a, strip_b, arrived) = refs[:6], refs[6:12], refs[12:]
    copies = [pltpu.make_async_copy(a, b, arrived.at[i]) for i, (a, b) in enumerate(zip(sources, held))]
    for copy in copies:
        copy.start()
    for copy in copies:
        copy.wait()
    rhs, eta, friction, ice, grounded, _ = held
    layers = eta.shape[0]
    plane = own_planes(rhs, eta, friction, ice, grounded)
    even, _, _ = place_of("gx")
    upper_a = (lax.broadcasted_iota(jnp.int32, (ROWS, LANES), 0) < HALO) != even
    for q in range(strip_a.shape[0] // 2):
        first, second = pair_of(q, layers)
        x, y = plane(first), plane(second)
        for half in range(2):
            xs = x[:, half * LANES : (half + 1) * LANES]
            ys = y[:, half * LANES : (half + 1) * LANES]
            ys = pltpu.roll(ys, HALO, 0)
            strip_a[2 * q + half] = jnp.where(upper_a, xs, ys)
            strip_b[2 * q + half] = jnp.where(upper_a, ys, xs)


def column_kernel(rhs, eta, friction, ice, grounded, column_a, column_b):
    layers = eta.shape[0]
    plane = own_planes(rhs, eta, friction, ice, grounded)
    lane = lax.broadcasted_iota(jnp.int32, (ROWS, LANES), 1)
    even, _, _ = place_of(("gy", "gz"))
    zero = jnp.zeros((ROWS, LANES), jnp.float32)
    to_left, to_right = [zero] * column_a.shape[0], [zero] * column_a.shape[0]
    for p in range(3 * layers + 2):
        v = plane(p)
        tile, slots = ribbon_places(p, layers)
        group, at = packed_place(tile)
        for slot in slots:
            here = between(lane, slot * SLOT + at, HALO)
            to_left[group] = jnp.where(here, turned(v[:, :LANES], slot * SLOT + at), to_left[group])
            to_right[group] = jnp.where(here, turned(v[:, LANES:], slot * SLOT + at + HALO), to_right[group])
    for group in range(column_a.shape[0]):
        column_a[group] = jnp.where(even, to_right[group], to_left[group])
        column_b[group] = jnp.where(even, to_left[group], to_right[group])


def beside_kernel(from_a, from_b, columns):
    even, has_a, has_b = place_of(("gy", "gz"))
    count = from_a.shape[0]
    for group in range(count):
        a = jnp.where(has_a, from_a[group], 0.0)
        b = jnp.where(has_b, from_b[group], 0.0)
        columns[group] = jnp.where(even, a, b)
        columns[count + group] = jnp.where(even, b, a)


def two_sum(a, b):
    s = a + b
    t = s - a
    return s, (a - (s - t)) + (b - t)


def join(x, y):
    s, e = two_sum(x[0], y[0])
    return s, e + (x[1] + y[1])


def cut(v, bits):
    t = v * (2.0**bits + 1.0)
    h = t - (t - v)
    return h, v - h


def times(scalar, x):
    high, low = cut(x[0], 12)
    return scalar * high, scalar * low + scalar * x[1]


def beyond():
    even, has_a, has_b = place_of("gx")
    upper_a = (lax.broadcasted_iota(jnp.int32, (ROWS, LANES), 0) < HALO) == even
    lower_a = jnp.logical_not(upper_a)

    def below_and_above(from_a, from_b):
        return jnp.where(upper_a & has_a, from_a, jnp.where(lower_a & has_b, from_b, 0.0))

    def above_and_below(from_a, from_b):
        return jnp.where(lower_a & has_a, from_a, jnp.where(upper_a & has_b, from_b, 0.0))

    return below_and_above, above_and_below


def row_next(v):
    return pltpu.roll(v, 2 * ROWS - 1, 0)


def row_prev(v):
    return pltpu.roll(v, 1, 0)


def col_next(v):
    return pltpu.roll(v, v.shape[1] - 1, 1)


def col_prev(v):
    return pltpu.roll(v, 1, 1)


def ribbon_of(p, layers, head, tail, lane, strips):
    tile, slots = ribbon_places(p, layers)
    for slot in slots:
        at = slot * SLOT
        strips[tile] = jnp.where(between(lane, at, 8), turned(tail, at + 8), strips[tile])
        strips[tile] = jnp.where(between(lane, at + 20, 8), turned(head, at + 20), strips[tile])


def own_kernel(_, rhs, eta, friction, ice, grounded, ribbon, squares):
    layers = eta.shape[0]
    plane = own_planes(rhs, eta, friction, ice, grounded)
    lane = lax.broadcasted_iota(jnp.int32, (ROWS, LANES), 1)
    strips = [jnp.zeros((ROWS, LANES), jnp.float32)] * ribbon.shape[0]
    for p in range(3 * layers + 2):
        v = plane(p)
        ribbon_of(p, layers, v[:, :LANES], v[:, LANES:], lane, strips)
    for tile, v in enumerate(strips):
        ribbon[tile] = v
    bare = 1.0 - ice[...].astype(jnp.float32)
    whole = jnp.zeros((ROWS, 2 * LANES), jnp.float32)
    outside = jnp.zeros((ROWS, 2 * LANES), jnp.float32)
    for c in range(2):
        for k in range(layers):
            square = rhs[c, k] * rhs[c, k]
            whole = whole + square
            outside = outside + bare * square
    squares[0], squares[1] = whole, outside


class Tiles:
    def __init__(self, tiles):
        self.tiles = tiles

    @staticmethod
    def load(ref):
        return Tiles([ref[r : r + ROWS, c : c + LANES] for r in (0, ROWS) for c in (0, LANES)])

    def store(self, ref):
        for v, (r, c) in zip(self.tiles, ((0, 0), (0, LANES), (ROWS, 0), (ROWS, LANES))):
            ref[r : r + ROWS, c : c + LANES] = v

    def both(self, other, op):
        if isinstance(other, Tiles):
            return Tiles([op(x, y) for x, y in zip(self.tiles, other.tiles)])
        return Tiles([op(x, other) for x in self.tiles])

    def __add__(self, other):
        return self.both(other, lambda x, y: x + y)

    def __sub__(self, other):
        return self.both(other, lambda x, y: x - y)

    def __mul__(self, other):
        return self.both(other, lambda x, y: x * y)

    __rmul__ = __mul__


class Moves:
    def __init__(self):
        row = lax.broadcasted_iota(jnp.int32, (ROWS, LANES), 0)
        lane = lax.broadcasted_iota(jnp.int32, (ROWS, LANES), 1)
        self.first_row, self.last_row = row == 0, row == ROWS - 1
        self.first_lane, self.last_lane = lane == 0, lane == LANES - 1

    def rows(self, v, shift, edge):
        own0, own1, halo0, halo1 = [pltpu.roll(x, shift, 0) for x in v.tiles]
        return Tiles(
            [
                jnp.where(edge, halo0, own0),
                jnp.where(edge, halo1, own1),
                jnp.where(edge, own0, halo0),
                jnp.where(edge, own1, halo1),
            ]
        )

    def row_next(self, v):
        return self.rows(v, ROWS - 1, self.last_row)

    def row_prev(self, v):
        return self.rows(v, 1, self.first_row)

    def col_next(self, v):
        own0, own1, halo0, halo1 = [pltpu.roll(x, LANES - 1, 1) for x in v.tiles]
        return Tiles([jnp.where(self.last_lane, own1, own0), own1, jnp.where(self.last_lane, halo1, halo0), halo1])

    def col_prev(self, v):
        own0, own1, halo0, halo1 = [pltpu.roll(x, 1, 1) for x in v.tiles]
        return Tiles([own0, jnp.where(self.first_lane, own0, own1), halo0, jnp.where(self.first_lane, halo0, halo1)])


class Turns:
    row_next = staticmethod(row_next)
    row_prev = staticmethod(row_prev)
    col_next = staticmethod(col_next)
    col_prev = staticmethod(col_prev)


def horizontal(g0, g1, e_row, e_row_1, e_col, e_col_1, e_half, moves):
    row_next, row_prev, col_next, col_prev = moves.row_next, moves.row_prev, moves.col_next, moves.col_prev
    g0n, g1n = row_next(g0), col_next(g1)
    f = e_half * (g1n - col_prev(g1))
    h = e_half * (g0n - row_prev(g0))
    flux = e_row * (g0 - g0n)
    out0 = flux - row_next(f) - row_prev(flux - f)
    flux = e_col * (g0 - col_next(g0))
    out0 = out0 + (flux - col_prev(flux))
    flux = e_col_1 * (g1 - g1n)
    out1 = flux - col_next(h) - col_prev(flux - h)
    flux = e_row_1 * (g1 - row_next(g1))
    out1 = out1 + (flux - row_prev(flux))
    return out0, out1


def main_kernel(
    rhs, eta, friction, ice, grounded, squares, strip_b, strip_a,
    power_1, power_2, power_3, power_4, sums, ribbon,
    masked, eta_row, eta_col, eta_half, eta_up, cover, drag,
):
    layers = eta.shape[0]
    plane = own_planes(rhs, eta, friction, ice, grounded)
    below_and_above, above_and_below = beyond()
    lane = lax.broadcasted_iota(jnp.int32, (ROWS, LANES), 1)

    def target(p):
        if p < 2 * layers:
            return masked.at[p // layers, p % layers]
        if p < 3 * layers:
            return eta_up.at[p - 2 * layers]
        return cover if p == 3 * layers else drag

    strips = [jnp.zeros((ROWS, LANES), jnp.float32)] * ribbon.shape[0]
    for q in range(strip_a.shape[0] // 2):
        first, second = pair_of(q, layers)
        halves = ([], [])
        for half in range(2):
            from_a, from_b = strip_a[2 * q + half], strip_b[2 * q + half]
            halves[0].append(below_and_above(from_a, from_b))
            halves[1].append(pltpu.roll(above_and_below(from_a, from_b), HALO, 0))
        for p, halo in zip((first, second), halves):
            v = plane(p)
            dst = target(p)
            dst[0:ROWS, :] = v
            dst[ROWS:, 0:LANES], dst[ROWS:, LANES:] = halo
            ribbon_of(p, layers, *halo, lane, strips)
    for tile, v in enumerate(strips):
        ribbon[tile] = v

    moves = Moves()
    load = Tiles.load
    e = load(eta_up.at[0])
    for k in range(layers):
        pair = e + moves.row_next(e)
        (2.0 * pair).store(eta_row.at[0, k])
        (0.5 * pair).store(eta_row.at[1, k])
        pair = e + moves.col_next(e)
        (0.5 * pair).store(eta_col.at[0, k])
        (2.0 * pair).store(eta_col.at[1, k])
        (0.5 * e).store(eta_half.at[k])
        after = load(eta_up.at[k + 1]) if k + 1 < layers else None
        (e + after if k + 1 < layers else 0.0 * e).store(eta_up.at[k])
        e = after

    def apply(t, src, dst):
        def block(b, carry):
            g0, g1, below0, below1, odd, even = carry
            g0, g1, below0, below1 = Tiles(g0), Tiles(g1), Tiles(below0), Tiles(below1)
            odd, even = list(odd), list(even)
            m = load(cover)
            for i in range(UNROLL):
                k = b * UNROLL + i
                after = k + 1 if i + 1 < UNROLL else jnp.minimum(k + 1, layers - 1)
                next0, next1 = load(src.at[0, after]), load(src.at[1, after])
                e_up = load(eta_up.at[k])
                up0, up1 = e_up * (g0 - next0), e_up * (g1 - next1)
                pairs = [load(ref.at[c, k]) for ref in (eta_row, eta_col) for c in range(2)]
                out0, out1 = horizontal(g0, g1, *pairs, load(eta_half.at[k]), moves)
                out0, out1 = m * (out0 + (up0 - below0)), m * (out1 + (up1 - below1))
                for c, g, out in ((0, g0, out0), (1, g1, out1)):
                    if t < STEPS:
                        out.store(dst.at[c, k])
                    for half in range(2):
                        now = out.tiles[half]
                        if t == STEPS:
                            dst[c, k, :, half * LANES : (half + 1) * LANES] = now
                        odd[half] = odd[half] + g.tiles[half] * now
                        even[half] = even[half] + now * now
                g0, g1, below0, below1 = next0, next1, up0, up1
            return g0.tiles, g1.tiles, below0.tiles, below1.tiles, odd, even

        zero = [jnp.zeros((ROWS, LANES), jnp.float32)] * 2
        d = -1.0 * load(drag)
        g0, g1 = load(src.at[0, 0]), load(src.at[1, 0])
        start = (g0.tiles, g1.tiles, (d * g0).tiles, (d * g1).tiles, zero, zero)
        ends = lax.fori_loop(0, layers // UNROLL, block, start)[4:]
        return [jnp.concatenate(v, 1) for v in ends]

    outside = squares[1]
    sums[0] = squares[0]
    wide = lax.broadcasted_iota(jnp.int32, (ROWS, 2 * LANES), 1)
    inner = between(wide, HALO, 2 * LANES - 2 * HALO)
    fields = (masked, power_1, power_2, power_3, power_4)
    for t in range(1, STEPS + 1):
        odd, even = apply(t, fields[t - 1], fields[t])
        sums[2 * t - 1] = jnp.where(inner, odd, 0.0) + outside
        sums[2 * t] = jnp.where(inner, even, 0.0) + outside


def ribbon_kernel(own, halo, columns, columns_b, columns_a, sums, edges, moments):
    tiles = edges.shape[2]
    below_and_above, _ = beyond()
    lane = lax.broadcasted_iota(jnp.int32, (2 * ROWS, LANES), 1)

    count = columns.shape[0] // 2
    beside = [
        jnp.concatenate([columns[i], below_and_above(columns_a[i], columns_b[i])], 0) for i in range(2 * count)
    ]
    spot = lane % SLOT

    def whole(tile):
        group, at = packed_place(tile)
        right = jnp.where(between(spot, 8, HALO), turned(beside[group], 8 - at), jnp.concatenate([own[tile], halo[tile]], 0))
        return jnp.where(between(spot, 16, HALO), turned(beside[count + group], 16 - at), right)

    field = [[whole(c * tiles + n) for n in range(tiles)] for c in range(2)]
    eta = [whole(2 * tiles + n) for n in range(tiles)]
    cover, drag = whole(3 * tiles), whole(3 * tiles + 1)

    def after(v):
        return v[1:] + [turned(v[0], -SLOT)]

    eta_row = [2.0 * (e + row_next(e)) for e in eta]
    eta_col = [0.5 * (e + col_next(e)) for e in eta]
    eta_row_1, eta_col_1 = [0.25 * e for e in eta_row], [4.0 * e for e in eta_col]
    eta_half = [0.5 * e for e in eta]
    eta_up = [e + n for e, n in zip(eta, after(eta))]
    eta_up[-1] = jnp.where(lane < LANES - SLOT, eta_up[-1], 0.0)
    place = lax.broadcasted_iota(jnp.int32, (ROWS, LANES), 1) % SLOT
    edge = between(place, 4, HALO) | between(place, 20, HALO)
    extra = [None]
    for t in range(1, STEPS + 1):
        ups = [[u * (g - n) for u, g, n in zip(eta_up, field[c], after(field[c]))] for c in range(2)]
        result = ([], [])
        odd = even = jnp.zeros((ROWS, LANES), jnp.float32)
        for n in range(tiles):
            coefficients = (eta_row[n], eta_row_1[n], eta_col[n], eta_col_1[n], eta_half[n])
            outs = horizontal(field[0][n], field[1][n], *coefficients, Turns)
            for c in range(2):
                below = ups[c][n - 1] if n else turned(ups[c][-1], SLOT) - drag * field[c][0]
                out = cover * (outs[c] + (ups[c][n] - below))
                result[c].append(out)
                now = out[:ROWS]
                edges[t - 1, c, n] = now
                odd = odd + field[c][n][:ROWS] * now
                even = even + now * now
        field = result
        extra.extend([jnp.where(edge, odd, 0.0), jnp.where(edge, even, 0.0)])

    tall = lax.broadcasted_iota(jnp.int32, (2 * ROWS, LANES), 0)
    high = jnp.zeros((2 * ROWS, LANES), jnp.float32)
    low = jnp.zeros((2 * ROWS, LANES), jnp.float32)
    for j, more in enumerate(extra):
        total = sums[j]
        pair = two_sum(total[:, :LANES], total[:, LANES:])
        if more is not None:
            pair = join(pair, (more, jnp.zeros_like(more)))
        for step in (4, 2, 1):
            pair = join(pair, tuple(pltpu.roll(v, step, 0) for v in pair))
        high = jnp.where(tall == j, jnp.concatenate([pair[0]] * 2, 0), high)
        low = jnp.where(tall == j, jnp.concatenate([pair[1]] * 2, 0), low)
    total = (high, low)
    for step in (64, 32):
        total = join(total, tuple(pltpu.roll(v, step, 1) for v in total))
    group = lax.broadcasted_iota(jnp.int32, (ROWS, LANES), 1) // 32
    parts = [total[0][:ROWS], total[1][:ROWS], total[0][ROWS:], total[1][ROWS:]]
    moments[...] = jnp.where(
        group == 0, parts[0], jnp.where(group == 1, parts[1], jnp.where(group == 2, parts[2], parts[3]))
    )


def added(parts):
    terms = [(v, turned(v, -32)) for v in parts]
    return join(join(terms[0], terms[1]), join(terms[2], terms[3])) if len(terms) == 4 else join(*terms)


def add_kernel(*refs):
    *ins, out = refs
    high, low = added([x[...] for x in ins])
    lane = lax.broadcasted_iota(jnp.int32, (ROWS, LANES), 1)
    out[...] = jnp.where(lane % 64 < 32, high, turned(low, 32))


def solve(total):
    for step in (16, 8, 4, 2, 1):
        total = join(total, tuple(pltpu.roll(v, step, 1) for v in total))
    total = tuple(
        jnp.concatenate([jnp.broadcast_to(v[:, i : i + 1], (ROWS, LANES)) for i in (31, 95)], 0) for v in total
    )

    def spread(v, j):
        return jnp.broadcast_to(v[j : j + 1], (ROWS, LANES))

    centre, _ = cut(spread(total[0], 1) / spread(total[0], 0), 13)
    wide = jnp.concatenate([centre, centre], 0)
    mu = [spread(total[0] + total[1], 0)]
    for _ in range(2 * STEPS):
        step = times(wide, total)
        total = join(tuple(pltpu.roll(v, 2 * ROWS - 1, 0) for v in total), (-step[0], -step[1]))
        mu.append(spread(total[0] + total[1], 0))

    def plus(a, b):
        n = max(len(a), len(b))
        return [a[i] + b[i] if i < min(len(a), len(b)) else (a[i] if i < len(a) else b[i]) for i in range(n)]

    def scaled(s, a):
        return [s * x for x in a]

    def operator(a):
        return plus([centre * x for x in a], [jnp.zeros_like(centre)] + a)

    def dot(a, b):
        square = [None] * (len(a) + len(b) - 1)
        for i, x in enumerate(a):
            for j, y in enumerate(b):
                z = x * y
                square[i + j] = z if square[i + j] is None else square[i + j] + z
        value = square[0] * mu[0]
        for n in range(1, len(square)):
            value = value + square[n] * mu[n]
        return value

    one = jnp.ones_like(centre)
    right = [one]
    quasi, search, update, iterate = right, right, [], []
    applied = operator(search)
    carried = applied
    rho = mu[0]
    tau_sq = rho
    alpha = theta_sq = eta = None
    for half in range(STEPS):
        if half % 2 == 0:
            alpha = rho / dot(carried, right)
            search_next = plus(search, scaled(-alpha, carried))
        quasi = plus(quasi, scaled(-alpha, applied))
        if half:
            update = plus(search, scaled(theta_sq / alpha * eta, update))
        else:
            update = search
        theta_sq = dot(quasi, quasi) / tau_sq
        cosine_sq = 1.0 / (1.0 + theta_sq)
        tau_sq = tau_sq * theta_sq * cosine_sq
        eta = cosine_sq * alpha
        iterate = plus(iterate, scaled(eta, update))
        if half % 2 == 0:
            search = search_next
            applied = operator(search)
        elif half < STEPS - 1:
            rho_next = dot(quasi, right)
            beta = rho_next / rho
            search = plus(quasi, scaled(beta, search))
            applied_next = operator(search)
            carried = plus(applied_next, scaled(beta, plus(applied, scaled(beta, carried))))
            applied, rho = applied_next, rho_next
    powers = [iterate[-1]]
    for c in iterate[-2::-1]:
        powers = plus([c] + powers, scaled(-centre, powers))
    return powers


def final_kernel(rhs, power_1, power_2, power_3, power_4, edges, friction, ice, grounded, speed, *rest):
    *parts, iterate, residual, hessian = rest
    layers, tiles = rhs.shape[1], edges.shape[2]
    factors = solve(added([x[...] for x in parts]))
    powers = (power_1, power_2, power_3, power_4)
    wide = [jnp.concatenate([c, c], 1) for c in factors]
    rest = sum(wide[1:], wide[0])
    cover = ice[...].astype(jnp.float32)
    lane = lax.broadcasted_iota(jnp.int32, (ROWS, LANES), 1)

    def combined(vectors, weights):
        x = weights[1] * vectors[0]
        y = weights[0] * vectors[0]
        for t in range(1, STEPS):
            if t + 1 < STEPS:
                x = x + weights[t + 1] * vectors[t]
            y = y + weights[t] * vectors[t]
        return x, y

    for c in range(2):
        side = [combined([edges[t, c, n] for t in range(STEPS)], factors) for n in range(tiles)]
        for k in range(layers):
            at = k // tiles * SLOT
            inner = combined([p[c, k, :ROWS] for p in powers], wide)
            patched = []
            for v, e in zip(inner, side[k % tiles]):
                head = jnp.where(lane < HALO, turned(e, -at - 20), v[:, :LANES])
                tail = jnp.where(lane >= LANES - HALO, turned(e, 120 - at), v[:, LANES:])
                patched.append(jnp.concatenate([head, tail], 1))
            r = rhs[c, k]
            x, y = patched
            iterate[c, k] = jnp.where(cover > 0.0, wide[0] * r + x, rest * r)
            residual[c, k] = r - jnp.where(cover > 0.0, y, rest * r)
    weight = cover * (friction[...] * grounded[...].astype(jnp.float32))
    hessian[...] = weight * (speed[0] * iterate[0, 0] + speed[1] * iterate[1, 0])


def exchange(x, axis, order):
    count = lax.axis_size(axis)
    stride = 1
    rounds = []
    while stride < count:
        size = 4 if (count // stride) % 4 == 0 else 2
        rounds.append((stride, size))
        stride *= size
    for at, (stride, size) in enumerate(rounds):
        parts = [x]
        for turn in order if size == 4 else (1,):
            pairs = []
            for i in range(count):
                place = (i // stride) % size
                pairs.append((i, i + ((place ^ turn) - place) * stride))
            parts.append(lax.ppermute(x, axis, pairs))
        if at == len(rounds) - 1:
            return parts
        x = call(add_kernel, [x.shape])(*parts)[0]
    return [x]


def body(adjoint_rhs, viscosity, friction, ice_mask, grounded, basal_velocity):
    layers = viscosity.shape[0]
    inputs = (adjoint_rhs, viscosity, friction, ice_mask, grounded, basal_velocity)
    tile = (ROWS, LANES)
    strips = (2 * (layers + layers // 2 + 1),) + tile
    ribbons = ribbon_tiles(layers)
    packed = ((ribbons + 7) // 8,) + tile
    both = (2 * packed[0],) + tile
    *held, strip_a, strip_b = call(
        strip_kernel,
        [jax.ShapeDtypeStruct(x.shape, x.dtype) for x in inputs] + [strips, strips],
        [pltpu.SemaphoreType.DMA((len(inputs),))],
        in_specs=[pl.BlockSpec(memory_space=pltpu.HBM)] * len(inputs),
    )(*[pltpu.with_memory_space_constraint(x, pltpu.HBM) for x in inputs])
    strip_b, strip_a = swapped(strip_b, ("gx",), 1, "gz"), swapped(strip_a, ("gx",), 0)
    column_a, column_b = call(column_kernel, [packed, packed])(*held[:5])
    beside = ("gy", "gz")
    (columns,) = call(beside_kernel, [both])(swapped(column_a, beside, 0), swapped(column_b, beside, 1))
    columns_b, columns_a = swapped(columns, ("gx",), 1, "gz"), swapped(columns, ("gx",), 0)
    block = (layers, 2 * ROWS, 2 * LANES)
    own, squares = call(
        own_kernel,
        [(ribbons,) + tile, (2, ROWS, 2 * LANES)],
        in_specs=[pl.BlockSpec(memory_space=pl.ANY)] + [pl.BlockSpec(memory_space=pltpu.VMEM)] * 5,
    )(columns, *held[:5])
    *powers, sums, halo = call(
        main_kernel,
        [(2,) + block] * (STEPS - 1) + [adjoint_rhs.shape, (2 * STEPS + 1, ROWS, 2 * LANES), (ribbons,) + tile],
        [(2,) + block] * 3 + [block] * 2 + [block[1:]] * 2,
        cost_estimate=pl.CostEstimate(flops=200_000_000, bytes_accessed=8_000_000, transcendentals=0),
    )(*held[:5], squares, strip_b, strip_a)
    edges, sums = call(
        ribbon_kernel,
        [(STEPS, 2, layers // 4) + tile, tile],
    )(own, halo, columns, columns_b, columns_a, sums)
    parts = exchange(sums, ("gy", "gz"), (3, 2, 1))
    if len(parts) > 1:
        sums = call(add_kernel, [sums.shape])(*parts)[0]
    parts = exchange(sums, "gx", (1, 2, 3))
    rhs, _, friction, ice_mask, grounded, speed = held
    return tuple(
        call(final_kernel, [adjoint_rhs.shape, adjoint_rhs.shape, friction.shape])(
            rhs, *powers, edges, friction, ice_mask, grounded, speed, *parts
        )
    )


def solution(mesh):
    in_specs = (
        P(None, None, ("parts", "gx"), ("gy", "gz")),
        P(None, ("parts", "gx"), ("gy", "gz")),
        P(("parts", "gx"), ("gy", "gz")),
        P(("parts", "gx"), ("gy", "gz")),
        P(("parts", "gx"), ("gy", "gz")),
        P(None, ("parts", "gx"), ("gy", "gz")),
    )
    out_specs = (
        P(None, None, ("parts", "gx"), ("gy", "gz")),
        P(None, None, ("parts", "gx"), ("gy", "gz")),
        P(("parts", "gx"), ("gy", "gz")),
    )
    return jax.shard_map(body, mesh=mesh, in_specs=in_specs, out_specs=out_specs, check_vma=False)
```

```python
import functools

import jax
import jax.numpy as jnp
from jax import lax
from jax.experimental import pallas as pl
from jax.experimental.pallas import tpu as pltpu
from jax.sharding import PartitionSpec as P

STEPS = 4
HALO = 4
ROWS = 8
LANES = 128
UNROLL = 5
SLOT = 32


def call(kernel, outs, scratch=(), **more):
    return pl.pallas_call(
        kernel,
        out_shape=[jax.ShapeDtypeStruct(s, jnp.float32) if isinstance(s, tuple) else s for s in outs],
        scratch_shapes=[pltpu.VMEM(s, jnp.float32) if isinstance(s, tuple) else s for s in scratch],
        compiler_params=pltpu.CompilerParams(vmem_limit_bytes=40 * 1024 * 1024),
        **more,
    )


def place_of(axis):
    place, count = lax.axis_index(axis), lax.axis_size(axis)
    even = place % 2 == 0
    has_a = jnp.logical_or(jnp.logical_not(even), place < count - 1)
    has_b = jnp.where(even, place > 0, place < count - 1)
    return even, has_a, has_b


def swapped(x, axes, first, spare=None):
    count, others = lax.axis_size(axes), lax.axis_size(spare) if spare else 1
    pairs = []
    for at in range(others):
        for i in range(count):
            other, to = (i + 1 if (i - first) % 2 == 0 else i - 1), at
            if not 0 <= other < count:
                other, to = (i, at ^ 1) if spare else (count - 1 - i, at)
                if to >= others or count % 2:
                    other, to = i, at
            pairs.append((i * others + at, other * others + to))
    return lax.ppermute(x, (*axes, spare) if spare else axes, pairs)


def own_planes(rhs, eta, friction, ice, grounded):
    layers = eta.shape[0]
    cover = ice[...].astype(jnp.float32)
    drag = friction[...] * grounded[...].astype(jnp.float32)

    def plane(p):
        if p < 2 * layers:
            return rhs[p // layers, p % layers] * cover
        if p < 3 * layers:
            return eta[p - 2 * layers]
        return cover if p == 3 * layers else drag

    return plane


def pair_of(q, layers):
    if q < layers:
        return q, q + layers
    if q < layers + layers // 2:
        return q + layers, q + layers + layers // 2
    return 3 * layers, 3 * layers + 1


def ribbon_places(p, layers):
    tiles = layers // 4
    if p < 3 * layers:
        k = p % layers
        return p // layers * tiles + k % tiles, (k // tiles,)
    return (3 * tiles, (0, 1, 2, 3)) if p == 3 * layers else (3 * tiles + 1, (0,))


def ribbon_tiles(layers):
    return 3 * (layers // 4) + 2


def packed_place(tile):
    return tile // 8, HALO * (tile % 8)


def between(lane, first, width):
    return (lane >= first) & (lane < first + width)


def turned(v, shift):
    shift = shift % LANES
    return pltpu.roll(v, shift, 1) if shift else v


def strip_kernel(*refs):
    sources, held, (strip_a, strip_b, arrived) = refs[:6], refs[6:12], refs[12:]
    copies = [pltpu.make_async_copy(a, b, arrived.at[i]) for i, (a, b) in enumerate(zip(sources, held))]
    for copy in copies:
        copy.start()
    for copy in copies:
        copy.wait()
    rhs, eta, friction, ice, grounded, _ = held
    layers = eta.shape[0]
    plane = own_planes(rhs, eta, friction, ice, grounded)
    even, _, _ = place_of("gx")
    upper_a = (lax.broadcasted_iota(jnp.int32, (ROWS, LANES), 0) < HALO) != even
    for q in range(strip_a.shape[0] // 2):
        first, second = pair_of(q, layers)
        x, y = plane(first), plane(second)
        for half in range(2):
            xs = x[:, half * LANES : (half + 1) * LANES]
            ys = y[:, half * LANES : (half + 1) * LANES]
            ys = pltpu.roll(ys, HALO, 0)
            strip_a[2 * q + half] = jnp.where(upper_a, xs, ys)
            strip_b[2 * q + half] = jnp.where(upper_a, ys, xs)


def column_kernel(rhs, eta, friction, ice, grounded, column_a, column_b):
    layers = eta.shape[0]
    plane = own_planes(rhs, eta, friction, ice, grounded)
    lane = lax.broadcasted_iota(jnp.int32, (ROWS, LANES), 1)
    even, _, _ = place_of(("gy", "gz"))
    zero = jnp.zeros((ROWS, LANES), jnp.float32)
    to_left, to_right = [zero] * column_a.shape[0], [zero] * column_a.shape[0]
    for p in range(3 * layers + 2):
        v = plane(p)
        tile, slots = ribbon_places(p, layers)
        group, at = packed_place(tile)
        for slot in slots:
            here = between(lane, slot * SLOT + at, HALO)
            to_left[group] = jnp.where(here, turned(v[:, :LANES], slot * SLOT + at), to_left[group])
            to_right[group] = jnp.where(here, turned(v[:, LANES:], slot * SLOT + at + HALO), to_right[group])
    for group in range(column_a.shape[0]):
        column_a[group] = jnp.where(even, to_right[group], to_left[group])
        column_b[group] = jnp.where(even, to_left[group], to_right[group])


def beside_kernel(from_a, from_b, columns):
    even, has_a, has_b = place_of(("gy", "gz"))
    count = from_a.shape[0]
    for group in range(count):
        a = jnp.where(has_a, from_a[group], 0.0)
        b = jnp.where(has_b, from_b[group], 0.0)
        columns[group] = jnp.where(even, a, b)
        columns[count + group] = jnp.where(even, b, a)


def two_sum(a, b):
    s = a + b
    t = s - a
    return s, (a - (s - t)) + (b - t)


def join(x, y):
    s, e = two_sum(x[0], y[0])
    return s, e + (x[1] + y[1])


def cut(v, bits):
    t = v * (2.0**bits + 1.0)
    h = t - (t - v)
    return h, v - h


def times(scalar, x):
    high, low = cut(x[0], 12)
    return scalar * high, scalar * low + scalar * x[1]


def beyond():
    even, has_a, has_b = place_of("gx")
    upper_a = (lax.broadcasted_iota(jnp.int32, (ROWS, LANES), 0) < HALO) == even
    lower_a = jnp.logical_not(upper_a)

    def below_and_above(from_a, from_b):
        return jnp.where(upper_a & has_a, from_a, jnp.where(lower_a & has_b, from_b, 0.0))

    def above_and_below(from_a, from_b):
        return jnp.where(lower_a & has_a, from_a, jnp.where(upper_a & has_b, from_b, 0.0))

    return below_and_above, above_and_below


def row_next(v):
    return pltpu.roll(v, 2 * ROWS - 1, 0)


def row_prev(v):
    return pltpu.roll(v, 1, 0)


def col_next(v):
    return pltpu.roll(v, v.shape[1] - 1, 1)


def col_prev(v):
    return pltpu.roll(v, 1, 1)


def ribbon_of(p, layers, head, tail, lane, strips):
    tile, slots = ribbon_places(p, layers)
    for slot in slots:
        at = slot * SLOT
        strips[tile] = jnp.where(between(lane, at, 8), turned(tail, at + 8), strips[tile])
        strips[tile] = jnp.where(between(lane, at + 20, 8), turned(head, at + 20), strips[tile])


def own_kernel(_, rhs, eta, friction, ice, grounded, ribbon, squares):
    layers = eta.shape[0]
    plane = own_planes(rhs, eta, friction, ice, grounded)
    lane = lax.broadcasted_iota(jnp.int32, (ROWS, LANES), 1)
    strips = [jnp.zeros((ROWS, LANES), jnp.float32)] * ribbon.shape[0]
    for p in range(3 * layers + 2):
        v = plane(p)
        ribbon_of(p, layers, v[:, :LANES], v[:, LANES:], lane, strips)
    for tile, v in enumerate(strips):
        ribbon[tile] = v
    bare = 1.0 - ice[...].astype(jnp.float32)
    whole = jnp.zeros((ROWS, 2 * LANES), jnp.float32)
    outside = jnp.zeros((ROWS, 2 * LANES), jnp.float32)
    for c in range(2):
        for k in range(layers):
            square = rhs[c, k] * rhs[c, k]
            whole = whole + square
            outside = outside + bare * square
    squares[0], squares[1] = whole, outside


class Tiles:
    def __init__(self, tiles):
        self.tiles = tiles

    @staticmethod
    def load(ref):
        return Tiles([ref[r : r + ROWS, c : c + LANES] for r in (0, ROWS) for c in (0, LANES)])

    def store(self, ref):
        for v, (r, c) in zip(self.tiles, ((0, 0), (0, LANES), (ROWS, 0), (ROWS, LANES))):
            ref[r : r + ROWS, c : c + LANES] = v

    def both(self, other, op):
        if isinstance(other, Tiles):
            return Tiles([op(x, y) for x, y in zip(self.tiles, other.tiles)])
        return Tiles([op(x, other) for x in self.tiles])

    def __add__(self, other):
        return self.both(other, lambda x, y: x + y)

    def __sub__(self, other):
        return self.both(other, lambda x, y: x - y)

    def __mul__(self, other):
        return self.both(other, lambda x, y: x * y)

    __rmul__ = __mul__


class Moves:
    def __init__(self):
        row = lax.broadcasted_iota(jnp.int32, (ROWS, LANES), 0)
        lane = lax.broadcasted_iota(jnp.int32, (ROWS, LANES), 1)
        self.first_row, self.last_row = row == 0, row == ROWS - 1
        self.first_lane, self.last_lane = lane == 0, lane == LANES - 1

    def rows(self, v, shift, edge):
        own0, own1, halo0, halo1 = [pltpu.roll(x, shift, 0) for x in v.tiles]
        return Tiles(
            [
                jnp.where(edge, halo0, own0),
                jnp.where(edge, halo1, own1),
                jnp.where(edge, own0, halo0),
                jnp.where(edge, own1, halo1),
            ]
        )

    def row_next(self, v):
        return self.rows(v, ROWS - 1, self.last_row)

    def row_prev(self, v):
        return self.rows(v, 1, self.first_row)

    def col_next(self, v):
        own0, own1, halo0, halo1 = [pltpu.roll(x, LANES - 1, 1) for x in v.tiles]
        return Tiles([jnp.where(self.last_lane, own1, own0), own1, jnp.where(self.last_lane, halo1, halo0), halo1])

    def col_prev(self, v):
        own0, own1, halo0, halo1 = [pltpu.roll(x, 1, 1) for x in v.tiles]
        return Tiles([own0, jnp.where(self.first_lane, own0, own1), halo0, jnp.where(self.first_lane, halo0, halo1)])


class Turns:
    row_next = staticmethod(row_next)
    row_prev = staticmethod(row_prev)
    col_next = staticmethod(col_next)
    col_prev = staticmethod(col_prev)


def horizontal(g0, g1, e_row, e_row_1, e_col, e_col_1, e_half, moves):
    row_next, row_prev, col_next, col_prev = moves.row_next, moves.row_prev, moves.col_next, moves.col_prev
    g0n, g1n = row_next(g0), col_next(g1)
    f = e_half * (g1n - col_prev(g1))
    h = e_half * (g0n - row_prev(g0))
    flux = e_row * (g0 - g0n)
    out0 = flux - row_next(f) - row_prev(flux - f)
    flux = e_col * (g0 - col_next(g0))
    out0 = out0 + (flux - col_prev(flux))
    flux = e_col_1 * (g1 - g1n)
    out1 = flux - col_next(h) - col_prev(flux - h)
    flux = e_row_1 * (g1 - row_next(g1))
    out1 = out1 + (flux - row_prev(flux))
    return out0, out1


def main_kernel(
    rhs, eta, friction, ice, grounded, squares, strip_b, strip_a,
    power_1, power_2, power_3, power_4, sums, ribbon,
    masked, eta_row, eta_col, eta_half, eta_up, cover, drag,
):
    layers = eta.shape[0]
    plane = own_planes(rhs, eta, friction, ice, grounded)
    below_and_above, above_and_below = beyond()
    lane = lax.broadcasted_iota(jnp.int32, (ROWS, LANES), 1)

    def target(p):
        if p < 2 * layers:
            return masked.at[p // layers, p % layers]
        if p < 3 * layers:
            return eta_up.at[p - 2 * layers]
        return cover if p == 3 * layers else drag

    strips = [jnp.zeros((ROWS, LANES), jnp.float32)] * ribbon.shape[0]
    for q in range(strip_a.shape[0] // 2):
        first, second = pair_of(q, layers)
        halves = ([], [])
        for half in range(2):
            from_a, from_b = strip_a[2 * q + half], strip_b[2 * q + half]
            halves[0].append(below_and_above(from_a, from_b))
            halves[1].append(pltpu.roll(above_and_below(from_a, from_b), HALO, 0))
        for p, halo in zip((first, second), halves):
            v = plane(p)
            dst = target(p)
            dst[0:ROWS, :] = v
            dst[ROWS:, 0:LANES], dst[ROWS:, LANES:] = halo
            ribbon_of(p, layers, *halo, lane, strips)
    for tile, v in enumerate(strips):
        ribbon[tile] = v

    moves = Moves()
    load = Tiles.load
    e = load(eta_up.at[0])
    for k in range(layers):
        pair = e + moves.row_next(e)
        (2.0 * pair).store(eta_row.at[0, k])
        (0.5 * pair).store(eta_row.at[1, k])
        pair = e + moves.col_next(e)
        (0.5 * pair).store(eta_col.at[0, k])
        (2.0 * pair).store(eta_col.at[1, k])
        (0.5 * e).store(eta_half.at[k])
        after = load(eta_up.at[k + 1]) if k + 1 < layers else None
        (e + after if k + 1 < layers else 0.0 * e).store(eta_up.at[k])
        e = after

    def apply(t, src, dst):
        def block(b, carry):
            g0, g1, below0, below1, odd, even = carry
            g0, g1, below0, below1 = Tiles(g0), Tiles(g1), Tiles(below0), Tiles(below1)
            odd, even = list(odd), list(even)
            m = load(cover)
            for i in range(UNROLL):
                k = b * UNROLL + i
                after = k + 1 if i + 1 < UNROLL else jnp.minimum(k + 1, layers - 1)
                next0, next1 = load(src.at[0, after]), load(src.at[1, after])
                e_up = load(eta_up.at[k])
                up0, up1 = e_up * (g0 - next0), e_up * (g1 - next1)
                pairs = [load(ref.at[c, k]) for ref in (eta_row, eta_col) for c in range(2)]
                out0, out1 = horizontal(g0, g1, *pairs, load(eta_half.at[k]), moves)
                out0, out1 = m * (out0 + (up0 - below0)), m * (out1 + (up1 - below1))
                for c, g, out in ((0, g0, out0), (1, g1, out1)):
                    if t < STEPS:
                        out.store(dst.at[c, k])
                    for half in range(2):
                        now = out.tiles[half]
                        if t == STEPS:
                            dst[c, k, :, half * LANES : (half + 1) * LANES] = now
                        odd[half] = odd[half] + g.tiles[half] * now
                        even[half] = even[half] + now * now
                g0, g1, below0, below1 = next0, next1, up0, up1
            return g0.tiles, g1.tiles, below0.tiles, below1.tiles, odd, even

        zero = [jnp.zeros((ROWS, LANES), jnp.float32)] * 2
        d = -1.0 * load(drag)
        g0, g1 = load(src.at[0, 0]), load(src.at[1, 0])
        start = (g0.tiles, g1.tiles, (d * g0).tiles, (d * g1).tiles, zero, zero)
        ends = lax.fori_loop(0, layers // UNROLL, block, start)[4:]
        return [jnp.concatenate(v, 1) for v in ends]

    outside = squares[1]
    sums[0] = squares[0]
    wide = lax.broadcasted_iota(jnp.int32, (ROWS, 2 * LANES), 1)
    inner = between(wide, HALO, 2 * LANES - 2 * HALO)
    fields = (masked, power_1, power_2, power_3, power_4)
    for t in range(1, STEPS + 1):
        odd, even = apply(t, fields[t - 1], fields[t])
        sums[2 * t - 1] = jnp.where(inner, odd, 0.0) + outside
        sums[2 * t] = jnp.where(inner, even, 0.0) + outside


def ribbon_kernel(own, halo, columns, columns_b, columns_a, sums, edges, moments):
    tiles = edges.shape[2]
    below_and_above, _ = beyond()
    lane = lax.broadcasted_iota(jnp.int32, (2 * ROWS, LANES), 1)

    count = columns.shape[0] // 2
    beside = [
        jnp.concatenate([columns[i], below_and_above(columns_a[i], columns_b[i])], 0) for i in range(2 * count)
    ]
    spot = lane % SLOT

    def whole(tile):
        group, at = packed_place(tile)
        right = jnp.where(between(spot, 8, HALO), turned(beside[group], 8 - at), jnp.concatenate([own[tile], halo[tile]], 0))
        return jnp.where(between(spot, 16, HALO), turned(beside[count + group], 16 - at), right)

    field = [[whole(c * tiles + n) for n in range(tiles)] for c in range(2)]
    eta = [whole(2 * tiles + n) for n in range(tiles)]
    cover, drag = whole(3 * tiles), whole(3 * tiles + 1)

    def after(v):
        return v[1:] + [turned(v[0], -SLOT)]

    eta_row = [2.0 * (e + row_next(e)) for e in eta]
    eta_col = [0.5 * (e + col_next(e)) for e in eta]
    eta_row_1, eta_col_1 = [0.25 * e for e in eta_row], [4.0 * e for e in eta_col]
    eta_half = [0.5 * e for e in eta]
    eta_up = [e + n for e, n in zip(eta, after(eta))]
    eta_up[-1] = jnp.where(lane < LANES - SLOT, eta_up[-1], 0.0)
    place = lax.broadcasted_iota(jnp.int32, (ROWS, LANES), 1) % SLOT
    edge = between(place, 4, HALO) | between(place, 20, HALO)
    extra = [None]
    for t in range(1, STEPS + 1):
        ups = [[u * (g - n) for u, g, n in zip(eta_up, field[c], after(field[c]))] for c in range(2)]
        result = ([], [])
        odd = even = jnp.zeros((ROWS, LANES), jnp.float32)
        for n in range(tiles):
            coefficients = (eta_row[n], eta_row_1[n], eta_col[n], eta_col_1[n], eta_half[n])
            outs = horizontal(field[0][n], field[1][n], *coefficients, Turns)
            for c in range(2):
                below = ups[c][n - 1] if n else turned(ups[c][-1], SLOT) - drag * field[c][0]
                out = cover * (outs[c] + (ups[c][n] - below))
                result[c].append(out)
                now = out[:ROWS]
                edges[t - 1, c, n] = now
                odd = odd + field[c][n][:ROWS] * now
                even = even + now * now
        field = result
        extra.extend([jnp.where(edge, odd, 0.0), jnp.where(edge, even, 0.0)])

    tall = lax.broadcasted_iota(jnp.int32, (2 * ROWS, LANES), 0)
    high = jnp.zeros((2 * ROWS, LANES), jnp.float32)
    low = jnp.zeros((2 * ROWS, LANES), jnp.float32)
    for j, more in enumerate(extra):
        total = sums[j]
        pair = two_sum(total[:, :LANES], total[:, LANES:])
        if more is not None:
            pair = join(pair, (more, jnp.zeros_like(more)))
        for step in (4, 2, 1):
            pair = join(pair, tuple(pltpu.roll(v, step, 0) for v in pair))
        high = jnp.where(tall == j, jnp.concatenate([pair[0]] * 2, 0), high)
        low = jnp.where(tall == j, jnp.concatenate([pair[1]] * 2, 0), low)
    total = join((high, low), (pltpu.roll(high, 64, 1), pltpu.roll(low, 64, 1)))
    first = lax.broadcasted_iota(jnp.int32, (ROWS, LANES), 1) < 64
    for i, v in enumerate(total):
        moments[i] = jnp.where(first, v[:ROWS], v[ROWS:])


def added(terms):
    while len(terms) > 1:
        terms = [join(*terms[i : i + 2]) if i + 1 < len(terms) else terms[i] for i in range(0, len(terms), 2)]
    return terms[0]


def add_kernel(*refs):
    *ins, out = refs
    out[0], out[1] = added([(x[0], x[1]) for x in ins])


def solve(total):
    for unit in (8, 1):
        total = added([tuple(turned(v, unit * i) for v in total) for i in range(8)])

    def spread(j):
        row, lane = (j, 63) if j < ROWS else (j - ROWS, 127)
        return tuple(jnp.broadcast_to(v[row : row + 1, lane : lane + 1], (ROWS, LANES)) for v in total)

    table = [spread(j) for j in range(2 * STEPS + 1)]
    centre, _ = cut(table[1][0] / table[0][0], 13)
    mu = [sum(table[0])]
    while len(table) > 1:
        steps = [times(centre, x) for x in table[:-1]]
        table = [join(x, (-y[0], -y[1])) for x, y in zip(table[1:], steps)]
        mu.append(sum(table[0]))

    def plus(a, b):
        n = max(len(a), len(b))
        return [a[i] + b[i] if i < min(len(a), len(b)) else (a[i] if i < len(a) else b[i]) for i in range(n)]

    def scaled(s, a):
        return [s * x for x in a]

    def operator(a):
        return plus([centre * x for x in a], [jnp.zeros_like(centre)] + a)

    def dot(a, b):
        square = [None] * (len(a) + len(b) - 1)
        for i, x in enumerate(a):
            for j, y in enumerate(b):
                z = x * y
                square[i + j] = z if square[i + j] is None else square[i + j] + z
        value = square[0] * mu[0]
        for n in range(1, len(square)):
            value = value + square[n] * mu[n]
        return value

    one = jnp.ones_like(centre)
    right = [one]
    quasi, search, update, iterate = right, right, [], []
    applied = operator(search)
    carried = applied
    rho = mu[0]
    tau_sq = rho
    alpha = theta_sq = eta = None
    for half in range(STEPS):
        if half % 2 == 0:
            alpha = rho / dot(carried, right)
            search_next = plus(search, scaled(-alpha, carried))
        quasi = plus(quasi, scaled(-alpha, applied))
        if half:
            update = plus(search, scaled(theta_sq / alpha * eta, update))
        else:
            update = search
        theta_sq = dot(quasi, quasi) / tau_sq
        cosine_sq = 1.0 / (1.0 + theta_sq)
        tau_sq = tau_sq * theta_sq * cosine_sq
        eta = cosine_sq * alpha
        iterate = plus(iterate, scaled(eta, update))
        if half % 2 == 0:
            search = search_next
            applied = operator(search)
        elif half < STEPS - 1:
            rho_next = dot(quasi, right)
            beta = rho_next / rho
            search = plus(quasi, scaled(beta, search))
            applied_next = operator(search)
            carried = plus(applied_next, scaled(beta, plus(applied, scaled(beta, carried))))
            applied, rho = applied_next, rho_next
    powers = [iterate[-1]]
    for c in iterate[-2::-1]:
        powers = plus([c] + powers, scaled(-centre, powers))
    return powers


def final_kernel(rhs, power_1, power_2, power_3, power_4, edges, friction, ice, grounded, speed, *rest):
    *parts, iterate, residual, hessian = rest
    layers, tiles = rhs.shape[1], edges.shape[2]
    factors = solve(added([(x[0], x[1]) for x in parts]))
    powers = (power_1, power_2, power_3, power_4)
    wide = [jnp.concatenate([c, c], 1) for c in factors]
    rest = sum(wide[1:], wide[0])
    cover = ice[...].astype(jnp.float32)
    lane = lax.broadcasted_iota(jnp.int32, (ROWS, LANES), 1)

    def combined(vectors, weights):
        x = weights[1] * vectors[0]
        y = weights[0] * vectors[0]
        for t in range(1, STEPS):
            if t + 1 < STEPS:
                x = x + weights[t + 1] * vectors[t]
            y = y + weights[t] * vectors[t]
        return x, y

    for c in range(2):
        side = [combined([edges[t, c, n] for t in range(STEPS)], factors) for n in range(tiles)]
        for k in range(layers):
            at = k // tiles * SLOT
            inner = combined([p[c, k, :ROWS] for p in powers], wide)
            patched = []
            for v, e in zip(inner, side[k % tiles]):
                head = jnp.where(lane < HALO, turned(e, -at - 20), v[:, :LANES])
                tail = jnp.where(lane >= LANES - HALO, turned(e, 120 - at), v[:, LANES:])
                patched.append(jnp.concatenate([head, tail], 1))
            r = rhs[c, k]
            x, y = patched
            iterate[c, k] = jnp.where(cover > 0.0, wide[0] * r + x, rest * r)
            residual[c, k] = r - jnp.where(cover > 0.0, y, rest * r)
    weight = cover * (friction[...] * grounded[...].astype(jnp.float32))
    hessian[...] = weight * (speed[0] * iterate[0, 0] + speed[1] * iterate[1, 0])


def exchange(x, axis, order):
    count = lax.axis_size(axis)
    stride = 1
    rounds = []
    while stride < count:
        size = 4 if (count // stride) % 4 == 0 else 2
        rounds.append((stride, size))
        stride *= size
    for at, (stride, size) in enumerate(rounds):
        parts = [x]
        for turn in order if size == 4 else (1,):
            pairs = []
            for i in range(count):
                place = (i // stride) % size
                pairs.append((i, i + ((place ^ turn) - place) * stride))
            parts.append(lax.ppermute(x, axis, pairs))
        if at == len(rounds) - 1:
            return parts
        x = call(add_kernel, [x.shape])(*parts)[0]
    return [x]


def body(adjoint_rhs, viscosity, friction, ice_mask, grounded, basal_velocity):
    layers = viscosity.shape[0]
    inputs = (adjoint_rhs, viscosity, friction, ice_mask, grounded, basal_velocity)
    tile = (ROWS, LANES)
    strips = (2 * (layers + layers // 2 + 1),) + tile
    ribbons = ribbon_tiles(layers)
    packed = ((ribbons + 7) // 8,) + tile
    both = (2 * packed[0],) + tile
    *held, strip_a, strip_b = call(
        strip_kernel,
        [jax.ShapeDtypeStruct(x.shape, x.dtype) for x in inputs] + [strips, strips],
        [pltpu.SemaphoreType.DMA((len(inputs),))],
        in_specs=[pl.BlockSpec(memory_space=pltpu.HBM)] * len(inputs),
    )(*[pltpu.with_memory_space_constraint(x, pltpu.HBM) for x in inputs])
    strip_b, strip_a = swapped(strip_b, ("gx",), 1, "gz"), swapped(strip_a, ("gx",), 0)
    column_a, column_b = call(column_kernel, [packed, packed])(*held[:5])
    beside = ("gy", "gz")
    (columns,) = call(beside_kernel, [both])(swapped(column_a, beside, 0), swapped(column_b, beside, 1))
    columns_b, columns_a = swapped(columns, ("gx",), 1, "gz"), swapped(columns, ("gx",), 0)
    block = (layers, 2 * ROWS, 2 * LANES)
    own, squares = call(
        own_kernel,
        [(ribbons,) + tile, (2, ROWS, 2 * LANES)],
        in_specs=[pl.BlockSpec(memory_space=pl.ANY)] + [pl.BlockSpec(memory_space=pltpu.VMEM)] * 5,
    )(columns, *held[:5])
    *powers, sums, halo = call(
        main_kernel,
        [(2,) + block] * (STEPS - 1) + [adjoint_rhs.shape, (2 * STEPS + 1, ROWS, 2 * LANES), (ribbons,) + tile],
        [(2,) + block] * 3 + [block] * 2 + [block[1:]] * 2,
        cost_estimate=pl.CostEstimate(flops=200_000_000, bytes_accessed=8_000_000, transcendentals=0),
    )(*held[:5], squares, strip_b, strip_a)
    edges, sums = call(
        ribbon_kernel,
        [(STEPS, 2, layers // 4) + tile, (2,) + tile],
    )(own, halo, columns, columns_b, columns_a, sums)
    parts = exchange(sums, ("gy", "gz"), (3, 2, 1))
    if len(parts) > 1:
        sums = call(add_kernel, [sums.shape])(*parts)[0]
    parts = exchange(sums, "gx", (1, 2, 3))
    rhs, _, friction, ice_mask, grounded, speed = held
    return tuple(
        call(final_kernel, [adjoint_rhs.shape, adjoint_rhs.shape, friction.shape])(
            rhs, *powers, edges, friction, ice_mask, grounded, speed, *parts
        )
    )


def solution(mesh):
    in_specs = (
        P(None, None, ("parts", "gx"), ("gy", "gz")),
        P(None, ("parts", "gx"), ("gy", "gz")),
        P(("parts", "gx"), ("gy", "gz")),
        P(("parts", "gx"), ("gy", "gz")),
        P(("parts", "gx"), ("gy", "gz")),
        P(None, ("parts", "gx"), ("gy", "gz")),
    )
    out_specs = (
        P(None, None, ("parts", "gx"), ("gy", "gz")),
        P(None, None, ("parts", "gx"), ("gy", "gz")),
        P(("parts", "gx"), ("gy", "gz")),
    )
    return jax.shard_map(body, mesh=mesh, in_specs=in_specs, out_specs=out_specs, check_vma=False)
```

```python
import functools

import jax
import jax.numpy as jnp
from jax import lax
from jax.experimental import pallas as pl
from jax.experimental.pallas import tpu as pltpu
from jax.sharding import PartitionSpec as P

STEPS = 4
HALO = 4
ROWS = 8
LANES = 128
UNROLL = 5
SLOT = 32


def call(kernel, outs, scratch=(), **more):
    return pl.pallas_call(
        kernel,
        out_shape=[jax.ShapeDtypeStruct(s, jnp.float32) if isinstance(s, tuple) else s for s in outs],
        scratch_shapes=[pltpu.VMEM(s, jnp.float32) if isinstance(s, tuple) else s for s in scratch],
        compiler_params=pltpu.CompilerParams(vmem_limit_bytes=40 * 1024 * 1024),
        **more,
    )


def place_of(axis):
    place, count = lax.axis_index(axis), lax.axis_size(axis)
    even = place % 2 == 0
    has_a = jnp.logical_or(jnp.logical_not(even), place < count - 1)
    has_b = jnp.where(even, place > 0, place < count - 1)
    return even, has_a, has_b


def swapped(x, axes, first, spare=None):
    count, others = lax.axis_size(axes), lax.axis_size(spare) if spare else 1
    pairs = []
    for at in range(others):
        for i in range(count):
            other, to = (i + 1 if (i - first) % 2 == 0 else i - 1), at
            if not 0 <= other < count:
                other, to = (i, at ^ 1) if spare else (count - 1 - i, at)
                if to >= others or count % 2:
                    other, to = i, at
            pairs.append((i * others + at, other * others + to))
    return lax.ppermute(x, (*axes, spare) if spare else axes, pairs)


def own_planes(rhs, eta, friction, ice, grounded):
    layers = eta.shape[0]
    cover = ice[...].astype(jnp.float32)
    drag = friction[...] * grounded[...].astype(jnp.float32)

    def plane(p):
        if p < 2 * layers:
            return rhs[p // layers, p % layers] * cover
        if p < 3 * layers:
            return eta[p - 2 * layers]
        return cover if p == 3 * layers else drag

    return plane


def pair_of(q, layers):
    if q < layers:
        return q, q + layers
    if q < layers + layers // 2:
        return q + layers, q + layers + layers // 2
    return 3 * layers, 3 * layers + 1


def ribbon_places(p, layers):
    tiles = layers // 4
    if p < 3 * layers:
        k = p % layers
        return p // layers * tiles + k % tiles, (k // tiles,)
    return (3 * tiles, (0, 1, 2, 3)) if p == 3 * layers else (3 * tiles + 1, (0,))


def ribbon_tiles(layers):
    return 3 * (layers // 4) + 2


def packed_place(tile):
    return tile // 8, HALO * (tile % 8)


def between(lane, first, width):
    return (lane >= first) & (lane < first + width)


def turned(v, shift):
    shift = shift % LANES
    return pltpu.roll(v, shift, 1) if shift else v


def strip_kernel(*refs):
    sources, held, (strip_a, strip_b, arrived) = refs[:6], refs[6:12], refs[12:]
    copies = [pltpu.make_async_copy(a, b, arrived.at[i]) for i, (a, b) in enumerate(zip(sources, held))]
    for copy in copies:
        copy.start()
    for copy in copies:
        copy.wait()
    rhs, eta, friction, ice, grounded, _ = held
    layers = eta.shape[0]
    plane = own_planes(rhs, eta, friction, ice, grounded)
    even, _, _ = place_of("gx")
    upper_a = (lax.broadcasted_iota(jnp.int32, (ROWS, LANES), 0) < HALO) != even
    for q in range(strip_a.shape[0] // 2):
        first, second = pair_of(q, layers)
        x, y = plane(first), plane(second)
        for half in range(2):
            xs = x[:, half * LANES : (half + 1) * LANES]
            ys = y[:, half * LANES : (half + 1) * LANES]
            ys = pltpu.roll(ys, HALO, 0)
            strip_a[2 * q + half] = jnp.where(upper_a, xs, ys)
            strip_b[2 * q + half] = jnp.where(upper_a, ys, xs)


def column_kernel(rhs, eta, friction, ice, grounded, column_a, column_b):
    layers = eta.shape[0]
    plane = own_planes(rhs, eta, friction, ice, grounded)
    lane = lax.broadcasted_iota(jnp.int32, (ROWS, LANES), 1)
    even, _, _ = place_of(("gy", "gz"))
    zero = jnp.zeros((ROWS, LANES), jnp.float32)
    to_left, to_right = [zero] * column_a.shape[0], [zero] * column_a.shape[0]
    for p in range(3 * layers + 2):
        v = plane(p)
        tile, slots = ribbon_places(p, layers)
        group, at = packed_place(tile)
        for slot in slots:
            here = between(lane, slot * SLOT + at, HALO)
            to_left[group] = jnp.where(here, turned(v[:, :LANES], slot * SLOT + at), to_left[group])
            to_right[group] = jnp.where(here, turned(v[:, LANES:], slot * SLOT + at + HALO), to_right[group])
    for group in range(column_a.shape[0]):
        column_a[group] = jnp.where(even, to_right[group], to_left[group])
        column_b[group] = jnp.where(even, to_left[group], to_right[group])


def beside_kernel(from_a, from_b, columns):
    even, has_a, has_b = place_of(("gy", "gz"))
    count = from_a.shape[0]
    for group in range(count):
        a = jnp.where(has_a, from_a[group], 0.0)
        b = jnp.where(has_b, from_b[group], 0.0)
        columns[group] = jnp.where(even, a, b)
        columns[count + group] = jnp.where(even, b, a)


def two_sum(a, b):
    s = a + b
    t = s - a
    return s, (a - (s - t)) + (b - t)


def join(x, y):
    s, e = two_sum(x[0], y[0])
    return s, e + (x[1] + y[1])


def cut(v, bits):
    t = v * (2.0**bits + 1.0)
    h = t - (t - v)
    return h, v - h


def times(scalar, x):
    high, low = cut(x[0], 12)
    return scalar * high, scalar * low + scalar * x[1]


def beyond():
    even, has_a, has_b = place_of("gx")
    upper_a = (lax.broadcasted_iota(jnp.int32, (ROWS, LANES), 0) < HALO) == even
    lower_a = jnp.logical_not(upper_a)

    def below_and_above(from_a, from_b):
        return jnp.where(upper_a & has_a, from_a, jnp.where(lower_a & has_b, from_b, 0.0))

    def above_and_below(from_a, from_b):
        return jnp.where(lower_a & has_a, from_a, jnp.where(upper_a & has_b, from_b, 0.0))

    return below_and_above, above_and_below


def row_next(v):
    return pltpu.roll(v, 2 * ROWS - 1, 0)


def row_prev(v):
    return pltpu.roll(v, 1, 0)


def col_next(v):
    return pltpu.roll(v, v.shape[1] - 1, 1)


def col_prev(v):
    return pltpu.roll(v, 1, 1)


def ribbon_of(p, layers, head, tail, lane, strips):
    tile, slots = ribbon_places(p, layers)
    for slot in slots:
        at = slot * SLOT
        strips[tile] = jnp.where(between(lane, at, 8), turned(tail, at + 8), strips[tile])
        strips[tile] = jnp.where(between(lane, at + 20, 8), turned(head, at + 20), strips[tile])


def own_kernel(_, rhs, eta, friction, ice, grounded, ribbon, squares):
    layers = eta.shape[0]
    plane = own_planes(rhs, eta, friction, ice, grounded)
    lane = lax.broadcasted_iota(jnp.int32, (ROWS, LANES), 1)
    strips = [jnp.zeros((ROWS, LANES), jnp.float32)] * ribbon.shape[0]
    for p in range(3 * layers + 2):
        v = plane(p)
        ribbon_of(p, layers, v[:, :LANES], v[:, LANES:], lane, strips)
    for tile, v in enumerate(strips):
        ribbon[tile] = v
    bare = 1.0 - ice[...].astype(jnp.float32)
    whole = jnp.zeros((ROWS, 2 * LANES), jnp.float32)
    outside = jnp.zeros((ROWS, 2 * LANES), jnp.float32)
    for c in range(2):
        for k in range(layers):
            square = rhs[c, k] * rhs[c, k]
            whole = whole + square
            outside = outside + bare * square
    squares[0], squares[1] = whole, outside


class Tiles:
    def __init__(self, tiles):
        self.tiles = tiles

    @staticmethod
    def load(ref):
        return Tiles([ref[r : r + ROWS, c : c + LANES] for r in (0, ROWS) for c in (0, LANES)])

    def store(self, ref):
        for v, (r, c) in zip(self.tiles, ((0, 0), (0, LANES), (ROWS, 0), (ROWS, LANES))):
            ref[r : r + ROWS, c : c + LANES] = v

    def both(self, other, op):
        if isinstance(other, Tiles):
            return Tiles([op(x, y) for x, y in zip(self.tiles, other.tiles)])
        return Tiles([op(x, other) for x in self.tiles])

    def __add__(self, other):
        return self.both(other, lambda x, y: x + y)

    def __sub__(self, other):
        return self.both(other, lambda x, y: x - y)

    def __mul__(self, other):
        return self.both(other, lambda x, y: x * y)

    __rmul__ = __mul__


class Moves:
    def __init__(self):
        row = lax.broadcasted_iota(jnp.int32, (ROWS, LANES), 0)
        lane = lax.broadcasted_iota(jnp.int32, (ROWS, LANES), 1)
        self.first_row, self.last_row = row == 0, row == ROWS - 1
        self.first_lane, self.last_lane = lane == 0, lane == LANES - 1

    def rows(self, v, shift, edge):
        own0, own1, halo0, halo1 = [pltpu.roll(x, shift, 0) for x in v.tiles]
        return Tiles(
            [
                jnp.where(edge, halo0, own0),
                jnp.where(edge, halo1, own1),
                jnp.where(edge, own0, halo0),
                jnp.where(edge, own1, halo1),
            ]
        )

    def row_next(self, v):
        return self.rows(v, ROWS - 1, self.last_row)

    def row_prev(self, v):
        return self.rows(v, 1, self.first_row)

    def col_next(self, v):
        own0, own1, halo0, halo1 = [pltpu.roll(x, LANES - 1, 1) for x in v.tiles]
        return Tiles([jnp.where(self.last_lane, own1, own0), own1, jnp.where(self.last_lane, halo1, halo0), halo1])

    def col_prev(self, v):
        own0, own1, halo0, halo1 = [pltpu.roll(x, 1, 1) for x in v.tiles]
        return Tiles([own0, jnp.where(self.first_lane, own0, own1), halo0, jnp.where(self.first_lane, halo0, halo1)])


class Turns:
    row_next = staticmethod(row_next)
    row_prev = staticmethod(row_prev)
    col_next = staticmethod(col_next)
    col_prev = staticmethod(col_prev)


def horizontal(g0, g1, e_row, e_row_1, e_col, e_col_1, e_half, moves):
    row_next, row_prev, col_next, col_prev = moves.row_next, moves.row_prev, moves.col_next, moves.col_prev
    g0n, g1n = row_next(g0), col_next(g1)
    f = e_half * (g1n - col_prev(g1))
    h = e_half * (g0n - row_prev(g0))
    flux = e_row * (g0 - g0n)
    out0 = flux - row_next(f) - row_prev(flux - f)
    flux = e_col * (g0 - col_next(g0))
    out0 = out0 + (flux - col_prev(flux))
    flux = e_col_1 * (g1 - g1n)
    out1 = flux - col_next(h) - col_prev(flux - h)
    flux = e_row_1 * (g1 - row_next(g1))
    out1 = out1 + (flux - row_prev(flux))
    return out0, out1


def main_kernel(
    rhs, eta, friction, ice, grounded, squares, strip_b, strip_a,
    power_1, power_2, power_3, power_4, sums, ribbon,
    masked, eta_row, eta_col, eta_half, eta_up, cover, drag,
):
    layers = eta.shape[0]
    plane = own_planes(rhs, eta, friction, ice, grounded)
    below_and_above, above_and_below = beyond()
    lane = lax.broadcasted_iota(jnp.int32, (ROWS, LANES), 1)

    def target(p):
        if p < 2 * layers:
            return masked.at[p // layers, p % layers]
        if p < 3 * layers:
            return eta_up.at[p - 2 * layers]
        return cover if p == 3 * layers else drag

    strips = [jnp.zeros((ROWS, LANES), jnp.float32)] * ribbon.shape[0]
    for q in range(strip_a.shape[0] // 2):
        first, second = pair_of(q, layers)
        halves = ([], [])
        for half in range(2):
            from_a, from_b = strip_a[2 * q + half], strip_b[2 * q + half]
            halves[0].append(below_and_above(from_a, from_b))
            halves[1].append(pltpu.roll(above_and_below(from_a, from_b), HALO, 0))
        for p, halo in zip((first, second), halves):
            v = plane(p)
            dst = target(p)
            dst[0:ROWS, :] = v
            dst[ROWS:, 0:LANES], dst[ROWS:, LANES:] = halo
            ribbon_of(p, layers, *halo, lane, strips)
    for tile, v in enumerate(strips):
        ribbon[tile] = v

    moves = Moves()
    load = Tiles.load
    e = load(eta_up.at[0])
    for k in range(layers):
        pair = e + moves.row_next(e)
        (2.0 * pair).store(eta_row.at[0, k])
        (0.5 * pair).store(eta_row.at[1, k])
        pair = e + moves.col_next(e)
        (0.5 * pair).store(eta_col.at[0, k])
        (2.0 * pair).store(eta_col.at[1, k])
        (0.5 * e).store(eta_half.at[k])
        after = load(eta_up.at[k + 1]) if k + 1 < layers else None
        (e + after if k + 1 < layers else 0.0 * e).store(eta_up.at[k])
        e = after

    def apply(t, src, dst):
        def block(b, carry):
            g0, g1, below0, below1, odd, even = carry
            g0, g1, below0, below1 = Tiles(g0), Tiles(g1), Tiles(below0), Tiles(below1)
            odd, even = list(odd), list(even)
            m = load(cover)
            for i in range(UNROLL):
                k = b * UNROLL + i
                after = k + 1 if i + 1 < UNROLL else jnp.minimum(k + 1, layers - 1)
                next0, next1 = load(src.at[0, after]), load(src.at[1, after])
                e_up = load(eta_up.at[k])
                up0, up1 = e_up * (g0 - next0), e_up * (g1 - next1)
                pairs = [load(ref.at[c, k]) for ref in (eta_row, eta_col) for c in range(2)]
                out0, out1 = horizontal(g0, g1, *pairs, load(eta_half.at[k]), moves)
                out0, out1 = m * (out0 + (up0 - below0)), m * (out1 + (up1 - below1))
                for c, g, out in ((0, g0, out0), (1, g1, out1)):
                    if t < STEPS:
                        out.store(dst.at[c, k])
                    for half in range(2):
                        now = out.tiles[half]
                        if t == STEPS:
                            dst[c, k, :, half * LANES : (half + 1) * LANES] = now
                        odd[half] = odd[half] + g.tiles[half] * now
                        even[half] = even[half] + now * now
                g0, g1, below0, below1 = next0, next1, up0, up1
            return g0.tiles, g1.tiles, below0.tiles, below1.tiles, odd, even

        zero = [jnp.zeros((ROWS, LANES), jnp.float32)] * 2
        d = -1.0 * load(drag)
        g0, g1 = load(src.at[0, 0]), load(src.at[1, 0])
        start = (g0.tiles, g1.tiles, (d * g0).tiles, (d * g1).tiles, zero, zero)
        ends = lax.fori_loop(0, layers // UNROLL, block, start)[4:]
        return [jnp.concatenate(v, 1) for v in ends]

    outside = squares[1]
    sums[0] = squares[0]
    wide = lax.broadcasted_iota(jnp.int32, (ROWS, 2 * LANES), 1)
    inner = between(wide, HALO, 2 * LANES - 2 * HALO)
    fields = (masked, power_1, power_2, power_3, power_4)
    for t in range(1, STEPS + 1):
        odd, even = apply(t, fields[t - 1], fields[t])
        sums[2 * t - 1] = jnp.where(inner, odd, 0.0) + outside
        sums[2 * t] = jnp.where(inner, even, 0.0) + outside


def ribbon_kernel(own, halo, columns, columns_a, columns_b, sums, edges, moments):
    tiles = edges.shape[2]
    below_and_above, _ = beyond()
    lane = lax.broadcasted_iota(jnp.int32, (2 * ROWS, LANES), 1)

    count = columns.shape[0] // 2
    beside = [
        jnp.concatenate([columns[i], below_and_above(columns_a[i], columns_b[i])], 0) for i in range(2 * count)
    ]
    spot = lane % SLOT

    def whole(tile):
        group, at = packed_place(tile)
        right = jnp.where(between(spot, 8, HALO), turned(beside[group], 8 - at), jnp.concatenate([own[tile], halo[tile]], 0))
        return jnp.where(between(spot, 16, HALO), turned(beside[count + group], 16 - at), right)

    field = [[whole(c * tiles + n) for n in range(tiles)] for c in range(2)]
    eta = [whole(2 * tiles + n) for n in range(tiles)]
    cover, drag = whole(3 * tiles), whole(3 * tiles + 1)

    def after(v):
        return v[1:] + [turned(v[0], -SLOT)]

    eta_row = [2.0 * (e + row_next(e)) for e in eta]
    eta_col = [0.5 * (e + col_next(e)) for e in eta]
    eta_row_1, eta_col_1 = [0.25 * e for e in eta_row], [4.0 * e for e in eta_col]
    eta_half = [0.5 * e for e in eta]
    eta_up = [e + n for e, n in zip(eta, after(eta))]
    eta_up[-1] = jnp.where(lane < LANES - SLOT, eta_up[-1], 0.0)
    place = lax.broadcasted_iota(jnp.int32, (ROWS, LANES), 1) % SLOT
    edge = between(place, 4, HALO) | between(place, 20, HALO)
    extra = [None]
    for t in range(1, STEPS + 1):
        ups = [[u * (g - n) for u, g, n in zip(eta_up, field[c], after(field[c]))] for c in range(2)]
        result = ([], [])
        odd = even = jnp.zeros((ROWS, LANES), jnp.float32)
        for n in range(tiles):
            coefficients = (eta_row[n], eta_row_1[n], eta_col[n], eta_col_1[n], eta_half[n])
            outs = horizontal(field[0][n], field[1][n], *coefficients, Turns)
            for c in range(2):
                below = ups[c][n - 1] if n else turned(ups[c][-1], SLOT) - drag * field[c][0]
                out = cover * (outs[c] + (ups[c][n] - below))
                result[c].append(out)
                now = out[:ROWS]
                edges[t - 1, c, n] = now
                odd = odd + field[c][n][:ROWS] * now
                even = even + now * now
        field = result
        extra.extend([jnp.where(edge, odd, 0.0), jnp.where(edge, even, 0.0)])

    tall = lax.broadcasted_iota(jnp.int32, (2 * ROWS, LANES), 0)
    high = jnp.zeros((2 * ROWS, LANES), jnp.float32)
    low = jnp.zeros((2 * ROWS, LANES), jnp.float32)
    for j, more in enumerate(extra):
        total = sums[j]
        pair = two_sum(total[:, :LANES], total[:, LANES:])
        if more is not None:
            pair = join(pair, (more, jnp.zeros_like(more)))
        for step in (4, 2, 1):
            pair = join(pair, tuple(pltpu.roll(v, step, 0) for v in pair))
        high = jnp.where(tall == j, jnp.concatenate([pair[0]] * 2, 0), high)
        low = jnp.where(tall == j, jnp.concatenate([pair[1]] * 2, 0), low)
    total = join((high, low), (pltpu.roll(high, 64, 1), pltpu.roll(low, 64, 1)))
    first = lax.broadcasted_iota(jnp.int32, (ROWS, LANES), 1) < 64
    for i, v in enumerate(total):
        moments[i] = jnp.where(first, v[:ROWS], v[ROWS:])


def added(terms):
    while len(terms) > 1:
        terms = [join(*terms[i : i + 2]) if i + 1 < len(terms) else terms[i] for i in range(0, len(terms), 2)]
    return terms[0]


def add_kernel(*refs):
    *ins, out = refs
    out[0], out[1] = added([(x[0], x[1]) for x in ins])


def solve(total):
    for unit in (8, 1):
        total = added([tuple(turned(v, unit * i) for v in total) for i in range(8)])

    def spread(j):
        row, lane = (j, 63) if j < ROWS else (j - ROWS, 127)
        return tuple(jnp.broadcast_to(v[row : row + 1, lane : lane + 1], (ROWS, LANES)) for v in total)

    table = [spread(j) for j in range(2 * STEPS + 1)]
    centre, _ = cut(table[1][0] / table[0][0], 13)
    mu = [sum(table[0])]
    while len(table) > 1:
        steps = [times(centre, x) for x in table[:-1]]
        table = [join(x, (-y[0], -y[1])) for x, y in zip(table[1:], steps)]
        mu.append(sum(table[0]))

    def plus(a, b):
        n = max(len(a), len(b))
        return [a[i] + b[i] if i < min(len(a), len(b)) else (a[i] if i < len(a) else b[i]) for i in range(n)]

    def scaled(s, a):
        return [s * x for x in a]

    def operator(a):
        return plus([centre * x for x in a], [jnp.zeros_like(centre)] + a)

    def dot(a, b):
        square = [None] * (len(a) + len(b) - 1)
        for i, x in enumerate(a):
            for j, y in enumerate(b):
                z = x * y
                square[i + j] = z if square[i + j] is None else square[i + j] + z
        value = square[0] * mu[0]
        for n in range(1, len(square)):
            value = value + square[n] * mu[n]
        return value

    one = jnp.ones_like(centre)
    right = [one]
    quasi, search, update, iterate = right, right, [], []
    applied = operator(search)
    carried = applied
    rho = mu[0]
    tau_sq = rho
    alpha = theta_sq = eta = None
    for half in range(STEPS):
        if half % 2 == 0:
            alpha = rho / dot(carried, right)
            search_next = plus(search, scaled(-alpha, carried))
        quasi = plus(quasi, scaled(-alpha, applied))
        if half:
            update = plus(search, scaled(theta_sq / alpha * eta, update))
        else:
            update = search
        theta_sq = dot(quasi, quasi) / tau_sq
        cosine_sq = 1.0 / (1.0 + theta_sq)
        tau_sq = tau_sq * theta_sq * cosine_sq
        eta = cosine_sq * alpha
        iterate = plus(iterate, scaled(eta, update))
        if half % 2 == 0:
            search = search_next
            applied = operator(search)
        elif half < STEPS - 1:
            rho_next = dot(quasi, right)
            beta = rho_next / rho
            search = plus(quasi, scaled(beta, search))
            applied_next = operator(search)
            carried = plus(applied_next, scaled(beta, plus(applied, scaled(beta, carried))))
            applied, rho = applied_next, rho_next
    powers = [iterate[-1]]
    for c in iterate[-2::-1]:
        powers = plus([c] + powers, scaled(-centre, powers))
    return powers


def patch_kernel(_, rhs, ice, power_1, power_2, power_3, power_4, edges, vectors):
    layers, tiles = rhs.shape[1], edges.shape[2]
    covered = ice[...] > 0
    lane = lax.broadcasted_iota(jnp.int32, (ROWS, LANES), 1)
    for t, power in enumerate((power_1, power_2, power_3, power_4)):
        for c in range(2):
            for k in range(layers):
                e, at = edges[t, c, k % tiles], k // tiles * SLOT
                v = power[c, k, :ROWS]
                head = jnp.where(lane < HALO, turned(e, -at - 20), v[:, :LANES])
                tail = jnp.where(lane >= LANES - HALO, turned(e, 120 - at), v[:, LANES:])
                vectors[t, c, k] = jnp.where(covered, jnp.concatenate([head, tail], 1), rhs[c, k])


def final_kernel(rhs, vectors, friction, ice, grounded, speed, *rest):
    *parts, iterate, residual, hessian = rest
    layers = rhs.shape[1]
    wide = [jnp.concatenate([c, c], 1) for c in solve(added([(x[0], x[1]) for x in parts]))]
    for c in range(2):
        for k in range(layers):
            r = rhs[c, k]
            x, y = wide[0] * r, r
            for t in range(STEPS):
                v = vectors[t, c, k]
                if t + 1 < STEPS:
                    x = x + wide[t + 1] * v
                y = y - wide[t] * v
            iterate[c, k] = x
            residual[c, k] = y
    weight = ice[...].astype(jnp.float32) * (friction[...] * grounded[...].astype(jnp.float32))
    hessian[...] = weight * (speed[0] * iterate[0, 0] + speed[1] * iterate[1, 0])


def exchange(x, axis, order):
    count = lax.axis_size(axis)
    stride = 1
    rounds = []
    while stride < count:
        size = 4 if (count // stride) % 4 == 0 else 2
        rounds.append((stride, size))
        stride *= size
    for at, (stride, size) in enumerate(rounds):
        parts = [x]
        for turn in order if size == 4 else (1,):
            pairs = []
            for i in range(count):
                place = (i // stride) % size
                pairs.append((i, i + ((place ^ turn) - place) * stride))
            parts.append(lax.ppermute(x, axis, pairs))
        if at == len(rounds) - 1:
            return parts
        x = call(add_kernel, [x.shape])(*parts)[0]
    return [x]


def body(adjoint_rhs, viscosity, friction, ice_mask, grounded, basal_velocity):
    layers = viscosity.shape[0]
    inputs = (adjoint_rhs, viscosity, friction, ice_mask, grounded, basal_velocity)
    tile = (ROWS, LANES)
    strips = (2 * (layers + layers // 2 + 1),) + tile
    ribbons = ribbon_tiles(layers)
    packed = ((ribbons + 7) // 8,) + tile
    both = (2 * packed[0],) + tile
    *held, strip_a, strip_b = call(
        strip_kernel,
        [jax.ShapeDtypeStruct(x.shape, x.dtype) for x in inputs] + [strips, strips],
        [pltpu.SemaphoreType.DMA((len(inputs),))],
        in_specs=[pl.BlockSpec(memory_space=pltpu.HBM)] * len(inputs),
    )(*[pltpu.with_memory_space_constraint(x, pltpu.HBM) for x in inputs])
    strip_b, strip_a = swapped(strip_b, ("gx",), 1, "gz"), swapped(strip_a, ("gx",), 0)
    column_a, column_b = call(column_kernel, [packed, packed])(*held[:5])
    beside = ("gy", "gz")
    (columns,) = call(beside_kernel, [both])(swapped(column_a, beside, 0), swapped(column_b, beside, 1))
    columns_a, columns_b = swapped(columns, ("gx",), 0), swapped(columns, ("gx",), 1, "gz")
    block = (layers, 2 * ROWS, 2 * LANES)
    own, squares = call(
        own_kernel,
        [(ribbons,) + tile, (2, ROWS, 2 * LANES)],
        in_specs=[pl.BlockSpec(memory_space=pl.ANY)] + [pl.BlockSpec(memory_space=pltpu.VMEM)] * 5,
    )(columns, *held[:5])
    *powers, sums, halo = call(
        main_kernel,
        [(2,) + block] * (STEPS - 1) + [adjoint_rhs.shape, (2 * STEPS + 1, ROWS, 2 * LANES), (ribbons,) + tile],
        [(2,) + block] * 3 + [block] * 2 + [block[1:]] * 2,
        cost_estimate=pl.CostEstimate(flops=200_000_000, bytes_accessed=8_000_000, transcendentals=0),
    )(*held[:5], squares, strip_b, strip_a)
    edges, sums = call(
        ribbon_kernel,
        [(STEPS, 2, layers // 4) + tile, (2,) + tile],
    )(own, halo, columns, columns_a, columns_b, sums)
    parts = exchange(sums, ("gy", "gz"), (1, 2, 3))
    if len(parts) > 1:
        sums = call(add_kernel, [sums.shape])(*parts)[0]
    parts = exchange(sums, "gx", (1, 3, 2))
    rhs, _, friction, ice_mask, grounded, speed = held
    (vectors,) = call(
        patch_kernel,
        [(STEPS,) + adjoint_rhs.shape],
        in_specs=[pl.BlockSpec(memory_space=pl.ANY)] + [pl.BlockSpec(memory_space=pltpu.VMEM)] * 7,
    )(sums, rhs, ice_mask, *powers, edges)
    return tuple(
        call(final_kernel, [adjoint_rhs.shape, adjoint_rhs.shape, friction.shape])(
            rhs, vectors, friction, ice_mask, grounded, speed, *parts
        )
    )


def solution(mesh):
    in_specs = (
        P(None, None, ("parts", "gx"), ("gy", "gz")),
        P(None, ("parts", "gx"), ("gy", "gz")),
        P(("parts", "gx"), ("gy", "gz")),
        P(("parts", "gx"), ("gy", "gz")),
        P(("parts", "gx"), ("gy", "gz")),
        P(None, ("parts", "gx"), ("gy", "gz")),
    )
    out_specs = (
        P(None, None, ("parts", "gx"), ("gy", "gz")),
        P(None, None, ("parts", "gx"), ("gy", "gz")),
        P(("parts", "gx"), ("gy", "gz")),
    )
    return jax.shard_map(body, mesh=mesh, in_specs=in_specs, out_specs=out_specs, check_vma=False)
```

```python
import functools

import jax
import jax.numpy as jnp
from jax import lax
from jax.experimental import pallas as pl
from jax.experimental.pallas import tpu as pltpu
from jax.sharding import PartitionSpec as P

STEPS = 4
HALO = 4
ROWS = 8
LANES = 128
UNROLL = 4
SLOT = 32


def call(kernel, outs, scratch=(), **more):
    return pl.pallas_call(
        kernel,
        out_shape=[jax.ShapeDtypeStruct(s, jnp.float32) if isinstance(s, tuple) else s for s in outs],
        scratch_shapes=[pltpu.VMEM(s, jnp.float32) if isinstance(s, tuple) else s for s in scratch],
        compiler_params=pltpu.CompilerParams(vmem_limit_bytes=40 * 1024 * 1024),
        **more,
    )


def place_of(axis):
    place, count = lax.axis_index(axis), lax.axis_size(axis)
    even = place % 2 == 0
    has_a = jnp.logical_or(jnp.logical_not(even), place < count - 1)
    has_b = jnp.where(even, place > 0, place < count - 1)
    return even, has_a, has_b


def swapped(x, axes, first, spare=None):
    count, others = lax.axis_size(axes), lax.axis_size(spare) if spare else 1
    pairs = []
    for at in range(others):
        for i in range(count):
            other, to = (i + 1 if (i - first) % 2 == 0 else i - 1), at
            if not 0 <= other < count:
                other, to = (i, at ^ 1) if spare else (count - 1 - i, at)
                if to >= others or count % 2:
                    other, to = i, at
            pairs.append((i * others + at, other * others + to))
    return lax.ppermute(x, (*axes, spare) if spare else axes, pairs)


def own_planes(rhs, eta, friction, ice, grounded):
    layers = eta.shape[0]
    cover = ice[...].astype(jnp.float32)
    drag = friction[...] * grounded[...].astype(jnp.float32)

    def plane(p):
        if p < 2 * layers:
            return rhs[p // layers, p % layers] * cover
        if p < 3 * layers:
            return eta[p - 2 * layers]
        return cover if p == 3 * layers else drag

    return plane


def pair_of(q, layers):
    if q < layers:
        return q, q + layers
    if q < layers + layers // 2:
        return q + layers, q + layers + layers // 2
    return 3 * layers, 3 * layers + 1


def ribbon_places(p, layers):
    tiles = layers // 4
    if p < 3 * layers:
        k = p % layers
        return p // layers * tiles + k % tiles, (k // tiles,)
    return (3 * tiles, (0, 1, 2, 3)) if p == 3 * layers else (3 * tiles + 1, (0,))


def ribbon_tiles(layers):
    return 3 * (layers // 4) + 2


def packed_place(tile):
    return tile // 8, HALO * (tile % 8)


def between(lane, first, width):
    return (lane >= first) & (lane < first + width)


def turned(v, shift):
    shift = shift % LANES
    return pltpu.roll(v, shift, 1) if shift else v


def strip_kernel(*refs):
    sources, held, (strip_a, strip_b, arrived) = refs[:6], refs[6:12], refs[12:]
    copies = [pltpu.make_async_copy(a, b, arrived.at[i]) for i, (a, b) in enumerate(zip(sources, held))]
    for copy in copies:
        copy.start()
    for copy in copies:
        copy.wait()
    rhs, eta, friction, ice, grounded, _ = held
    layers = eta.shape[0]
    plane = own_planes(rhs, eta, friction, ice, grounded)
    even, _, _ = place_of("gx")
    upper_a = (lax.broadcasted_iota(jnp.int32, (ROWS, LANES), 0) < HALO) != even
    for q in range(strip_a.shape[0] // 2):
        first, second = pair_of(q, layers)
        x, y = plane(first), plane(second)
        for half in range(2):
            xs = x[:, half * LANES : (half + 1) * LANES]
            ys = y[:, half * LANES : (half + 1) * LANES]
            ys = pltpu.roll(ys, HALO, 0)
            strip_a[2 * q + half] = jnp.where(upper_a, xs, ys)
            strip_b[2 * q + half] = jnp.where(upper_a, ys, xs)


def column_kernel(rhs, eta, friction, ice, grounded, column_a, column_b):
    layers = eta.shape[0]
    plane = own_planes(rhs, eta, friction, ice, grounded)
    lane = lax.broadcasted_iota(jnp.int32, (ROWS, LANES), 1)
    even, _, _ = place_of(("gy", "gz"))
    zero = jnp.zeros((ROWS, LANES), jnp.float32)
    to_left, to_right = [zero] * column_a.shape[0], [zero] * column_a.shape[0]
    for p in range(3 * layers + 2):
        v = plane(p)
        tile, slots = ribbon_places(p, layers)
        group, at = packed_place(tile)
        for slot in slots:
            here = between(lane, slot * SLOT + at, HALO)
            to_left[group] = jnp.where(here, turned(v[:, :LANES], slot * SLOT + at), to_left[group])
            to_right[group] = jnp.where(here, turned(v[:, LANES:], slot * SLOT + at + HALO), to_right[group])
    for group in range(column_a.shape[0]):
        column_a[group] = jnp.where(even, to_right[group], to_left[group])
        column_b[group] = jnp.where(even, to_left[group], to_right[group])


def beside_kernel(from_a, from_b, columns):
    even, has_a, has_b = place_of(("gy", "gz"))
    count = from_a.shape[0]
    for group in range(count):
        a = jnp.where(has_a, from_a[group], 0.0)
        b = jnp.where(has_b, from_b[group], 0.0)
        columns[group] = jnp.where(even, a, b)
        columns[count + group] = jnp.where(even, b, a)


def two_sum(a, b):
    s = a + b
    t = s - a
    return s, (a - (s - t)) + (b - t)


def join(x, y):
    s, e = two_sum(x[0], y[0])
    return s, e + (x[1] + y[1])


def cut(v, bits):
    t = v * (2.0**bits + 1.0)
    h = t - (t - v)
    return h, v - h


def times(scalar, x):
    high, low = cut(x[0], 12)
    return scalar * high, scalar * low + scalar * x[1]


def beyond():
    even, has_a, has_b = place_of("gx")
    upper_a = (lax.broadcasted_iota(jnp.int32, (ROWS, LANES), 0) < HALO) == even
    lower_a = jnp.logical_not(upper_a)

    def below_and_above(from_a, from_b):
        return jnp.where(upper_a & has_a, from_a, jnp.where(lower_a & has_b, from_b, 0.0))

    def above_and_below(from_a, from_b):
        return jnp.where(lower_a & has_a, from_a, jnp.where(upper_a & has_b, from_b, 0.0))

    return below_and_above, above_and_below


def row_next(v):
    return pltpu.roll(v, 2 * ROWS - 1, 0)


def row_prev(v):
    return pltpu.roll(v, 1, 0)


def col_next(v):
    return pltpu.roll(v, v.shape[1] - 1, 1)


def col_prev(v):
    return pltpu.roll(v, 1, 1)


def ribbon_of(p, layers, head, tail, lane, strips):
    tile, slots = ribbon_places(p, layers)
    for slot in slots:
        at = slot * SLOT
        strips[tile] = jnp.where(between(lane, at, 8), turned(tail, at + 8), strips[tile])
        strips[tile] = jnp.where(between(lane, at + 20, 8), turned(head, at + 20), strips[tile])


def own_kernel(_, rhs, eta, friction, ice, grounded, ribbon, squares):
    layers = eta.shape[0]
    plane = own_planes(rhs, eta, friction, ice, grounded)
    lane = lax.broadcasted_iota(jnp.int32, (ROWS, LANES), 1)
    strips = [jnp.zeros((ROWS, LANES), jnp.float32)] * ribbon.shape[0]
    for p in range(3 * layers + 2):
        v = plane(p)
        ribbon_of(p, layers, v[:, :LANES], v[:, LANES:], lane, strips)
    for tile, v in enumerate(strips):
        ribbon[tile] = v
    bare = 1.0 - ice[...].astype(jnp.float32)
    whole = jnp.zeros((ROWS, 2 * LANES), jnp.float32)
    outside = jnp.zeros((ROWS, 2 * LANES), jnp.float32)
    for c in range(2):
        for k in range(layers):
            square = rhs[c, k] * rhs[c, k]
            whole = whole + square
            outside = outside + bare * square
    squares[0], squares[1] = whole, outside


class Tiles:
    def __init__(self, tiles):
        self.tiles = tiles

    @staticmethod
    def load(ref):
        return Tiles([ref[r : r + ROWS, c : c + LANES] for r in (0, ROWS) for c in (0, LANES)])

    def store(self, ref):
        for v, (r, c) in zip(self.tiles, ((0, 0), (0, LANES), (ROWS, 0), (ROWS, LANES))):
            ref[r : r + ROWS, c : c + LANES] = v

    def both(self, other, op):
        if isinstance(other, Tiles):
            return Tiles([op(x, y) for x, y in zip(self.tiles, other.tiles)])
        return Tiles([op(x, other) for x in self.tiles])

    def __add__(self, other):
        return self.both(other, lambda x, y: x + y)

    def __sub__(self, other):
        return self.both(other, lambda x, y: x - y)

    def __mul__(self, other):
        return self.both(other, lambda x, y: x * y)

    __rmul__ = __mul__


class Moves:
    def __init__(self):
        row = lax.broadcasted_iota(jnp.int32, (ROWS, LANES), 0)
        lane = lax.broadcasted_iota(jnp.int32, (ROWS, LANES), 1)
        self.first_row, self.last_row = row == 0, row == ROWS - 1
        self.first_lane, self.last_lane = lane == 0, lane == LANES - 1

    def rows(self, v, shift, edge):
        own0, own1, halo0, halo1 = [pltpu.roll(x, shift, 0) for x in v.tiles]
        return Tiles(
            [
                jnp.where(edge, halo0, own0),
                jnp.where(edge, halo1, own1),
                jnp.where(edge, own0, halo0),
                jnp.where(edge, own1, halo1),
            ]
        )

    def row_next(self, v):
        return self.rows(v, ROWS - 1, self.last_row)

    def row_prev(self, v):
        return self.rows(v, 1, self.first_row)

    def col_next(self, v):
        own0, own1, halo0, halo1 = [pltpu.roll(x, LANES - 1, 1) for x in v.tiles]
        return Tiles([jnp.where(self.last_lane, own1, own0), own1, jnp.where(self.last_lane, halo1, halo0), halo1])

    def col_prev(self, v):
        own0, own1, halo0, halo1 = [pltpu.roll(x, 1, 1) for x in v.tiles]
        return Tiles([own0, jnp.where(self.first_lane, own0, own1), halo0, jnp.where(self.first_lane, halo0, halo1)])


class Turns:
    row_next = staticmethod(row_next)
    row_prev = staticmethod(row_prev)
    col_next = staticmethod(col_next)
    col_prev = staticmethod(col_prev)


def horizontal(g0, g1, e_row, e_row_1, e_col, e_col_1, e_half, moves):
    row_next, row_prev, col_next, col_prev = moves.row_next, moves.row_prev, moves.col_next, moves.col_prev
    g0n, g1n = row_next(g0), col_next(g1)
    f = e_half * (g1n - col_prev(g1))
    h = e_half * (g0n - row_prev(g0))
    flux = e_row * (g0 - g0n)
    out0 = flux - row_next(f) - row_prev(flux - f)
    flux = e_col * (g0 - col_next(g0))
    out0 = out0 + (flux - col_prev(flux))
    flux = e_col_1 * (g1 - g1n)
    out1 = flux - col_next(h) - col_prev(flux - h)
    flux = e_row_1 * (g1 - row_next(g1))
    out1 = out1 + (flux - row_prev(flux))
    return out0, out1


def main_kernel(
    rhs, eta, friction, ice, grounded, squares, strip_b, strip_a,
    power_1, power_2, power_3, power_4, sums, ribbon,
    masked, eta_row, eta_col, eta_half, eta_up, cover, drag,
):
    layers = eta.shape[0]
    plane = own_planes(rhs, eta, friction, ice, grounded)
    below_and_above, above_and_below = beyond()
    lane = lax.broadcasted_iota(jnp.int32, (ROWS, LANES), 1)

    def target(p):
        if p < 2 * layers:
            return masked.at[p // layers, p % layers]
        if p < 3 * layers:
            return eta_up.at[p - 2 * layers]
        return cover if p == 3 * layers else drag

    strips = [jnp.zeros((ROWS, LANES), jnp.float32)] * ribbon.shape[0]
    for q in range(strip_a.shape[0] // 2):
        first, second = pair_of(q, layers)
        halves = ([], [])
        for half in range(2):
            from_a, from_b = strip_a[2 * q + half], strip_b[2 * q + half]
            halves[0].append(below_and_above(from_a, from_b))
            halves[1].append(pltpu.roll(above_and_below(from_a, from_b), HALO, 0))
        for p, halo in zip((first, second), halves):
            v = plane(p)
            dst = target(p)
            dst[0:ROWS, :] = v
            dst[ROWS:, 0:LANES], dst[ROWS:, LANES:] = halo
            ribbon_of(p, layers, *halo, lane, strips)
    for tile, v in enumerate(strips):
        ribbon[tile] = v

    moves = Moves()
    load = Tiles.load
    e = load(eta_up.at[0])
    for k in range(layers):
        pair = e + moves.row_next(e)
        (2.0 * pair).store(eta_row.at[0, k])
        (0.5 * pair).store(eta_row.at[1, k])
        pair = e + moves.col_next(e)
        (0.5 * pair).store(eta_col.at[0, k])
        (2.0 * pair).store(eta_col.at[1, k])
        (0.5 * e).store(eta_half.at[k])
        after = load(eta_up.at[k + 1]) if k + 1 < layers else None
        (e + after if k + 1 < layers else 0.0 * e).store(eta_up.at[k])
        e = after

    def apply(t, src, dst):
        def block(b, carry):
            g0, g1, below0, below1, odd, even = carry
            g0, g1, below0, below1 = Tiles(g0), Tiles(g1), Tiles(below0), Tiles(below1)
            odd, even = list(odd), list(even)
            m = load(cover)
            for i in range(UNROLL):
                k = b * UNROLL + i
                after = k + 1 if i + 1 < UNROLL else jnp.minimum(k + 1, layers - 1)
                next0, next1 = load(src.at[0, after]), load(src.at[1, after])
                e_up = load(eta_up.at[k])
                up0, up1 = e_up * (g0 - next0), e_up * (g1 - next1)
                pairs = [load(ref.at[c, k]) for ref in (eta_row, eta_col) for c in range(2)]
                out0, out1 = horizontal(g0, g1, *pairs, load(eta_half.at[k]), moves)
                out0, out1 = m * (out0 + (up0 - below0)), m * (out1 + (up1 - below1))
                for c, g, out in ((0, g0, out0), (1, g1, out1)):
                    if t < STEPS:
                        out.store(dst.at[c, k])
                    for half in range(2):
                        now = out.tiles[half]
                        if t == STEPS:
                            dst[c, k, :, half * LANES : (half + 1) * LANES] = now
                        odd[half] = odd[half] + g.tiles[half] * now
                        even[half] = even[half] + now * now
                g0, g1, below0, below1 = next0, next1, up0, up1
            return g0.tiles, g1.tiles, below0.tiles, below1.tiles, odd, even

        zero = [jnp.zeros((ROWS, LANES), jnp.float32)] * 2
        d = -1.0 * load(drag)
        g0, g1 = load(src.at[0, 0]), load(src.at[1, 0])
        start = (g0.tiles, g1.tiles, (d * g0).tiles, (d * g1).tiles, zero, zero)
        ends = lax.fori_loop(0, layers // UNROLL, block, start)[4:]
        return [jnp.concatenate(v, 1) for v in ends]

    outside = squares[1]
    sums[0] = squares[0]
    wide = lax.broadcasted_iota(jnp.int32, (ROWS, 2 * LANES), 1)
    inner = between(wide, HALO, 2 * LANES - 2 * HALO)
    fields = (masked, power_1, power_2, power_3, power_4)
    for t in range(1, STEPS + 1):
        odd, even = apply(t, fields[t - 1], fields[t])
        sums[2 * t - 1] = jnp.where(inner, odd, 0.0) + outside
        sums[2 * t] = jnp.where(inner, even, 0.0) + outside


def ribbon_kernel(own, halo, columns, columns_a, columns_b, sums, edges, moments):
    tiles = edges.shape[2]
    below_and_above, _ = beyond()
    lane = lax.broadcasted_iota(jnp.int32, (2 * ROWS, LANES), 1)

    count = columns.shape[0] // 2
    beside = [
        jnp.concatenate([columns[i], below_and_above(columns_a[i], columns_b[i])], 0) for i in range(2 * count)
    ]
    spot = lane % SLOT

    def whole(tile):
        group, at = packed_place(tile)
        right = jnp.where(between(spot, 8, HALO), turned(beside[group], 8 - at), jnp.concatenate([own[tile], halo[tile]], 0))
        return jnp.where(between(spot, 16, HALO), turned(beside[count + group], 16 - at), right)

    field = [[whole(c * tiles + n) for n in range(tiles)] for c in range(2)]
    eta = [whole(2 * tiles + n) for n in range(tiles)]
    cover, drag = whole(3 * tiles), whole(3 * tiles + 1)

    def after(v):
        return v[1:] + [turned(v[0], -SLOT)]

    eta_row = [2.0 * (e + row_next(e)) for e in eta]
    eta_col = [0.5 * (e + col_next(e)) for e in eta]
    eta_row_1, eta_col_1 = [0.25 * e for e in eta_row], [4.0 * e for e in eta_col]
    eta_half = [0.5 * e for e in eta]
    eta_up = [e + n for e, n in zip(eta, after(eta))]
    eta_up[-1] = jnp.where(lane < LANES - SLOT, eta_up[-1], 0.0)
    place = lax.broadcasted_iota(jnp.int32, (ROWS, LANES), 1) % SLOT
    edge = between(place, 4, HALO) | between(place, 20, HALO)
    extra = [None]
    for t in range(1, STEPS + 1):
        ups = [[u * (g - n) for u, g, n in zip(eta_up, field[c], after(field[c]))] for c in range(2)]
        result = ([], [])
        odd = even = jnp.zeros((ROWS, LANES), jnp.float32)
        for n in range(tiles):
            coefficients = (eta_row[n], eta_row_1[n], eta_col[n], eta_col_1[n], eta_half[n])
            outs = horizontal(field[0][n], field[1][n], *coefficients, Turns)
            for c in range(2):
                below = ups[c][n - 1] if n else turned(ups[c][-1], SLOT) - drag * field[c][0]
                out = cover * (outs[c] + (ups[c][n] - below))
                result[c].append(out)
                now = out[:ROWS]
                edges[t - 1, c, n] = now
                odd = odd + field[c][n][:ROWS] * now
                even = even + now * now
        field = result
        extra.extend([jnp.where(edge, odd, 0.0), jnp.where(edge, even, 0.0)])

    tall = lax.broadcasted_iota(jnp.int32, (2 * ROWS, LANES), 0)
    high = jnp.zeros((2 * ROWS, LANES), jnp.float32)
    low = jnp.zeros((2 * ROWS, LANES), jnp.float32)
    for j, more in enumerate(extra):
        total = sums[j]
        pair = two_sum(total[:, :LANES], total[:, LANES:])
        if more is not None:
            pair = join(pair, (more, jnp.zeros_like(more)))
        for step in (4, 2, 1):
            pair = join(pair, tuple(pltpu.roll(v, step, 0) for v in pair))
        high = jnp.where(tall == j, jnp.concatenate([pair[0]] * 2, 0), high)
        low = jnp.where(tall == j, jnp.concatenate([pair[1]] * 2, 0), low)
    total = join((high, low), (pltpu.roll(high, 64, 1), pltpu.roll(low, 64, 1)))
    first = lax.broadcasted_iota(jnp.int32, (ROWS, LANES), 1) < 64
    for i, v in enumerate(total):
        moments[i] = jnp.where(first, v[:ROWS], v[ROWS:])


def added(terms):
    while len(terms) > 1:
        terms = [join(*terms[i : i + 2]) if i + 1 < len(terms) else terms[i] for i in range(0, len(terms), 2)]
    return terms[0]


def add_kernel(*refs):
    *ins, out = refs
    out[0], out[1] = added([(x[0], x[1]) for x in ins])


def solve(total):
    for unit in (8, 1):
        total = added([tuple(turned(v, unit * i) for v in total) for i in range(8)])

    def spread(j):
        row, lane = (j, 63) if j < ROWS else (j - ROWS, 127)
        return tuple(jnp.broadcast_to(v[row : row + 1, lane : lane + 1], (ROWS, LANES)) for v in total)

    table = [spread(j) for j in range(2 * STEPS + 1)]
    centre, _ = cut(table[1][0] / table[0][0], 13)
    mu = [sum(table[0])]
    while len(table) > 1:
        steps = [times(centre, x) for x in table[:-1]]
        table = [join(x, (-y[0], -y[1])) for x, y in zip(table[1:], steps)]
        mu.append(sum(table[0]))

    def plus(a, b):
        n = max(len(a), len(b))
        return [a[i] + b[i] if i < min(len(a), len(b)) else (a[i] if i < len(a) else b[i]) for i in range(n)]

    def scaled(s, a):
        return [s * x for x in a]

    def operator(a):
        return plus([centre * x for x in a], [jnp.zeros_like(centre)] + a)

    def dot(a, b):
        square = [None] * (len(a) + len(b) - 1)
        for i, x in enumerate(a):
            for j, y in enumerate(b):
                z = x * y
                square[i + j] = z if square[i + j] is None else square[i + j] + z
        value = square[0] * mu[0]
        for n in range(1, len(square)):
            value = value + square[n] * mu[n]
        return value

    one = jnp.ones_like(centre)
    right = [one]
    quasi, search, update, iterate = right, right, [], []
    applied = operator(search)
    carried = applied
    rho = mu[0]
    tau_sq = rho
    alpha = theta_sq = eta = None
    for half in range(STEPS):
        if half % 2 == 0:
            alpha = rho / dot(carried, right)
            search_next = plus(search, scaled(-alpha, carried))
        quasi = plus(quasi, scaled(-alpha, applied))
        if half:
            update = plus(search, scaled(theta_sq / alpha * eta, update))
        else:
            update = search
        theta_sq = dot(quasi, quasi) / tau_sq
        cosine_sq = 1.0 / (1.0 + theta_sq)
        tau_sq = tau_sq * theta_sq * cosine_sq
        eta = cosine_sq * alpha
        iterate = plus(iterate, scaled(eta, update))
        if half % 2 == 0:
            search = search_next
            applied = operator(search)
        elif half < STEPS - 1:
            rho_next = dot(quasi, right)
            beta = rho_next / rho
            search = plus(quasi, scaled(beta, search))
            applied_next = operator(search)
            carried = plus(applied_next, scaled(beta, plus(applied, scaled(beta, carried))))
            applied, rho = applied_next, rho_next
    powers = [iterate[-1]]
    for c in iterate[-2::-1]:
        powers = plus([c] + powers, scaled(-centre, powers))
    return powers


def patch_kernel(_, rhs, ice, power_1, power_2, power_3, power_4, edges, vectors):
    layers, tiles = rhs.shape[1], edges.shape[2]
    covered = ice[...] > 0
    lane = lax.broadcasted_iota(jnp.int32, (ROWS, LANES), 1)
    for t, power in enumerate((power_1, power_2, power_3, power_4)):
        for c in range(2):
            for k in range(layers):
                e, at = edges[t, c, k % tiles], k // tiles * SLOT
                v = power[c, k, :ROWS]
                head = jnp.where(lane < HALO, turned(e, -at - 20), v[:, :LANES])
                tail = jnp.where(lane >= LANES - HALO, turned(e, 120 - at), v[:, LANES:])
                vectors[t, c, k] = jnp.where(covered, jnp.concatenate([head, tail], 1), rhs[c, k])


def final_kernel(rhs, vectors, friction, ice, grounded, speed, *rest):
    *parts, iterate, residual, hessian = rest
    layers = rhs.shape[1]
    wide = [jnp.concatenate([c, c], 1) for c in solve(added([(x[0], x[1]) for x in parts]))]
    for c in range(2):
        for k in range(layers):
            r = rhs[c, k]
            x, y = wide[0] * r, r
            for t in range(STEPS):
                v = vectors[t, c, k]
                if t + 1 < STEPS:
                    x = x + wide[t + 1] * v
                y = y - wide[t] * v
            iterate[c, k] = x
            residual[c, k] = y
    weight = ice[...].astype(jnp.float32) * (friction[...] * grounded[...].astype(jnp.float32))
    hessian[...] = weight * (speed[0] * iterate[0, 0] + speed[1] * iterate[1, 0])


def exchange(x, axis, order):
    count = lax.axis_size(axis)
    stride = 1
    rounds = []
    while stride < count:
        size = 4 if (count // stride) % 4 == 0 else 2
        rounds.append((stride, size))
        stride *= size
    for at, (stride, size) in enumerate(rounds):
        parts = [x]
        for turn in order if size == 4 else (1,):
            pairs = []
            for i in range(count):
                place = (i // stride) % size
                pairs.append((i, i + ((place ^ turn) - place) * stride))
            parts.append(lax.ppermute(x, axis, pairs))
        if at == len(rounds) - 1:
            return parts
        x = call(add_kernel, [x.shape])(*parts)[0]
    return [x]


def body(adjoint_rhs, viscosity, friction, ice_mask, grounded, basal_velocity):
    layers = viscosity.shape[0]
    inputs = (adjoint_rhs, viscosity, friction, ice_mask, grounded, basal_velocity)
    tile = (ROWS, LANES)
    strips = (2 * (layers + layers // 2 + 1),) + tile
    ribbons = ribbon_tiles(layers)
    packed = ((ribbons + 7) // 8,) + tile
    both = (2 * packed[0],) + tile
    *held, strip_a, strip_b = call(
        strip_kernel,
        [jax.ShapeDtypeStruct(x.shape, x.dtype) for x in inputs] + [strips, strips],
        [pltpu.SemaphoreType.DMA((len(inputs),))],
        in_specs=[pl.BlockSpec(memory_space=pltpu.HBM)] * len(inputs),
    )(*[pltpu.with_memory_space_constraint(x, pltpu.HBM) for x in inputs])
    strip_b, strip_a = swapped(strip_b, ("gx",), 1, "gz"), swapped(strip_a, ("gx",), 0)
    column_a, column_b = call(column_kernel, [packed, packed])(*held[:5])
    beside = ("gy", "gz")
    (columns,) = call(beside_kernel, [both])(swapped(column_a, beside, 0), swapped(column_b, beside, 1))
    columns_a, columns_b = swapped(columns, ("gx",), 0), swapped(columns, ("gx",), 1, "gz")
    block = (layers, 2 * ROWS, 2 * LANES)
    own, squares = call(
        own_kernel,
        [(ribbons,) + tile, (2, ROWS, 2 * LANES)],
        in_specs=[pl.BlockSpec(memory_space=pl.ANY)] + [pl.BlockSpec(memory_space=pltpu.VMEM)] * 5,
    )(columns, *held[:5])
    *powers, sums, halo = call(
        main_kernel,
        [(2,) + block] * (STEPS - 1) + [adjoint_rhs.shape, (2 * STEPS + 1, ROWS, 2 * LANES), (ribbons,) + tile],
        [(2,) + block] * 3 + [block] * 2 + [block[1:]] * 2,
        cost_estimate=pl.CostEstimate(flops=200_000_000, bytes_accessed=8_000_000, transcendentals=0),
    )(*held[:5], squares, strip_b, strip_a)
    edges, sums = call(
        ribbon_kernel,
        [(STEPS, 2, layers // 4) + tile, (2,) + tile],
    )(own, halo, columns, columns_a, columns_b, sums)
    parts = exchange(sums, ("gy", "gz"), (1, 2, 3))
    if len(parts) > 1:
        sums = call(add_kernel, [sums.shape])(*parts)[0]
    parts = exchange(sums, "gx", (1, 3, 2))
    rhs, _, friction, ice_mask, grounded, speed = held
    (vectors,) = call(
        patch_kernel,
        [(STEPS,) + adjoint_rhs.shape],
        in_specs=[pl.BlockSpec(memory_space=pl.ANY)] + [pl.BlockSpec(memory_space=pltpu.VMEM)] * 7,
    )(sums, rhs, ice_mask, *powers, edges)
    return tuple(
        call(final_kernel, [adjoint_rhs.shape, adjoint_rhs.shape, friction.shape])(
            rhs, vectors, friction, ice_mask, grounded, speed, *parts
        )
    )


def solution(mesh):
    in_specs = (
        P(None, None, ("parts", "gx"), ("gy", "gz")),
        P(None, ("parts", "gx"), ("gy", "gz")),
        P(("parts", "gx"), ("gy", "gz")),
        P(("parts", "gx"), ("gy", "gz")),
        P(("parts", "gx"), ("gy", "gz")),
        P(None, ("parts", "gx"), ("gy", "gz")),
    )
    out_specs = (
        P(None, None, ("parts", "gx"), ("gy", "gz")),
        P(None, None, ("parts", "gx"), ("gy", "gz")),
        P(("parts", "gx"), ("gy", "gz")),
    )
    return jax.shard_map(body, mesh=mesh, in_specs=in_specs, out_specs=out_specs, check_vma=False)
```

```python
import functools

import jax
import jax.numpy as jnp
from jax import lax
from jax.experimental import pallas as pl
from jax.experimental.pallas import tpu as pltpu
from jax.sharding import PartitionSpec as P

STEPS = 4
HALO = 4
ROWS = 8
LANES = 128
UNROLL = 10
SLOT = 32


def call(kernel, outs, scratch=(), **more):
    return pl.pallas_call(
        kernel,
        out_shape=[jax.ShapeDtypeStruct(s, jnp.float32) if isinstance(s, tuple) else s for s in outs],
        scratch_shapes=[pltpu.VMEM(s, jnp.float32) if isinstance(s, tuple) else s for s in scratch],
        compiler_params=pltpu.CompilerParams(vmem_limit_bytes=40 * 1024 * 1024),
        **more,
    )


def place_of(axis):
    place, count = lax.axis_index(axis), lax.axis_size(axis)
    even = place % 2 == 0
    has_a = jnp.logical_or(jnp.logical_not(even), place < count - 1)
    has_b = jnp.where(even, place > 0, place < count - 1)
    return even, has_a, has_b


def swapped(x, axes, first, spare=None):
    count, others = lax.axis_size(axes), lax.axis_size(spare) if spare else 1
    pairs = []
    for at in range(others):
        for i in range(count):
            other, to = (i + 1 if (i - first) % 2 == 0 else i - 1), at
            if not 0 <= other < count:
                other, to = (i, at ^ 1) if spare else (count - 1 - i, at)
                if to >= others or count % 2:
                    other, to = i, at
            pairs.append((i * others + at, other * others + to))
    return lax.ppermute(x, (*axes, spare) if spare else axes, pairs)


def own_planes(rhs, eta, friction, ice, grounded):
    layers = eta.shape[0]
    cover = ice[...].astype(jnp.float32)
    drag = friction[...] * grounded[...].astype(jnp.float32)

    def plane(p):
        if p < 2 * layers:
            return rhs[p // layers, p % layers] * cover
        if p < 3 * layers:
            return eta[p - 2 * layers]
        return cover if p == 3 * layers else drag

    return plane


def pair_of(q, layers):
    if q < layers:
        return q, q + layers
    if q < layers + layers // 2:
        return q + layers, q + layers + layers // 2
    return 3 * layers, 3 * layers + 1


def ribbon_places(p, layers):
    tiles = layers // 4
    if p < 3 * layers:
        k = p % layers
        return p // layers * tiles + k % tiles, (k // tiles,)
    return (3 * tiles, (0, 1, 2, 3)) if p == 3 * layers else (3 * tiles + 1, (0,))


def ribbon_tiles(layers):
    return 3 * (layers // 4) + 2


def packed_place(tile):
    return tile // 8, HALO * (tile % 8)


def between(lane, first, width):
    return (lane >= first) & (lane < first + width)


def turned(v, shift):
    shift = shift % LANES
    return pltpu.roll(v, shift, 1) if shift else v


def strip_kernel(*refs):
    sources, held, (strip_a, strip_b, arrived) = refs[:6], refs[6:12], refs[12:]
    copies = [pltpu.make_async_copy(a, b, arrived.at[i]) for i, (a, b) in enumerate(zip(sources, held))]
    for copy in copies:
        copy.start()
    for copy in copies:
        copy.wait()
    rhs, eta, friction, ice, grounded, _ = held
    layers = eta.shape[0]
    plane = own_planes(rhs, eta, friction, ice, grounded)
    even, _, _ = place_of("gx")
    upper_a = (lax.broadcasted_iota(jnp.int32, (ROWS, LANES), 0) < HALO) != even
    for q in range(strip_a.shape[0] // 2):
        first, second = pair_of(q, layers)
        x, y = plane(first), plane(second)
        for half in range(2):
            xs = x[:, half * LANES : (half + 1) * LANES]
            ys = y[:, half * LANES : (half + 1) * LANES]
            ys = pltpu.roll(ys, HALO, 0)
            strip_a[2 * q + half] = jnp.where(upper_a, xs, ys)
            strip_b[2 * q + half] = jnp.where(upper_a, ys, xs)


def column_kernel(rhs, eta, friction, ice, grounded, column_a, column_b):
    layers = eta.shape[0]
    plane = own_planes(rhs, eta, friction, ice, grounded)
    lane = lax.broadcasted_iota(jnp.int32, (ROWS, LANES), 1)
    even, _, _ = place_of(("gy", "gz"))
    zero = jnp.zeros((ROWS, LANES), jnp.float32)
    to_left, to_right = [zero] * column_a.shape[0], [zero] * column_a.shape[0]
    for p in range(3 * layers + 2):
        v = plane(p)
        tile, slots = ribbon_places(p, layers)
        group, at = packed_place(tile)
        for slot in slots:
            here = between(lane, slot * SLOT + at, HALO)
            to_left[group] = jnp.where(here, turned(v[:, :LANES], slot * SLOT + at), to_left[group])
            to_right[group] = jnp.where(here, turned(v[:, LANES:], slot * SLOT + at + HALO), to_right[group])
    for group in range(column_a.shape[0]):
        column_a[group] = jnp.where(even, to_right[group], to_left[group])
        column_b[group] = jnp.where(even, to_left[group], to_right[group])


def beside_kernel(from_a, from_b, columns):
    even, has_a, has_b = place_of(("gy", "gz"))
    count = from_a.shape[0]
    for group in range(count):
        a = jnp.where(has_a, from_a[group], 0.0)
        b = jnp.where(has_b, from_b[group], 0.0)
        columns[group] = jnp.where(even, a, b)
        columns[count + group] = jnp.where(even, b, a)


def two_sum(a, b):
    s = a + b
    t = s - a
    return s, (a - (s - t)) + (b - t)


def join(x, y):
    s, e = two_sum(x[0], y[0])
    return s, e + (x[1] + y[1])


def cut(v, bits):
    t = v * (2.0**bits + 1.0)
    h = t - (t - v)
    return h, v - h


def times(scalar, x):
    high, low = cut(x[0], 12)
    return scalar * high, scalar * low + scalar * x[1]


def beyond():
    even, has_a, has_b = place_of("gx")
    upper_a = (lax.broadcasted_iota(jnp.int32, (ROWS, LANES), 0) < HALO) == even
    lower_a = jnp.logical_not(upper_a)

    def below_and_above(from_a, from_b):
        return jnp.where(upper_a & has_a, from_a, jnp.where(lower_a & has_b, from_b, 0.0))

    def above_and_below(from_a, from_b):
        return jnp.where(lower_a & has_a, from_a, jnp.where(upper_a & has_b, from_b, 0.0))

    return below_and_above, above_and_below


def row_next(v):
    return pltpu.roll(v, 2 * ROWS - 1, 0)


def row_prev(v):
    return pltpu.roll(v, 1, 0)


def col_next(v):
    return pltpu.roll(v, v.shape[1] - 1, 1)


def col_prev(v):
    return pltpu.roll(v, 1, 1)


def ribbon_of(p, layers, head, tail, lane, strips):
    tile, slots = ribbon_places(p, layers)
    for slot in slots:
        at = slot * SLOT
        strips[tile] = jnp.where(between(lane, at, 8), turned(tail, at + 8), strips[tile])
        strips[tile] = jnp.where(between(lane, at + 20, 8), turned(head, at + 20), strips[tile])


def own_kernel(_, rhs, eta, friction, ice, grounded, ribbon, squares):
    layers = eta.shape[0]
    plane = own_planes(rhs, eta, friction, ice, grounded)
    lane = lax.broadcasted_iota(jnp.int32, (ROWS, LANES), 1)
    strips = [jnp.zeros((ROWS, LANES), jnp.float32)] * ribbon.shape[0]
    for p in range(3 * layers + 2):
        v = plane(p)
        ribbon_of(p, layers, v[:, :LANES], v[:, LANES:], lane, strips)
    for tile, v in enumerate(strips):
        ribbon[tile] = v
    bare = 1.0 - ice[...].astype(jnp.float32)
    whole = jnp.zeros((ROWS, 2 * LANES), jnp.float32)
    outside = jnp.zeros((ROWS, 2 * LANES), jnp.float32)
    for c in range(2):
        for k in range(layers):
            square = rhs[c, k] * rhs[c, k]
            whole = whole + square
            outside = outside + bare * square
    squares[0], squares[1] = whole, outside


class Tiles:
    def __init__(self, tiles):
        self.tiles = tiles

    @staticmethod
    def load(ref):
        return Tiles([ref[r : r + ROWS, c : c + LANES] for r in (0, ROWS) for c in (0, LANES)])

    def store(self, ref):
        for v, (r, c) in zip(self.tiles, ((0, 0), (0, LANES), (ROWS, 0), (ROWS, LANES))):
            ref[r : r + ROWS, c : c + LANES] = v

    def both(self, other, op):
        if isinstance(other, Tiles):
            return Tiles([op(x, y) for x, y in zip(self.tiles, other.tiles)])
        return Tiles([op(x, other) for x in self.tiles])

    def __add__(self, other):
        return self.both(other, lambda x, y: x + y)

    def __sub__(self, other):
        return self.both(other, lambda x, y: x - y)

    def __mul__(self, other):
        return self.both(other, lambda x, y: x * y)

    __rmul__ = __mul__


class Moves:
    def __init__(self):
        row = lax.broadcasted_iota(jnp.int32, (ROWS, LANES), 0)
        lane = lax.broadcasted_iota(jnp.int32, (ROWS, LANES), 1)
        self.first_row, self.last_row = row == 0, row == ROWS - 1
        self.first_lane, self.last_lane = lane == 0, lane == LANES - 1

    def rows(self, v, shift, edge):
        own0, own1, halo0, halo1 = [pltpu.roll(x, shift, 0) for x in v.tiles]
        return Tiles(
            [
                jnp.where(edge, halo0, own0),
                jnp.where(edge, halo1, own1),
                jnp.where(edge, own0, halo0),
                jnp.where(edge, own1, halo1),
            ]
        )

    def row_next(self, v):
        return self.rows(v, ROWS - 1, self.last_row)

    def row_prev(self, v):
        return self.rows(v, 1, self.first_row)

    def col_next(self, v):
        own0, own1, halo0, halo1 = [pltpu.roll(x, LANES - 1, 1) for x in v.tiles]
        return Tiles([jnp.where(self.last_lane, own1, own0), own1, jnp.where(self.last_lane, halo1, halo0), halo1])

    def col_prev(self, v):
        own0, own1, halo0, halo1 = [pltpu.roll(x, 1, 1) for x in v.tiles]
        return Tiles([own0, jnp.where(self.first_lane, own0, own1), halo0, jnp.where(self.first_lane, halo0, halo1)])


class Turns:
    row_next = staticmethod(row_next)
    row_prev = staticmethod(row_prev)
    col_next = staticmethod(col_next)
    col_prev = staticmethod(col_prev)


def horizontal(g0, g1, e_row, e_row_1, e_col, e_col_1, e_half, moves):
    row_next, row_prev, col_next, col_prev = moves.row_next, moves.row_prev, moves.col_next, moves.col_prev
    g0n, g1n = row_next(g0), col_next(g1)
    f = e_half * (g1n - col_prev(g1))
    h = e_half * (g0n - row_prev(g0))
    flux = e_row * (g0 - g0n)
    out0 = flux - row_next(f) - row_prev(flux - f)
    flux = e_col * (g0 - col_next(g0))
    out0 = out0 + (flux - col_prev(flux))
    flux = e_col_1 * (g1 - g1n)
    out1 = flux - col_next(h) - col_prev(flux - h)
    flux = e_row_1 * (g1 - row_next(g1))
    out1 = out1 + (flux - row_prev(flux))
    return out0, out1


def main_kernel(
    rhs, eta, friction, ice, grounded, squares, strip_b, strip_a,
    power_1, power_2, power_3, power_4, sums, ribbon,
    masked, eta_row, eta_col, eta_half, eta_up, cover, drag,
):
    layers = eta.shape[0]
    plane = own_planes(rhs, eta, friction, ice, grounded)
    below_and_above, above_and_below = beyond()
    lane = lax.broadcasted_iota(jnp.int32, (ROWS, LANES), 1)

    def target(p):
        if p < 2 * layers:
            return masked.at[p // layers, p % layers]
        if p < 3 * layers:
            return eta_up.at[p - 2 * layers]
        return cover if p == 3 * layers else drag

    strips = [jnp.zeros((ROWS, LANES), jnp.float32)] * ribbon.shape[0]
    for q in range(strip_a.shape[0] // 2):
        first, second = pair_of(q, layers)
        halves = ([], [])
        for half in range(2):
            from_a, from_b = strip_a[2 * q + half], strip_b[2 * q + half]
            halves[0].append(below_and_above(from_a, from_b))
            halves[1].append(pltpu.roll(above_and_below(from_a, from_b), HALO, 0))
        for p, halo in zip((first, second), halves):
            v = plane(p)
            dst = target(p)
            dst[0:ROWS, :] = v
            dst[ROWS:, 0:LANES], dst[ROWS:, LANES:] = halo
            ribbon_of(p, layers, *halo, lane, strips)
    for tile, v in enumerate(strips):
        ribbon[tile] = v

    moves = Moves()
    load = Tiles.load
    e = load(eta_up.at[0])
    for k in range(layers):
        pair = e + moves.row_next(e)
        (2.0 * pair).store(eta_row.at[0, k])
        (0.5 * pair).store(eta_row.at[1, k])
        pair = e + moves.col_next(e)
        (0.5 * pair).store(eta_col.at[0, k])
        (2.0 * pair).store(eta_col.at[1, k])
        (0.5 * e).store(eta_half.at[k])
        after = load(eta_up.at[k + 1]) if k + 1 < layers else None
        (e + after if k + 1 < layers else 0.0 * e).store(eta_up.at[k])
        e = after

    def apply(t, src, dst):
        def block(b, carry):
            g0, g1, below0, below1, odd, even = carry
            g0, g1, below0, below1 = Tiles(g0), Tiles(g1), Tiles(below0), Tiles(below1)
            odd, even = list(odd), list(even)
            m = load(cover)
            for i in range(UNROLL):
                k = b * UNROLL + i
                after = k + 1 if i + 1 < UNROLL else jnp.minimum(k + 1, layers - 1)
                next0, next1 = load(src.at[0, after]), load(src.at[1, after])
                e_up = load(eta_up.at[k])
                up0, up1 = e_up * (g0 - next0), e_up * (g1 - next1)
                pairs = [load(ref.at[c, k]) for ref in (eta_row, eta_col) for c in range(2)]
                out0, out1 = horizontal(g0, g1, *pairs, load(eta_half.at[k]), moves)
                out0, out1 = m * (out0 + (up0 - below0)), m * (out1 + (up1 - below1))
                for c, g, out in ((0, g0, out0), (1, g1, out1)):
                    if t < STEPS:
                        out.store(dst.at[c, k])
                    for half in range(2):
                        now = out.tiles[half]
                        if t == STEPS:
                            dst[c, k, :, half * LANES : (half + 1) * LANES] = now
                        odd[half] = odd[half] + g.tiles[half] * now
                        even[half] = even[half] + now * now
                g0, g1, below0, below1 = next0, next1, up0, up1
            return g0.tiles, g1.tiles, below0.tiles, below1.tiles, odd, even

        zero = [jnp.zeros((ROWS, LANES), jnp.float32)] * 2
        d = -1.0 * load(drag)
        g0, g1 = load(src.at[0, 0]), load(src.at[1, 0])
        start = (g0.tiles, g1.tiles, (d * g0).tiles, (d * g1).tiles, zero, zero)
        ends = lax.fori_loop(0, layers // UNROLL, block, start)[4:]
        return [jnp.concatenate(v, 1) for v in ends]

    outside = squares[1]
    sums[0] = squares[0]
    wide = lax.broadcasted_iota(jnp.int32, (ROWS, 2 * LANES), 1)
    inner = between(wide, HALO, 2 * LANES - 2 * HALO)
    fields = (masked, power_1, power_2, power_3, power_4)
    for t in range(1, STEPS + 1):
        odd, even = apply(t, fields[t - 1], fields[t])
        sums[2 * t - 1] = jnp.where(inner, odd, 0.0) + outside
        sums[2 * t] = jnp.where(inner, even, 0.0) + outside


def ribbon_kernel(own, halo, columns, columns_a, columns_b, sums, edges, moments):
    tiles = edges.shape[2]
    below_and_above, _ = beyond()
    lane = lax.broadcasted_iota(jnp.int32, (2 * ROWS, LANES), 1)

    count = columns.shape[0] // 2
    beside = [
        jnp.concatenate([columns[i], below_and_above(columns_a[i], columns_b[i])], 0) for i in range(2 * count)
    ]
    spot = lane % SLOT

    def whole(tile):
        group, at = packed_place(tile)
        right = jnp.where(between(spot, 8, HALO), turned(beside[group], 8 - at), jnp.concatenate([own[tile], halo[tile]], 0))
        return jnp.where(between(spot, 16, HALO), turned(beside[count + group], 16 - at), right)

    field = [[whole(c * tiles + n) for n in range(tiles)] for c in range(2)]
    eta = [whole(2 * tiles + n) for n in range(tiles)]
    cover, drag = whole(3 * tiles), whole(3 * tiles + 1)

    def after(v):
        return v[1:] + [turned(v[0], -SLOT)]

    eta_row = [2.0 * (e + row_next(e)) for e in eta]
    eta_col = [0.5 * (e + col_next(e)) for e in eta]
    eta_row_1, eta_col_1 = [0.25 * e for e in eta_row], [4.0 * e for e in eta_col]
    eta_half = [0.5 * e for e in eta]
    eta_up = [e + n for e, n in zip(eta, after(eta))]
    eta_up[-1] = jnp.where(lane < LANES - SLOT, eta_up[-1], 0.0)
    place = lax.broadcasted_iota(jnp.int32, (ROWS, LANES), 1) % SLOT
    edge = between(place, 4, HALO) | between(place, 20, HALO)
    extra = [None]
    for t in range(1, STEPS + 1):
        ups = [[u * (g - n) for u, g, n in zip(eta_up, field[c], after(field[c]))] for c in range(2)]
        result = ([], [])
        odd = even = jnp.zeros((ROWS, LANES), jnp.float32)
        for n in range(tiles):
            coefficients = (eta_row[n], eta_row_1[n], eta_col[n], eta_col_1[n], eta_half[n])
            outs = horizontal(field[0][n], field[1][n], *coefficients, Turns)
            for c in range(2):
                below = ups[c][n - 1] if n else turned(ups[c][-1], SLOT) - drag * field[c][0]
                out = cover * (outs[c] + (ups[c][n] - below))
                result[c].append(out)
                now = out[:ROWS]
                edges[t - 1, c, n] = now
                odd = odd + field[c][n][:ROWS] * now
                even = even + now * now
        field = result
        extra.extend([jnp.where(edge, odd, 0.0), jnp.where(edge, even, 0.0)])

    tall = lax.broadcasted_iota(jnp.int32, (2 * ROWS, LANES), 0)
    high = jnp.zeros((2 * ROWS, LANES), jnp.float32)
    low = jnp.zeros((2 * ROWS, LANES), jnp.float32)
    for j, more in enumerate(extra):
        total = sums[j]
        pair = two_sum(total[:, :LANES], total[:, LANES:])
        if more is not None:
            pair = join(pair, (more, jnp.zeros_like(more)))
        for step in (4, 2, 1):
            pair = join(pair, tuple(pltpu.roll(v, step, 0) for v in pair))
        high = jnp.where(tall == j, jnp.concatenate([pair[0]] * 2, 0), high)
        low = jnp.where(tall == j, jnp.concatenate([pair[1]] * 2, 0), low)
    total = join((high, low), (pltpu.roll(high, 64, 1), pltpu.roll(low, 64, 1)))
    first = lax.broadcasted_iota(jnp.int32, (ROWS, LANES), 1) < 64
    for i, v in enumerate(total):
        moments[i] = jnp.where(first, v[:ROWS], v[ROWS:])


def added(terms):
    while len(terms) > 1:
        terms = [join(*terms[i : i + 2]) if i + 1 < len(terms) else terms[i] for i in range(0, len(terms), 2)]
    return terms[0]


def add_kernel(*refs):
    *ins, out = refs
    out[0], out[1] = added([(x[0], x[1]) for x in ins])


def solve(total):
    for unit in (8, 1):
        total = added([tuple(turned(v, unit * i) for v in total) for i in range(8)])

    def spread(j):
        row, lane = (j, 63) if j < ROWS else (j - ROWS, 127)
        return tuple(jnp.broadcast_to(v[row : row + 1, lane : lane + 1], (ROWS, LANES)) for v in total)

    table = [spread(j) for j in range(2 * STEPS + 1)]
    centre, _ = cut(table[1][0] / table[0][0], 13)
    mu = [sum(table[0])]
    while len(table) > 1:
        steps = [times(centre, x) for x in table[:-1]]
        table = [join(x, (-y[0], -y[1])) for x, y in zip(table[1:], steps)]
        mu.append(sum(table[0]))

    def plus(a, b):
        n = max(len(a), len(b))
        return [a[i] + b[i] if i < min(len(a), len(b)) else (a[i] if i < len(a) else b[i]) for i in range(n)]

    def scaled(s, a):
        return [s * x for x in a]

    def operator(a):
        return plus([centre * x for x in a], [jnp.zeros_like(centre)] + a)

    def dot(a, b):
        square = [None] * (len(a) + len(b) - 1)
        for i, x in enumerate(a):
            for j, y in enumerate(b):
                z = x * y
                square[i + j] = z if square[i + j] is None else square[i + j] + z
        value = square[0] * mu[0]
        for n in range(1, len(square)):
            value = value + square[n] * mu[n]
        return value

    one = jnp.ones_like(centre)
    right = [one]
    quasi, search, update, iterate = right, right, [], []
    applied = operator(search)
    carried = applied
    rho = mu[0]
    tau_sq = rho
    alpha = theta_sq = eta = None
    for half in range(STEPS):
        if half % 2 == 0:
            alpha = rho / dot(carried, right)
            search_next = plus(search, scaled(-alpha, carried))
        quasi = plus(quasi, scaled(-alpha, applied))
        if half:
            update = plus(search, scaled(theta_sq / alpha * eta, update))
        else:
            update = search
        theta_sq = dot(quasi, quasi) / tau_sq
        cosine_sq = 1.0 / (1.0 + theta_sq)
        tau_sq = tau_sq * theta_sq * cosine_sq
        eta = cosine_sq * alpha
        iterate = plus(iterate, scaled(eta, update))
        if half % 2 == 0:
            search = search_next
            applied = operator(search)
        elif half < STEPS - 1:
            rho_next = dot(quasi, right)
            beta = rho_next / rho
            search = plus(quasi, scaled(beta, search))
            applied_next = operator(search)
            carried = plus(applied_next, scaled(beta, plus(applied, scaled(beta, carried))))
            applied, rho = applied_next, rho_next
    powers = [iterate[-1]]
    for c in iterate[-2::-1]:
        powers = plus([c] + powers, scaled(-centre, powers))
    return powers


def patch_kernel(_, rhs, ice, power_1, power_2, power_3, power_4, edges, vectors):
    layers, tiles = rhs.shape[1], edges.shape[2]
    covered = ice[...] > 0
    lane = lax.broadcasted_iota(jnp.int32, (ROWS, LANES), 1)
    for t, power in enumerate((power_1, power_2, power_3, power_4)):
        for c in range(2):
            for k in range(layers):
                e, at = edges[t, c, k % tiles], k // tiles * SLOT
                v = power[c, k, :ROWS]
                head = jnp.where(lane < HALO, turned(e, -at - 20), v[:, :LANES])
                tail = jnp.where(lane >= LANES - HALO, turned(e, 120 - at), v[:, LANES:])
                vectors[t, c, k] = jnp.where(covered, jnp.concatenate([head, tail], 1), rhs[c, k])


def final_kernel(rhs, vectors, friction, ice, grounded, speed, *rest):
    *parts, iterate, residual, hessian = rest
    layers = rhs.shape[1]
    wide = [jnp.concatenate([c, c], 1) for c in solve(added([(x[0], x[1]) for x in parts]))]
    for c in range(2):
        for k in range(layers):
            r = rhs[c, k]
            x, y = wide[0] * r, r
            for t in range(STEPS):
                v = vectors[t, c, k]
                if t + 1 < STEPS:
                    x = x + wide[t + 1] * v
                y = y - wide[t] * v
            iterate[c, k] = x
            residual[c, k] = y
    weight = ice[...].astype(jnp.float32) * (friction[...] * grounded[...].astype(jnp.float32))
    hessian[...] = weight * (speed[0] * iterate[0, 0] + speed[1] * iterate[1, 0])


def exchange(x, axis, order):
    count = lax.axis_size(axis)
    stride = 1
    rounds = []
    while stride < count:
        size = 4 if (count // stride) % 4 == 0 else 2
        rounds.append((stride, size))
        stride *= size
    for at, (stride, size) in enumerate(rounds):
        parts = [x]
        for turn in order if size == 4 else (1,):
            pairs = []
            for i in range(count):
                place = (i // stride) % size
                pairs.append((i, i + ((place ^ turn) - place) * stride))
            parts.append(lax.ppermute(x, axis, pairs))
        if at == len(rounds) - 1:
            return parts
        x = call(add_kernel, [x.shape])(*parts)[0]
    return [x]


def body(adjoint_rhs, viscosity, friction, ice_mask, grounded, basal_velocity):
    layers = viscosity.shape[0]
    inputs = (adjoint_rhs, viscosity, friction, ice_mask, grounded, basal_velocity)
    tile = (ROWS, LANES)
    strips = (2 * (layers + layers // 2 + 1),) + tile
    ribbons = ribbon_tiles(layers)
    packed = ((ribbons + 7) // 8,) + tile
    both = (2 * packed[0],) + tile
    *held, strip_a, strip_b = call(
        strip_kernel,
        [jax.ShapeDtypeStruct(x.shape, x.dtype) for x in inputs] + [strips, strips],
        [pltpu.SemaphoreType.DMA((len(inputs),))],
        in_specs=[pl.BlockSpec(memory_space=pltpu.HBM)] * len(inputs),
    )(*[pltpu.with_memory_space_constraint(x, pltpu.HBM) for x in inputs])
    strip_b, strip_a = swapped(strip_b, ("gx",), 1, "gz"), swapped(strip_a, ("gx",), 0)
    column_a, column_b = call(column_kernel, [packed, packed])(*held[:5])
    beside = ("gy", "gz")
    (columns,) = call(beside_kernel, [both])(swapped(column_a, beside, 0), swapped(column_b, beside, 1))
    columns_a, columns_b = swapped(columns, ("gx",), 0), swapped(columns, ("gx",), 1, "gz")
    block = (layers, 2 * ROWS, 2 * LANES)
    own, squares = call(
        own_kernel,
        [(ribbons,) + tile, (2, ROWS, 2 * LANES)],
        in_specs=[pl.BlockSpec(memory_space=pl.ANY)] + [pl.BlockSpec(memory_space=pltpu.VMEM)] * 5,
    )(columns, *held[:5])
    *powers, sums, halo = call(
        main_kernel,
        [(2,) + block] * (STEPS - 1) + [adjoint_rhs.shape, (2 * STEPS + 1, ROWS, 2 * LANES), (ribbons,) + tile],
        [(2,) + block] * 3 + [block] * 2 + [block[1:]] * 2,
        cost_estimate=pl.CostEstimate(flops=200_000_000, bytes_accessed=8_000_000, transcendentals=0),
    )(*held[:5], squares, strip_b, strip_a)
    edges, sums = call(
        ribbon_kernel,
        [(STEPS, 2, layers // 4) + tile, (2,) + tile],
    )(own, halo, columns, columns_a, columns_b, sums)
    parts = exchange(sums, ("gy", "gz"), (1, 2, 3))
    if len(parts) > 1:
        sums = call(add_kernel, [sums.shape])(*parts)[0]
    parts = exchange(sums, "gx", (1, 3, 2))
    rhs, _, friction, ice_mask, grounded, speed = held
    (vectors,) = call(
        patch_kernel,
        [(STEPS,) + adjoint_rhs.shape],
        in_specs=[pl.BlockSpec(memory_space=pl.ANY)] + [pl.BlockSpec(memory_space=pltpu.VMEM)] * 7,
    )(sums, rhs, ice_mask, *powers, edges)
    return tuple(
        call(final_kernel, [adjoint_rhs.shape, adjoint_rhs.shape, friction.shape])(
            rhs, vectors, friction, ice_mask, grounded, speed, *parts
        )
    )


def solution(mesh):
    in_specs = (
        P(None, None, ("parts", "gx"), ("gy", "gz")),
        P(None, ("parts", "gx"), ("gy", "gz")),
        P(("parts", "gx"), ("gy", "gz")),
        P(("parts", "gx"), ("gy", "gz")),
        P(("parts", "gx"), ("gy", "gz")),
        P(None, ("parts", "gx"), ("gy", "gz")),
    )
    out_specs = (
        P(None, None, ("parts", "gx"), ("gy", "gz")),
        P(None, None, ("parts", "gx"), ("gy", "gz")),
        P(("parts", "gx"), ("gy", "gz")),
    )
    return jax.shard_map(body, mesh=mesh, in_specs=in_specs, out_specs=out_specs, check_vma=False)
```

```python
import functools

import jax
import jax.numpy as jnp
from jax import lax
from jax.experimental import pallas as pl
from jax.experimental.pallas import tpu as pltpu
from jax.sharding import PartitionSpec as P

STEPS = 4
HALO = 4
ROWS = 8
LANES = 128
UNROLL = 5
SLOT = 32


def call(kernel, outs, scratch=(), **more):
    return pl.pallas_call(
        kernel,
        out_shape=[jax.ShapeDtypeStruct(s, jnp.float32) if isinstance(s, tuple) else s for s in outs],
        scratch_shapes=[pltpu.VMEM(s, jnp.float32) if isinstance(s, tuple) else s for s in scratch],
        compiler_params=pltpu.CompilerParams(vmem_limit_bytes=40 * 1024 * 1024),
        **more,
    )


def place_of(axis):
    place, count = lax.axis_index(axis), lax.axis_size(axis)
    even = place % 2 == 0
    has_a = jnp.logical_or(jnp.logical_not(even), place < count - 1)
    has_b = jnp.where(even, place > 0, place < count - 1)
    return even, has_a, has_b


def swapped(x, axes, first, spare=None):
    count, others = lax.axis_size(axes), lax.axis_size(spare) if spare else 1
    pairs = []
    for at in range(others):
        for i in range(count):
            other, to = (i + 1 if (i - first) % 2 == 0 else i - 1), at
            if not 0 <= other < count:
                other, to = (i, at ^ 1) if spare else (count - 1 - i, at)
                if to >= others or count % 2:
                    other, to = i, at
            pairs.append((i * others + at, other * others + to))
    return lax.ppermute(x, (*axes, spare) if spare else axes, pairs)


def own_planes(rhs, eta, friction, ice, grounded):
    layers = eta.shape[0]
    cover = ice[...].astype(jnp.float32)
    drag = friction[...] * grounded[...].astype(jnp.float32)

    def plane(p):
        if p < 2 * layers:
            return rhs[p // layers, p % layers] * cover
        if p < 3 * layers:
            return eta[p - 2 * layers]
        return cover if p == 3 * layers else drag

    return plane


def pair_of(q, layers):
    if q < layers:
        return q, q + layers
    if q < layers + layers // 2:
        return q + layers, q + layers + layers // 2
    return 3 * layers, 3 * layers + 1


def ribbon_places(p, layers):
    tiles = layers // 4
    if p < 3 * layers:
        k = p % layers
        return p // layers * tiles + k % tiles, (k // tiles,)
    return (3 * tiles, (0, 1, 2, 3)) if p == 3 * layers else (3 * tiles + 1, (0,))


def ribbon_tiles(layers):
    return 3 * (layers // 4) + 2


def packed_place(tile):
    return tile // 8, HALO * (tile % 8)


def between(lane, first, width):
    return (lane >= first) & (lane < first + width)


def turned(v, shift):
    shift = shift % LANES
    return pltpu.roll(v, shift, 1) if shift else v


def strip_kernel(*refs):
    sources, held, (strip_a, strip_b, arrived) = refs[:6], refs[6:12], refs[12:]
    copies = [pltpu.make_async_copy(a, b, arrived.at[i]) for i, (a, b) in enumerate(zip(sources, held))]
    for copy in copies:
        copy.start()
    for copy in copies:
        copy.wait()
    rhs, eta, friction, ice, grounded, _ = held
    layers = eta.shape[0]
    plane = own_planes(rhs, eta, friction, ice, grounded)
    even, _, _ = place_of("gx")
    upper_a = (lax.broadcasted_iota(jnp.int32, (ROWS, LANES), 0) < HALO) != even
    for q in range(strip_a.shape[0] // 2):
        first, second = pair_of(q, layers)
        x, y = plane(first), plane(second)
        for half in range(2):
            xs = x[:, half * LANES : (half + 1) * LANES]
            ys = y[:, half * LANES : (half + 1) * LANES]
            ys = pltpu.roll(ys, HALO, 0)
            strip_a[2 * q + half] = jnp.where(upper_a, xs, ys)
            strip_b[2 * q + half] = jnp.where(upper_a, ys, xs)


def column_kernel(rhs, eta, friction, ice, grounded, column_a, column_b):
    layers = eta.shape[0]
    plane = own_planes(rhs, eta, friction, ice, grounded)
    lane = lax.broadcasted_iota(jnp.int32, (ROWS, LANES), 1)
    even, _, _ = place_of(("gy", "gz"))
    zero = jnp.zeros((ROWS, LANES), jnp.float32)
    to_left, to_right = [zero] * column_a.shape[0], [zero] * column_a.shape[0]
    for p in range(3 * layers + 2):
        v = plane(p)
        tile, slots = ribbon_places(p, layers)
        group, at = packed_place(tile)
        for slot in slots:
            here = between(lane, slot * SLOT + at, HALO)
            to_left[group] = jnp.where(here, turned(v[:, :LANES], slot * SLOT + at), to_left[group])
            to_right[group] = jnp.where(here, turned(v[:, LANES:], slot * SLOT + at + HALO), to_right[group])
    for group in range(column_a.shape[0]):
        column_a[group] = jnp.where(even, to_right[group], to_left[group])
        column_b[group] = jnp.where(even, to_left[group], to_right[group])


def beside_kernel(from_a, from_b, columns):
    even, has_a, has_b = place_of(("gy", "gz"))
    count = from_a.shape[0]
    for group in range(count):
        a = jnp.where(has_a, from_a[group], 0.0)
        b = jnp.where(has_b, from_b[group], 0.0)
        columns[group] = jnp.where(even, a, b)
        columns[count + group] = jnp.where(even, b, a)


def two_sum(a, b):
    s = a + b
    t = s - a
    return s, (a - (s - t)) + (b - t)


def join(x, y):
    s, e = two_sum(x[0], y[0])
    return s, e + (x[1] + y[1])


def cut(v, bits):
    t = v * (2.0**bits + 1.0)
    h = t - (t - v)
    return h, v - h


def times(scalar, x):
    high, low = cut(x[0], 12)
    return scalar * high, scalar * low + scalar * x[1]


def beyond():
    even, has_a, has_b = place_of("gx")
    upper_a = (lax.broadcasted_iota(jnp.int32, (ROWS, LANES), 0) < HALO) == even
    lower_a = jnp.logical_not(upper_a)

    def below_and_above(from_a, from_b):
        return jnp.where(upper_a & has_a, from_a, jnp.where(lower_a & has_b, from_b, 0.0))

    def above_and_below(from_a, from_b):
        return jnp.where(lower_a & has_a, from_a, jnp.where(upper_a & has_b, from_b, 0.0))

    return below_and_above, above_and_below


def row_next(v):
    return pltpu.roll(v, 2 * ROWS - 1, 0)


def row_prev(v):
    return pltpu.roll(v, 1, 0)


def col_next(v):
    return pltpu.roll(v, v.shape[1] - 1, 1)


def col_prev(v):
    return pltpu.roll(v, 1, 1)


def ribbon_of(p, layers, head, tail, lane, strips):
    tile, slots = ribbon_places(p, layers)
    for slot in slots:
        at = slot * SLOT
        strips[tile] = jnp.where(between(lane, at, 8), turned(tail, at + 8), strips[tile])
        strips[tile] = jnp.where(between(lane, at + 20, 8), turned(head, at + 20), strips[tile])


def own_kernel(_, rhs, eta, friction, ice, grounded, ribbon, squares):
    layers = eta.shape[0]
    plane = own_planes(rhs, eta, friction, ice, grounded)
    lane = lax.broadcasted_iota(jnp.int32, (ROWS, LANES), 1)
    strips = [jnp.zeros((ROWS, LANES), jnp.float32)] * ribbon.shape[0]
    for p in range(3 * layers + 2):
        v = plane(p)
        ribbon_of(p, layers, v[:, :LANES], v[:, LANES:], lane, strips)
    for tile, v in enumerate(strips):
        ribbon[tile] = v
    bare = 1.0 - ice[...].astype(jnp.float32)
    whole = jnp.zeros((ROWS, 2 * LANES), jnp.float32)
    outside = jnp.zeros((ROWS, 2 * LANES), jnp.float32)
    for c in range(2):
        for k in range(layers):
            square = rhs[c, k] * rhs[c, k]
            whole = whole + square
            outside = outside + bare * square
    squares[0], squares[1] = whole, outside


class Tiles:
    def __init__(self, tiles):
        self.tiles = tiles

    @staticmethod
    def load(ref):
        return Tiles([ref[r : r + ROWS, c : c + LANES] for r in (0, ROWS) for c in (0, LANES)])

    def store(self, ref):
        for v, (r, c) in zip(self.tiles, ((0, 0), (0, LANES), (ROWS, 0), (ROWS, LANES))):
            ref[r : r + ROWS, c : c + LANES] = v

    def both(self, other, op):
        if isinstance(other, Tiles):
            return Tiles([op(x, y) for x, y in zip(self.tiles, other.tiles)])
        return Tiles([op(x, other) for x in self.tiles])

    def __add__(self, other):
        return self.both(other, lambda x, y: x + y)

    def __sub__(self, other):
        return self.both(other, lambda x, y: x - y)

    def __mul__(self, other):
        return self.both(other, lambda x, y: x * y)

    __rmul__ = __mul__


class Moves:
    def __init__(self):
        row = lax.broadcasted_iota(jnp.int32, (ROWS, LANES), 0)
        lane = lax.broadcasted_iota(jnp.int32, (ROWS, LANES), 1)
        self.first_row, self.last_row = row == 0, row == ROWS - 1
        self.first_lane, self.last_lane = lane == 0, lane == LANES - 1

    def rows(self, v, shift, edge):
        own0, own1, halo0, halo1 = [pltpu.roll(x, shift, 0) for x in v.tiles]
        return Tiles(
            [
                jnp.where(edge, halo0, own0),
                jnp.where(edge, halo1, own1),
                jnp.where(edge, own0, halo0),
                jnp.where(edge, own1, halo1),
            ]
        )

    def row_next(self, v):
        return self.rows(v, ROWS - 1, self.last_row)

    def row_prev(self, v):
        return self.rows(v, 1, self.first_row)

    def col_next(self, v):
        own0, own1, halo0, halo1 = [pltpu.roll(x, LANES - 1, 1) for x in v.tiles]
        return Tiles([jnp.where(self.last_lane, own1, own0), own1, jnp.where(self.last_lane, halo1, halo0), halo1])

    def col_prev(self, v):
        own0, own1, halo0, halo1 = [pltpu.roll(x, 1, 1) for x in v.tiles]
        return Tiles([own0, jnp.where(self.first_lane, own0, own1), halo0, jnp.where(self.first_lane, halo0, halo1)])


class Turns:
    row_next = staticmethod(row_next)
    row_prev = staticmethod(row_prev)
    col_next = staticmethod(col_next)
    col_prev = staticmethod(col_prev)


def along(g0, g1, e_row, e_col, e_half, moves):
    f = e_half * (moves.col_next(g1) - moves.col_prev(g1))
    flux = e_row * (g0 - moves.row_next(g0))
    out = flux - moves.row_next(f) - moves.row_prev(flux - f)
    flux = e_col * (g0 - moves.col_next(g0))
    return out + (flux - moves.col_prev(flux))


def across(g0, g1, e_row, e_col, e_half, moves):
    h = e_half * (moves.row_next(g0) - moves.row_prev(g0))
    flux = e_col * (g1 - moves.col_next(g1))
    out = flux - moves.col_next(h) - moves.col_prev(flux - h)
    flux = e_row * (g1 - moves.row_next(g1))
    return out + (flux - moves.row_prev(flux))


def main_kernel(
    rhs, eta, friction, ice, grounded, squares, strip_b, strip_a,
    power_1, power_2, power_3, power_4, sums, ribbon,
    masked, eta_row, eta_col, eta_half, eta_up, cover, drag,
):
    layers = eta.shape[0]
    plane = own_planes(rhs, eta, friction, ice, grounded)
    below_and_above, above_and_below = beyond()
    lane = lax.broadcasted_iota(jnp.int32, (ROWS, LANES), 1)

    def target(p):
        if p < 2 * layers:
            return masked.at[p // layers, p % layers]
        if p < 3 * layers:
            return eta_up.at[p - 2 * layers]
        return cover if p == 3 * layers else drag

    strips = [jnp.zeros((ROWS, LANES), jnp.float32)] * ribbon.shape[0]
    for q in range(strip_a.shape[0] // 2):
        first, second = pair_of(q, layers)
        halves = ([], [])
        for half in range(2):
            from_a, from_b = strip_a[2 * q + half], strip_b[2 * q + half]
            halves[0].append(below_and_above(from_a, from_b))
            halves[1].append(pltpu.roll(above_and_below(from_a, from_b), HALO, 0))
        for p, halo in zip((first, second), halves):
            v = plane(p)
            dst = target(p)
            dst[0:ROWS, :] = v
            dst[ROWS:, 0:LANES], dst[ROWS:, LANES:] = halo
            ribbon_of(p, layers, *halo, lane, strips)
    for tile, v in enumerate(strips):
        ribbon[tile] = v

    moves = Moves()
    load = Tiles.load
    e = load(eta_up.at[0])
    for k in range(layers):
        pair = e + moves.row_next(e)
        (2.0 * pair).store(eta_row.at[0, k])
        (0.5 * pair).store(eta_row.at[1, k])
        pair = e + moves.col_next(e)
        (0.5 * pair).store(eta_col.at[0, k])
        (2.0 * pair).store(eta_col.at[1, k])
        (0.5 * e).store(eta_half.at[k])
        after = load(eta_up.at[k + 1]) if k + 1 < layers else None
        (e + after if k + 1 < layers else 0.0 * e).store(eta_up.at[k])
        e = after

    def apply(t, src, dst):
        def block(b, carry):
            g0, g1, below0, below1, odd, even = carry
            g0, g1, below0, below1 = Tiles(g0), Tiles(g1), Tiles(below0), Tiles(below1)
            odd, even = list(odd), list(even)
            m = load(cover)
            for i in range(UNROLL):
                k = b * UNROLL + i
                after = k + 1 if i + 1 < UNROLL else jnp.minimum(k + 1, layers - 1)
                next0, next1 = load(src.at[0, after]), load(src.at[1, after])
                e_up, e_half = load(eta_up.at[k]), load(eta_half.at[k])
                ups = []
                for c, g, following, below, part in ((0, g0, next0, below0, along), (1, g1, next1, below1, across)):
                    up = e_up * (g - following)
                    out = part(g0, g1, load(eta_row.at[c, k]), load(eta_col.at[c, k]), e_half, moves)
                    out = m * (out + (up - below))
                    if t < STEPS:
                        out.store(dst.at[c, k])
                    for half in range(2):
                        now = out.tiles[half]
                        if t == STEPS:
                            dst[c, k, :, half * LANES : (half + 1) * LANES] = now
                        odd[half] = odd[half] + g.tiles[half] * now
                        even[half] = even[half] + now * now
                    ups.append(up)
                up0, up1 = ups
                g0, g1, below0, below1 = next0, next1, up0, up1
            return g0.tiles, g1.tiles, below0.tiles, below1.tiles, odd, even

        zero = [jnp.zeros((ROWS, LANES), jnp.float32)] * 2
        d = -1.0 * load(drag)
        g0, g1 = load(src.at[0, 0]), load(src.at[1, 0])
        start = (g0.tiles, g1.tiles, (d * g0).tiles, (d * g1).tiles, zero, zero)
        ends = lax.fori_loop(0, layers // UNROLL, block, start)[4:]
        return [jnp.concatenate(v, 1) for v in ends]

    outside = squares[1]
    sums[0] = squares[0]
    wide = lax.broadcasted_iota(jnp.int32, (ROWS, 2 * LANES), 1)
    inner = between(wide, HALO, 2 * LANES - 2 * HALO)
    fields = (masked, power_1, power_2, power_3, power_4)
    for t in range(1, STEPS + 1):
        odd, even = apply(t, fields[t - 1], fields[t])
        sums[2 * t - 1] = jnp.where(inner, odd, 0.0) + outside
        sums[2 * t] = jnp.where(inner, even, 0.0) + outside


def ribbon_kernel(own, halo, columns, columns_a, columns_b, sums, edges, moments):
    tiles = edges.shape[2]
    below_and_above, _ = beyond()
    lane = lax.broadcasted_iota(jnp.int32, (2 * ROWS, LANES), 1)

    count = columns.shape[0] // 2
    beside = [
        jnp.concatenate([columns[i], below_and_above(columns_a[i], columns_b[i])], 0) for i in range(2 * count)
    ]
    spot = lane % SLOT

    def whole(tile):
        group, at = packed_place(tile)
        right = jnp.where(between(spot, 8, HALO), turned(beside[group], 8 - at), jnp.concatenate([own[tile], halo[tile]], 0))
        return jnp.where(between(spot, 16, HALO), turned(beside[count + group], 16 - at), right)

    field = [[whole(c * tiles + n) for n in range(tiles)] for c in range(2)]
    eta = [whole(2 * tiles + n) for n in range(tiles)]
    cover, drag = whole(3 * tiles), whole(3 * tiles + 1)

    def after(v):
        return v[1:] + [turned(v[0], -SLOT)]

    eta_row = [2.0 * (e + row_next(e)) for e in eta]
    eta_col = [0.5 * (e + col_next(e)) for e in eta]
    eta_row_1, eta_col_1 = [0.25 * e for e in eta_row], [4.0 * e for e in eta_col]
    eta_half = [0.5 * e for e in eta]
    eta_up = [e + n for e, n in zip(eta, after(eta))]
    eta_up[-1] = jnp.where(lane < LANES - SLOT, eta_up[-1], 0.0)
    place = lax.broadcasted_iota(jnp.int32, (ROWS, LANES), 1) % SLOT
    edge = between(place, 4, HALO) | between(place, 20, HALO)
    extra = [None]
    for t in range(1, STEPS + 1):
        ups = [[u * (g - n) for u, g, n in zip(eta_up, field[c], after(field[c]))] for c in range(2)]
        result = ([], [])
        odd = even = jnp.zeros((ROWS, LANES), jnp.float32)
        for n in range(tiles):
            outs = (
                along(field[0][n], field[1][n], eta_row[n], eta_col[n], eta_half[n], Turns),
                across(field[0][n], field[1][n], eta_row_1[n], eta_col_1[n], eta_half[n], Turns),
            )
            for c in range(2):
                below = ups[c][n - 1] if n else turned(ups[c][-1], SLOT) - drag * field[c][0]
                out = cover * (outs[c] + (ups[c][n] - below))
                result[c].append(out)
                now = out[:ROWS]
                edges[t - 1, c, n] = now
                odd = odd + field[c][n][:ROWS] * now
                even = even + now * now
        field = result
        extra.extend([jnp.where(edge, odd, 0.0), jnp.where(edge, even, 0.0)])

    tall = lax.broadcasted_iota(jnp.int32, (2 * ROWS, LANES), 0)
    high = jnp.zeros((2 * ROWS, LANES), jnp.float32)
    low = jnp.zeros((2 * ROWS, LANES), jnp.float32)
    for j, more in enumerate(extra):
        total = sums[j]
        pair = two_sum(total[:, :LANES], total[:, LANES:])
        if more is not None:
            pair = join(pair, (more, jnp.zeros_like(more)))
        for step in (4, 2, 1):
            pair = join(pair, tuple(pltpu.roll(v, step, 0) for v in pair))
        high = jnp.where(tall == j, jnp.concatenate([pair[0]] * 2, 0), high)
        low = jnp.where(tall == j, jnp.concatenate([pair[1]] * 2, 0), low)
    total = join((high, low), (pltpu.roll(high, 64, 1), pltpu.roll(low, 64, 1)))
    first = lax.broadcasted_iota(jnp.int32, (ROWS, LANES), 1) < 64
    for i, v in enumerate(total):
        moments[i] = jnp.where(first, v[:ROWS], v[ROWS:])


def added(terms):
    while len(terms) > 1:
        terms = [join(*terms[i : i + 2]) if i + 1 < len(terms) else terms[i] for i in range(0, len(terms), 2)]
    return terms[0]


def add_kernel(*refs):
    *ins, out = refs
    out[0], out[1] = added([(x[0], x[1]) for x in ins])


def solve(total):
    for unit in (8, 1):
        total = added([tuple(turned(v, unit * i) for v in total) for i in range(8)])

    def spread(j):
        row, lane = (j, 63) if j < ROWS else (j - ROWS, 127)
        return tuple(jnp.broadcast_to(v[row : row + 1, lane : lane + 1], (ROWS, LANES)) for v in total)

    table = [spread(j) for j in range(2 * STEPS + 1)]
    centre, _ = cut(table[1][0] / table[0][0], 13)
    mu = [sum(table[0])]
    while len(table) > 1:
        steps = [times(centre, x) for x in table[:-1]]
        table = [join(x, (-y[0], -y[1])) for x, y in zip(table[1:], steps)]
        mu.append(sum(table[0]))

    def plus(a, b):
        n = max(len(a), len(b))
        return [a[i] + b[i] if i < min(len(a), len(b)) else (a[i] if i < len(a) else b[i]) for i in range(n)]

    def scaled(s, a):
        return [s * x for x in a]

    def operator(a):
        return plus([centre * x for x in a], [jnp.zeros_like(centre)] + a)

    def dot(a, b):
        square = [None] * (len(a) + len(b) - 1)
        for i, x in enumerate(a):
            for j, y in enumerate(b):
                z = x * y
                square[i + j] = z if square[i + j] is None else square[i + j] + z
        value = square[0] * mu[0]
        for n in range(1, len(square)):
            value = value + square[n] * mu[n]
        return value

    one = jnp.ones_like(centre)
    right = [one]
    quasi, search, update, iterate = right, right, [], []
    applied = operator(search)
    carried = applied
    rho = mu[0]
    tau_sq = rho
    alpha = theta_sq = eta = None
    for half in range(STEPS):
        if half % 2 == 0:
            alpha = rho / dot(carried, right)
            search_next = plus(search, scaled(-alpha, carried))
        quasi = plus(quasi, scaled(-alpha, applied))
        if half:
            update = plus(search, scaled(theta_sq / alpha * eta, update))
        else:
            update = search
        theta_sq = dot(quasi, quasi) / tau_sq
        cosine_sq = 1.0 / (1.0 + theta_sq)
        tau_sq = tau_sq * theta_sq * cosine_sq
        eta = cosine_sq * alpha
        iterate = plus(iterate, scaled(eta, update))
        if half % 2 == 0:
            search = search_next
            applied = operator(search)
        elif half < STEPS - 1:
            rho_next = dot(quasi, right)
            beta = rho_next / rho
            search = plus(quasi, scaled(beta, search))
            applied_next = operator(search)
            carried = plus(applied_next, scaled(beta, plus(applied, scaled(beta, carried))))
            applied, rho = applied_next, rho_next
    powers = [iterate[-1]]
    for c in iterate[-2::-1]:
        powers = plus([c] + powers, scaled(-centre, powers))
    return powers


def patch_kernel(_, rhs, ice, power_1, power_2, power_3, power_4, edges, vectors):
    layers, tiles = rhs.shape[1], edges.shape[2]
    covered = ice[...] > 0
    lane = lax.broadcasted_iota(jnp.int32, (ROWS, LANES), 1)
    for t, power in enumerate((power_1, power_2, power_3, power_4)):
        for c in range(2):
            for k in range(layers):
                e, at = edges[t, c, k % tiles], k // tiles * SLOT
                v = power[c, k, :ROWS]
                head = jnp.where(lane < HALO, turned(e, -at - 20), v[:, :LANES])
                tail = jnp.where(lane >= LANES - HALO, turned(e, 120 - at), v[:, LANES:])
                vectors[t, c, k] = jnp.where(covered, jnp.concatenate([head, tail], 1), rhs[c, k])


def final_kernel(rhs, vectors, friction, ice, grounded, speed, *rest):
    *parts, iterate, residual, hessian = rest
    layers = rhs.shape[1]
    wide = [jnp.concatenate([c, c], 1) for c in solve(added([(x[0], x[1]) for x in parts]))]
    for c in range(2):
        for k in range(layers):
            r = rhs[c, k]
            x, y = wide[0] * r, r
            for t in range(STEPS):
                v = vectors[t, c, k]
                if t + 1 < STEPS:
                    x = x + wide[t + 1] * v
                y = y - wide[t] * v
            iterate[c, k] = x
            residual[c, k] = y
    weight = ice[...].astype(jnp.float32) * (friction[...] * grounded[...].astype(jnp.float32))
    hessian[...] = weight * (speed[0] * iterate[0, 0] + speed[1] * iterate[1, 0])


def exchange(x, axis, order):
    count = lax.axis_size(axis)
    stride = 1
    rounds = []
    while stride < count:
        size = 4 if (count // stride) % 4 == 0 else 2
        rounds.append((stride, size))
        stride *= size
    for at, (stride, size) in enumerate(rounds):
        parts = [x]
        for turn in order if size == 4 else (1,):
            pairs = []
            for i in range(count):
                place = (i // stride) % size
                pairs.append((i, i + ((place ^ turn) - place) * stride))
            parts.append(lax.ppermute(x, axis, pairs))
        if at == len(rounds) - 1:
            return parts
        x = call(add_kernel, [x.shape])(*parts)[0]
    return [x]


def body(adjoint_rhs, viscosity, friction, ice_mask, grounded, basal_velocity):
    layers = viscosity.shape[0]
    inputs = (adjoint_rhs, viscosity, friction, ice_mask, grounded, basal_velocity)
    tile = (ROWS, LANES)
    strips = (2 * (layers + layers // 2 + 1),) + tile
    ribbons = ribbon_tiles(layers)
    packed = ((ribbons + 7) // 8,) + tile
    both = (2 * packed[0],) + tile
    *held, strip_a, strip_b = call(
        strip_kernel,
        [jax.ShapeDtypeStruct(x.shape, x.dtype) for x in inputs] + [strips, strips],
        [pltpu.SemaphoreType.DMA((len(inputs),))],
        in_specs=[pl.BlockSpec(memory_space=pltpu.HBM)] * len(inputs),
    )(*[pltpu.with_memory_space_constraint(x, pltpu.HBM) for x in inputs])
    strip_b, strip_a = swapped(strip_b, ("gx",), 1, "gz"), swapped(strip_a, ("gx",), 0)
    column_a, column_b = call(column_kernel, [packed, packed])(*held[:5])
    beside = ("gy", "gz")
    (columns,) = call(beside_kernel, [both])(swapped(column_a, beside, 0), swapped(column_b, beside, 1))
    columns_a, columns_b = swapped(columns, ("gx",), 0), swapped(columns, ("gx",), 1, "gz")
    block = (layers, 2 * ROWS, 2 * LANES)
    own, squares = call(
        own_kernel,
        [(ribbons,) + tile, (2, ROWS, 2 * LANES)],
        in_specs=[pl.BlockSpec(memory_space=pl.ANY)] + [pl.BlockSpec(memory_space=pltpu.VMEM)] * 5,
    )(columns, *held[:5])
    *powers, sums, halo = call(
        main_kernel,
        [(2,) + block] * (STEPS - 1) + [adjoint_rhs.shape, (2 * STEPS + 1, ROWS, 2 * LANES), (ribbons,) + tile],
        [(2,) + block] * 3 + [block] * 2 + [block[1:]] * 2,
        cost_estimate=pl.CostEstimate(flops=200_000_000, bytes_accessed=8_000_000, transcendentals=0),
    )(*held[:5], squares, strip_b, strip_a)
    edges, sums = call(
        ribbon_kernel,
        [(STEPS, 2, layers // 4) + tile, (2,) + tile],
    )(own, halo, columns, columns_a, columns_b, sums)
    parts = exchange(sums, ("gy", "gz"), (1, 2, 3))
    if len(parts) > 1:
        sums = call(add_kernel, [sums.shape])(*parts)[0]
    parts = exchange(sums, "gx", (1, 3, 2))
    rhs, _, friction, ice_mask, grounded, speed = held
    (vectors,) = call(
        patch_kernel,
        [(STEPS,) + adjoint_rhs.shape],
        in_specs=[pl.BlockSpec(memory_space=pl.ANY)] + [pl.BlockSpec(memory_space=pltpu.VMEM)] * 7,
    )(sums, rhs, ice_mask, *powers, edges)
    return tuple(
        call(final_kernel, [adjoint_rhs.shape, adjoint_rhs.shape, friction.shape])(
            rhs, vectors, friction, ice_mask, grounded, speed, *parts
        )
    )


def solution(mesh):
    in_specs = (
        P(None, None, ("parts", "gx"), ("gy", "gz")),
        P(None, ("parts", "gx"), ("gy", "gz")),
        P(("parts", "gx"), ("gy", "gz")),
        P(("parts", "gx"), ("gy", "gz")),
        P(("parts", "gx"), ("gy", "gz")),
        P(None, ("parts", "gx"), ("gy", "gz")),
    )
    out_specs = (
        P(None, None, ("parts", "gx"), ("gy", "gz")),
        P(None, None, ("parts", "gx"), ("gy", "gz")),
        P(("parts", "gx"), ("gy", "gz")),
    )
    return jax.shard_map(body, mesh=mesh, in_specs=in_specs, out_specs=out_specs, check_vma=False)
```

```python
import functools

import jax
import jax.numpy as jnp
from jax import lax
from jax.experimental import pallas as pl
from jax.experimental.pallas import tpu as pltpu
from jax.sharding import PartitionSpec as P

STEPS = 4
HALO = 4
ROWS = 8
LANES = 128
UNROLL = 5
SLOT = 32


def call(kernel, outs, scratch=(), **more):
    return pl.pallas_call(
        kernel,
        out_shape=[jax.ShapeDtypeStruct(s, jnp.float32) if isinstance(s, tuple) else s for s in outs],
        scratch_shapes=[pltpu.VMEM(s, jnp.float32) if isinstance(s, tuple) else s for s in scratch],
        compiler_params=pltpu.CompilerParams(vmem_limit_bytes=40 * 1024 * 1024),
        **more,
    )


def place_of(axis):
    place, count = lax.axis_index(axis), lax.axis_size(axis)
    even = place % 2 == 0
    has_a = jnp.logical_or(jnp.logical_not(even), place < count - 1)
    has_b = jnp.where(even, place > 0, place < count - 1)
    return even, has_a, has_b


def swapped(x, axes, first, spare=None):
    count, others = lax.axis_size(axes), lax.axis_size(spare) if spare else 1
    pairs = []
    for at in range(others):
        for i in range(count):
            other, to = (i + 1 if (i - first) % 2 == 0 else i - 1), at
            if not 0 <= other < count:
                other, to = (i, at ^ 1) if spare else (count - 1 - i, at)
                if to >= others or count % 2:
                    other, to = i, at
            pairs.append((i * others + at, other * others + to))
    return lax.ppermute(x, (*axes, spare) if spare else axes, pairs)


def own_planes(rhs, eta, friction, ice, grounded):
    layers = eta.shape[0]
    cover = ice[...].astype(jnp.float32)
    drag = friction[...] * grounded[...].astype(jnp.float32)

    def plane(p):
        if p < 2 * layers:
            return rhs[p // layers, p % layers] * cover
        if p < 3 * layers:
            return eta[p - 2 * layers]
        return cover if p == 3 * layers else drag

    return plane


def pair_of(q, layers):
    if q < layers:
        return q, q + layers
    if q < layers + layers // 2:
        return q + layers, q + layers + layers // 2
    return 3 * layers, 3 * layers + 1


def ribbon_places(p, layers):
    tiles = layers // 4
    if p < 3 * layers:
        k = p % layers
        return p // layers * tiles + k % tiles, (k // tiles,)
    return (3 * tiles, (0, 1, 2, 3)) if p == 3 * layers else (3 * tiles + 1, (0,))


def ribbon_tiles(layers):
    return 3 * (layers // 4) + 2


def packed_place(tile):
    return tile // 8, HALO * (tile % 8)


def between(lane, first, width):
    return (lane >= first) & (lane < first + width)


def turned(v, shift):
    shift = shift % LANES
    return pltpu.roll(v, shift, 1) if shift else v


def strip_kernel(*refs):
    sources, held, (strip_a, strip_b, arrived) = refs[:6], refs[6:12], refs[12:]
    half = held[1].shape[0] // 2
    pieces = [[(c, pl.ds(h, half)) for c in range(2) for h in (0, half)], [(pl.ds(h, half),) for h in (0, half)]]
    copies = []
    for i, (a, b) in enumerate(zip(sources, held)):
        for at in pieces[i] if i < 2 else [()]:
            src, dst = (a.at[at], b.at[at]) if at else (a, b)
            copies.append(pltpu.make_async_copy(src, dst, arrived.at[len(copies)]))
            copies[-1].start()
    for copy in copies:
        copy.wait()
    rhs, eta, friction, ice, grounded, _ = held
    layers = eta.shape[0]
    plane = own_planes(rhs, eta, friction, ice, grounded)
    even, _, _ = place_of("gx")
    upper_a = (lax.broadcasted_iota(jnp.int32, (ROWS, LANES), 0) < HALO) != even
    for q in range(strip_a.shape[0] // 2):
        first, second = pair_of(q, layers)
        x, y = plane(first), plane(second)
        for half in range(2):
            xs = x[:, half * LANES : (half + 1) * LANES]
            ys = y[:, half * LANES : (half + 1) * LANES]
            ys = pltpu.roll(ys, HALO, 0)
            strip_a[2 * q + half] = jnp.where(upper_a, xs, ys)
            strip_b[2 * q + half] = jnp.where(upper_a, ys, xs)


def column_kernel(rhs, eta, friction, ice, grounded, column_a, column_b):
    layers = eta.shape[0]
    plane = own_planes(rhs, eta, friction, ice, grounded)
    lane = lax.broadcasted_iota(jnp.int32, (ROWS, LANES), 1)
    even, _, _ = place_of(("gy", "gz"))
    zero = jnp.zeros((ROWS, LANES), jnp.float32)
    to_left, to_right = [zero] * column_a.shape[0], [zero] * column_a.shape[0]
    for p in range(3 * layers + 2):
        v = plane(p)
        tile, slots = ribbon_places(p, layers)
        group, at = packed_place(tile)
        for slot in slots:
            here = between(lane, slot * SLOT + at, HALO)
            to_left[group] = jnp.where(here, turned(v[:, :LANES], slot * SLOT + at), to_left[group])
            to_right[group] = jnp.where(here, turned(v[:, LANES:], slot * SLOT + at + HALO), to_right[group])
    for group in range(column_a.shape[0]):
        column_a[group] = jnp.where(even, to_right[group], to_left[group])
        column_b[group] = jnp.where(even, to_left[group], to_right[group])


def beside_kernel(from_a, from_b, columns):
    even, has_a, has_b = place_of(("gy", "gz"))
    count = from_a.shape[0]
    for group in range(count):
        a = jnp.where(has_a, from_a[group], 0.0)
        b = jnp.where(has_b, from_b[group], 0.0)
        columns[group] = jnp.where(even, a, b)
        columns[count + group] = jnp.where(even, b, a)


def two_sum(a, b):
    s = a + b
    t = s - a
    return s, (a - (s - t)) + (b - t)


def join(x, y):
    s, e = two_sum(x[0], y[0])
    return s, e + (x[1] + y[1])


def cut(v, bits):
    t = v * (2.0**bits + 1.0)
    h = t - (t - v)
    return h, v - h


def times(scalar, x):
    high, low = cut(x[0], 12)
    return scalar * high, scalar * low + scalar * x[1]


def beyond():
    even, has_a, has_b = place_of("gx")
    upper_a = (lax.broadcasted_iota(jnp.int32, (ROWS, LANES), 0) < HALO) == even
    lower_a = jnp.logical_not(upper_a)

    def below_and_above(from_a, from_b):
        return jnp.where(upper_a & has_a, from_a, jnp.where(lower_a & has_b, from_b, 0.0))

    def above_and_below(from_a, from_b):
        return jnp.where(lower_a & has_a, from_a, jnp.where(upper_a & has_b, from_b, 0.0))

    return below_and_above, above_and_below


def row_next(v):
    return pltpu.roll(v, 2 * ROWS - 1, 0)


def row_prev(v):
    return pltpu.roll(v, 1, 0)


def col_next(v):
    return pltpu.roll(v, v.shape[1] - 1, 1)


def col_prev(v):
    return pltpu.roll(v, 1, 1)


def ribbon_of(p, layers, head, tail, lane, strips):
    tile, slots = ribbon_places(p, layers)
    for slot in slots:
        at = slot * SLOT
        strips[tile] = jnp.where(between(lane, at, 8), turned(tail, at + 8), strips[tile])
        strips[tile] = jnp.where(between(lane, at + 20, 8), turned(head, at + 20), strips[tile])


def own_kernel(_, rhs, eta, friction, ice, grounded, ribbon, squares):
    layers = eta.shape[0]
    plane = own_planes(rhs, eta, friction, ice, grounded)
    lane = lax.broadcasted_iota(jnp.int32, (ROWS, LANES), 1)
    strips = [jnp.zeros((ROWS, LANES), jnp.float32)] * ribbon.shape[0]
    for p in range(3 * layers + 2):
        v = plane(p)
        ribbon_of(p, layers, v[:, :LANES], v[:, LANES:], lane, strips)
    for tile, v in enumerate(strips):
        ribbon[tile] = v
    bare = 1.0 - ice[...].astype(jnp.float32)
    whole = jnp.zeros((ROWS, 2 * LANES), jnp.float32)
    outside = jnp.zeros((ROWS, 2 * LANES), jnp.float32)
    for c in range(2):
        for k in range(layers):
            square = rhs[c, k] * rhs[c, k]
            whole = whole + square
            outside = outside + bare * square
    squares[0], squares[1] = whole, outside


class Tiles:
    def __init__(self, tiles):
        self.tiles = tiles

    @staticmethod
    def load(ref):
        return Tiles([ref[r : r + ROWS, c : c + LANES] for r in (0, ROWS) for c in (0, LANES)])

    def store(self, ref):
        for v, (r, c) in zip(self.tiles, ((0, 0), (0, LANES), (ROWS, 0), (ROWS, LANES))):
            ref[r : r + ROWS, c : c + LANES] = v

    def both(self, other, op):
        if isinstance(other, Tiles):
            return Tiles([op(x, y) for x, y in zip(self.tiles, other.tiles)])
        return Tiles([op(x, other) for x in self.tiles])

    def __add__(self, other):
        return self.both(other, lambda x, y: x + y)

    def __sub__(self, other):
        return self.both(other, lambda x, y: x - y)

    def __mul__(self, other):
        return self.both(other, lambda x, y: x * y)

    __rmul__ = __mul__


class Moves:
    def __init__(self):
        row = lax.broadcasted_iota(jnp.int32, (ROWS, LANES), 0)
        lane = lax.broadcasted_iota(jnp.int32, (ROWS, LANES), 1)
        self.first_row, self.last_row = row == 0, row == ROWS - 1
        self.first_lane, self.last_lane = lane == 0, lane == LANES - 1

    def rows(self, v, shift, edge):
        own0, own1, halo0, halo1 = [pltpu.roll(x, shift, 0) for x in v.tiles]
        return Tiles(
            [
                jnp.where(edge, halo0, own0),
                jnp.where(edge, halo1, own1),
                jnp.where(edge, own0, halo0),
                jnp.where(edge, own1, halo1),
            ]
        )

    def row_next(self, v):
        return self.rows(v, ROWS - 1, self.last_row)

    def row_prev(self, v):
        return self.rows(v, 1, self.first_row)

    def col_next(self, v):
        own0, own1, halo0, halo1 = [pltpu.roll(x, LANES - 1, 1) for x in v.tiles]
        return Tiles([jnp.where(self.last_lane, own1, own0), own1, jnp.where(self.last_lane, halo1, halo0), halo1])

    def col_prev(self, v):
        own0, own1, halo0, halo1 = [pltpu.roll(x, 1, 1) for x in v.tiles]
        return Tiles([own0, jnp.where(self.first_lane, own0, own1), halo0, jnp.where(self.first_lane, halo0, halo1)])


class Turns:
    row_next = staticmethod(row_next)
    row_prev = staticmethod(row_prev)
    col_next = staticmethod(col_next)
    col_prev = staticmethod(col_prev)


def horizontal(g0, g1, e_row, e_row_1, e_col, e_col_1, e_half, moves):
    row_next, row_prev, col_next, col_prev = moves.row_next, moves.row_prev, moves.col_next, moves.col_prev
    g0n, g1n = row_next(g0), col_next(g1)
    f = e_half * (g1n - col_prev(g1))
    h = e_half * (g0n - row_prev(g0))
    flux = e_row * (g0 - g0n)
    out0 = flux - row_next(f) - row_prev(flux - f)
    flux = e_col * (g0 - col_next(g0))
    out0 = out0 + (flux - col_prev(flux))
    flux = e_col_1 * (g1 - g1n)
    out1 = flux - col_next(h) - col_prev(flux - h)
    flux = e_row_1 * (g1 - row_next(g1))
    out1 = out1 + (flux - row_prev(flux))
    return out0, out1


def main_kernel(
    rhs, eta, friction, ice, grounded, squares, strip_b, strip_a,
    power_1, power_2, power_3, power_4, sums, ribbon,
    masked, eta_row, eta_col, eta_half, eta_up, cover, drag,
):
    layers = eta.shape[0]
    plane = own_planes(rhs, eta, friction, ice, grounded)
    below_and_above, above_and_below = beyond()
    lane = lax.broadcasted_iota(jnp.int32, (ROWS, LANES), 1)

    def target(p):
        if p < 2 * layers:
            return masked.at[p // layers, p % layers]
        if p < 3 * layers:
            return eta_up.at[p - 2 * layers]
        return cover if p == 3 * layers else drag

    strips = [jnp.zeros((ROWS, LANES), jnp.float32)] * ribbon.shape[0]
    for q in range(strip_a.shape[0] // 2):
        first, second = pair_of(q, layers)
        halves = ([], [])
        for half in range(2):
            from_a, from_b = strip_a[2 * q + half], strip_b[2 * q + half]
            halves[0].append(below_and_above(from_a, from_b))
            halves[1].append(pltpu.roll(above_and_below(from_a, from_b), HALO, 0))
        for p, halo in zip((first, second), halves):
            v = plane(p)
            dst = target(p)
            dst[0:ROWS, :] = v
            dst[ROWS:, 0:LANES], dst[ROWS:, LANES:] = halo
            ribbon_of(p, layers, *halo, lane, strips)
    for tile, v in enumerate(strips):
        ribbon[tile] = v

    moves = Moves()
    load = Tiles.load
    e = load(eta_up.at[0])
    for k in range(layers):
        pair = e + moves.row_next(e)
        (2.0 * pair).store(eta_row.at[0, k])
        (0.5 * pair).store(eta_row.at[1, k])
        pair = e + moves.col_next(e)
        (0.5 * pair).store(eta_col.at[0, k])
        (2.0 * pair).store(eta_col.at[1, k])
        (0.5 * e).store(eta_half.at[k])
        after = load(eta_up.at[k + 1]) if k + 1 < layers else None
        (e + after if k + 1 < layers else 0.0 * e).store(eta_up.at[k])
        e = after

    def apply(t, src, dst):
        def block(b, carry):
            g0, g1, below0, below1, odd, even = carry
            g0, g1, below0, below1 = Tiles(g0), Tiles(g1), Tiles(below0), Tiles(below1)
            odd, even = list(odd), list(even)
            m = load(cover)
            for i in range(UNROLL):
                k = b * UNROLL + i
                after = k + 1 if i + 1 < UNROLL else jnp.minimum(k + 1, layers - 1)
                next0, next1 = load(src.at[0, after]), load(src.at[1, after])
                e_up = load(eta_up.at[k])
                up0, up1 = e_up * (g0 - next0), e_up * (g1 - next1)
                pairs = [load(ref.at[c, k]) for ref in (eta_row, eta_col) for c in range(2)]
                out0, out1 = horizontal(g0, g1, *pairs, load(eta_half.at[k]), moves)
                out0, out1 = m * (out0 + (up0 - below0)), m * (out1 + (up1 - below1))
                for c, g, out in ((0, g0, out0), (1, g1, out1)):
                    if t < STEPS:
                        out.store(dst.at[c, k])
                    for half in range(2):
                        now = out.tiles[half]
                        if t == STEPS:
                            dst[c, k, :, half * LANES : (half + 1) * LANES] = now
                        odd[half] = odd[half] + g.tiles[half] * now
                        even[half] = even[half] + now * now
                g0, g1, below0, below1 = next0, next1, up0, up1
            return g0.tiles, g1.tiles, below0.tiles, below1.tiles, odd, even

        zero = [jnp.zeros((ROWS, LANES), jnp.float32)] * 2
        d = -1.0 * load(drag)
        g0, g1 = load(src.at[0, 0]), load(src.at[1, 0])
        start = (g0.tiles, g1.tiles, (d * g0).tiles, (d * g1).tiles, zero, zero)
        ends = lax.fori_loop(0, layers // UNROLL, block, start)[4:]
        return [jnp.concatenate(v, 1) for v in ends]

    outside = squares[1]
    sums[0] = squares[0]
    wide = lax.broadcasted_iota(jnp.int32, (ROWS, 2 * LANES), 1)
    inner = between(wide, HALO, 2 * LANES - 2 * HALO)
    fields = (masked, power_1, power_2, power_3, power_4)
    for t in range(1, STEPS + 1):
        odd, even = apply(t, fields[t - 1], fields[t])
        sums[2 * t - 1] = jnp.where(inner, odd, 0.0) + outside
        sums[2 * t] = jnp.where(inner, even, 0.0) + outside


def ribbon_kernel(own, halo, columns, columns_a, columns_b, sums, edges, moments):
    tiles = edges.shape[2]
    below_and_above, _ = beyond()
    lane = lax.broadcasted_iota(jnp.int32, (2 * ROWS, LANES), 1)

    count = columns.shape[0] // 2
    beside = [
        jnp.concatenate([columns[i], below_and_above(columns_a[i], columns_b[i])], 0) for i in range(2 * count)
    ]
    spot = lane % SLOT

    def whole(tile):
        group, at = packed_place(tile)
        right = jnp.where(between(spot, 8, HALO), turned(beside[group], 8 - at), jnp.concatenate([own[tile], halo[tile]], 0))
        return jnp.where(between(spot, 16, HALO), turned(beside[count + group], 16 - at), right)

    field = [[whole(c * tiles + n) for n in range(tiles)] for c in range(2)]
    eta = [whole(2 * tiles + n) for n in range(tiles)]
    cover, drag = whole(3 * tiles), whole(3 * tiles + 1)

    def after(v):
        return v[1:] + [turned(v[0], -SLOT)]

    eta_row = [2.0 * (e + row_next(e)) for e in eta]
    eta_col = [0.5 * (e + col_next(e)) for e in eta]
    eta_row_1, eta_col_1 = [0.25 * e for e in eta_row], [4.0 * e for e in eta_col]
    eta_half = [0.5 * e for e in eta]
    eta_up = [e + n for e, n in zip(eta, after(eta))]
    eta_up[-1] = jnp.where(lane < LANES - SLOT, eta_up[-1], 0.0)
    place = lax.broadcasted_iota(jnp.int32, (ROWS, LANES), 1) % SLOT
    edge = between(place, 4, HALO) | between(place, 20, HALO)
    extra = [None]
    for t in range(1, STEPS + 1):
        ups = [[u * (g - n) for u, g, n in zip(eta_up, field[c], after(field[c]))] for c in range(2)]
        result = ([], [])
        odd = even = jnp.zeros((ROWS, LANES), jnp.float32)
        for n in range(tiles):
            coefficients = (eta_row[n], eta_row_1[n], eta_col[n], eta_col_1[n], eta_half[n])
            outs = horizontal(field[0][n], field[1][n], *coefficients, Turns)
            for c in range(2):
                below = ups[c][n - 1] if n else turned(ups[c][-1], SLOT) - drag * field[c][0]
                out = cover * (outs[c] + (ups[c][n] - below))
                result[c].append(out)
                now = out[:ROWS]
                edges[t - 1, c, n] = now
                odd = odd + field[c][n][:ROWS] * now
                even = even + now * now
        field = result
        extra.extend([jnp.where(edge, odd, 0.0), jnp.where(edge, even, 0.0)])

    tall = lax.broadcasted_iota(jnp.int32, (2 * ROWS, LANES), 0)
    high = jnp.zeros((2 * ROWS, LANES), jnp.float32)
    low = jnp.zeros((2 * ROWS, LANES), jnp.float32)
    for j, more in enumerate(extra):
        total = sums[j]
        pair = two_sum(total[:, :LANES], total[:, LANES:])
        if more is not None:
            pair = join(pair, (more, jnp.zeros_like(more)))
        for step in (4, 2, 1):
            pair = join(pair, tuple(pltpu.roll(v, step, 0) for v in pair))
        high = jnp.where(tall == j, jnp.concatenate([pair[0]] * 2, 0), high)
        low = jnp.where(tall == j, jnp.concatenate([pair[1]] * 2, 0), low)
    total = join((high, low), (pltpu.roll(high, 64, 1), pltpu.roll(low, 64, 1)))
    first = lax.broadcasted_iota(jnp.int32, (ROWS, LANES), 1) < 64
    for i, v in enumerate(total):
        moments[i] = jnp.where(first, v[:ROWS], v[ROWS:])


def added(terms):
    while len(terms) > 1:
        terms = [join(*terms[i : i + 2]) if i + 1 < len(terms) else terms[i] for i in range(0, len(terms), 2)]
    return terms[0]


def add_kernel(*refs):
    *ins, out = refs
    out[0], out[1] = added([(x[0], x[1]) for x in ins])


def solve(total):
    for unit in (8, 1):
        total = added([tuple(turned(v, unit * i) for v in total) for i in range(8)])

    def spread(j):
        row, lane = (j, 63) if j < ROWS else (j - ROWS, 127)
        return tuple(jnp.broadcast_to(v[row : row + 1, lane : lane + 1], (ROWS, LANES)) for v in total)

    table = [spread(j) for j in range(2 * STEPS + 1)]
    centre, _ = cut(table[1][0] / table[0][0], 13)
    mu = [sum(table[0])]
    while len(table) > 1:
        steps = [times(centre, x) for x in table[:-1]]
        table = [join(x, (-y[0], -y[1])) for x, y in zip(table[1:], steps)]
        mu.append(sum(table[0]))

    def plus(a, b):
        n = max(len(a), len(b))
        return [a[i] + b[i] if i < min(len(a), len(b)) else (a[i] if i < len(a) else b[i]) for i in range(n)]

    def scaled(s, a):
        return [s * x for x in a]

    def operator(a):
        return plus([centre * x for x in a], [jnp.zeros_like(centre)] + a)

    def dot(a, b):
        square = [None] * (len(a) + len(b) - 1)
        for i, x in enumerate(a):
            for j, y in enumerate(b):
                z = x * y
                square[i + j] = z if square[i + j] is None else square[i + j] + z
        value = square[0] * mu[0]
        for n in range(1, len(square)):
            value = value + square[n] * mu[n]
        return value

    one = jnp.ones_like(centre)
    right = [one]
    quasi, search, update, iterate = right, right, [], []
    applied = operator(search)
    carried = applied
    rho = mu[0]
    tau_sq = rho
    alpha = theta_sq = eta = None
    for half in range(STEPS):
        if half % 2 == 0:
            alpha = rho / dot(carried, right)
            search_next = plus(search, scaled(-alpha, carried))
        quasi = plus(quasi, scaled(-alpha, applied))
        if half:
            update = plus(search, scaled(theta_sq / alpha * eta, update))
        else:
            update = search
        theta_sq = dot(quasi, quasi) / tau_sq
        cosine_sq = 1.0 / (1.0 + theta_sq)
        tau_sq = tau_sq * theta_sq * cosine_sq
        eta = cosine_sq * alpha
        iterate = plus(iterate, scaled(eta, update))
        if half % 2 == 0:
            search = search_next
            applied = operator(search)
        elif half < STEPS - 1:
            rho_next = dot(quasi, right)
            beta = rho_next / rho
            search = plus(quasi, scaled(beta, search))
            applied_next = operator(search)
            carried = plus(applied_next, scaled(beta, plus(applied, scaled(beta, carried))))
            applied, rho = applied_next, rho_next
    powers = [iterate[-1]]
    for c in iterate[-2::-1]:
        powers = plus([c] + powers, scaled(-centre, powers))
    return powers


def patch_kernel(_, rhs, ice, power_1, power_2, power_3, power_4, edges, vectors):
    layers, tiles = rhs.shape[1], edges.shape[2]
    covered = ice[...] > 0
    lane = lax.broadcasted_iota(jnp.int32, (ROWS, LANES), 1)
    for t, power in enumerate((power_1, power_2, power_3, power_4)):
        for c in range(2):
            for k in range(layers):
                e, at = edges[t, c, k % tiles], k // tiles * SLOT
                v = power[c, k, :ROWS]
                head = jnp.where(lane < HALO, turned(e, -at - 20), v[:, :LANES])
                tail = jnp.where(lane >= LANES - HALO, turned(e, 120 - at), v[:, LANES:])
                vectors[t, c, k] = jnp.where(covered, jnp.concatenate([head, tail], 1), rhs[c, k])


def final_kernel(rhs, vectors, friction, ice, grounded, speed, *rest):
    *parts, iterate, residual, hessian = rest
    layers = rhs.shape[1]
    wide = [jnp.concatenate([c, c], 1) for c in solve(added([(x[0], x[1]) for x in parts]))]
    for c in range(2):
        for k in range(layers):
            r = rhs[c, k]
            x, y = wide[0] * r, r
            for t in range(STEPS):
                v = vectors[t, c, k]
                if t + 1 < STEPS:
                    x = x + wide[t + 1] * v
                y = y - wide[t] * v
            iterate[c, k] = x
            residual[c, k] = y
    weight = ice[...].astype(jnp.float32) * (friction[...] * grounded[...].astype(jnp.float32))
    hessian[...] = weight * (speed[0] * iterate[0, 0] + speed[1] * iterate[1, 0])


def exchange(x, axis, order):
    count = lax.axis_size(axis)
    stride = 1
    rounds = []
    while stride < count:
        size = 4 if (count // stride) % 4 == 0 else 2
        rounds.append((stride, size))
        stride *= size
    for at, (stride, size) in enumerate(rounds):
        parts = [x]
        for turn in order if size == 4 else (1,):
            pairs = []
            for i in range(count):
                place = (i // stride) % size
                pairs.append((i, i + ((place ^ turn) - place) * stride))
            parts.append(lax.ppermute(x, axis, pairs))
        if at == len(rounds) - 1:
            return parts
        x = call(add_kernel, [x.shape])(*parts)[0]
    return [x]


def body(adjoint_rhs, viscosity, friction, ice_mask, grounded, basal_velocity):
    layers = viscosity.shape[0]
    inputs = (adjoint_rhs, viscosity, friction, ice_mask, grounded, basal_velocity)
    tile = (ROWS, LANES)
    strips = (2 * (layers + layers // 2 + 1),) + tile
    ribbons = ribbon_tiles(layers)
    packed = ((ribbons + 7) // 8,) + tile
    both = (2 * packed[0],) + tile
    *held, strip_a, strip_b = call(
        strip_kernel,
        [jax.ShapeDtypeStruct(x.shape, x.dtype) for x in inputs] + [strips, strips],
        [pltpu.SemaphoreType.DMA((len(inputs) + 4,))],
        in_specs=[pl.BlockSpec(memory_space=pltpu.HBM)] * len(inputs),
    )(*[pltpu.with_memory_space_constraint(x, pltpu.HBM) for x in inputs])
    strip_b, strip_a = swapped(strip_b, ("gx",), 1, "gz"), swapped(strip_a, ("gx",), 0)
    column_a, column_b = call(column_kernel, [packed, packed])(*held[:5])
    beside = ("gy", "gz")
    (columns,) = call(beside_kernel, [both])(swapped(column_a, beside, 0), swapped(column_b, beside, 1))
    columns_a, columns_b = swapped(columns, ("gx",), 0), swapped(columns, ("gx",), 1, "gz")
    block = (layers, 2 * ROWS, 2 * LANES)
    own, squares = call(
        own_kernel,
        [(ribbons,) + tile, (2, ROWS, 2 * LANES)],
        in_specs=[pl.BlockSpec(memory_space=pl.ANY)] + [pl.BlockSpec(memory_space=pltpu.VMEM)] * 5,
    )(columns, *held[:5])
    *powers, sums, halo = call(
        main_kernel,
        [(2,) + block] * (STEPS - 1) + [adjoint_rhs.shape, (2 * STEPS + 1, ROWS, 2 * LANES), (ribbons,) + tile],
        [(2,) + block] * 3 + [block] * 2 + [block[1:]] * 2,
        cost_estimate=pl.CostEstimate(flops=200_000_000, bytes_accessed=8_000_000, transcendentals=0),
    )(*held[:5], squares, strip_b, strip_a)
    edges, sums = call(
        ribbon_kernel,
        [(STEPS, 2, layers // 4) + tile, (2,) + tile],
    )(own, halo, columns, columns_a, columns_b, sums)
    parts = exchange(sums, ("gy", "gz"), (1, 2, 3))
    if len(parts) > 1:
        sums = call(add_kernel, [sums.shape])(*parts)[0]
    parts = exchange(sums, "gx", (1, 3, 2))
    rhs, _, friction, ice_mask, grounded, speed = held
    (vectors,) = call(
        patch_kernel,
        [(STEPS,) + adjoint_rhs.shape],
        in_specs=[pl.BlockSpec(memory_space=pl.ANY)] + [pl.BlockSpec(memory_space=pltpu.VMEM)] * 7,
    )(sums, rhs, ice_mask, *powers, edges)
    return tuple(
        call(final_kernel, [adjoint_rhs.shape, adjoint_rhs.shape, friction.shape])(
            rhs, vectors, friction, ice_mask, grounded, speed, *parts
        )
    )


def solution(mesh):
    in_specs = (
        P(None, None, ("parts", "gx"), ("gy", "gz")),
        P(None, ("parts", "gx"), ("gy", "gz")),
        P(("parts", "gx"), ("gy", "gz")),
        P(("parts", "gx"), ("gy", "gz")),
        P(("parts", "gx"), ("gy", "gz")),
        P(None, ("parts", "gx"), ("gy", "gz")),
    )
    out_specs = (
        P(None, None, ("parts", "gx"), ("gy", "gz")),
        P(None, None, ("parts", "gx"), ("gy", "gz")),
        P(("parts", "gx"), ("gy", "gz")),
    )
    return jax.shard_map(body, mesh=mesh, in_specs=in_specs, out_specs=out_specs, check_vma=False)
```

```python
import functools

import jax
import jax.numpy as jnp
from jax import lax
from jax.experimental import pallas as pl
from jax.experimental.pallas import tpu as pltpu
from jax.sharding import PartitionSpec as P

STEPS = 4
HALO = 4
ROWS = 8
LANES = 128
UNROLL = 5
SLOT = 32


def call(kernel, outs, scratch=(), **more):
    return pl.pallas_call(
        kernel,
        out_shape=[jax.ShapeDtypeStruct(s, jnp.float32) if isinstance(s, tuple) else s for s in outs],
        scratch_shapes=[pltpu.VMEM(s, jnp.float32) if isinstance(s, tuple) else s for s in scratch],
        compiler_params=pltpu.CompilerParams(vmem_limit_bytes=40 * 1024 * 1024),
        **more,
    )


def place_of(axis):
    place, count = lax.axis_index(axis), lax.axis_size(axis)
    even = place % 2 == 0
    has_a = jnp.logical_or(jnp.logical_not(even), place < count - 1)
    has_b = jnp.where(even, place > 0, place < count - 1)
    return even, has_a, has_b


def swapped(x, axes, first, spare=None):
    count, others = lax.axis_size(axes), lax.axis_size(spare) if spare else 1
    pairs = []
    for at in range(others):
        for i in range(count):
            other, to = (i + 1 if (i - first) % 2 == 0 else i - 1), at
            if not 0 <= other < count:
                other, to = (i, at ^ 1) if spare else (count - 1 - i, at)
                if to >= others or count % 2:
                    other, to = i, at
            pairs.append((i * others + at, other * others + to))
    return lax.ppermute(x, (*axes, spare) if spare else axes, pairs)


def own_planes(rhs, eta, friction, ice, grounded):
    layers = eta.shape[0]
    cover = ice[...].astype(jnp.float32)
    drag = friction[...] * grounded[...].astype(jnp.float32)

    def plane(p):
        if p < 2 * layers:
            return rhs[p // layers, p % layers] * cover
        if p < 3 * layers:
            return eta[p - 2 * layers]
        return cover if p == 3 * layers else drag

    return plane


def pair_of(q, layers):
    if q < layers:
        return q, q + layers
    if q < layers + layers // 2:
        return q + layers, q + layers + layers // 2
    return 3 * layers, 3 * layers + 1


def ribbon_places(p, layers):
    tiles = layers // 4
    if p < 3 * layers:
        k = p % layers
        return p // layers * tiles + k % tiles, (k // tiles,)
    return (3 * tiles, (0, 1, 2, 3)) if p == 3 * layers else (3 * tiles + 1, (0,))


def ribbon_tiles(layers):
    return 3 * (layers // 4) + 2


def packed_place(tile):
    return tile // 8, HALO * (tile % 8)


def between(lane, first, width):
    return (lane >= first) & (lane < first + width)


def turned(v, shift):
    shift = shift % LANES
    return pltpu.roll(v, shift, 1) if shift else v


def strip_kernel(*refs):
    sources, held, (strip_a, strip_b, arrived) = refs[:6], refs[6:12], refs[12:]
    copies = [pltpu.make_async_copy(a, b, arrived.at[i]) for i, (a, b) in enumerate(zip(sources, held))]
    for copy in copies:
        copy.start()
    for copy in copies:
        copy.wait()
    rhs, eta, friction, ice, grounded, _ = held
    layers = eta.shape[0]
    plane = own_planes(rhs, eta, friction, ice, grounded)
    even, _, _ = place_of("gx")
    upper_a = (lax.broadcasted_iota(jnp.int32, (ROWS, LANES), 0) < HALO) != even
    for q in range(strip_a.shape[0] // 2):
        first, second = pair_of(q, layers)
        x, y = plane(first), plane(second)
        for half in range(2):
            xs = x[:, half * LANES : (half + 1) * LANES]
            ys = y[:, half * LANES : (half + 1) * LANES]
            ys = pltpu.roll(ys, HALO, 0)
            strip_a[2 * q + half] = jnp.where(upper_a, xs, ys)
            strip_b[2 * q + half] = jnp.where(upper_a, ys, xs)


def column_kernel(rhs, eta, friction, ice, grounded, column_a, column_b):
    layers = eta.shape[0]
    plane = own_planes(rhs, eta, friction, ice, grounded)
    lane = lax.broadcasted_iota(jnp.int32, (ROWS, LANES), 1)
    even, _, _ = place_of(("gy", "gz"))
    zero = jnp.zeros((ROWS, LANES), jnp.float32)
    to_left, to_right = [zero] * column_a.shape[0], [zero] * column_a.shape[0]
    for p in range(3 * layers + 2):
        v = plane(p)
        tile, slots = ribbon_places(p, layers)
        group, at = packed_place(tile)
        for slot in slots:
            here = between(lane, slot * SLOT + at, HALO)
            to_left[group] = jnp.where(here, turned(v[:, :LANES], slot * SLOT + at), to_left[group])
            to_right[group] = jnp.where(here, turned(v[:, LANES:], slot * SLOT + at + HALO), to_right[group])
    for group in range(column_a.shape[0]):
        column_a[group] = jnp.where(even, to_right[group], to_left[group])
        column_b[group] = jnp.where(even, to_left[group], to_right[group])


def beside_kernel(from_a, from_b, columns):
    even, has_a, has_b = place_of(("gy", "gz"))
    count = from_a.shape[0]
    for group in range(count):
        a = jnp.where(has_a, from_a[group], 0.0)
        b = jnp.where(has_b, from_b[group], 0.0)
        columns[group] = jnp.where(even, a, b)
        columns[count + group] = jnp.where(even, b, a)


def two_sum(a, b):
    s = a + b
    t = s - a
    return s, (a - (s - t)) + (b - t)


def join(x, y):
    s, e = two_sum(x[0], y[0])
    return s, e + (x[1] + y[1])


def cut(v, bits):
    t = v * (2.0**bits + 1.0)
    h = t - (t - v)
    return h, v - h


def times(scalar, x):
    high, low = cut(x[0], 12)
    return scalar * high, scalar * low + scalar * x[1]


def beyond():
    even, has_a, has_b = place_of("gx")
    upper_a = (lax.broadcasted_iota(jnp.int32, (ROWS, LANES), 0) < HALO) == even
    lower_a = jnp.logical_not(upper_a)

    def below_and_above(from_a, from_b):
        return jnp.where(upper_a & has_a, from_a, jnp.where(lower_a & has_b, from_b, 0.0))

    def above_and_below(from_a, from_b):
        return jnp.where(lower_a & has_a, from_a, jnp.where(upper_a & has_b, from_b, 0.0))

    return below_and_above, above_and_below


def row_next(v):
    return pltpu.roll(v, 2 * ROWS - 1, 0)


def row_prev(v):
    return pltpu.roll(v, 1, 0)


def col_next(v):
    return pltpu.roll(v, v.shape[1] - 1, 1)


def col_prev(v):
    return pltpu.roll(v, 1, 1)


def ribbon_of(p, layers, head, tail, lane, strips):
    tile, slots = ribbon_places(p, layers)
    for slot in slots:
        at = slot * SLOT
        strips[tile] = jnp.where(between(lane, at, 8), turned(tail, at + 8), strips[tile])
        strips[tile] = jnp.where(between(lane, at + 20, 8), turned(head, at + 20), strips[tile])


def own_kernel(_, rhs, eta, friction, ice, grounded, ribbon, squares):
    layers = eta.shape[0]
    plane = own_planes(rhs, eta, friction, ice, grounded)
    lane = lax.broadcasted_iota(jnp.int32, (ROWS, LANES), 1)
    strips = [jnp.zeros((ROWS, LANES), jnp.float32)] * ribbon.shape[0]
    for p in range(3 * layers + 2):
        v = plane(p)
        ribbon_of(p, layers, v[:, :LANES], v[:, LANES:], lane, strips)
    for tile, v in enumerate(strips):
        ribbon[tile] = v
    bare = 1.0 - ice[...].astype(jnp.float32)
    whole = jnp.zeros((ROWS, 2 * LANES), jnp.float32)
    outside = jnp.zeros((ROWS, 2 * LANES), jnp.float32)
    for c in range(2):
        for k in range(layers):
            square = rhs[c, k] * rhs[c, k]
            whole = whole + square
            outside = outside + bare * square
    squares[0], squares[1] = whole, outside


class Tiles:
    def __init__(self, tiles):
        self.tiles = tiles

    @staticmethod
    def load(ref):
        return Tiles([ref[r : r + ROWS, c : c + LANES] for r in (0, ROWS) for c in (0, LANES)])

    def store(self, ref):
        for v, (r, c) in zip(self.tiles, ((0, 0), (0, LANES), (ROWS, 0), (ROWS, LANES))):
            ref[r : r + ROWS, c : c + LANES] = v

    def both(self, other, op):
        if isinstance(other, Tiles):
            return Tiles([op(x, y) for x, y in zip(self.tiles, other.tiles)])
        return Tiles([op(x, other) for x in self.tiles])

    def __add__(self, other):
        return self.both(other, lambda x, y: x + y)

    def __sub__(self, other):
        return self.both(other, lambda x, y: x - y)

    def __mul__(self, other):
        return self.both(other, lambda x, y: x * y)

    __rmul__ = __mul__


class Moves:
    def __init__(self):
        row = lax.broadcasted_iota(jnp.int32, (ROWS, LANES), 0)
        lane = lax.broadcasted_iota(jnp.int32, (ROWS, LANES), 1)
        self.first_row, self.last_row = row == 0, row == ROWS - 1
        self.first_lane, self.last_lane = lane == 0, lane == LANES - 1

    def rows(self, v, shift, edge):
        own0, own1, halo0, halo1 = [pltpu.roll(x, shift, 0) for x in v.tiles]
        return Tiles(
            [
                jnp.where(edge, halo0, own0),
                jnp.where(edge, halo1, own1),
                jnp.where(edge, own0, halo0),
                jnp.where(edge, own1, halo1),
            ]
        )

    def row_next(self, v):
        return self.rows(v, ROWS - 1, self.last_row)

    def row_prev(self, v):
        return self.rows(v, 1, self.first_row)

    def col_next(self, v):
        own0, own1, halo0, halo1 = [pltpu.roll(x, LANES - 1, 1) for x in v.tiles]
        return Tiles([jnp.where(self.last_lane, own1, own0), own1, jnp.where(self.last_lane, halo1, halo0), halo1])

    def col_prev(self, v):
        own0, own1, halo0, halo1 = [pltpu.roll(x, 1, 1) for x in v.tiles]
        return Tiles([own0, jnp.where(self.first_lane, own0, own1), halo0, jnp.where(self.first_lane, halo0, halo1)])


class Turns:
    row_next = staticmethod(row_next)
    row_prev = staticmethod(row_prev)
    col_next = staticmethod(col_next)
    col_prev = staticmethod(col_prev)


def horizontal(g0, g1, e_row, e_row_1, e_col, e_col_1, e_half, moves):
    row_next, row_prev, col_next, col_prev = moves.row_next, moves.row_prev, moves.col_next, moves.col_prev
    g0n, g1n = row_next(g0), col_next(g1)
    f = e_half * (g1n - col_prev(g1))
    h = e_half * (g0n - row_prev(g0))
    flux = e_row * (g0 - g0n)
    out0 = flux - row_next(f) - row_prev(flux - f)
    flux = e_col * (g0 - col_next(g0))
    out0 = out0 + (flux - col_prev(flux))
    flux = e_col_1 * (g1 - g1n)
    out1 = flux - col_next(h) - col_prev(flux - h)
    flux = e_row_1 * (g1 - row_next(g1))
    out1 = out1 + (flux - row_prev(flux))
    return out0, out1


def main_kernel(
    rhs, eta, friction, ice, grounded, squares, strip_b, strip_a,
    power_1, power_2, power_3, power_4, sums, ribbon,
    masked, eta_row, eta_col, eta_half, eta_up, cover, drag,
):
    layers = eta.shape[0]
    plane = own_planes(rhs, eta, friction, ice, grounded)
    below_and_above, above_and_below = beyond()
    lane = lax.broadcasted_iota(jnp.int32, (ROWS, LANES), 1)

    def target(p):
        if p < 2 * layers:
            return masked.at[p // layers, p % layers]
        if p < 3 * layers:
            return eta_up.at[p - 2 * layers]
        return cover if p == 3 * layers else drag

    strips = [jnp.zeros((ROWS, LANES), jnp.float32)] * ribbon.shape[0]
    for q in range(strip_a.shape[0] // 2):
        first, second = pair_of(q, layers)
        halves = ([], [])
        for half in range(2):
            from_a, from_b = strip_a[2 * q + half], strip_b[2 * q + half]
            halves[0].append(below_and_above(from_a, from_b))
            halves[1].append(pltpu.roll(above_and_below(from_a, from_b), HALO, 0))
        for p, halo in zip((first, second), halves):
            v = plane(p)
            dst = target(p)
            dst[0:ROWS, :] = v
            dst[ROWS:, 0:LANES], dst[ROWS:, LANES:] = halo
            ribbon_of(p, layers, *halo, lane, strips)
    for tile, v in enumerate(strips):
        ribbon[tile] = v

    moves = Moves()
    load = Tiles.load
    e = load(eta_up.at[0])
    for k in range(layers):
        pair = e + moves.row_next(e)
        (2.0 * pair).store(eta_row.at[0, k])
        (0.5 * pair).store(eta_row.at[1, k])
        pair = e + moves.col_next(e)
        (0.5 * pair).store(eta_col.at[0, k])
        (2.0 * pair).store(eta_col.at[1, k])
        (0.5 * e).store(eta_half.at[k])
        after = load(eta_up.at[k + 1]) if k + 1 < layers else None
        (e + after if k + 1 < layers else 0.0 * e).store(eta_up.at[k])
        e = after

    def apply(t, src, dst):
        used = 4 if t < STEPS else 2

        def block(b, carry):
            g0, g1, below0, below1, odd, even = carry
            g0, g1, below0, below1 = Tiles(g0), Tiles(g1), Tiles(below0), Tiles(below1)
            odd, even = list(odd), list(even)
            m = load(cover)
            for i in range(UNROLL):
                k = b * UNROLL + i
                after = k + 1 if i + 1 < UNROLL else jnp.minimum(k + 1, layers - 1)
                next0, next1 = load(src.at[0, after]), load(src.at[1, after])
                e_up = Tiles(load(eta_up.at[k]).tiles[:used])
                up0, up1 = e_up * (g0 - next0), e_up * (g1 - next1)
                pairs = [load(ref.at[c, k]) for ref in (eta_row, eta_col) for c in range(2)]
                out0, out1 = horizontal(g0, g1, *pairs, load(eta_half.at[k]), moves)
                out0, out1 = m * (out0 + (up0 - below0)), m * (out1 + (up1 - below1))
                for c, g, out in ((0, g0, out0), (1, g1, out1)):
                    if t < STEPS:
                        out.store(dst.at[c, k])
                    for half in range(2):
                        now = out.tiles[half]
                        if t == STEPS:
                            dst[c, k, :, half * LANES : (half + 1) * LANES] = now
                        odd[half] = odd[half] + g.tiles[half] * now
                        even[half] = even[half] + now * now
                g0, g1, below0, below1 = next0, next1, up0, up1
            return g0.tiles, g1.tiles, below0.tiles, below1.tiles, odd, even

        zero = [jnp.zeros((ROWS, LANES), jnp.float32)] * 2
        d = -1.0 * load(drag)
        g0, g1 = load(src.at[0, 0]), load(src.at[1, 0])
        start = (g0.tiles, g1.tiles, (d * g0).tiles[:used], (d * g1).tiles[:used], zero, zero)
        ends = lax.fori_loop(0, layers // UNROLL, block, start)[4:]
        return [jnp.concatenate(v, 1) for v in ends]

    outside = squares[1]
    sums[0] = squares[0]
    wide = lax.broadcasted_iota(jnp.int32, (ROWS, 2 * LANES), 1)
    inner = between(wide, HALO, 2 * LANES - 2 * HALO)
    fields = (masked, power_1, power_2, power_3, power_4)
    for t in range(1, STEPS + 1):
        odd, even = apply(t, fields[t - 1], fields[t])
        sums[2 * t - 1] = jnp.where(inner, odd, 0.0) + outside
        sums[2 * t] = jnp.where(inner, even, 0.0) + outside


def ribbon_kernel(own, halo, columns, columns_a, columns_b, sums, edges, moments):
    tiles = edges.shape[2]
    below_and_above, _ = beyond()
    lane = lax.broadcasted_iota(jnp.int32, (2 * ROWS, LANES), 1)

    count = columns.shape[0] // 2
    beside = [
        jnp.concatenate([columns[i], below_and_above(columns_a[i], columns_b[i])], 0) for i in range(2 * count)
    ]
    spot = lane % SLOT

    def whole(tile):
        group, at = packed_place(tile)
        right = jnp.where(between(spot, 8, HALO), turned(beside[group], 8 - at), jnp.concatenate([own[tile], halo[tile]], 0))
        return jnp.where(between(spot, 16, HALO), turned(beside[count + group], 16 - at), right)

    field = [[whole(c * tiles + n) for n in range(tiles)] for c in range(2)]
    eta = [whole(2 * tiles + n) for n in range(tiles)]
    cover, drag = whole(3 * tiles), whole(3 * tiles + 1)

    def after(v):
        return v[1:] + [turned(v[0], -SLOT)]

    eta_row = [2.0 * (e + row_next(e)) for e in eta]
    eta_col = [0.5 * (e + col_next(e)) for e in eta]
    eta_row_1, eta_col_1 = [0.25 * e for e in eta_row], [4.0 * e for e in eta_col]
    eta_half = [0.5 * e for e in eta]
    eta_up = [e + n for e, n in zip(eta, after(eta))]
    eta_up[-1] = jnp.where(lane < LANES - SLOT, eta_up[-1], 0.0)
    place = lax.broadcasted_iota(jnp.int32, (ROWS, LANES), 1) % SLOT
    edge = between(place, 4, HALO) | between(place, 20, HALO)
    extra = [None]
    for t in range(1, STEPS + 1):
        ups = [[u * (g - n) for u, g, n in zip(eta_up, field[c], after(field[c]))] for c in range(2)]
        result = ([], [])
        odd = even = jnp.zeros((ROWS, LANES), jnp.float32)
        for n in range(tiles):
            coefficients = (eta_row[n], eta_row_1[n], eta_col[n], eta_col_1[n], eta_half[n])
            outs = horizontal(field[0][n], field[1][n], *coefficients, Turns)
            for c in range(2):
                below = ups[c][n - 1] if n else turned(ups[c][-1], SLOT) - drag * field[c][0]
                out = cover * (outs[c] + (ups[c][n] - below))
                result[c].append(out)
                now = out[:ROWS]
                edges[t - 1, c, n] = now
                odd = odd + field[c][n][:ROWS] * now
                even = even + now * now
        field = result
        extra.extend([jnp.where(edge, odd, 0.0), jnp.where(edge, even, 0.0)])

    tall = lax.broadcasted_iota(jnp.int32, (2 * ROWS, LANES), 0)
    high = jnp.zeros((2 * ROWS, LANES), jnp.float32)
    low = jnp.zeros((2 * ROWS, LANES), jnp.float32)
    for j, more in enumerate(extra):
        total = sums[j]
        pair = two_sum(total[:, :LANES], total[:, LANES:])
        if more is not None:
            pair = join(pair, (more, jnp.zeros_like(more)))
        for step in (4, 2, 1):
            pair = join(pair, tuple(pltpu.roll(v, step, 0) for v in pair))
        high = jnp.where(tall == j, jnp.concatenate([pair[0]] * 2, 0), high)
        low = jnp.where(tall == j, jnp.concatenate([pair[1]] * 2, 0), low)
    total = join((high, low), (pltpu.roll(high, 64, 1), pltpu.roll(low, 64, 1)))
    first = lax.broadcasted_iota(jnp.int32, (ROWS, LANES), 1) < 64
    for i, v in enumerate(total):
        moments[i] = jnp.where(first, v[:ROWS], v[ROWS:])


def added(terms):
    while len(terms) > 1:
        terms = [join(*terms[i : i + 2]) if i + 1 < len(terms) else terms[i] for i in range(0, len(terms), 2)]
    return terms[0]


def add_kernel(*refs):
    *ins, out = refs
    out[0], out[1] = added([(x[0], x[1]) for x in ins])


def solve(total):
    for unit in (8, 1):
        total = added([tuple(turned(v, unit * i) for v in total) for i in range(8)])

    def spread(j):
        row, lane = (j, 63) if j < ROWS else (j - ROWS, 127)
        return tuple(jnp.broadcast_to(v[row : row + 1, lane : lane + 1], (ROWS, LANES)) for v in total)

    table = [spread(j) for j in range(2 * STEPS + 1)]
    centre, _ = cut(table[1][0] / table[0][0], 13)
    mu = [sum(table[0])]
    while len(table) > 1:
        steps = [times(centre, x) for x in table[:-1]]
        table = [join(x, (-y[0], -y[1])) for x, y in zip(table[1:], steps)]
        mu.append(sum(table[0]))

    def plus(a, b):
        n = max(len(a), len(b))
        return [a[i] + b[i] if i < min(len(a), len(b)) else (a[i] if i < len(a) else b[i]) for i in range(n)]

    def scaled(s, a):
        return [s * x for x in a]

    def operator(a):
        return plus([centre * x for x in a], [jnp.zeros_like(centre)] + a)

    def dot(a, b):
        square = [None] * (len(a) + len(b) - 1)
        for i, x in enumerate(a):
            for j, y in enumerate(b):
                z = x * y
                square[i + j] = z if square[i + j] is None else square[i + j] + z
        value = square[0] * mu[0]
        for n in range(1, len(square)):
            value = value + square[n] * mu[n]
        return value

    one = jnp.ones_like(centre)
    right = [one]
    quasi, search, update, iterate = right, right, [], []
    applied = operator(search)
    carried = applied
    rho = mu[0]
    tau_sq = rho
    alpha = theta_sq = eta = None
    for half in range(STEPS):
        if half % 2 == 0:
            alpha = rho / dot(carried, right)
            search_next = plus(search, scaled(-alpha, carried))
        quasi = plus(quasi, scaled(-alpha, applied))
        if half:
            update = plus(search, scaled(theta_sq / alpha * eta, update))
        else:
            update = search
        theta_sq = dot(quasi, quasi) / tau_sq
        cosine_sq = 1.0 / (1.0 + theta_sq)
        tau_sq = tau_sq * theta_sq * cosine_sq
        eta = cosine_sq * alpha
        iterate = plus(iterate, scaled(eta, update))
        if half % 2 == 0:
            search = search_next
            applied = operator(search)
        elif half < STEPS - 1:
            rho_next = dot(quasi, right)
            beta = rho_next / rho
            search = plus(quasi, scaled(beta, search))
            applied_next = operator(search)
            carried = plus(applied_next, scaled(beta, plus(applied, scaled(beta, carried))))
            applied, rho = applied_next, rho_next
    powers = [iterate[-1]]
    for c in iterate[-2::-1]:
        powers = plus([c] + powers, scaled(-centre, powers))
    return powers


def patch_kernel(_, rhs, ice, power_1, power_2, power_3, power_4, edges, vectors):
    layers, tiles = rhs.shape[1], edges.shape[2]
    covered = ice[...] > 0
    lane = lax.broadcasted_iota(jnp.int32, (ROWS, LANES), 1)
    for t, power in enumerate((power_1, power_2, power_3, power_4)):
        for c in range(2):
            for k in range(layers):
                e, at = edges[t, c, k % tiles], k // tiles * SLOT
                v = power[c, k, :ROWS]
                head = jnp.where(lane < HALO, turned(e, -at - 20), v[:, :LANES])
                tail = jnp.where(lane >= LANES - HALO, turned(e, 120 - at), v[:, LANES:])
                vectors[t, c, k] = jnp.where(covered, jnp.concatenate([head, tail], 1), rhs[c, k])


def final_kernel(rhs, vectors, friction, ice, grounded, speed, *rest):
    *parts, iterate, residual, hessian = rest
    layers = rhs.shape[1]
    wide = [jnp.concatenate([c, c], 1) for c in solve(added([(x[0], x[1]) for x in parts]))]
    for c in range(2):
        for k in range(layers):
            r = rhs[c, k]
            x, y = wide[0] * r, r
            for t in range(STEPS):
                v = vectors[t, c, k]
                if t + 1 < STEPS:
                    x = x + wide[t + 1] * v
                y = y - wide[t] * v
            iterate[c, k] = x
            residual[c, k] = y
    weight = ice[...].astype(jnp.float32) * (friction[...] * grounded[...].astype(jnp.float32))
    hessian[...] = weight * (speed[0] * iterate[0, 0] + speed[1] * iterate[1, 0])


def exchange(x, axis, order):
    count = lax.axis_size(axis)
    stride = 1
    rounds = []
    while stride < count:
        size = 4 if (count // stride) % 4 == 0 else 2
        rounds.append((stride, size))
        stride *= size
    for at, (stride, size) in enumerate(rounds):
        parts = [x]
        for turn in order if size == 4 else (1,):
            pairs = []
            for i in range(count):
                place = (i // stride) % size
                pairs.append((i, i + ((place ^ turn) - place) * stride))
            parts.append(lax.ppermute(x, axis, pairs))
        if at == len(rounds) - 1:
            return parts
        x = call(add_kernel, [x.shape])(*parts)[0]
    return [x]


def body(adjoint_rhs, viscosity, friction, ice_mask, grounded, basal_velocity):
    layers = viscosity.shape[0]
    inputs = (adjoint_rhs, viscosity, friction, ice_mask, grounded, basal_velocity)
    tile = (ROWS, LANES)
    strips = (2 * (layers + layers // 2 + 1),) + tile
    ribbons = ribbon_tiles(layers)
    packed = ((ribbons + 7) // 8,) + tile
    both = (2 * packed[0],) + tile
    *held, strip_a, strip_b = call(
        strip_kernel,
        [jax.ShapeDtypeStruct(x.shape, x.dtype) for x in inputs] + [strips, strips],
        [pltpu.SemaphoreType.DMA((len(inputs),))],
        in_specs=[pl.BlockSpec(memory_space=pltpu.HBM)] * len(inputs),
    )(*[pltpu.with_memory_space_constraint(x, pltpu.HBM) for x in inputs])
    strip_b, strip_a = swapped(strip_b, ("gx",), 1, "gz"), swapped(strip_a, ("gx",), 0)
    column_a, column_b = call(column_kernel, [packed, packed])(*held[:5])
    beside = ("gy", "gz")
    (columns,) = call(beside_kernel, [both])(swapped(column_a, beside, 0), swapped(column_b, beside, 1))
    columns_a, columns_b = swapped(columns, ("gx",), 0), swapped(columns, ("gx",), 1, "gz")
    block = (layers, 2 * ROWS, 2 * LANES)
    own, squares = call(
        own_kernel,
        [(ribbons,) + tile, (2, ROWS, 2 * LANES)],
        in_specs=[pl.BlockSpec(memory_space=pl.ANY)] + [pl.BlockSpec(memory_space=pltpu.VMEM)] * 5,
    )(columns, *held[:5])
    *powers, sums, halo = call(
        main_kernel,
        [(2,) + block] * (STEPS - 1) + [adjoint_rhs.shape, (2 * STEPS + 1, ROWS, 2 * LANES), (ribbons,) + tile],
        [(2,) + block] * 3 + [block] * 2 + [block[1:]] * 2,
        cost_estimate=pl.CostEstimate(flops=200_000_000, bytes_accessed=8_000_000, transcendentals=0),
    )(*held[:5], squares, strip_b, strip_a)
    edges, sums = call(
        ribbon_kernel,
        [(STEPS, 2, layers // 4) + tile, (2,) + tile],
    )(own, halo, columns, columns_a, columns_b, sums)
    parts = exchange(sums, ("gy", "gz"), (1, 2, 3))
    if len(parts) > 1:
        sums = call(add_kernel, [sums.shape])(*parts)[0]
    parts = exchange(sums, "gx", (1, 3, 2))
    rhs, _, friction, ice_mask, grounded, speed = held
    (vectors,) = call(
        patch_kernel,
        [(STEPS,) + adjoint_rhs.shape],
        in_specs=[pl.BlockSpec(memory_space=pl.ANY)] + [pl.BlockSpec(memory_space=pltpu.VMEM)] * 7,
    )(sums, rhs, ice_mask, *powers, edges)
    return tuple(
        call(final_kernel, [adjoint_rhs.shape, adjoint_rhs.shape, friction.shape])(
            rhs, vectors, friction, ice_mask, grounded, speed, *parts
        )
    )


def solution(mesh):
    in_specs = (
        P(None, None, ("parts", "gx"), ("gy", "gz")),
        P(None, ("parts", "gx"), ("gy", "gz")),
        P(("parts", "gx"), ("gy", "gz")),
        P(("parts", "gx"), ("gy", "gz")),
        P(("parts", "gx"), ("gy", "gz")),
        P(None, ("parts", "gx"), ("gy", "gz")),
    )
    out_specs = (
        P(None, None, ("parts", "gx"), ("gy", "gz")),
        P(None, None, ("parts", "gx"), ("gy", "gz")),
        P(("parts", "gx"), ("gy", "gz")),
    )
    return jax.shard_map(body, mesh=mesh, in_specs=in_specs, out_specs=out_specs, check_vma=False)
```

```python
import functools

import jax
import jax.numpy as jnp
from jax import lax
from jax.experimental import pallas as pl
from jax.experimental.pallas import tpu as pltpu
from jax.sharding import PartitionSpec as P

STEPS = 4
HALO = 4
ROWS = 8
LANES = 128
UNROLL = 5
SLOT = 32


def call(kernel, outs, scratch=(), **more):
    return pl.pallas_call(
        kernel,
        out_shape=[jax.ShapeDtypeStruct(s, jnp.float32) if isinstance(s, tuple) else s for s in outs],
        scratch_shapes=[pltpu.VMEM(s, jnp.float32) if isinstance(s, tuple) else s for s in scratch],
        compiler_params=pltpu.CompilerParams(vmem_limit_bytes=40 * 1024 * 1024),
        **more,
    )


def place_of(axis):
    place, count = lax.axis_index(axis), lax.axis_size(axis)
    even = place % 2 == 0
    has_a = jnp.logical_or(jnp.logical_not(even), place < count - 1)
    has_b = jnp.where(even, place > 0, place < count - 1)
    return even, has_a, has_b


def swapped(x, axes, first, spare=None):
    count, others = lax.axis_size(axes), lax.axis_size(spare) if spare else 1
    pairs = []
    for at in range(others):
        for i in range(count):
            other, to = (i + 1 if (i - first) % 2 == 0 else i - 1), at
            if not 0 <= other < count:
                other, to = (i, at ^ 1) if spare else (count - 1 - i, at)
                if to >= others or count % 2:
                    other, to = i, at
            pairs.append((i * others + at, other * others + to))
    return lax.ppermute(x, (*axes, spare) if spare else axes, pairs)


def own_planes(rhs, eta, friction, ice, grounded):
    layers = eta.shape[0]
    cover = ice[...].astype(jnp.float32)
    drag = friction[...] * grounded[...].astype(jnp.float32)

    def plane(p):
        if p < 2 * layers:
            return rhs[p // layers, p % layers] * cover
        if p < 3 * layers:
            return eta[p - 2 * layers]
        return cover if p == 3 * layers else drag

    return plane


def pair_of(q, layers):
    if q < layers:
        return q, q + layers
    if q < layers + layers // 2:
        return q + layers, q + layers + layers // 2
    return 3 * layers, 3 * layers + 1


def ribbon_places(p, layers):
    tiles = layers // 4
    if p < 3 * layers:
        k = p % layers
        return p // layers * tiles + k % tiles, (k // tiles,)
    return (3 * tiles, (0, 1, 2, 3)) if p == 3 * layers else (3 * tiles + 1, (0,))


def ribbon_tiles(layers):
    return 3 * (layers // 4) + 2


def packed_place(tile):
    return tile // 8, HALO * (tile % 8)


def between(lane, first, width):
    return (lane >= first) & (lane < first + width)


def turned(v, shift):
    shift = shift % LANES
    return pltpu.roll(v, shift, 1) if shift else v


def strip_kernel(*refs):
    sources, held, (strip_a, strip_b, arrived) = refs[:6], refs[6:12], refs[12:]
    copies = [pltpu.make_async_copy(a, b, arrived.at[i]) for i, (a, b) in enumerate(zip(sources, held))]
    for copy in copies:
        copy.start()
    for copy in copies:
        copy.wait()
    rhs, eta, friction, ice, grounded, _ = held
    layers = eta.shape[0]
    plane = own_planes(rhs, eta, friction, ice, grounded)
    even, _, _ = place_of("gx")
    upper_a = (lax.broadcasted_iota(jnp.int32, (ROWS, LANES), 0) < HALO) != even
    for q in range(strip_a.shape[0] // 2):
        first, second = pair_of(q, layers)
        x, y = plane(first), plane(second)
        for half in range(2):
            xs = x[:, half * LANES : (half + 1) * LANES]
            ys = y[:, half * LANES : (half + 1) * LANES]
            ys = pltpu.roll(ys, HALO, 0)
            strip_a[2 * q + half] = jnp.where(upper_a, xs, ys)
            strip_b[2 * q + half] = jnp.where(upper_a, ys, xs)


def column_kernel(rhs, eta, friction, ice, grounded, column_a, column_b):
    layers = eta.shape[0]
    plane = own_planes(rhs, eta, friction, ice, grounded)
    lane = lax.broadcasted_iota(jnp.int32, (ROWS, LANES), 1)
    even, _, _ = place_of(("gy", "gz"))
    zero = jnp.zeros((ROWS, LANES), jnp.float32)
    to_left, to_right = [zero] * column_a.shape[0], [zero] * column_a.shape[0]
    for p in range(3 * layers + 2):
        v = plane(p)
        tile, slots = ribbon_places(p, layers)
        group, at = packed_place(tile)
        for slot in slots:
            here = between(lane, slot * SLOT + at, HALO)
            to_left[group] = jnp.where(here, turned(v[:, :LANES], slot * SLOT + at), to_left[group])
            to_right[group] = jnp.where(here, turned(v[:, LANES:], slot * SLOT + at + HALO), to_right[group])
    for group in range(column_a.shape[0]):
        column_a[group] = jnp.where(even, to_right[group], to_left[group])
        column_b[group] = jnp.where(even, to_left[group], to_right[group])


def beside_kernel(from_a, from_b, columns):
    even, has_a, has_b = place_of(("gy", "gz"))
    count = from_a.shape[0]
    for group in range(count):
        a = jnp.where(has_a, from_a[group], 0.0)
        b = jnp.where(has_b, from_b[group], 0.0)
        columns[group] = jnp.where(even, a, b)
        columns[count + group] = jnp.where(even, b, a)


def two_sum(a, b):
    s = a + b
    t = s - a
    return s, (a - (s - t)) + (b - t)


def join(x, y):
    s, e = two_sum(x[0], y[0])
    return s, e + (x[1] + y[1])


def cut(v, bits):
    t = v * (2.0**bits + 1.0)
    h = t - (t - v)
    return h, v - h


def times(scalar, x):
    high, low = cut(x[0], 12)
    return scalar * high, scalar * low + scalar * x[1]


def beyond():
    even, has_a, has_b = place_of("gx")
    upper_a = (lax.broadcasted_iota(jnp.int32, (ROWS, LANES), 0) < HALO) == even
    lower_a = jnp.logical_not(upper_a)

    def below_and_above(from_a, from_b):
        return jnp.where(upper_a & has_a, from_a, jnp.where(lower_a & has_b, from_b, 0.0))

    def above_and_below(from_a, from_b):
        return jnp.where(lower_a & has_a, from_a, jnp.where(upper_a & has_b, from_b, 0.0))

    return below_and_above, above_and_below


def row_next(v):
    return pltpu.roll(v, 2 * ROWS - 1, 0)


def row_prev(v):
    return pltpu.roll(v, 1, 0)


def col_next(v):
    return pltpu.roll(v, v.shape[1] - 1, 1)


def col_prev(v):
    return pltpu.roll(v, 1, 1)


def ribbon_of(p, layers, head, tail, lane, strips):
    tile, slots = ribbon_places(p, layers)
    for slot in slots:
        at = slot * SLOT
        strips[tile] = jnp.where(between(lane, at, 8), turned(tail, at + 8), strips[tile])
        strips[tile] = jnp.where(between(lane, at + 20, 8), turned(head, at + 20), strips[tile])


def own_kernel(_, rhs, eta, friction, ice, grounded, ribbon, squares):
    layers = eta.shape[0]
    plane = own_planes(rhs, eta, friction, ice, grounded)
    lane = lax.broadcasted_iota(jnp.int32, (ROWS, LANES), 1)
    strips = [jnp.zeros((ROWS, LANES), jnp.float32)] * ribbon.shape[0]
    for p in range(3 * layers + 2):
        v = plane(p)
        ribbon_of(p, layers, v[:, :LANES], v[:, LANES:], lane, strips)
    for tile, v in enumerate(strips):
        ribbon[tile] = v
    bare = 1.0 - ice[...].astype(jnp.float32)
    whole = jnp.zeros((ROWS, 2 * LANES), jnp.float32)
    outside = jnp.zeros((ROWS, 2 * LANES), jnp.float32)
    for c in range(2):
        for k in range(layers):
            square = rhs[c, k] * rhs[c, k]
            whole = whole + square
            outside = outside + bare * square
    squares[0], squares[1] = whole, outside


class Tiles:
    def __init__(self, tiles):
        self.tiles = tiles

    @staticmethod
    def load(ref):
        return Tiles([ref[r : r + ROWS, c : c + LANES] for r in (0, ROWS) for c in (0, LANES)])

    def store(self, ref):
        for v, (r, c) in zip(self.tiles, ((0, 0), (0, LANES), (ROWS, 0), (ROWS, LANES))):
            ref[r : r + ROWS, c : c + LANES] = v

    def both(self, other, op):
        if isinstance(other, Tiles):
            return Tiles([op(x, y) for x, y in zip(self.tiles, other.tiles)])
        return Tiles([op(x, other) for x in self.tiles])

    def __add__(self, other):
        return self.both(other, lambda x, y: x + y)

    def __sub__(self, other):
        return self.both(other, lambda x, y: x - y)

    def __mul__(self, other):
        return self.both(other, lambda x, y: x * y)

    __rmul__ = __mul__


class Moves:
    def __init__(self):
        row = lax.broadcasted_iota(jnp.int32, (ROWS, LANES), 0)
        lane = lax.broadcasted_iota(jnp.int32, (ROWS, LANES), 1)
        self.first_row, self.last_row = row == 0, row == ROWS - 1
        self.first_lane, self.last_lane = lane == 0, lane == LANES - 1

    def rows(self, v, shift, edge):
        own0, own1, halo0, halo1 = [pltpu.roll(x, shift, 0) for x in v.tiles]
        return Tiles(
            [
                jnp.where(edge, halo0, own0),
                jnp.where(edge, halo1, own1),
                jnp.where(edge, own0, halo0),
                jnp.where(edge, own1, halo1),
            ]
        )

    def row_next(self, v):
        return self.rows(v, ROWS - 1, self.last_row)

    def row_prev(self, v):
        return self.rows(v, 1, self.first_row)

    def col_next(self, v):
        own0, own1, halo0, halo1 = [pltpu.roll(x, LANES - 1, 1) for x in v.tiles]
        return Tiles([jnp.where(self.last_lane, own1, own0), own1, jnp.where(self.last_lane, halo1, halo0), halo1])

    def col_prev(self, v):
        own0, own1, halo0, halo1 = [pltpu.roll(x, 1, 1) for x in v.tiles]
        return Tiles([own0, jnp.where(self.first_lane, own0, own1), halo0, jnp.where(self.first_lane, halo0, halo1)])


class Turns:
    row_next = staticmethod(row_next)
    row_prev = staticmethod(row_prev)
    col_next = staticmethod(col_next)
    col_prev = staticmethod(col_prev)


def horizontal(g0, g1, e_row, e_row_1, e_col, e_col_1, e_half, moves):
    row_next, row_prev, col_next, col_prev = moves.row_next, moves.row_prev, moves.col_next, moves.col_prev
    g0n, g1n = row_next(g0), col_next(g1)
    f = e_half * (g1n - col_prev(g1))
    h = e_half * (g0n - row_prev(g0))
    flux = e_row * (g0 - g0n)
    out0 = flux - row_next(f) - row_prev(flux - f)
    flux = e_col * (g0 - col_next(g0))
    out0 = out0 + (flux - col_prev(flux))
    flux = e_col_1 * (g1 - g1n)
    out1 = flux - col_next(h) - col_prev(flux - h)
    flux = e_row_1 * (g1 - row_next(g1))
    out1 = out1 + (flux - row_prev(flux))
    return out0, out1


def main_kernel(
    rhs, eta, friction, ice, grounded, squares, strip_b, strip_a,
    power_1, power_2, power_3, power_4, sums, ribbon,
    masked, eta_row, eta_col, eta_half, eta_up, cover, drag,
):
    layers = eta.shape[0]
    plane = own_planes(rhs, eta, friction, ice, grounded)
    below_and_above, above_and_below = beyond()
    lane = lax.broadcasted_iota(jnp.int32, (ROWS, LANES), 1)

    def target(p):
        if p < 2 * layers:
            return masked.at[p // layers, p % layers]
        if p < 3 * layers:
            return eta_up.at[p - 2 * layers]
        return cover if p == 3 * layers else drag

    strips = [jnp.zeros((ROWS, LANES), jnp.float32)] * ribbon.shape[0]
    for q in range(strip_a.shape[0] // 2):
        first, second = pair_of(q, layers)
        halves = ([], [])
        for half in range(2):
            from_a, from_b = strip_a[2 * q + half], strip_b[2 * q + half]
            halves[0].append(below_and_above(from_a, from_b))
            halves[1].append(pltpu.roll(above_and_below(from_a, from_b), HALO, 0))
        for p, halo in zip((first, second), halves):
            v = plane(p)
            dst = target(p)
            dst[0:ROWS, :] = v
            dst[ROWS:, 0:LANES], dst[ROWS:, LANES:] = halo
            ribbon_of(p, layers, *halo, lane, strips)
    for tile, v in enumerate(strips):
        ribbon[tile] = v

    moves = Moves()
    load = Tiles.load
    e = load(eta_up.at[0])
    for k in range(layers):
        pair = e + moves.row_next(e)
        (2.0 * pair).store(eta_row.at[0, k])
        (0.5 * pair).store(eta_row.at[1, k])
        pair = e + moves.col_next(e)
        (0.5 * pair).store(eta_col.at[0, k])
        (2.0 * pair).store(eta_col.at[1, k])
        (0.5 * e).store(eta_half.at[k])
        after = load(eta_up.at[k + 1]) if k + 1 < layers else None
        (e + after if k + 1 < layers else 0.0 * e).store(eta_up.at[k])
        e = after

    def apply(t, src, dst):
        def block(b, carry):
            g0, g1, below0, below1, odd, even = carry
            g0, g1, below0, below1 = Tiles(g0), Tiles(g1), Tiles(below0), Tiles(below1)
            odd, even = list(odd), list(even)
            m = load(cover)
            for i in range(UNROLL):
                k = b * UNROLL + i
                after = k + 1 if i + 1 < UNROLL else jnp.minimum(k + 1, layers - 1)
                next0, next1 = load(src.at[0, after]), load(src.at[1, after])
                e_up = load(eta_up.at[k])
                up0, up1 = e_up * (g0 - next0), e_up * (g1 - next1)
                pairs = [load(ref.at[c, k]) for ref in (eta_row, eta_col) for c in range(2)]
                out0, out1 = horizontal(g0, g1, *pairs, load(eta_half.at[k]), moves)
                out0, out1 = m * (out0 + (up0 - below0)), m * (out1 + (up1 - below1))
                for c, g, out in ((0, g0, out0), (1, g1, out1)):
                    if t < STEPS:
                        out.store(dst.at[c, k])
                    for half in range(2):
                        now = out.tiles[half]
                        if t == STEPS:
                            dst[c, k, :, half * LANES : (half + 1) * LANES] = now
                        odd[half] = odd[half] + g.tiles[half] * now
                        even[half] = even[half] + now * now
                g0, g1, below0, below1 = next0, next1, up0, up1
            return g0.tiles, g1.tiles, below0.tiles, below1.tiles, odd, even

        zero = [jnp.zeros((ROWS, LANES), jnp.float32)] * 2
        d = -1.0 * load(drag)
        g0, g1 = load(src.at[0, 0]), load(src.at[1, 0])
        start = (g0.tiles, g1.tiles, (d * g0).tiles, (d * g1).tiles, zero, zero)
        ends = lax.fori_loop(0, layers // UNROLL, block, start)[4:]
        return [jnp.concatenate(v, 1) for v in ends]

    outside = squares[1]
    sums[0] = squares[0]
    wide = lax.broadcasted_iota(jnp.int32, (ROWS, 2 * LANES), 1)
    inner = between(wide, HALO, 2 * LANES - 2 * HALO)
    fields = (masked, power_1, power_2, power_3, power_4)
    for t in range(1, STEPS + 1):
        odd, even = apply(t, fields[t - 1], fields[t])
        sums[2 * t - 1] = jnp.where(inner, odd, 0.0) + outside
        sums[2 * t] = jnp.where(inner, even, 0.0) + outside


def ribbon_kernel(own, halo, columns, columns_a, columns_b, sums, edges, moments):
    tiles = edges.shape[2]
    below_and_above, _ = beyond()
    lane = lax.broadcasted_iota(jnp.int32, (2 * ROWS, LANES), 1)

    count = columns.shape[0] // 2
    beside = [
        jnp.concatenate([columns[i], below_and_above(columns_a[i], columns_b[i])], 0) for i in range(2 * count)
    ]
    spot = lane % SLOT

    def whole(tile):
        group, at = packed_place(tile)
        right = jnp.where(between(spot, 8, HALO), turned(beside[group], 8 - at), jnp.concatenate([own[tile], halo[tile]], 0))
        return jnp.where(between(spot, 16, HALO), turned(beside[count + group], 16 - at), right)

    field = [[whole(c * tiles + n) for n in range(tiles)] for c in range(2)]
    eta = [whole(2 * tiles + n) for n in range(tiles)]
    cover, drag = whole(3 * tiles), whole(3 * tiles + 1)

    def after(v):
        return v[1:] + [turned(v[0], -SLOT)]

    eta_row = [2.0 * (e + row_next(e)) for e in eta]
    eta_col = [0.5 * (e + col_next(e)) for e in eta]
    eta_row_1, eta_col_1 = [0.25 * e for e in eta_row], [4.0 * e for e in eta_col]
    eta_half = [0.5 * e for e in eta]
    eta_up = [e + n for e, n in zip(eta, after(eta))]
    eta_up[-1] = jnp.where(lane < LANES - SLOT, eta_up[-1], 0.0)
    place = lax.broadcasted_iota(jnp.int32, (ROWS, LANES), 1) % SLOT
    edge = between(place, 4, HALO) | between(place, 20, HALO)
    extra = [None]
    for t in range(1, STEPS + 1):
        ups = [[u * (g - n) for u, g, n in zip(eta_up, field[c], after(field[c]))] for c in range(2)]
        result = ([], [])
        odd = even = jnp.zeros((ROWS, LANES), jnp.float32)
        for n in range(tiles):
            coefficients = (eta_row[n], eta_row_1[n], eta_col[n], eta_col_1[n], eta_half[n])
            outs = horizontal(field[0][n], field[1][n], *coefficients, Turns)
            for c in range(2):
                below = ups[c][n - 1] if n else turned(ups[c][-1], SLOT) - drag * field[c][0]
                out = cover * (outs[c] + (ups[c][n] - below))
                result[c].append(out)
                now = out[:ROWS]
                edges[t - 1, c, n] = now
                odd = odd + field[c][n][:ROWS] * now
                even = even + now * now
        field = result
        extra.extend([jnp.where(edge, odd, 0.0), jnp.where(edge, even, 0.0)])

    tall = lax.broadcasted_iota(jnp.int32, (2 * ROWS, LANES), 0)
    high = jnp.zeros((2 * ROWS, LANES), jnp.float32)
    low = jnp.zeros((2 * ROWS, LANES), jnp.float32)
    for j, more in enumerate(extra):
        total = sums[j]
        pair = two_sum(total[:, :LANES], total[:, LANES:])
        if more is not None:
            pair = join(pair, (more, jnp.zeros_like(more)))
        pair = added([pair] + [tuple(pltpu.roll(v, step, 0) for v in pair) for step in (2, 4, 6)])
        pair = join(pair, tuple(pltpu.roll(v, 1, 0) for v in pair))
        high = jnp.where(tall == j, jnp.concatenate([pair[0]] * 2, 0), high)
        low = jnp.where(tall == j, jnp.concatenate([pair[1]] * 2, 0), low)
    total = join((high, low), (pltpu.roll(high, 64, 1), pltpu.roll(low, 64, 1)))
    first = lax.broadcasted_iota(jnp.int32, (ROWS, LANES), 1) < 64
    for i, v in enumerate(total):
        moments[i] = jnp.where(first, v[:ROWS], v[ROWS:])


def added(terms):
    while len(terms) > 1:
        terms = [join(*terms[i : i + 2]) if i + 1 < len(terms) else terms[i] for i in range(0, len(terms), 2)]
    return terms[0]


def add_kernel(*refs):
    *ins, out = refs
    out[0], out[1] = added([(x[0], x[1]) for x in ins])


def solve(total):
    for unit in (8, 1):
        total = added([tuple(turned(v, unit * i) for v in total) for i in range(8)])

    def spread(j):
        row, lane = (j, 63) if j < ROWS else (j - ROWS, 127)
        return tuple(jnp.broadcast_to(v[row : row + 1, lane : lane + 1], (ROWS, LANES)) for v in total)

    table = [spread(j) for j in range(2 * STEPS + 1)]
    centre, _ = cut(table[1][0] / table[0][0], 13)
    mu = [sum(table[0])]
    while len(table) > 1:
        steps = [times(centre, x) for x in table[:-1]]
        table = [join(x, (-y[0], -y[1])) for x, y in zip(table[1:], steps)]
        mu.append(sum(table[0]))

    def plus(a, b):
        n = max(len(a), len(b))
        return [a[i] + b[i] if i < min(len(a), len(b)) else (a[i] if i < len(a) else b[i]) for i in range(n)]

    def scaled(s, a):
        return [s * x for x in a]

    def operator(a):
        return plus([centre * x for x in a], [jnp.zeros_like(centre)] + a)

    def dot(a, b):
        square = [None] * (len(a) + len(b) - 1)
        for i, x in enumerate(a):
            for j, y in enumerate(b):
                z = x * y
                square[i + j] = z if square[i + j] is None else square[i + j] + z
        value = square[0] * mu[0]
        for n in range(1, len(square)):
            value = value + square[n] * mu[n]
        return value

    one = jnp.ones_like(centre)
    right = [one]
    quasi, search, update, iterate = right, right, [], []
    applied = operator(search)
    carried = applied
    rho = mu[0]
    tau_sq = rho
    alpha = theta_sq = eta = None
    for half in range(STEPS):
        if half % 2 == 0:
            alpha = rho / dot(carried, right)
            search_next = plus(search, scaled(-alpha, carried))
        quasi = plus(quasi, scaled(-alpha, applied))
        if half:
            update = plus(search, scaled(theta_sq / alpha * eta, update))
        else:
            update = search
        theta_sq = dot(quasi, quasi) / tau_sq
        cosine_sq = 1.0 / (1.0 + theta_sq)
        tau_sq = tau_sq * theta_sq * cosine_sq
        eta = cosine_sq * alpha
        iterate = plus(iterate, scaled(eta, update))
        if half % 2 == 0:
            search = search_next
            applied = operator(search)
        elif half < STEPS - 1:
            rho_next = dot(quasi, right)
            beta = rho_next / rho
            search = plus(quasi, scaled(beta, search))
            applied_next = operator(search)
            carried = plus(applied_next, scaled(beta, plus(applied, scaled(beta, carried))))
            applied, rho = applied_next, rho_next
    powers = [iterate[-1]]
    for c in iterate[-2::-1]:
        powers = plus([c] + powers, scaled(-centre, powers))
    return powers


def patch_kernel(_, rhs, ice, power_1, power_2, power_3, power_4, edges, vectors):
    layers, tiles = rhs.shape[1], edges.shape[2]
    covered = ice[...] > 0
    lane = lax.broadcasted_iota(jnp.int32, (ROWS, LANES), 1)
    for t, power in enumerate((power_1, power_2, power_3, power_4)):
        for c in range(2):
            for k in range(layers):
                e, at = edges[t, c, k % tiles], k // tiles * SLOT
                v = power[c, k, :ROWS]
                head = jnp.where(lane < HALO, turned(e, -at - 20), v[:, :LANES])
                tail = jnp.where(lane >= LANES - HALO, turned(e, 120 - at), v[:, LANES:])
                vectors[t, c, k] = jnp.where(covered, jnp.concatenate([head, tail], 1), rhs[c, k])


def final_kernel(rhs, vectors, friction, ice, grounded, speed, *rest):
    *parts, iterate, residual, hessian = rest
    layers = rhs.shape[1]
    wide = [jnp.concatenate([c, c], 1) for c in solve(added([(x[0], x[1]) for x in parts]))]
    for c in range(2):
        for k in range(layers):
            r = rhs[c, k]
            x, y = wide[0] * r, r
            for t in range(STEPS):
                v = vectors[t, c, k]
                if t + 1 < STEPS:
                    x = x + wide[t + 1] * v
                y = y - wide[t] * v
            iterate[c, k] = x
            residual[c, k] = y
    weight = ice[...].astype(jnp.float32) * (friction[...] * grounded[...].astype(jnp.float32))
    hessian[...] = weight * (speed[0] * iterate[0, 0] + speed[1] * iterate[1, 0])


def exchange(x, axis, order):
    count = lax.axis_size(axis)
    stride = 1
    rounds = []
    while stride < count:
        size = 4 if (count // stride) % 4 == 0 else 2
        rounds.append((stride, size))
        stride *= size
    for at, (stride, size) in enumerate(rounds):
        parts = [x]
        for turn in order if size == 4 else (1,):
            pairs = []
            for i in range(count):
                place = (i // stride) % size
                pairs.append((i, i + ((place ^ turn) - place) * stride))
            parts.append(lax.ppermute(x, axis, pairs))
        if at == len(rounds) - 1:
            return parts
        x = call(add_kernel, [x.shape])(*parts)[0]
    return [x]


def body(adjoint_rhs, viscosity, friction, ice_mask, grounded, basal_velocity):
    layers = viscosity.shape[0]
    inputs = (adjoint_rhs, viscosity, friction, ice_mask, grounded, basal_velocity)
    tile = (ROWS, LANES)
    strips = (2 * (layers + layers // 2 + 1),) + tile
    ribbons = ribbon_tiles(layers)
    packed = ((ribbons + 7) // 8,) + tile
    both = (2 * packed[0],) + tile
    *held, strip_a, strip_b = call(
        strip_kernel,
        [jax.ShapeDtypeStruct(x.shape, x.dtype) for x in inputs] + [strips, strips],
        [pltpu.SemaphoreType.DMA((len(inputs),))],
        in_specs=[pl.BlockSpec(memory_space=pltpu.HBM)] * len(inputs),
    )(*[pltpu.with_memory_space_constraint(x, pltpu.HBM) for x in inputs])
    strip_b, strip_a = swapped(strip_b, ("gx",), 1, "gz"), swapped(strip_a, ("gx",), 0)
    column_a, column_b = call(column_kernel, [packed, packed])(*held[:5])
    beside = ("gy", "gz")
    (columns,) = call(beside_kernel, [both])(swapped(column_a, beside, 0), swapped(column_b, beside, 1))
    columns_a, columns_b = swapped(columns, ("gx",), 0), swapped(columns, ("gx",), 1, "gz")
    block = (layers, 2 * ROWS, 2 * LANES)
    own, squares = call(
        own_kernel,
        [(ribbons,) + tile, (2, ROWS, 2 * LANES)],
        in_specs=[pl.BlockSpec(memory_space=pl.ANY)] + [pl.BlockSpec(memory_space=pltpu.VMEM)] * 5,
    )(columns, *held[:5])
    *powers, sums, halo = call(
        main_kernel,
        [(2,) + block] * (STEPS - 1) + [adjoint_rhs.shape, (2 * STEPS + 1, ROWS, 2 * LANES), (ribbons,) + tile],
        [(2,) + block] * 3 + [block] * 2 + [block[1:]] * 2,
        cost_estimate=pl.CostEstimate(flops=200_000_000, bytes_accessed=8_000_000, transcendentals=0),
    )(*held[:5], squares, strip_b, strip_a)
    edges, sums = call(
        ribbon_kernel,
        [(STEPS, 2, layers // 4) + tile, (2,) + tile],
    )(own, halo, columns, columns_a, columns_b, sums)
    parts = exchange(sums, ("gy", "gz"), (1, 2, 3))
    if len(parts) > 1:
        sums = call(add_kernel, [sums.shape])(*parts)[0]
    parts = exchange(sums, "gx", (1, 3, 2))
    rhs, _, friction, ice_mask, grounded, speed = held
    (vectors,) = call(
        patch_kernel,
        [(STEPS,) + adjoint_rhs.shape],
        in_specs=[pl.BlockSpec(memory_space=pl.ANY)] + [pl.BlockSpec(memory_space=pltpu.VMEM)] * 7,
    )(sums, rhs, ice_mask, *powers, edges)
    return tuple(
        call(final_kernel, [adjoint_rhs.shape, adjoint_rhs.shape, friction.shape])(
            rhs, vectors, friction, ice_mask, grounded, speed, *parts
        )
    )


def solution(mesh):
    in_specs = (
        P(None, None, ("parts", "gx"), ("gy", "gz")),
        P(None, ("parts", "gx"), ("gy", "gz")),
        P(("parts", "gx"), ("gy", "gz")),
        P(("parts", "gx"), ("gy", "gz")),
        P(("parts", "gx"), ("gy", "gz")),
        P(None, ("parts", "gx"), ("gy", "gz")),
    )
    out_specs = (
        P(None, None, ("parts", "gx"), ("gy", "gz")),
        P(None, None, ("parts", "gx"), ("gy", "gz")),
        P(("parts", "gx"), ("gy", "gz")),
    )
    return jax.shard_map(body, mesh=mesh, in_specs=in_specs, out_specs=out_specs, check_vma=False)
```
